32 devices in a mesh: wide: 16 (over z, x, core), narrow: 2 (over y).
Axes of the slice: x: 2, y: 2, z: 4, core: 2. Of those that a mesh axis runs over, the one named last changes fastest.
Arguments:
- matrix_slab: float32 [16, 262144], P(None, ('wide', 'narrow')), may hold values from -6 to 6
- row_signs: int32 [262144], P(('wide', 'narrow')), may hold values from -1 to 1, as said below
- sample_rows: int32 [32768], P(('wide', 'narrow')), may hold values from 0 to 7, as said below
Outputs:
- sketch: float32 [16, 32768], P(None, ('wide', 'narrow'))
- sketch_gram: float32 [16, 16], replicated
The draws below stay inside these ranges and needn't reach their ends.
Inputs may be any that keep to these rules, and one draw needn't show every extreme that they name: `row_signs`: each entry is +1 or -1. `sample_rows`: entry k is the offset of the k-th sampled row inside the run of 8 rows that starts at k * 8.
All inputs are finite; a program needn't handle non-finite values.
Results may differ from the reference program's by a relative error of at most 0.00013.
Values sent between devices are 32-bit elements; how exact they have to be, the bound alone decides.
No kernel may reach another device: no remote copies, remote signals or barrier semaphores. Data moves between devices by JAX's collectives and lax.ppermute only.
A program may use at most 64 MiB of HBM per device.

```python
import math
import jax
import jax.numpy as jnp
from jax import lax

COLS = 16
R_DEV = 8192
S_DEV = 1024
ROWS = 262144
SAMPLES = 32768


def draw_row_signs(key, part):
    picks = jax.random.randint(jax.random.fold_in(key, 11), (ROWS,), 0, 2)
    return (2 * picks - 1).astype(jnp.int32)


def draw_sample_rows(key, part):
    run_length = R_DEV // S_DEV
    offsets = jax.random.randint(jax.random.fold_in(key, 23), (SAMPLES,), 0, run_length)
    offsets = offsets.at[0].set(run_length - 1)
    offsets = offsets.at[1].set(0)
    return offsets.astype(jnp.int32)


def level_of(rng, shape, shards, least, high):
    factor_of, own = 1.0, jax.random.fold_in(rng, 6)
    for dim, shards_of in shards:
        steps = jnp.exp(jax.random.uniform(jax.random.fold_in(own, dim), (shards_of,), jnp.float32, least / len(shards), high / len(shards)))
        factor_of = factor_of * jnp.repeat(steps, shape[dim] // shards_of).reshape([-1 if axis == dim else 1 for axis in range(len(shape))])
    return factor_of


def centred(stream_key, extent, deviation, limit, cuts=(), kind=jnp.bfloat16):
    array = deviation * jax.random.normal(stream_key, extent, jnp.float32)
    if cuts:
        array = array * level_of(stream_key, extent, cuts, -0.22, 0.18)
    return jnp.clip(array, -limit, limit).astype(kind)


def setup_inputs(seed: int = 0) -> dict:
    seeds = jax.random.split(jax.random.key(seed), 4)
    return {
        "matrix_slab": centred(seeds[0], (COLS, ROWS), 1.0, 6.0, ((1, 32),), jnp.float32),
        "row_signs": draw_row_signs(jax.random.fold_in(seeds[3], 71), 0),
        "sample_rows": draw_sample_rows(jax.random.fold_in(seeds[3], 71), 0),
    }


def reference(matrix_slab, row_signs, sample_rows):
    values = matrix_slab * row_signs.astype(jnp.float32)[None, :]
    columns = values.shape[0]
    row_total = values.shape[1]
    stride_len = 1
    for section in range(row_total.bit_length() - 1):
        shaped = values.reshape(columns, row_total // (2 * stride_len), 2, stride_len)
        first_half = shaped[:, :, 0, :]
        second_half = shaped[:, :, 1, :]
        values = jnp.stack([first_half + second_half, first_half - second_half], axis=2).reshape(columns, row_total)
        stride_len = stride_len * 2
    values = values * jnp.float32(1.0 / math.sqrt(ROWS))
    run_length = R_DEV // S_DEV
    full_index = (jnp.arange(SAMPLES, dtype=jnp.int32) * run_length + sample_rows.astype(jnp.int32)).astype(jnp.int32)
    sketch = jnp.take(values, full_index, axis=1)
    sketch_gram = jnp.dot(sketch, sketch.T, precision=lax.Precision.HIGHEST, preferred_element_type=jnp.float32) / jnp.float32(SAMPLES)
    return (sketch, sketch_gram)
```

```python
import functools
import math

import jax
import jax.numpy as jnp
from jax import lax
from jax.experimental import pallas as pl
from jax.experimental.pallas import tpu as pltpu
from jax.sharding import PartitionSpec as P

LANES = 128
SUBLANES = 8
AXES = ("wide", "narrow")
VMEM_LIMIT = 32 * 1024 * 1024


def butterfly(values):
    values = list(values)
    apart = 1
    while apart < len(values):
        for low in range(len(values)):
            if not low & apart:
                first, second = values[low], values[low | apart]
                values[low], values[low | apart] = first + second, first - second
        apart *= 2
    return values


def sylvester(order_size):
    rows = lax.broadcasted_iota(jnp.int32, (order_size, order_size), 0)
    cols = lax.broadcasted_iota(jnp.int32, (order_size, order_size), 1)
    common = rows & cols
    parity = jnp.zeros_like(common)
    for bit_pos in range(order_size.bit_length() - 1):
        parity = parity ^ (common >> bit_pos)
    return (1 - 2 * (parity & 1)).astype(jnp.float32)


def split_dot(values, table):
    total = None
    for _ in range(3):
        part = values.astype(jnp.bfloat16)
        values = values - part.astype(jnp.float32)
        product = jnp.dot(part, table, preferred_element_type=jnp.float32)
        total = product if total is None else total + product
    return total


def local_kernel(x_ref, signs_ref, out_ref):
    blocks, columns, _ = out_ref.shape
    for block in range(blocks):
        signs = signs_ref[block : block + 1, :].astype(jnp.float32)
        out_ref[block] = x_ref[:, block * LANES : (block + 1) * LANES] * signs
    table = sylvester(LANES).astype(jnp.bfloat16)
    mixed = split_dot(out_ref[...].reshape(blocks * columns, LANES), table)
    out_ref[...] = mixed.reshape(blocks, columns, LANES)
    radix = 8
    apart = 1
    while apart < blocks:
        step = min(radix, blocks // apart)
        for start in range(blocks):
            if (start // apart) % step == 0:
                places = [start + apart * index for index in range(step)]
                for place, value in zip(places, butterfly([out_ref[p] for p in places])):
                    out_ref[place] = value
        apart *= step


def local_transform(matrix_slab, row_signs):
    columns, row_count = matrix_slab.shape
    blocks = row_count // LANES
    return pl.pallas_call(
        local_kernel,
        out_shape=jax.ShapeDtypeStruct((blocks, columns, LANES), jnp.float32),
        in_specs=[pl.BlockSpec(memory_space=pltpu.VMEM)] * 2,
        out_specs=pl.BlockSpec(memory_space=pltpu.VMEM),
        compiler_params=pltpu.CompilerParams(vmem_limit_bytes=VMEM_LIMIT),
    )(matrix_slab, row_signs.reshape(blocks, LANES))


def mix_kernel(run_length, scale, gram_scale, x_ref, samples_ref, out_ref):
    devices = x_ref.shape[0]
    runs = LANES // run_length
    samples = samples_ref[...].astype(jnp.float32).astype(jnp.bfloat16)
    run_of = lax.broadcasted_iota(jnp.int32, (2 * runs, 2 * LANES), 0)
    row_of = lax.broadcasted_iota(jnp.int32, (2 * runs, 2 * LANES), 1)
    spread = jnp.where(row_of // run_length == run_of, 1.0, 0.0).astype(jnp.bfloat16)
    offsets = jnp.dot(samples, spread, preferred_element_type=jnp.float32)
    own = lax.broadcasted_iota(jnp.int32, offsets.shape, 1) % run_length
    mask = jnp.where(offsets == own.astype(jnp.float32), scale, 0.0)
    picked = []
    for part in range(4):
        block = part // 2
        rows = [x_ref[s, part * SUBLANES : (part + 1) * SUBLANES, :] for s in range(devices)]
        mixed = butterfly(rows)
        picked.append(
            jnp.concatenate(
                [
                    mixed[d] * mask[d : d + 1, block * LANES : (block + 1) * LANES]
                    for d in range(devices)
                ],
                axis=0,
            )
        )
    quarter = 2 * runs
    row = lax.broadcasted_iota(jnp.int32, (4 * LANES, 2 * LANES), 0)
    lane = lax.broadcasted_iota(jnp.int32, (4 * LANES, 2 * LANES), 1)
    in_block, in_half = row // (2 * LANES), row // LANES % 2
    group = lane // quarter
    half_here = jnp.where(group >= 6, 7 - group, group % 2)
    target = in_block * runs + row % LANES // run_length
    place = jnp.where((half_here == in_half) & (lane % quarter == target), 1.0, 0.0)
    gathered = split_dot(jnp.concatenate(picked, axis=1), place.astype(jnp.bfloat16))
    straight, crossed = gathered[:, :LANES], gathered[:, LANES:]
    totals = []
    for turn in range(SUBLANES):
        total = None
        for d in range(devices):
            one = straight[d * SUBLANES : (d + 1) * SUBLANES]
            two = crossed[d * SUBLANES : (d + 1) * SUBLANES]
            if turn:
                two = pltpu.roll(two, SUBLANES - turn, 0)
            total = one * two if total is None else total + one * two
        totals.append(total)
    row = lax.broadcasted_iota(jnp.int32, (LANES, LANES), 0)
    lane = lax.broadcasted_iota(jnp.int32, (LANES, LANES), 1)
    together = jnp.where(row // quarter == lane // quarter, 1.0, 0.0).astype(jnp.bfloat16)
    sums = split_dot(jnp.concatenate(totals, axis=0), together) * gram_scale
    sub = lax.broadcasted_iota(jnp.int32, (SUBLANES, LANES), 0)
    lane = lax.broadcasted_iota(jnp.int32, (SUBLANES, LANES), 1)
    gram = jnp.zeros((SUBLANES, LANES), jnp.float32)
    for turn in range(SUBLANES):
        here = sums[turn * SUBLANES : (turn + 1) * SUBLANES]
        gram = jnp.where(lane % SUBLANES == (sub + turn) % SUBLANES, here, gram)
    moved = pltpu.roll(gram, LANES // 2, 1)
    same = (lane // SUBLANES % 2 == 0) == (lane < LANES * 3 // 4)
    gram = jnp.where(same, moved, gram)
    for d in range(devices):
        one = straight[d * SUBLANES : (d + 1) * SUBLANES]
        out_ref[d] = jnp.where(lane < LANES // 2, one, gram)


def mix_and_pick(received, samples, run_length, scale, gram_scale):
    devices = received.shape[0]
    return pl.pallas_call(
        functools.partial(mix_kernel, run_length, scale, gram_scale),
        out_shape=jax.ShapeDtypeStruct((devices, SUBLANES, LANES), jnp.float32),
        in_specs=[pl.BlockSpec(memory_space=pltpu.VMEM)] * 2,
        out_specs=pl.BlockSpec(memory_space=pltpu.VMEM),
        compiler_params=pltpu.CompilerParams(vmem_limit_bytes=VMEM_LIMIT),
    )(received, samples)


def finish_kernel(x_ref, sketch_ref, gram_ref):
    sources = x_ref.shape[0]
    quarter = LANES // 4
    lane = lax.broadcasted_iota(jnp.int32, (SUBLANES, LANES), 1)
    gram = None
    for start in range(0, sources, 4):
        halves = [None, None]
        for index in range(4):
            piece = x_ref[start + index]
            gram = piece if gram is None else gram + piece
            for half in range(2):
                shift = (index - half) % 4 * quarter
                moved = pltpu.roll(piece, shift, 1) if shift else piece
                if halves[half] is None:
                    halves[half] = moved
                else:
                    halves[half] = jnp.where(lane // quarter == index, moved, halves[half])
        for half in range(2):
            sketch_ref[
                half * SUBLANES : (half + 1) * SUBLANES, start * quarter : (start + 4) * quarter
            ] = halves[half]
    columns = gram_ref.shape[0]
    gram_ref[:SUBLANES, :] = pltpu.roll(gram, LANES // 2, 1)[:, :columns]
    gram_ref[SUBLANES:, :] = pltpu.roll(gram, LANES // 4, 1)[:, :columns]


def finish(received, columns, sample_count):
    return pl.pallas_call(
        finish_kernel,
        out_shape=(
            jax.ShapeDtypeStruct((columns, sample_count), jnp.float32),
            jax.ShapeDtypeStruct((columns, columns), jnp.float32),
        ),
        in_specs=[pl.BlockSpec(memory_space=pltpu.VMEM)],
        out_specs=(pl.BlockSpec(memory_space=pltpu.VMEM),) * 2,
        compiler_params=pltpu.CompilerParams(vmem_limit_bytes=VMEM_LIMIT),
    )(received)


def exchange(values):
    return lax.all_to_all(values, AXES, split_axis=0, concat_axis=0, tiled=True)


def general_shards(transformed, sample_rows, devices, run_length, scale, gram_scale):
    blocks, columns, _ = transformed.shape
    slice_rows = blocks * LANES // devices
    slice_runs = slice_rows // run_length
    values = jnp.swapaxes(transformed, 0, 1).reshape(columns, devices, slice_rows)
    received = exchange(jnp.swapaxes(values, 0, 1))
    offsets = exchange(sample_rows.reshape(devices, slice_runs))
    mixed = jnp.einsum("ds,scr->dcr", sylvester(devices), received, precision=lax.Precision.HIGHEST)
    mixed = mixed.reshape(devices, columns, slice_runs, run_length)
    chosen = offsets[:, None, :, None] == lax.iota(jnp.int32, run_length)
    picked = jnp.sum(jnp.where(chosen, mixed, 0.0), axis=3) * scale
    gram = jnp.einsum("dck,dek->ce", picked, picked, precision=lax.Precision.HIGHEST)
    grams = jnp.broadcast_to((gram * gram_scale)[None], (devices, columns, columns))
    back = exchange(jnp.concatenate([picked, grams], axis=2))
    sketch = jnp.swapaxes(back[:, :, :slice_runs], 0, 1).reshape(columns, devices * slice_runs)
    return sketch, jnp.sum(back[:, :, slice_runs:], axis=0)


def shards(matrix_slab, row_signs, sample_rows):
    columns, row_count = matrix_slab.shape
    sample_count = sample_rows.shape[0]
    devices = lax.axis_size("wide") * lax.axis_size("narrow")
    run_length = row_count // sample_count
    scale = 1.0 / math.sqrt(row_count * devices)
    gram_scale = 1.0 / (sample_count * devices)
    transformed = local_transform(matrix_slab, row_signs)
    if row_count != devices * 2 * LANES or columns != 2 * SUBLANES or run_length != SUBLANES:
        return general_shards(transformed, sample_rows, devices, run_length, scale, gram_scale)
    slice_runs = sample_count // devices
    everyone = lax.all_gather(sample_rows.reshape(devices, slice_runs), AXES)
    me = lax.axis_index(AXES)
    samples = lax.dynamic_index_in_dim(everyone, me, axis=1, keepdims=False)
    received = exchange(transformed.reshape(devices, 2 * columns, LANES))
    returned = exchange(mix_and_pick(received, samples, run_length, scale, gram_scale))
    return finish(returned, columns, sample_count)


def solution(mesh):
    in_specs = (P(None, AXES), P(AXES), P(AXES))
    out_specs = (P(None, AXES), P())
    return jax.shard_map(shards, mesh=mesh, in_specs=in_specs, out_specs=out_specs, check_vma=False)
```

```python
import functools
import math

import jax
import jax.numpy as jnp
from jax import lax
from jax.experimental import pallas as pl
from jax.experimental.pallas import tpu as pltpu
from jax.sharding import PartitionSpec as P

LANES = 128
SUBLANES = 8
AXES = ("wide", "narrow")
VMEM_LIMIT = 32 * 1024 * 1024


def butterfly(values):
    values = list(values)
    apart = 1
    while apart < len(values):
        for low in range(len(values)):
            if not low & apart:
                first, second = values[low], values[low | apart]
                values[low], values[low | apart] = first + second, first - second
        apart *= 2
    return values


def sylvester(order_size):
    rows = lax.broadcasted_iota(jnp.int32, (order_size, order_size), 0)
    cols = lax.broadcasted_iota(jnp.int32, (order_size, order_size), 1)
    common = rows & cols
    parity = jnp.zeros_like(common)
    for bit_pos in range(order_size.bit_length() - 1):
        parity = parity ^ (common >> bit_pos)
    return (1 - 2 * (parity & 1)).astype(jnp.float32)


def split_dot(values, table):
    total = None
    for _ in range(3):
        part = values.astype(jnp.bfloat16)
        values = values - part.astype(jnp.float32)
        product = jnp.dot(part, table, preferred_element_type=jnp.float32)
        total = product if total is None else total + product
    return total


def local_kernel(x_ref, signs_ref, samples_ref, final_ref, out_ref):
    blocks, columns, _ = out_ref.shape
    for block in range(blocks):
        signs = signs_ref[block : block + 1, :].astype(jnp.float32)
        out_ref[block] = x_ref[:, block * LANES : (block + 1) * LANES] * signs
    table = sylvester(LANES).astype(jnp.bfloat16)
    mixed = split_dot(out_ref[...].reshape(blocks * columns, LANES), table)
    out_ref[...] = mixed.reshape(blocks, columns, LANES)
    radix = 8
    apart = 1
    while apart < blocks:
        step = min(radix, blocks // apart)
        for start in range(blocks):
            if (start // apart) % step == 0:
                places = [start + apart * index for index in range(step)]
                for place, value in zip(places, butterfly([out_ref[p] for p in places])):
                    out_ref[place] = value
        apart *= step
    slices = final_ref.shape[0]
    rows = blocks * columns // slices
    runs = samples_ref.shape[0] * LANES // slices
    samples = samples_ref[...].astype(jnp.float32)
    per_row = LANES // runs
    for index in range(slices):
        final_ref[index, :rows] = out_ref[
            index * blocks // slices : (index + 1) * blocks // slices
        ].reshape(rows, LANES)
        if not per_row:
            own = samples[:1]
        else:
            own = samples[index // per_row : index // per_row + 1]
            if index % per_row:
                own = pltpu.roll(own, LANES - index % per_row * runs, 1)
        final_ref[index, rows:] = jnp.broadcast_to(own, (SUBLANES, LANES))


def local_transform(matrix_slab, row_signs, sample_rows, slices):
    columns, row_count = matrix_slab.shape
    blocks = row_count // LANES
    rows = blocks * columns // slices + SUBLANES
    return pl.pallas_call(
        local_kernel,
        out_shape=jax.ShapeDtypeStruct((slices, rows, LANES), jnp.float32),
        in_specs=[pl.BlockSpec(memory_space=pltpu.VMEM)] * 3,
        out_specs=pl.BlockSpec(memory_space=pltpu.VMEM),
        scratch_shapes=[pltpu.VMEM((blocks, columns, LANES), jnp.float32)],
        compiler_params=pltpu.CompilerParams(vmem_limit_bytes=VMEM_LIMIT),
    )(matrix_slab, row_signs.reshape(blocks, LANES), sample_rows.reshape(-1, LANES))


def mix_kernel(run_length, scale, gram_scale, x_ref, out_ref):
    devices = x_ref.shape[0]
    runs = LANES // run_length
    samples = jnp.concatenate(
        [x_ref[s, 4 * SUBLANES : 4 * SUBLANES + 1, :] for s in range(devices)], axis=0
    ).astype(jnp.bfloat16)
    run_of = lax.broadcasted_iota(jnp.int32, (LANES, 2 * LANES), 0)
    row_of = lax.broadcasted_iota(jnp.int32, (LANES, 2 * LANES), 1)
    spread = jnp.where(row_of // run_length == run_of, 1.0, 0.0).astype(jnp.bfloat16)
    offsets = jnp.dot(samples, spread, preferred_element_type=jnp.float32)
    own = lax.broadcasted_iota(jnp.int32, offsets.shape, 1) % run_length
    mask = jnp.where(offsets == own.astype(jnp.float32), scale, 0.0)
    picked = []
    for part in range(4):
        block = part // 2
        rows = [x_ref[s, part * SUBLANES : (part + 1) * SUBLANES, :] for s in range(devices)]
        mixed = butterfly(rows)
        picked.append(
            jnp.concatenate(
                [
                    mixed[d] * mask[d : d + 1, block * LANES : (block + 1) * LANES]
                    for d in range(devices)
                ],
                axis=0,
            )
        )
    quarter = 2 * runs
    row = lax.broadcasted_iota(jnp.int32, (4 * LANES, 2 * LANES), 0)
    lane = lax.broadcasted_iota(jnp.int32, (4 * LANES, 2 * LANES), 1)
    in_block, in_half = row // (2 * LANES), row // LANES % 2
    group = lane // quarter
    half_here = jnp.where(group >= 6, 7 - group, group % 2)
    target = in_block * runs + row % LANES // run_length
    place = jnp.where((half_here == in_half) & (lane % quarter == target), 1.0, 0.0)
    gathered = split_dot(jnp.concatenate(picked, axis=1), place.astype(jnp.bfloat16))
    straight, crossed = gathered[:, :LANES], gathered[:, LANES:]
    totals = []
    for turn in range(SUBLANES):
        total = None
        for d in range(devices):
            one = straight[d * SUBLANES : (d + 1) * SUBLANES]
            two = crossed[d * SUBLANES : (d + 1) * SUBLANES]
            if turn:
                two = pltpu.roll(two, SUBLANES - turn, 0)
            total = one * two if total is None else total + one * two
        totals.append(total)
    row = lax.broadcasted_iota(jnp.int32, (LANES, LANES), 0)
    lane = lax.broadcasted_iota(jnp.int32, (LANES, LANES), 1)
    together = jnp.where(row // quarter == lane // quarter, 1.0, 0.0).astype(jnp.bfloat16)
    sums = split_dot(jnp.concatenate(totals, axis=0), together) * gram_scale
    sub = lax.broadcasted_iota(jnp.int32, (SUBLANES, LANES), 0)
    lane = lax.broadcasted_iota(jnp.int32, (SUBLANES, LANES), 1)
    gram = jnp.zeros((SUBLANES, LANES), jnp.float32)
    for turn in range(SUBLANES):
        here = sums[turn * SUBLANES : (turn + 1) * SUBLANES]
        gram = jnp.where(lane % SUBLANES == (sub + turn) % SUBLANES, here, gram)
    moved = pltpu.roll(gram, LANES // 2, 1)
    same = (lane // SUBLANES % 2 == 0) == (lane < LANES * 3 // 4)
    gram = jnp.where(same, moved, gram)
    for d in range(devices):
        one = straight[d * SUBLANES : (d + 1) * SUBLANES]
        out_ref[d] = jnp.where(lane < LANES // 2, one, gram)


def mix_and_pick(received, run_length, scale, gram_scale):
    devices = received.shape[0]
    return pl.pallas_call(
        functools.partial(mix_kernel, run_length, scale, gram_scale),
        out_shape=jax.ShapeDtypeStruct((devices, SUBLANES, LANES), jnp.float32),
        in_specs=[pl.BlockSpec(memory_space=pltpu.VMEM)],
        out_specs=pl.BlockSpec(memory_space=pltpu.VMEM),
        compiler_params=pltpu.CompilerParams(vmem_limit_bytes=VMEM_LIMIT),
    )(received)


def finish_kernel(x_ref, sketch_ref, gram_ref):
    sources = x_ref.shape[0]
    quarter = LANES // 4
    lane = lax.broadcasted_iota(jnp.int32, (SUBLANES, LANES), 1)
    gram = None
    for start in range(0, sources, 4):
        halves = [None, None]
        for index in range(4):
            piece = x_ref[start + index]
            gram = piece if gram is None else gram + piece
            for half in range(2):
                shift = (index - half) % 4 * quarter
                moved = pltpu.roll(piece, shift, 1) if shift else piece
                if halves[half] is None:
                    halves[half] = moved
                else:
                    halves[half] = jnp.where(lane // quarter == index, moved, halves[half])
        for half in range(2):
            sketch_ref[
                half * SUBLANES : (half + 1) * SUBLANES, start * quarter : (start + 4) * quarter
            ] = halves[half]
    columns = gram_ref.shape[0]
    gram_ref[:SUBLANES, :] = pltpu.roll(gram, LANES // 2, 1)[:, :columns]
    gram_ref[SUBLANES:, :] = pltpu.roll(gram, LANES // 4, 1)[:, :columns]


def finish(received, columns, sample_count):
    return pl.pallas_call(
        finish_kernel,
        out_shape=(
            jax.ShapeDtypeStruct((columns, sample_count), jnp.float32),
            jax.ShapeDtypeStruct((columns, columns), jnp.float32),
        ),
        in_specs=[pl.BlockSpec(memory_space=pltpu.VMEM)],
        out_specs=(pl.BlockSpec(memory_space=pltpu.VMEM),) * 2,
        compiler_params=pltpu.CompilerParams(vmem_limit_bytes=VMEM_LIMIT),
    )(received)


def exchange(values):
    return lax.all_to_all(values, AXES, split_axis=0, concat_axis=0, tiled=True)


def general_shards(transformed, sample_rows, columns, devices, run_length, scale, gram_scale):
    rows = transformed.shape[1] - SUBLANES
    blocks = rows // columns
    slice_rows = blocks * LANES // devices
    slice_runs = slice_rows // run_length
    values = transformed[0, :rows].reshape(blocks, columns, LANES)
    values = jnp.swapaxes(values, 0, 1).reshape(columns, devices, slice_rows)
    received = exchange(jnp.swapaxes(values, 0, 1))
    offsets = exchange(sample_rows.reshape(devices, slice_runs))
    mixed = jnp.einsum("ds,scr->dcr", sylvester(devices), received, precision=lax.Precision.HIGHEST)
    mixed = mixed.reshape(devices, columns, slice_runs, run_length)
    chosen = offsets[:, None, :, None] == lax.iota(jnp.int32, run_length)
    picked = jnp.sum(jnp.where(chosen, mixed, 0.0), axis=3) * scale
    gram = jnp.einsum("dck,dek->ce", picked, picked, precision=lax.Precision.HIGHEST)
    grams = jnp.broadcast_to((gram * gram_scale)[None], (devices, columns, columns))
    back = exchange(jnp.concatenate([picked, grams], axis=2))
    sketch = jnp.swapaxes(back[:, :, :slice_runs], 0, 1).reshape(columns, devices * slice_runs)
    return sketch, jnp.sum(back[:, :, slice_runs:], axis=0)


def shards(matrix_slab, row_signs, sample_rows):
    columns, row_count = matrix_slab.shape
    sample_count = sample_rows.shape[0]
    devices = lax.axis_size("wide") * lax.axis_size("narrow")
    run_length = row_count // sample_count
    scale = 1.0 / math.sqrt(row_count * devices)
    gram_scale = 1.0 / (sample_count * devices)
    if row_count != devices * 2 * LANES or columns != 2 * SUBLANES or run_length != SUBLANES:
        transformed = local_transform(matrix_slab, row_signs, sample_rows, 1)
        return general_shards(
            transformed, sample_rows, columns, devices, run_length, scale, gram_scale
        )
    received = exchange(local_transform(matrix_slab, row_signs, sample_rows, devices))
    returned = exchange(mix_and_pick(received, run_length, scale, gram_scale))
    return finish(returned, columns, sample_count)


def solution(mesh):
    in_specs = (P(None, AXES), P(AXES), P(AXES))
    out_specs = (P(None, AXES), P())
    return jax.shard_map(shards, mesh=mesh, in_specs=in_specs, out_specs=out_specs, check_vma=False)
```

```python
import functools
import math

import jax
import jax.numpy as jnp
from jax import lax
from jax.experimental import pallas as pl
from jax.experimental.pallas import tpu as pltpu
from jax.sharding import PartitionSpec as P

LANES = 128
SUBLANES = 8
AXES = ("wide", "narrow")
VMEM_LIMIT = 32 * 1024 * 1024


def butterfly(values):
    values = list(values)
    apart = 1
    while apart < len(values):
        for low in range(len(values)):
            if not low & apart:
                first, second = values[low], values[low | apart]
                values[low], values[low | apart] = first + second, first - second
        apart *= 2
    return values


def sylvester(order_size):
    rows = lax.broadcasted_iota(jnp.int32, (order_size, order_size), 0)
    cols = lax.broadcasted_iota(jnp.int32, (order_size, order_size), 1)
    common = rows & cols
    parity = jnp.zeros_like(common)
    for bit_pos in range(order_size.bit_length() - 1):
        parity = parity ^ (common >> bit_pos)
    return (1 - 2 * (parity & 1)).astype(jnp.float32)


def split_dot(values, table, parts=3):
    total = None
    for _ in range(parts):
        part = values.astype(jnp.bfloat16)
        values = values - part.astype(jnp.float32)
        product = jnp.dot(part, table, preferred_element_type=jnp.float32)
        total = product if total is None else total + product
    return total


def mix_blocks(out_ref):
    blocks = out_ref.shape[0]
    radix = 8
    apart = 1
    while apart < blocks:
        step = min(radix, blocks // apart)
        for start in range(blocks):
            if (start // apart) % step == 0:
                places = [start + apart * index for index in range(step)]
                for place, value in zip(places, butterfly([out_ref[p] for p in places])):
                    out_ref[place] = value
        apart *= step


def local_kernel(x_ref, signs_ref, out_ref):
    blocks, columns, _ = out_ref.shape
    for block in range(blocks):
        signs = signs_ref[block : block + 1, :].astype(jnp.float32)
        out_ref[block] = x_ref[:, block * LANES : (block + 1) * LANES] * signs
    table = sylvester(LANES).astype(jnp.bfloat16)
    mixed = split_dot(out_ref[...].reshape(blocks * columns, LANES), table)
    out_ref[...] = mixed.reshape(blocks, columns, LANES)
    mix_blocks(out_ref)


def sliced_kernel(x_ref, signs_ref, own_ref, other_ref, final_ref, out_ref):
    local_kernel(x_ref, signs_ref, out_ref)
    blocks, columns, _ = out_ref.shape
    slices = final_ref.shape[0]
    rows = blocks * columns // slices
    share = blocks // slices
    high = lax.axis_index("high")
    own, other = own_ref[...].astype(jnp.float32), other_ref[...].astype(jnp.float32)
    first, second = jnp.where(high == 0, own, other), jnp.where(high == 0, other, own)
    lane = lax.broadcasted_iota(jnp.int32, first.shape, 1)
    turned_first, turned_second = pltpu.roll(first, LANES // 2, 1), pltpu.roll(second, LANES // 2, 1)
    offsets = [
        jnp.where(lane < LANES // 2, first, turned_second),
        jnp.where(lane < LANES // 2, turned_first, second),
    ]
    for index in range(slices):
        final_ref[index, :rows] = out_ref[index * share : (index + 1) * share].reshape(rows, LANES)
        tail = offsets[index % 2][index // 2 : index // 2 + 1]
        final_ref[index, rows:] = jnp.broadcast_to(tail, (SUBLANES, LANES))


def in_vmem(count):
    return [pl.BlockSpec(memory_space=pltpu.VMEM)] * count


def local_transform(matrix_slab, row_signs):
    columns, row_count = matrix_slab.shape
    blocks = row_count // LANES
    return pl.pallas_call(
        local_kernel,
        out_shape=jax.ShapeDtypeStruct((blocks, columns, LANES), jnp.float32),
        in_specs=in_vmem(2),
        out_specs=in_vmem(1)[0],
        compiler_params=pltpu.CompilerParams(vmem_limit_bytes=VMEM_LIMIT),
    )(matrix_slab, row_signs.reshape(blocks, LANES))


def sliced_transform(matrix_slab, row_signs, own_samples, other_samples, slices):
    columns, row_count = matrix_slab.shape
    blocks = row_count // LANES
    rows = blocks * columns // slices + SUBLANES
    return pl.pallas_call(
        sliced_kernel,
        out_shape=jax.ShapeDtypeStruct((slices, rows, LANES), jnp.float32),
        in_specs=in_vmem(4),
        out_specs=in_vmem(1)[0],
        scratch_shapes=[pltpu.VMEM((blocks, columns, LANES), jnp.float32)],
        compiler_params=pltpu.CompilerParams(vmem_limit_bytes=VMEM_LIMIT),
    )(
        matrix_slab,
        row_signs.reshape(blocks, LANES),
        own_samples.reshape(-1, LANES),
        other_samples.reshape(-1, LANES),
    )


def pick_kernel(run_length, scale, x_ref, keep_ref, send_ref):
    sources = x_ref.shape[0]
    parts = x_ref.shape[1] // SUBLANES - 1
    high = lax.axis_index("high")
    runs = parts * LANES // 2 // run_length
    samples = jnp.concatenate(
        [x_ref[s, parts * SUBLANES : parts * SUBLANES + 1, :] for s in range(sources)], axis=0
    ).astype(jnp.bfloat16)
    width = parts * LANES
    row = lax.broadcasted_iota(jnp.int32, (2 * runs, width), 0)
    lane = lax.broadcasted_iota(jnp.int32, (2 * runs, width), 1)
    spread = jnp.where(lane // run_length == row, 1.0, 0.0).astype(jnp.bfloat16)
    offsets = jnp.dot(samples, spread, preferred_element_type=jnp.float32)
    lane = lax.broadcasted_iota(jnp.int32, offsets.shape, 1)
    signed = jnp.where((lane >= width // 2) & (high == 1), -scale, scale)
    mask = jnp.where(offsets == (lane % run_length).astype(jnp.float32), signed, 0.0)
    picked = {}
    for part in range(parts):
        block, upper = part // 2, part % 2
        mixed = butterfly(
            [x_ref[s, part * SUBLANES : (part + 1) * SUBLANES, :] for s in range(sources)]
        )
        for half in range(2):
            start = half * width // 2 + block * LANES
            picked[block // 2, half, upper, block % 2] = jnp.concatenate(
                [mixed[e] * mask[e : e + 1, start : start + LANES] for e in range(sources)], axis=0
            )
    both = jnp.concatenate(
        [
            jnp.concatenate(
                [picked[b, h, u, low] for h in range(2) for u in range(2) for low in range(2)],
                axis=1,
            )
            for b in range(2)
        ],
        axis=0,
    )
    row = lax.broadcasted_iota(jnp.int32, (SUBLANES * LANES, LANES), 0)
    lane = lax.broadcasted_iota(jnp.int32, (SUBLANES * LANES, LANES), 1)
    place = jnp.where(row // run_length == lane, 1.0, 0.0).astype(jnp.bfloat16)
    gathered = split_dot(both, place, 2)
    lower, upper = gathered[: sources * SUBLANES], gathered[sources * SUBLANES :]
    shape = keep_ref.shape
    keep_ref[...] = jnp.where(high == 0, lower, upper).reshape(shape)
    send_ref[...] = jnp.where(high == 0, upper, lower).reshape(shape)


def pick(received, run_length, scale):
    shape = jax.ShapeDtypeStruct((received.shape[0], SUBLANES, LANES), jnp.float32)
    return pl.pallas_call(
        functools.partial(pick_kernel, run_length, scale),
        out_shape=(shape, shape),
        in_specs=in_vmem(1),
        out_specs=tuple(in_vmem(2)),
        compiler_params=pltpu.CompilerParams(vmem_limit_bytes=VMEM_LIMIT),
    )(received)


def gram_kernel(gram_scale, keep_ref, other_ref, out_ref):
    owners = keep_ref.shape[0]
    quarter = LANES // 4
    values = [keep_ref[e] + other_ref[e] for e in range(owners)]
    sub = lax.broadcasted_iota(jnp.int32, (SUBLANES, LANES), 0)
    lane = lax.broadcasted_iota(jnp.int32, (SUBLANES, LANES), 1)
    even = lane // quarter % 2 == 0
    crossed = [
        jnp.where(even, pltpu.roll(v, LANES - quarter, 1), pltpu.roll(v, quarter, 1)) for v in values
    ]
    totals = []
    for others in (values, crossed):
        for turn in range(SUBLANES):
            total = None
            for one, two in zip(values, others):
                product = one * (pltpu.roll(two, SUBLANES - turn, 0) if turn else two)
                total = product if total is None else total + product
            totals.append(total)
    row = lax.broadcasted_iota(jnp.int32, (LANES, LANES), 0)
    column = lax.broadcasted_iota(jnp.int32, (LANES, LANES), 1)
    together = jnp.where(row // quarter % 2 == column // quarter % 2, 1.0, 0.0)
    sums = split_dot(jnp.concatenate(totals, axis=0), together.astype(jnp.bfloat16)) * gram_scale
    same = (lane // SUBLANES % 2 == 0) == even
    gram = jnp.zeros((SUBLANES, LANES), jnp.float32)
    for turn in range(SUBLANES):
        straight = sums[turn * SUBLANES : (turn + 1) * SUBLANES]
        across = sums[(SUBLANES + turn) * SUBLANES : (SUBLANES + turn + 1) * SUBLANES]
        here = jnp.where(same, straight, across)
        gram = jnp.where(lane % SUBLANES == (sub + turn) % SUBLANES, here, gram)
    for e, value in enumerate(values):
        out_ref[e] = jnp.where(lane < LANES // 2, value, gram)
        out_ref[owners + e] = jnp.where(lane < LANES // 2, pltpu.roll(value, LANES // 2, 1), gram)


def join(keep, other, gram_scale):
    owners = keep.shape[0]
    return pl.pallas_call(
        functools.partial(gram_kernel, gram_scale),
        out_shape=jax.ShapeDtypeStruct((2 * owners, SUBLANES, LANES), jnp.float32),
        in_specs=in_vmem(2),
        out_specs=in_vmem(1)[0],
        compiler_params=pltpu.CompilerParams(vmem_limit_bytes=VMEM_LIMIT),
    )(keep, other)


def finish_kernel(x_ref, sketch_ref, gram_ref):
    sources = x_ref.shape[0]
    quarter = LANES // 4
    lane = lax.broadcasted_iota(jnp.int32, (SUBLANES, LANES), 1)
    gram = None
    for start in range(0, sources, 4):
        halves = [None, None]
        for index in range(4):
            place = start + index
            piece = x_ref[place % 2 * (sources // 2) + place // 2]
            gram = piece if gram is None else gram + piece
            for half in range(2):
                shift = (index - half) % 4 * quarter
                moved = pltpu.roll(piece, shift, 1) if shift else piece
                if halves[half] is None:
                    halves[half] = moved
                else:
                    halves[half] = jnp.where(lane // quarter == index, moved, halves[half])
        for half in range(2):
            sketch_ref[
                half * SUBLANES : (half + 1) * SUBLANES, start * quarter : (start + 4) * quarter
            ] = halves[half]
    columns = gram_ref.shape[0]
    gram_ref[:SUBLANES, :] = pltpu.roll(gram, LANES // 2, 1)[:, :columns]
    gram_ref[SUBLANES:, :] = pltpu.roll(gram, LANES // 4, 1)[:, :columns]


def finish(received, columns, sample_count):
    return pl.pallas_call(
        finish_kernel,
        out_shape=(
            jax.ShapeDtypeStruct((columns, sample_count), jnp.float32),
            jax.ShapeDtypeStruct((columns, columns), jnp.float32),
        ),
        in_specs=in_vmem(1),
        out_specs=tuple(in_vmem(2)),
        compiler_params=pltpu.CompilerParams(vmem_limit_bytes=VMEM_LIMIT),
    )(received)


def exchange(values, axes):
    return lax.all_to_all(values, axes, split_axis=0, concat_axis=0, tiled=True)


def general_shards(matrix_slab, row_signs, sample_rows):
    columns, row_count = matrix_slab.shape
    sample_count = sample_rows.shape[0]
    devices = lax.axis_size("wide") * lax.axis_size("narrow")
    run_length = row_count // sample_count
    slice_rows = row_count // devices
    slice_runs = slice_rows // run_length
    values = jnp.swapaxes(local_transform(matrix_slab, row_signs), 0, 1)
    values = values.reshape(columns, devices, slice_rows)
    received = exchange(jnp.swapaxes(values, 0, 1), AXES)
    offsets = exchange(sample_rows.reshape(devices, slice_runs), AXES)
    mixed = jnp.einsum("ds,scr->dcr", sylvester(devices), received, precision=lax.Precision.HIGHEST)
    mixed = mixed.reshape(devices, columns, slice_runs, run_length)
    chosen = offsets[:, None, :, None] == lax.iota(jnp.int32, run_length)
    picked = jnp.sum(jnp.where(chosen, mixed, 0.0), axis=3)
    picked = picked * jnp.float32(1.0 / math.sqrt(row_count * devices))
    gram = jnp.einsum("dck,dek->ce", picked, picked, precision=lax.Precision.HIGHEST)
    gram = gram / jnp.float32(sample_count * devices)
    grams = jnp.broadcast_to(gram[None], (devices, columns, columns))
    back = exchange(jnp.concatenate([picked, grams], axis=2), AXES)
    sketch = jnp.swapaxes(back[:, :, :slice_runs], 0, 1).reshape(columns, devices * slice_runs)
    return sketch, jnp.sum(back[:, :, slice_runs:], axis=0)


def halved_shards(matrix_slab, row_signs, sample_rows):
    columns, row_count = matrix_slab.shape
    sample_count = sample_rows.shape[0]
    sources = lax.axis_size("mid") * lax.axis_size("narrow")
    devices = 2 * sources
    run_length = row_count // sample_count
    swap = [(0, 1), (1, 0)]
    other_samples = lax.ppermute(sample_rows, "high", swap)
    sliced = sliced_transform(matrix_slab, row_signs, sample_rows, other_samples, sources)
    received = exchange(sliced, ("mid", "narrow"))
    keep, send = pick(received, run_length, 1.0 / math.sqrt(row_count * devices))
    joined = join(keep, lax.ppermute(send, "high", swap), 1.0 / (sample_count * devices))
    return finish(exchange(joined, ("high", "mid", "narrow")), columns, sample_count)


def solution(mesh):
    wide, narrow = mesh.shape["wide"], mesh.shape["narrow"]
    axes, function = AXES, general_shards
    if wide * narrow == 32 and wide > 1:
        axes, function = ("high", "mid", "narrow"), halved_shards
        mesh = jax.sharding.Mesh(mesh.devices.reshape(2, wide // 2, narrow), axes)
    in_specs = (P(None, axes), P(axes), P(axes))
    out_specs = (P(None, axes), P())
    return jax.shard_map(function, mesh=mesh, in_specs=in_specs, out_specs=out_specs, check_vma=False)
```

```python
import functools
import math

import jax
import jax.numpy as jnp
from jax import lax
from jax.experimental import pallas as pl
from jax.experimental.pallas import tpu as pltpu
from jax.sharding import PartitionSpec as P

LANES = 128
SUBLANES = 8
AXES = ("wide", "narrow")
VMEM_LIMIT = 32 * 1024 * 1024


def butterfly(values):
    values = list(values)
    apart = 1
    while apart < len(values):
        for low in range(len(values)):
            if not low & apart:
                first, second = values[low], values[low | apart]
                values[low], values[low | apart] = first + second, first - second
        apart *= 2
    return values


def sylvester(order_size):
    rows = lax.broadcasted_iota(jnp.int32, (order_size, order_size), 0)
    cols = lax.broadcasted_iota(jnp.int32, (order_size, order_size), 1)
    common = rows & cols
    parity = jnp.zeros_like(common)
    for bit_pos in range(order_size.bit_length() - 1):
        parity = parity ^ (common >> bit_pos)
    return (1 - 2 * (parity & 1)).astype(jnp.float32)


def split_dot(values, table, parts=3):
    total = None
    for _ in range(parts):
        part = values.astype(jnp.bfloat16)
        values = values - part.astype(jnp.float32)
        product = jnp.dot(part, table, preferred_element_type=jnp.float32)
        total = product if total is None else total + product
    return total


def mix_blocks(out_ref):
    blocks = out_ref.shape[0]
    radix = 8
    apart = 1
    while apart < blocks:
        step = min(radix, blocks // apart)
        for start in range(blocks):
            if (start // apart) % step == 0:
                places = [start + apart * index for index in range(step)]
                for place, value in zip(places, butterfly([out_ref[p] for p in places])):
                    out_ref[place] = value
        apart *= step


def local_kernel(x_hbm, signs_hbm, out_ref, x_ref, signs_ref, arrived):
    fetches = [
        pltpu.make_async_copy(x_hbm, x_ref, arrived.at[0]),
        pltpu.make_async_copy(signs_hbm, signs_ref, arrived.at[1]),
    ]
    for fetch in fetches:
        fetch.start()
    blocks, columns, _ = out_ref.shape
    table = sylvester(LANES).astype(jnp.bfloat16)
    for fetch in fetches:
        fetch.wait()
    for block in range(blocks):
        signs = signs_ref[block : block + 1, :].astype(jnp.float32)
        out_ref[block] = x_ref[:, block * LANES : (block + 1) * LANES] * signs
    mixed = split_dot(out_ref[...].reshape(blocks * columns, LANES), table)
    out_ref[...] = mixed.reshape(blocks, columns, LANES)
    mix_blocks(out_ref)


def in_vmem(count):
    return [pl.BlockSpec(memory_space=pltpu.VMEM)] * count


def local_transform(matrix_slab, row_signs):
    columns, row_count = matrix_slab.shape
    blocks = row_count // LANES
    return pl.pallas_call(
        local_kernel,
        out_shape=jax.ShapeDtypeStruct((blocks, columns, LANES), jnp.float32),
        in_specs=[pl.BlockSpec(memory_space=pltpu.HBM)] * 2,
        out_specs=in_vmem(1)[0],
        scratch_shapes=[
            pltpu.VMEM(matrix_slab.shape, jnp.float32),
            pltpu.VMEM((blocks, LANES), jnp.int32),
            pltpu.SemaphoreType.DMA((2,)),
        ],
        compiler_params=pltpu.CompilerParams(vmem_limit_bytes=VMEM_LIMIT),
    )(matrix_slab, row_signs.reshape(blocks, LANES))


def mix_kernel(run_length, scale, gram_scale, x_ref, samples_ref, out_ref):
    devices = x_ref.shape[0]
    runs = LANES // run_length
    samples = samples_ref[...].astype(jnp.float32).astype(jnp.bfloat16)
    run_of = lax.broadcasted_iota(jnp.int32, (2 * runs, 2 * LANES), 0)
    row_of = lax.broadcasted_iota(jnp.int32, (2 * runs, 2 * LANES), 1)
    spread = jnp.where(row_of // run_length == run_of, 1.0, 0.0).astype(jnp.bfloat16)
    offsets = jnp.dot(samples, spread, preferred_element_type=jnp.float32)
    own = lax.broadcasted_iota(jnp.int32, offsets.shape, 1) % run_length
    mask = jnp.where(offsets == own.astype(jnp.float32), scale, 0.0)
    picked = []
    for part in range(4):
        block = part // 2
        rows = [x_ref[s, part * SUBLANES : (part + 1) * SUBLANES, :] for s in range(devices)]
        mixed = butterfly(rows)
        picked.append(
            jnp.concatenate(
                [
                    mixed[d] * mask[d : d + 1, block * LANES : (block + 1) * LANES]
                    for d in range(devices)
                ],
                axis=0,
            )
        )
    quarter = 2 * runs
    row = lax.broadcasted_iota(jnp.int32, (4 * LANES, 2 * LANES), 0)
    lane = lax.broadcasted_iota(jnp.int32, (4 * LANES, 2 * LANES), 1)
    in_block, in_half = row // (2 * LANES), row // LANES % 2
    group = lane // quarter
    half_here = jnp.where(group >= 6, 7 - group, group % 2)
    target = in_block * runs + row % LANES // run_length
    place = jnp.where((half_here == in_half) & (lane % quarter == target), 1.0, 0.0)
    gathered = split_dot(jnp.concatenate(picked, axis=1), place.astype(jnp.bfloat16), 2)
    straight, crossed = gathered[:, :LANES], gathered[:, LANES:]
    totals = []
    for turn in range(SUBLANES):
        total = None
        for d in range(devices):
            one = straight[d * SUBLANES : (d + 1) * SUBLANES]
            two = crossed[d * SUBLANES : (d + 1) * SUBLANES]
            if turn:
                two = pltpu.roll(two, SUBLANES - turn, 0)
            total = one * two if total is None else total + one * two
        totals.append(total)
    row = lax.broadcasted_iota(jnp.int32, (LANES, LANES), 0)
    lane = lax.broadcasted_iota(jnp.int32, (LANES, LANES), 1)
    together = jnp.where(row // quarter == lane // quarter, 1.0, 0.0).astype(jnp.bfloat16)
    sums = split_dot(jnp.concatenate(totals, axis=0), together) * gram_scale
    sub = lax.broadcasted_iota(jnp.int32, (SUBLANES, LANES), 0)
    lane = lax.broadcasted_iota(jnp.int32, (SUBLANES, LANES), 1)
    gram = jnp.zeros((SUBLANES, LANES), jnp.float32)
    for turn in range(SUBLANES):
        here = sums[turn * SUBLANES : (turn + 1) * SUBLANES]
        gram = jnp.where(lane % SUBLANES == (sub + turn) % SUBLANES, here, gram)
    moved = pltpu.roll(gram, LANES // 2, 1)
    same = (lane // SUBLANES % 2 == 0) == (lane < LANES * 3 // 4)
    gram = jnp.where(same, moved, gram)
    for d in range(devices):
        one = straight[d * SUBLANES : (d + 1) * SUBLANES]
        out_ref[d] = jnp.where(lane < LANES // 2, one, gram)


def mix_and_pick(received, samples, run_length, scale, gram_scale):
    devices = received.shape[0]
    return pl.pallas_call(
        functools.partial(mix_kernel, run_length, scale, gram_scale),
        out_shape=jax.ShapeDtypeStruct((devices, SUBLANES, LANES), jnp.float32),
        in_specs=[pl.BlockSpec(memory_space=pltpu.VMEM)] * 2,
        out_specs=pl.BlockSpec(memory_space=pltpu.VMEM),
        compiler_params=pltpu.CompilerParams(vmem_limit_bytes=VMEM_LIMIT),
    )(received, samples)


def finish_kernel(x_ref, sketch_ref, gram_ref):
    sources = x_ref.shape[0]
    quarter = LANES // 4
    lane = lax.broadcasted_iota(jnp.int32, (SUBLANES, LANES), 1)
    gram = None
    for start in range(0, sources, 4):
        halves = [None, None]
        for index in range(4):
            piece = x_ref[start + index]
            gram = piece if gram is None else gram + piece
            for half in range(2):
                shift = (index - half) % 4 * quarter
                moved = pltpu.roll(piece, shift, 1) if shift else piece
                if halves[half] is None:
                    halves[half] = moved
                else:
                    halves[half] = jnp.where(lane // quarter == index, moved, halves[half])
        for half in range(2):
            sketch_ref[
                half * SUBLANES : (half + 1) * SUBLANES, start * quarter : (start + 4) * quarter
            ] = halves[half]
    columns = gram_ref.shape[0]
    gram_ref[:SUBLANES, :] = pltpu.roll(gram, LANES // 2, 1)[:, :columns]
    gram_ref[SUBLANES:, :] = pltpu.roll(gram, LANES // 4, 1)[:, :columns]


def finish(received, columns, sample_count):
    return pl.pallas_call(
        finish_kernel,
        out_shape=(
            jax.ShapeDtypeStruct((columns, sample_count), jnp.float32),
            jax.ShapeDtypeStruct((columns, columns), jnp.float32),
        ),
        in_specs=[pl.BlockSpec(memory_space=pltpu.VMEM)],
        out_specs=(pl.BlockSpec(memory_space=pltpu.VMEM),) * 2,
        compiler_params=pltpu.CompilerParams(vmem_limit_bytes=VMEM_LIMIT),
    )(received)


def exchange(values, axes):
    return lax.all_to_all(values, axes, split_axis=0, concat_axis=0, tiled=True)


def general_shards(matrix_slab, row_signs, sample_rows):
    columns, row_count = matrix_slab.shape
    sample_count = sample_rows.shape[0]
    devices = lax.axis_size("wide") * lax.axis_size("narrow")
    run_length = row_count // sample_count
    slice_rows = row_count // devices
    slice_runs = slice_rows // run_length
    values = jnp.swapaxes(local_transform(matrix_slab, row_signs), 0, 1)
    values = values.reshape(columns, devices, slice_rows)
    received = exchange(jnp.swapaxes(values, 0, 1), AXES)
    offsets = exchange(sample_rows.reshape(devices, slice_runs), AXES)
    mixed = jnp.einsum("ds,scr->dcr", sylvester(devices), received, precision=lax.Precision.HIGHEST)
    mixed = mixed.reshape(devices, columns, slice_runs, run_length)
    chosen = offsets[:, None, :, None] == lax.iota(jnp.int32, run_length)
    picked = jnp.sum(jnp.where(chosen, mixed, 0.0), axis=3)
    picked = picked * jnp.float32(1.0 / math.sqrt(row_count * devices))
    gram = jnp.einsum("dck,dek->ce", picked, picked, precision=lax.Precision.HIGHEST)
    gram = gram / jnp.float32(sample_count * devices)
    grams = jnp.broadcast_to(gram[None], (devices, columns, columns))
    back = exchange(jnp.concatenate([picked, grams], axis=2), AXES)
    sketch = jnp.swapaxes(back[:, :, :slice_runs], 0, 1).reshape(columns, devices * slice_runs)
    return sketch, jnp.sum(back[:, :, slice_runs:], axis=0)


def sliced_shards(matrix_slab, row_signs, sample_rows):
    columns, row_count = matrix_slab.shape
    sample_count = sample_rows.shape[0]
    devices = lax.axis_size("wide") * lax.axis_size("narrow")
    run_length = row_count // sample_count
    transformed = local_transform(matrix_slab, row_signs)
    transformed, sample_rows = lax.optimization_barrier((transformed, sample_rows))
    received = exchange(transformed.reshape(devices, -1, LANES), AXES)
    offsets = exchange(sample_rows.reshape(devices, -1), AXES)
    scale = 1.0 / math.sqrt(row_count * devices)
    picked = mix_and_pick(received, offsets, run_length, scale, 1.0 / (sample_count * devices))
    return finish(exchange(picked, AXES), columns, sample_count)


def solution(mesh):
    devices = mesh.shape["wide"] * mesh.shape["narrow"]
    function = sliced_shards if devices == 32 else general_shards
    in_specs = (P(None, AXES), P(AXES), P(AXES))
    out_specs = (P(None, AXES), P())
    return jax.shard_map(function, mesh=mesh, in_specs=in_specs, out_specs=out_specs, check_vma=False)
```

```python
import functools
import math

import jax
import jax.numpy as jnp
from jax import lax
from jax.experimental import pallas as pl
from jax.experimental.pallas import tpu as pltpu
from jax.sharding import PartitionSpec as P

LANES = 128
SUBLANES = 8
AXES = ("wide", "narrow")
VMEM_LIMIT = 32 * 1024 * 1024
FETCH_LIMIT = 60000000
FETCHES = 4


def butterfly(values):
    values = list(values)
    apart = 1
    while apart < len(values):
        for low in range(len(values)):
            if not low & apart:
                first, second = values[low], values[low | apart]
                values[low], values[low | apart] = first + second, first - second
        apart *= 2
    return values


def sylvester(order_size):
    rows = lax.broadcasted_iota(jnp.int32, (order_size, order_size), 0)
    cols = lax.broadcasted_iota(jnp.int32, (order_size, order_size), 1)
    common = rows & cols
    parity = jnp.zeros_like(common)
    for bit_pos in range(order_size.bit_length() - 1):
        parity = parity ^ (common >> bit_pos)
    return (1 - 2 * (parity & 1)).astype(jnp.float32)


def split_dot(values, table, parts=3):
    total = None
    for _ in range(parts):
        part = values.astype(jnp.bfloat16)
        values = values - part.astype(jnp.float32)
        product = jnp.dot(part, table, preferred_element_type=jnp.float32)
        total = product if total is None else total + product
    return total


def butterfly_steps(count):
    steps = []
    apart = 1
    while apart < count:
        radix = min(8, count // apart)
        for start in range(count):
            if start // apart % radix == 0:
                steps.append((apart, [start + apart * index for index in range(radix)]))
        apart *= radix
    return steps


def fetch_kernel(x_hbm, signs_hbm, out_ref, x_ref, signs_ref, arrived):
    blocks, columns, _ = out_ref.shape
    share = blocks // FETCHES
    fetches = [pltpu.make_async_copy(signs_hbm, signs_ref, arrived.at[0])]
    for piece in range(FETCHES):
        place = (slice(None), pl.ds(piece * share * LANES, share * LANES))
        fetches.append(
            pltpu.make_async_copy(x_hbm.at[place], x_ref.at[place], arrived.at[piece + 1])
        )
    for fetch in fetches:
        fetch.start()
    table = sylvester(LANES).astype(jnp.bfloat16)
    fetches[0].wait()
    for piece in range(FETCHES):
        fetches[piece + 1].wait()
        signed = []
        for block in range(piece * share, (piece + 1) * share):
            signs = signs_ref[block : block + 1, :].astype(jnp.float32)
            signed.append(x_ref[:, block * LANES : (block + 1) * LANES] * signs)
        mixed = split_dot(jnp.concatenate(signed, axis=0), table)
        out_ref[piece * share : (piece + 1) * share] = mixed.reshape(share, columns, LANES)


def local_kernel(x_hbm, signs_hbm, out_ref, x_ref, signs_ref, arrived):
    fetch_kernel(x_hbm, signs_hbm, out_ref, x_ref, signs_ref, arrived)
    for apart, places in butterfly_steps(out_ref.shape[0]):
        for place, value in zip(places, butterfly([out_ref[p] for p in places])):
            out_ref[place] = value


def sliced_kernel(
    x_hbm, signs_hbm, samples_hbm, final_ref, out_ref, x_ref, signs_ref, samples_ref, arrived, noted
):
    note = pltpu.make_async_copy(samples_hbm, samples_ref, noted)
    note.start()
    fetch_kernel(x_hbm, signs_hbm, out_ref, x_ref, signs_ref, arrived)
    blocks, columns, _ = out_ref.shape
    slices = blocks // 2
    rows = final_ref.shape[0] // slices
    steps = butterfly_steps(blocks)
    last = steps[-1][0]
    for apart, places in steps:
        for place, value in zip(places, butterfly([out_ref[p] for p in places])):
            if apart == last:
                start = place // 2 * rows + place % 2 * columns
                final_ref[start : start + columns, :] = value
            else:
                out_ref[place] = value
    note.wait()
    samples = samples_ref[...].astype(jnp.float32)
    per_row = slices // samples.shape[0]
    for turn in range(per_row):
        shift = LANES - turn * LANES // per_row
        turned = pltpu.roll(samples, shift, 1) if turn else samples
        for index in range(turn, slices, per_row):
            tail = (index + 1) * rows - 1
            final_ref[tail : tail + 1, :] = turned[index // per_row : index // per_row + 1]


def in_vmem(count):
    return [pl.BlockSpec(memory_space=pltpu.VMEM)] * count


def in_hbm(count):
    return [pl.BlockSpec(memory_space=pltpu.HBM)] * count


def fetch_scratch(matrix_slab, blocks):
    return [
        pltpu.VMEM(matrix_slab.shape, jnp.float32),
        pltpu.VMEM((blocks, LANES), jnp.int32),
    ]


def local_transform(matrix_slab, row_signs):
    columns, row_count = matrix_slab.shape
    blocks = row_count // LANES
    return pl.pallas_call(
        local_kernel,
        out_shape=jax.ShapeDtypeStruct((blocks, columns, LANES), jnp.float32),
        in_specs=in_hbm(2),
        out_specs=in_vmem(1)[0],
        scratch_shapes=[
            *fetch_scratch(matrix_slab, blocks),
            pltpu.SemaphoreType.DMA((FETCHES + 1,)),
        ],
        compiler_params=pltpu.CompilerParams(vmem_limit_bytes=VMEM_LIMIT),
    )(matrix_slab, row_signs.reshape(blocks, LANES))


def sliced_transform(matrix_slab, row_signs, sample_rows):
    columns, row_count = matrix_slab.shape
    blocks = row_count // LANES
    samples = sample_rows.reshape(-1, LANES)
    return pl.pallas_call(
        sliced_kernel,
        out_shape=jax.ShapeDtypeStruct((blocks // 2 * (2 * columns + 1), LANES), jnp.float32),
        in_specs=in_hbm(3),
        out_specs=in_vmem(1)[0],
        scratch_shapes=[
            pltpu.VMEM((blocks, columns, LANES), jnp.float32),
            *fetch_scratch(matrix_slab, blocks),
            pltpu.VMEM(samples.shape, jnp.int32),
            pltpu.SemaphoreType.DMA((FETCHES + 1,)),
            pltpu.SemaphoreType.DMA(()),
        ],
        compiler_params=pltpu.CompilerParams(vmem_limit_bytes=FETCH_LIMIT),
    )(matrix_slab, row_signs.reshape(blocks, LANES), samples)


def mix_kernel(run_length, scale, gram_scale, x_ref, out_ref):
    devices = out_ref.shape[0]
    rows = x_ref.shape[0] // devices
    runs = LANES // run_length
    samples = jnp.concatenate(
        [x_ref[(s + 1) * rows - 1 : (s + 1) * rows, :] for s in range(devices)], axis=0
    ).astype(jnp.bfloat16)
    run_of = lax.broadcasted_iota(jnp.int32, (LANES, 2 * LANES), 0)
    row_of = lax.broadcasted_iota(jnp.int32, (LANES, 2 * LANES), 1)
    spread = jnp.where(row_of // run_length == run_of, 1.0, 0.0).astype(jnp.bfloat16)
    offsets = jnp.dot(samples, spread, preferred_element_type=jnp.float32)
    own = lax.broadcasted_iota(jnp.int32, offsets.shape, 1) % run_length
    mask = jnp.where(offsets == own.astype(jnp.float32), scale, 0.0)
    picked = []
    for part in range(4):
        block = part // 2
        starts = [s * rows + part * SUBLANES for s in range(devices)]
        mixed = butterfly([x_ref[start : start + SUBLANES, :] for start in starts])
        picked.append(
            jnp.concatenate(
                [
                    mixed[d] * mask[d : d + 1, block * LANES : (block + 1) * LANES]
                    for d in range(devices)
                ],
                axis=0,
            )
        )
    quarter = 2 * runs
    row = lax.broadcasted_iota(jnp.int32, (4 * LANES, 2 * LANES), 0)
    lane = lax.broadcasted_iota(jnp.int32, (4 * LANES, 2 * LANES), 1)
    in_block, in_half = row // (2 * LANES), row // LANES % 2
    group = lane // quarter
    half_here = jnp.where(group >= 6, 7 - group, group % 2)
    target = in_block * runs + row % LANES // run_length
    place = jnp.where((half_here == in_half) & (lane % quarter == target), 1.0, 0.0)
    gathered = split_dot(jnp.concatenate(picked, axis=1), place.astype(jnp.bfloat16), 2)
    straight, crossed = gathered[:, :LANES], gathered[:, LANES:]
    totals = []
    for turn in range(SUBLANES):
        total = None
        for d in range(devices):
            one = straight[d * SUBLANES : (d + 1) * SUBLANES]
            two = crossed[d * SUBLANES : (d + 1) * SUBLANES]
            if turn:
                two = pltpu.roll(two, SUBLANES - turn, 0)
            total = one * two if total is None else total + one * two
        totals.append(total)
    row = lax.broadcasted_iota(jnp.int32, (LANES, LANES), 0)
    lane = lax.broadcasted_iota(jnp.int32, (LANES, LANES), 1)
    together = jnp.where(row // quarter == lane // quarter, 1.0, 0.0).astype(jnp.bfloat16)
    sums = split_dot(jnp.concatenate(totals, axis=0), together) * gram_scale
    sub = lax.broadcasted_iota(jnp.int32, (SUBLANES, LANES), 0)
    lane = lax.broadcasted_iota(jnp.int32, (SUBLANES, LANES), 1)
    gram = jnp.zeros((SUBLANES, LANES), jnp.float32)
    for turn in range(SUBLANES):
        here = sums[turn * SUBLANES : (turn + 1) * SUBLANES]
        gram = jnp.where(lane % SUBLANES == (sub + turn) % SUBLANES, here, gram)
    moved = pltpu.roll(gram, LANES // 2, 1)
    same = (lane // SUBLANES % 2 == 0) == (lane < LANES * 3 // 4)
    gram = jnp.where(same, moved, gram)
    for d in range(devices):
        one = straight[d * SUBLANES : (d + 1) * SUBLANES]
        out_ref[d] = jnp.where(lane < LANES // 2, one, gram)


def mix_and_pick(received, devices, run_length, scale, gram_scale):
    return pl.pallas_call(
        functools.partial(mix_kernel, run_length, scale, gram_scale),
        out_shape=jax.ShapeDtypeStruct((devices, SUBLANES, LANES), jnp.float32),
        in_specs=in_vmem(1),
        out_specs=in_vmem(1)[0],
        compiler_params=pltpu.CompilerParams(vmem_limit_bytes=VMEM_LIMIT),
    )(received)


def finish_kernel(x_ref, sketch_ref, gram_ref):
    sources = x_ref.shape[0]
    quarter = LANES // 4
    lane = lax.broadcasted_iota(jnp.int32, (SUBLANES, LANES), 1)
    gram = None
    for start in range(0, sources, 4):
        halves = [None, None]
        for index in range(4):
            piece = x_ref[start + index]
            gram = piece if gram is None else gram + piece
            for half in range(2):
                shift = (index - half) % 4 * quarter
                moved = pltpu.roll(piece, shift, 1) if shift else piece
                if halves[half] is None:
                    halves[half] = moved
                else:
                    halves[half] = jnp.where(lane // quarter == index, moved, halves[half])
        for half in range(2):
            sketch_ref[
                half * SUBLANES : (half + 1) * SUBLANES, start * quarter : (start + 4) * quarter
            ] = halves[half]
    columns = gram_ref.shape[0]
    gram_ref[:SUBLANES, :] = pltpu.roll(gram, LANES // 2, 1)[:, :columns]
    gram_ref[SUBLANES:, :] = pltpu.roll(gram, LANES // 4, 1)[:, :columns]


def finish(received, columns, sample_count):
    return pl.pallas_call(
        finish_kernel,
        out_shape=(
            jax.ShapeDtypeStruct((columns, sample_count), jnp.float32),
            jax.ShapeDtypeStruct((columns, columns), jnp.float32),
        ),
        in_specs=[pl.BlockSpec(memory_space=pltpu.VMEM)],
        out_specs=(pl.BlockSpec(memory_space=pltpu.VMEM),) * 2,
        compiler_params=pltpu.CompilerParams(vmem_limit_bytes=VMEM_LIMIT),
    )(received)


def exchange(values, axes):
    return lax.all_to_all(values, axes, split_axis=0, concat_axis=0, tiled=True)


def general_shards(matrix_slab, row_signs, sample_rows):
    columns, row_count = matrix_slab.shape
    sample_count = sample_rows.shape[0]
    devices = lax.axis_size("wide") * lax.axis_size("narrow")
    run_length = row_count // sample_count
    slice_rows = row_count // devices
    slice_runs = slice_rows // run_length
    values = jnp.swapaxes(local_transform(matrix_slab, row_signs), 0, 1)
    values = values.reshape(columns, devices, slice_rows)
    received = exchange(jnp.swapaxes(values, 0, 1), AXES)
    offsets = exchange(sample_rows.reshape(devices, slice_runs), AXES)
    mixed = jnp.einsum("ds,scr->dcr", sylvester(devices), received, precision=lax.Precision.HIGHEST)
    mixed = mixed.reshape(devices, columns, slice_runs, run_length)
    chosen = offsets[:, None, :, None] == lax.iota(jnp.int32, run_length)
    picked = jnp.sum(jnp.where(chosen, mixed, 0.0), axis=3)
    picked = picked * jnp.float32(1.0 / math.sqrt(row_count * devices))
    gram = jnp.einsum("dck,dek->ce", picked, picked, precision=lax.Precision.HIGHEST)
    gram = gram / jnp.float32(sample_count * devices)
    grams = jnp.broadcast_to(gram[None], (devices, columns, columns))
    back = exchange(jnp.concatenate([picked, grams], axis=2), AXES)
    sketch = jnp.swapaxes(back[:, :, :slice_runs], 0, 1).reshape(columns, devices * slice_runs)
    return sketch, jnp.sum(back[:, :, slice_runs:], axis=0)


def sliced_shards(matrix_slab, row_signs, sample_rows):
    columns, row_count = matrix_slab.shape
    sample_count = sample_rows.shape[0]
    devices = lax.axis_size("wide") * lax.axis_size("narrow")
    run_length = row_count // sample_count
    sent = sliced_transform(matrix_slab, row_signs, sample_rows)
    received = exchange(sent.reshape(devices, -1), AXES).reshape(sent.shape)
    scale = 1.0 / math.sqrt(row_count * devices)
    gram_scale = 1.0 / (sample_count * devices)
    picked = mix_and_pick(received, devices, run_length, scale, gram_scale)
    return finish(exchange(picked, AXES), columns, sample_count)


def solution(mesh):
    devices = mesh.shape["wide"] * mesh.shape["narrow"]
    function = sliced_shards if devices == 32 else general_shards
    in_specs = (P(None, AXES), P(AXES), P(AXES))
    out_specs = (P(None, AXES), P())
    return jax.shard_map(function, mesh=mesh, in_specs=in_specs, out_specs=out_specs, check_vma=False)
```

```python
import functools
import math

import jax
import jax.numpy as jnp
from jax import lax
from jax.experimental import pallas as pl
from jax.experimental.pallas import tpu as pltpu
from jax.sharding import PartitionSpec as P

LANES = 128
SUBLANES = 8
AXES = ("wide", "narrow")
SPLIT_AXES = ("line", "plane", "narrow")
ORDER = ("plane", "narrow", "line")
VMEM_LIMIT = 32 * 1024 * 1024
FETCH_LIMIT = 60000000
FETCHES = 4


def butterfly(values):
    values = list(values)
    apart = 1
    while apart < len(values):
        for low in range(len(values)):
            if not low & apart:
                first, second = values[low], values[low | apart]
                values[low], values[low | apart] = first + second, first - second
        apart *= 2
    return values


def sylvester(order_size):
    rows = lax.broadcasted_iota(jnp.int32, (order_size, order_size), 0)
    cols = lax.broadcasted_iota(jnp.int32, (order_size, order_size), 1)
    common = rows & cols
    parity = jnp.zeros_like(common)
    for bit_pos in range(order_size.bit_length() - 1):
        parity = parity ^ (common >> bit_pos)
    return (1 - 2 * (parity & 1)).astype(jnp.float32)


def split_dot(values, table, parts=3):
    total = None
    for _ in range(parts):
        part = values.astype(jnp.bfloat16)
        values = values - part.astype(jnp.float32)
        product = jnp.dot(part, table, preferred_element_type=jnp.float32)
        total = product if total is None else total + product
    return total


def butterfly_steps(count):
    steps = []
    apart = 1
    while apart < count:
        radix = min(8, count // apart)
        for start in range(count):
            if start // apart % radix == 0:
                steps.append((apart, [start + apart * index for index in range(radix)]))
        apart *= radix
    return steps


def fetch_kernel(x_hbm, signs_hbm, out_ref, x_ref, signs_ref, arrived):
    blocks, columns, _ = out_ref.shape
    share = blocks // FETCHES
    fetches = [pltpu.make_async_copy(signs_hbm, signs_ref, arrived.at[0])]
    for piece in range(FETCHES):
        place = (slice(None), pl.ds(piece * share * LANES, share * LANES))
        fetches.append(
            pltpu.make_async_copy(x_hbm.at[place], x_ref.at[place], arrived.at[piece + 1])
        )
    for fetch in fetches:
        fetch.start()
    table = sylvester(LANES).astype(jnp.bfloat16)
    fetches[0].wait()
    for piece in range(FETCHES):
        fetches[piece + 1].wait()
        signed = []
        for block in range(piece * share, (piece + 1) * share):
            signs = signs_ref[block : block + 1, :].astype(jnp.float32)
            signed.append(x_ref[:, block * LANES : (block + 1) * LANES] * signs)
        mixed = split_dot(jnp.concatenate(signed, axis=0), table)
        out_ref[piece * share : (piece + 1) * share] = mixed.reshape(share, columns, LANES)


def local_kernel(x_hbm, signs_hbm, out_ref, x_ref, signs_ref, arrived):
    fetch_kernel(x_hbm, signs_hbm, out_ref, x_ref, signs_ref, arrived)
    for apart, places in butterfly_steps(out_ref.shape[0]):
        for place, value in zip(places, butterfly([out_ref[p] for p in places])):
            out_ref[place] = value


def sliced_kernel(
    x_hbm, signs_hbm, samples_hbm, final_ref, out_ref, x_ref, signs_ref, samples_ref, arrived, noted
):
    note = pltpu.make_async_copy(samples_hbm, samples_ref, noted)
    note.start()
    fetch_kernel(x_hbm, signs_hbm, out_ref, x_ref, signs_ref, arrived)
    blocks, columns, _ = out_ref.shape
    slices = blocks // 2
    rows = final_ref.shape[0] // slices
    steps = butterfly_steps(blocks)
    last = steps[-1][0]
    for apart, places in steps:
        for place, value in zip(places, butterfly([out_ref[p] for p in places])):
            if apart == last:
                start = place // 2 * rows + place % 2 * columns
                final_ref[start : start + columns, :] = value
            else:
                out_ref[place] = value
    note.wait()
    samples = samples_ref[...].astype(jnp.float32)
    per_row = slices // samples.shape[0]
    for turn in range(per_row):
        shift = LANES - turn * LANES // per_row
        turned = pltpu.roll(samples, shift, 1) if turn else samples
        for index in range(turn, slices, per_row):
            tail = (index + 1) * rows - 1
            final_ref[tail : tail + 1, :] = turned[index // per_row : index // per_row + 1]


def in_vmem(count):
    return [pl.BlockSpec(memory_space=pltpu.VMEM)] * count


def in_hbm(count):
    return [pl.BlockSpec(memory_space=pltpu.HBM)] * count


def fetch_scratch(matrix_slab, blocks):
    return [
        pltpu.VMEM(matrix_slab.shape, jnp.float32),
        pltpu.VMEM((blocks, LANES), jnp.int32),
    ]


def local_transform(matrix_slab, row_signs):
    columns, row_count = matrix_slab.shape
    blocks = row_count // LANES
    return pl.pallas_call(
        local_kernel,
        out_shape=jax.ShapeDtypeStruct((blocks, columns, LANES), jnp.float32),
        in_specs=in_hbm(2),
        out_specs=in_vmem(1)[0],
        scratch_shapes=[
            *fetch_scratch(matrix_slab, blocks),
            pltpu.SemaphoreType.DMA((FETCHES + 1,)),
        ],
        compiler_params=pltpu.CompilerParams(vmem_limit_bytes=VMEM_LIMIT),
    )(matrix_slab, row_signs.reshape(blocks, LANES))


def sliced_transform(matrix_slab, row_signs, sample_rows):
    columns, row_count = matrix_slab.shape
    blocks = row_count // LANES
    samples = sample_rows.reshape(-1, LANES)
    return pl.pallas_call(
        sliced_kernel,
        out_shape=jax.ShapeDtypeStruct((blocks // 2 * (2 * columns + 1), LANES), jnp.float32),
        in_specs=in_hbm(3),
        out_specs=in_vmem(1)[0],
        scratch_shapes=[
            pltpu.VMEM((blocks, columns, LANES), jnp.float32),
            *fetch_scratch(matrix_slab, blocks),
            pltpu.VMEM(samples.shape, jnp.int32),
            pltpu.SemaphoreType.DMA((FETCHES + 1,)),
            pltpu.SemaphoreType.DMA(()),
        ],
        compiler_params=pltpu.CompilerParams(vmem_limit_bytes=FETCH_LIMIT),
    )(matrix_slab, row_signs.reshape(blocks, LANES), samples)


def mix_kernel(run_length, scale, gram_scale, x_ref, out_ref):
    devices = out_ref.shape[0]
    rows = x_ref.shape[0] // devices
    runs = LANES // run_length
    samples = jnp.concatenate(
        [x_ref[(s + 1) * rows - 1 : (s + 1) * rows, :] for s in range(devices)], axis=0
    ).astype(jnp.bfloat16)
    run_of = lax.broadcasted_iota(jnp.int32, (LANES, 2 * LANES), 0)
    row_of = lax.broadcasted_iota(jnp.int32, (LANES, 2 * LANES), 1)
    spread = jnp.where(row_of // run_length == run_of, 1.0, 0.0).astype(jnp.bfloat16)
    offsets = jnp.dot(samples, spread, preferred_element_type=jnp.float32)
    own = lax.broadcasted_iota(jnp.int32, offsets.shape, 1) % run_length
    mask = jnp.where(offsets == own.astype(jnp.float32), scale, 0.0)
    picked = []
    for part in range(4):
        block = part // 2
        starts = [s * rows + part * SUBLANES for s in range(devices)]
        mixed = butterfly([x_ref[start : start + SUBLANES, :] for start in starts])
        picked.append(
            jnp.concatenate(
                [
                    mixed[d] * mask[d : d + 1, block * LANES : (block + 1) * LANES]
                    for d in range(devices)
                ],
                axis=0,
            )
        )
    quarter = 2 * runs
    row = lax.broadcasted_iota(jnp.int32, (4 * LANES, 2 * LANES), 0)
    lane = lax.broadcasted_iota(jnp.int32, (4 * LANES, 2 * LANES), 1)
    in_block, in_half = row // (2 * LANES), row // LANES % 2
    group = lane // quarter
    half_here = jnp.where(group >= 6, 7 - group, group % 2)
    target = in_block * runs + row % LANES // run_length
    place = jnp.where((half_here == in_half) & (lane % quarter == target), 1.0, 0.0)
    gathered = split_dot(jnp.concatenate(picked, axis=1), place.astype(jnp.bfloat16), 2)
    straight, crossed = gathered[:, :LANES], gathered[:, LANES:]
    totals = []
    for turn in range(SUBLANES):
        total = None
        for d in range(devices):
            one = straight[d * SUBLANES : (d + 1) * SUBLANES]
            two = crossed[d * SUBLANES : (d + 1) * SUBLANES]
            if turn:
                two = pltpu.roll(two, SUBLANES - turn, 0)
            total = one * two if total is None else total + one * two
        totals.append(total)
    row = lax.broadcasted_iota(jnp.int32, (LANES, LANES), 0)
    lane = lax.broadcasted_iota(jnp.int32, (LANES, LANES), 1)
    together = jnp.where(row // quarter == lane // quarter, 1.0, 0.0).astype(jnp.bfloat16)
    sums = split_dot(jnp.concatenate(totals, axis=0), together) * gram_scale
    sub = lax.broadcasted_iota(jnp.int32, (SUBLANES, LANES), 0)
    lane = lax.broadcasted_iota(jnp.int32, (SUBLANES, LANES), 1)
    gram = jnp.zeros((SUBLANES, LANES), jnp.float32)
    for turn in range(SUBLANES):
        here = sums[turn * SUBLANES : (turn + 1) * SUBLANES]
        gram = jnp.where(lane % SUBLANES == (sub + turn) % SUBLANES, here, gram)
    moved = pltpu.roll(gram, LANES // 2, 1)
    same = (lane // SUBLANES % 2 == 0) == (lane < LANES * 3 // 4)
    gram = jnp.where(same, moved, gram)
    for d in range(devices):
        one = straight[d * SUBLANES : (d + 1) * SUBLANES]
        out_ref[d] = jnp.where(lane < LANES // 2, one, gram)


def mix_and_pick(received, devices, run_length, scale, gram_scale):
    return pl.pallas_call(
        functools.partial(mix_kernel, run_length, scale, gram_scale),
        out_shape=jax.ShapeDtypeStruct((devices, SUBLANES, LANES), jnp.float32),
        in_specs=in_vmem(1),
        out_specs=in_vmem(1)[0],
        compiler_params=pltpu.CompilerParams(vmem_limit_bytes=VMEM_LIMIT),
    )(received)


def finish_kernel(x_ref, sketch_ref, gram_ref):
    sources = x_ref.shape[0]
    quarter = LANES // 4
    lane = lax.broadcasted_iota(jnp.int32, (SUBLANES, LANES), 1)
    gram = None
    for start in range(0, sources, 4):
        halves = [None, None]
        for index in range(4):
            piece = x_ref[start + index]
            gram = piece if gram is None else gram + piece
            for half in range(2):
                shift = (index - half) % 4 * quarter
                moved = pltpu.roll(piece, shift, 1) if shift else piece
                if halves[half] is None:
                    halves[half] = moved
                else:
                    halves[half] = jnp.where(lane // quarter == index, moved, halves[half])
        for half in range(2):
            sketch_ref[
                half * SUBLANES : (half + 1) * SUBLANES, start * quarter : (start + 4) * quarter
            ] = halves[half]
    columns = gram_ref.shape[0]
    gram_ref[:SUBLANES, :] = pltpu.roll(gram, LANES // 2, 1)[:, :columns]
    gram_ref[SUBLANES:, :] = pltpu.roll(gram, LANES // 4, 1)[:, :columns]


def finish(received, columns, sample_count):
    return pl.pallas_call(
        finish_kernel,
        out_shape=(
            jax.ShapeDtypeStruct((columns, sample_count), jnp.float32),
            jax.ShapeDtypeStruct((columns, columns), jnp.float32),
        ),
        in_specs=[pl.BlockSpec(memory_space=pltpu.VMEM)],
        out_specs=(pl.BlockSpec(memory_space=pltpu.VMEM),) * 2,
        compiler_params=pltpu.CompilerParams(vmem_limit_bytes=VMEM_LIMIT),
    )(received)


def exchange(values, axes):
    return lax.all_to_all(values, axes, split_axis=0, concat_axis=0, tiled=True)


def general_shards(matrix_slab, row_signs, sample_rows):
    columns, row_count = matrix_slab.shape
    sample_count = sample_rows.shape[0]
    devices = lax.axis_size("wide") * lax.axis_size("narrow")
    run_length = row_count // sample_count
    slice_rows = row_count // devices
    slice_runs = slice_rows // run_length
    values = jnp.swapaxes(local_transform(matrix_slab, row_signs), 0, 1)
    values = values.reshape(columns, devices, slice_rows)
    received = exchange(jnp.swapaxes(values, 0, 1), AXES)
    offsets = exchange(sample_rows.reshape(devices, slice_runs), AXES)
    mixed = jnp.einsum("ds,scr->dcr", sylvester(devices), received, precision=lax.Precision.HIGHEST)
    mixed = mixed.reshape(devices, columns, slice_runs, run_length)
    chosen = offsets[:, None, :, None] == lax.iota(jnp.int32, run_length)
    picked = jnp.sum(jnp.where(chosen, mixed, 0.0), axis=3)
    picked = picked * jnp.float32(1.0 / math.sqrt(row_count * devices))
    gram = jnp.einsum("dck,dek->ce", picked, picked, precision=lax.Precision.HIGHEST)
    gram = gram / jnp.float32(sample_count * devices)
    grams = jnp.broadcast_to(gram[None], (devices, columns, columns))
    back = exchange(jnp.concatenate([picked, grams], axis=2), AXES)
    sketch = jnp.swapaxes(back[:, :, :slice_runs], 0, 1).reshape(columns, devices * slice_runs)
    return sketch, jnp.sum(back[:, :, slice_runs:], axis=0)


def sliced_shards(matrix_slab, row_signs, sample_rows):
    columns, row_count = matrix_slab.shape
    sample_count = sample_rows.shape[0]
    devices = lax.axis_size(ORDER)
    run_length = row_count // sample_count
    sent = sliced_transform(matrix_slab, row_signs, sample_rows)
    received = exchange(sent.reshape(devices, -1), ORDER).reshape(sent.shape)
    scale = 1.0 / math.sqrt(row_count * devices)
    gram_scale = 1.0 / (sample_count * devices)
    picked = mix_and_pick(received, devices, run_length, scale, gram_scale)
    return finish(exchange(picked, ORDER), columns, sample_count)


def solution(mesh):
    wide, narrow = mesh.shape["wide"], mesh.shape["narrow"]
    axes, function = AXES, general_shards
    if wide * narrow == 32 and wide % 4 == 0:
        axes, function = SPLIT_AXES, sliced_shards
        mesh = jax.sharding.Mesh(mesh.devices.reshape(4, wide // 4, narrow), axes)
    in_specs = (P(None, axes), P(axes), P(axes))
    out_specs = (P(None, axes), P())
    return jax.shard_map(function, mesh=mesh, in_specs=in_specs, out_specs=out_specs, check_vma=False)
```

```python
import functools
import math

import jax
import jax.numpy as jnp
from jax import lax
from jax.experimental import pallas as pl
from jax.experimental.pallas import tpu as pltpu
from jax.sharding import PartitionSpec as P

LANES = 128
SUBLANES = 8
AXES = ("wide", "narrow")
SPLIT_AXES = ("line", "plane", "narrow")
ORDER = ("plane", "narrow", "line")
VMEM_LIMIT = 32 * 1024 * 1024
FETCH_LIMIT = 60000000
FETCHES = 4
SENDS = 4
MESSAGE_ROWS = 6


def butterfly(values):
    values = list(values)
    apart = 1
    while apart < len(values):
        for low in range(len(values)):
            if not low & apart:
                first, second = values[low], values[low | apart]
                values[low], values[low | apart] = first + second, first - second
        apart *= 2
    return values


def sylvester(order_size):
    rows = lax.broadcasted_iota(jnp.int32, (order_size, order_size), 0)
    cols = lax.broadcasted_iota(jnp.int32, (order_size, order_size), 1)
    common = rows & cols
    parity = jnp.zeros_like(common)
    for bit_pos in range(order_size.bit_length() - 1):
        parity = parity ^ (common >> bit_pos)
    return (1 - 2 * (parity & 1)).astype(jnp.float32)


def split_dot(values, table, parts=3):
    total = None
    for _ in range(parts):
        part = values.astype(jnp.bfloat16)
        values = values - part.astype(jnp.float32)
        product = jnp.dot(part, table, preferred_element_type=jnp.float32)
        total = product if total is None else total + product
    return total


def butterfly_steps(count):
    steps = []
    apart = 1
    while apart < count:
        radix = min(8, count // apart)
        for start in range(count):
            if start // apart % radix == 0:
                steps.append((apart, [start + apart * index for index in range(radix)]))
        apart *= radix
    return steps


def fetch_kernel(x_hbm, signs_hbm, out_ref, x_ref, signs_ref, arrived):
    blocks, columns, _ = out_ref.shape
    share = blocks // FETCHES
    fetches = [pltpu.make_async_copy(signs_hbm, signs_ref, arrived.at[0])]
    for piece in range(FETCHES):
        place = (slice(None), pl.ds(piece * share * LANES, share * LANES))
        fetches.append(
            pltpu.make_async_copy(x_hbm.at[place], x_ref.at[place], arrived.at[piece + 1])
        )
    for fetch in fetches:
        fetch.start()
    table = sylvester(LANES).astype(jnp.bfloat16)
    fetches[0].wait()
    for piece in range(FETCHES):
        fetches[piece + 1].wait()
        signed = []
        for block in range(piece * share, (piece + 1) * share):
            signs = signs_ref[block : block + 1, :].astype(jnp.float32)
            signed.append(x_ref[:, block * LANES : (block + 1) * LANES] * signs)
        mixed = split_dot(jnp.concatenate(signed, axis=0), table)
        out_ref[piece * share : (piece + 1) * share] = mixed.reshape(share, columns, LANES)


def local_kernel(x_hbm, signs_hbm, out_ref, x_ref, signs_ref, arrived):
    fetch_kernel(x_hbm, signs_hbm, out_ref, x_ref, signs_ref, arrived)
    for apart, places in butterfly_steps(out_ref.shape[0]):
        for place, value in zip(places, butterfly([out_ref[p] for p in places])):
            out_ref[place] = value


def sliced_kernel(
    x_hbm, signs_hbm, samples_hbm, final_hbm,
    out_ref, final_ref, x_ref, signs_ref, samples_ref, arrived, noted, sent,
):
    note = pltpu.make_async_copy(samples_hbm, samples_ref, noted)
    note.start()
    fetch_kernel(x_hbm, signs_hbm, out_ref, x_ref, signs_ref, arrived)
    blocks, columns, _ = out_ref.shape
    slices = blocks // 2
    rows = final_ref.shape[0] // slices
    note.wait()
    samples = samples_ref[...].astype(jnp.float32)
    per_row = slices // samples.shape[0]
    for turn in range(per_row):
        shift = LANES - turn * LANES // per_row
        turned = pltpu.roll(samples, shift, 1) if turn else samples
        for index in range(turn, slices, per_row):
            tail = (index + 1) * rows - 1
            final_ref[tail : tail + 1, :] = turned[index // per_row : index // per_row + 1]
    steps = butterfly_steps(blocks)
    for apart, places in [step for step in steps if step[0] > 1]:
        for place, value in zip(places, butterfly([out_ref[p] for p in places])):
            out_ref[place] = value
    share = final_ref.shape[0] // SENDS
    sends = []
    for apart, places in [step for step in steps if step[0] == 1]:
        for place, value in zip(places, butterfly([out_ref[p] for p in places])):
            start = place // 2 * rows + place % 2 * columns
            final_ref[start : start + columns, :] = value
        if (places[-1] + 1) % (blocks // SENDS) == 0:
            piece = pl.ds(len(sends) * share, share)
            sends.append(
                pltpu.make_async_copy(
                    final_ref.at[piece], final_hbm.at[piece], sent.at[len(sends)]
                )
            )
            sends[-1].start()
    for send in sends:
        send.wait()


def in_vmem(count):
    return [pl.BlockSpec(memory_space=pltpu.VMEM)] * count


def in_hbm(count):
    return [pl.BlockSpec(memory_space=pltpu.HBM)] * count


def fetch_scratch(matrix_slab, blocks):
    return [
        pltpu.VMEM(matrix_slab.shape, jnp.float32),
        pltpu.VMEM((blocks, LANES), jnp.int32),
    ]


def local_transform(matrix_slab, row_signs):
    columns, row_count = matrix_slab.shape
    blocks = row_count // LANES
    return pl.pallas_call(
        local_kernel,
        out_shape=jax.ShapeDtypeStruct((blocks, columns, LANES), jnp.float32),
        in_specs=in_hbm(2),
        out_specs=in_vmem(1)[0],
        scratch_shapes=[
            *fetch_scratch(matrix_slab, blocks),
            pltpu.SemaphoreType.DMA((FETCHES + 1,)),
        ],
        compiler_params=pltpu.CompilerParams(vmem_limit_bytes=VMEM_LIMIT),
    )(matrix_slab, row_signs.reshape(blocks, LANES))


def sliced_transform(matrix_slab, row_signs, sample_rows):
    columns, row_count = matrix_slab.shape
    blocks = row_count // LANES
    samples = sample_rows.reshape(-1, LANES)
    final = (blocks // 2 * (2 * columns + 1), LANES)
    return pl.pallas_call(
        sliced_kernel,
        out_shape=jax.ShapeDtypeStruct(final, jnp.float32),
        in_specs=in_hbm(3),
        out_specs=in_hbm(1)[0],
        scratch_shapes=[
            pltpu.VMEM((blocks, columns, LANES), jnp.float32),
            pltpu.VMEM(final, jnp.float32),
            *fetch_scratch(matrix_slab, blocks),
            pltpu.VMEM(samples.shape, jnp.int32),
            pltpu.SemaphoreType.DMA((FETCHES + 1,)),
            pltpu.SemaphoreType.DMA(()),
            pltpu.SemaphoreType.DMA((SENDS,)),
        ],
        compiler_params=pltpu.CompilerParams(vmem_limit_bytes=FETCH_LIMIT),
    )(matrix_slab, row_signs.reshape(blocks, LANES), samples)


def mix_kernel(run_length, scale, gram_scale, x_ref, out_ref):
    devices = out_ref.shape[0] // MESSAGE_ROWS
    rows = x_ref.shape[0] // devices
    runs = LANES // run_length
    samples = jnp.concatenate(
        [x_ref[(s + 1) * rows - 1 : (s + 1) * rows, :] for s in range(devices)], axis=0
    ).astype(jnp.bfloat16)
    run_of = lax.broadcasted_iota(jnp.int32, (LANES, 2 * LANES), 0)
    row_of = lax.broadcasted_iota(jnp.int32, (LANES, 2 * LANES), 1)
    spread = jnp.where(row_of // run_length == run_of, 1.0, 0.0).astype(jnp.bfloat16)
    offsets = jnp.dot(samples, spread, preferred_element_type=jnp.float32)
    own = lax.broadcasted_iota(jnp.int32, offsets.shape, 1) % run_length
    mask = jnp.where(offsets == own.astype(jnp.float32), scale, 0.0)
    picked = []
    for part in range(4):
        block = part // 2
        starts = [s * rows + part * SUBLANES for s in range(devices)]
        mixed = butterfly([x_ref[start : start + SUBLANES, :] for start in starts])
        picked.append(
            jnp.concatenate(
                [
                    mixed[d] * mask[d : d + 1, block * LANES : (block + 1) * LANES]
                    for d in range(devices)
                ],
                axis=0,
            )
        )
    quarter = 2 * runs
    row = lax.broadcasted_iota(jnp.int32, (4 * LANES, 2 * LANES), 0)
    lane = lax.broadcasted_iota(jnp.int32, (4 * LANES, 2 * LANES), 1)
    in_block, in_half = row // (2 * LANES), row // LANES % 2
    group = lane // quarter
    half_here = jnp.where(group >= 6, 7 - group, group % 2)
    target = in_block * runs + row % LANES // run_length
    place = jnp.where((half_here == in_half) & (lane % quarter == target), 1.0, 0.0)
    gathered = split_dot(jnp.concatenate(picked, axis=1), place.astype(jnp.bfloat16), 2)
    straight, crossed = gathered[:, :LANES], gathered[:, LANES:]
    totals = []
    for turn in range(SUBLANES):
        total = None
        for d in range(devices):
            one = straight[d * SUBLANES : (d + 1) * SUBLANES]
            two = crossed[d * SUBLANES : (d + 1) * SUBLANES]
            if turn:
                two = pltpu.roll(two, SUBLANES - turn, 0)
            total = one * two if total is None else total + one * two
        totals.append(total)
    row = lax.broadcasted_iota(jnp.int32, (LANES, 4 * LANES), 0)
    lane = lax.broadcasted_iota(jnp.int32, (LANES, 4 * LANES), 1)
    together = jnp.where(row // quarter == lane // LANES, 1.0, 0.0).astype(jnp.bfloat16)
    sums = split_dot(jnp.concatenate(totals, axis=0), together) * gram_scale
    sub = lax.broadcasted_iota(jnp.int32, (SUBLANES, LANES), 0)
    lane = lax.broadcasted_iota(jnp.int32, (SUBLANES, LANES), 1)
    first, second = [jnp.zeros((SUBLANES, LANES), jnp.float32)] * 2
    for turn in range(SUBLANES):
        here = sums[turn * SUBLANES : (turn + 1) * SUBLANES]
        quarters = [here[:, q * LANES : (q + 1) * LANES] for q in range(4)]
        mine = lane % SUBLANES == (sub + turn) % SUBLANES
        left = lane // SUBLANES % 2 == 0
        first = jnp.where(mine, jnp.where(left, quarters[0], quarters[2]), first)
        second = jnp.where(mine, jnp.where(left, quarters[3], quarters[1]), second)
    in_place = lane // (2 * SUBLANES) == sub
    gram = jnp.concatenate(
        [jnp.sum(jnp.where(in_place, part, 0.0), axis=0, keepdims=True) for part in (first, second)],
        axis=0,
    )
    half = SUBLANES // 2
    lane = lax.broadcasted_iota(jnp.int32, (half, LANES), 1)
    for d in range(devices):
        one = straight[d * SUBLANES : (d + 1) * SUBLANES]
        start = d * MESSAGE_ROWS
        out_ref[start : start + half, :] = jnp.where(lane < LANES // 2, one[:half], one[half:])
        out_ref[start + half : start + MESSAGE_ROWS, :] = gram


def mix_and_pick(received, devices, run_length, scale, gram_scale):
    return pl.pallas_call(
        functools.partial(mix_kernel, run_length, scale, gram_scale),
        out_shape=jax.ShapeDtypeStruct((devices * MESSAGE_ROWS, LANES), jnp.float32),
        in_specs=in_vmem(1),
        out_specs=in_vmem(1)[0],
        compiler_params=pltpu.CompilerParams(vmem_limit_bytes=VMEM_LIMIT),
    )(received)


def finish_kernel(x_ref, sketch_ref, gram_ref):
    sources = x_ref.shape[0] // MESSAGE_ROWS
    quarter = LANES // 4
    half_rows = SUBLANES // 2
    sub = lax.broadcasted_iota(jnp.int32, (SUBLANES, LANES), 0)
    lane = lax.broadcasted_iota(jnp.int32, (SUBLANES, LANES), 1)
    gram = None
    for start in range(0, sources, 4):
        halves = [None, None]
        for index in range(4):
            place = (start + index) * MESSAGE_ROWS
            tail = x_ref[place + half_rows : place + MESSAGE_ROWS, :]
            gram = tail if gram is None else gram + tail
            piece = x_ref[place : place + half_rows, :]
            piece = jnp.concatenate([piece, piece], axis=0)
            piece = jnp.where(sub < half_rows, piece, pltpu.roll(piece, LANES // 2, 1))
            for half in range(2):
                shift = (index - half) % 4 * quarter
                moved = pltpu.roll(piece, shift, 1) if shift else piece
                if halves[half] is None:
                    halves[half] = moved
                else:
                    halves[half] = jnp.where(lane // quarter == index, moved, halves[half])
        for half in range(2):
            sketch_ref[
                half * SUBLANES : (half + 1) * SUBLANES, start * quarter : (start + 4) * quarter
            ] = halves[half]
    columns = gram_ref.shape[0]
    for half in range(2):
        for row in range(SUBLANES):
            line = gram[half : half + 1]
            line = pltpu.roll(line, LANES - row * columns, 1) if row else line
            gram_ref[half * SUBLANES + row : half * SUBLANES + row + 1, :] = line[:, :columns]


def finish(received, columns, sample_count):
    return pl.pallas_call(
        finish_kernel,
        out_shape=(
            jax.ShapeDtypeStruct((columns, sample_count), jnp.float32),
            jax.ShapeDtypeStruct((columns, columns), jnp.float32),
        ),
        in_specs=[pl.BlockSpec(memory_space=pltpu.VMEM)],
        out_specs=(pl.BlockSpec(memory_space=pltpu.VMEM),) * 2,
        compiler_params=pltpu.CompilerParams(vmem_limit_bytes=VMEM_LIMIT),
    )(received)


def exchange(values, axes):
    return lax.all_to_all(values, axes, split_axis=0, concat_axis=0, tiled=True)


def general_shards(matrix_slab, row_signs, sample_rows):
    columns, row_count = matrix_slab.shape
    sample_count = sample_rows.shape[0]
    devices = lax.axis_size("wide") * lax.axis_size("narrow")
    run_length = row_count // sample_count
    slice_rows = row_count // devices
    slice_runs = slice_rows // run_length
    values = jnp.swapaxes(local_transform(matrix_slab, row_signs), 0, 1)
    values = values.reshape(columns, devices, slice_rows)
    received = exchange(jnp.swapaxes(values, 0, 1), AXES)
    offsets = exchange(sample_rows.reshape(devices, slice_runs), AXES)
    mixed = jnp.einsum("ds,scr->dcr", sylvester(devices), received, precision=lax.Precision.HIGHEST)
    mixed = mixed.reshape(devices, columns, slice_runs, run_length)
    chosen = offsets[:, None, :, None] == lax.iota(jnp.int32, run_length)
    picked = jnp.sum(jnp.where(chosen, mixed, 0.0), axis=3)
    picked = picked * jnp.float32(1.0 / math.sqrt(row_count * devices))
    gram = jnp.einsum("dck,dek->ce", picked, picked, precision=lax.Precision.HIGHEST)
    gram = gram / jnp.float32(sample_count * devices)
    grams = jnp.broadcast_to(gram[None], (devices, columns, columns))
    back = exchange(jnp.concatenate([picked, grams], axis=2), AXES)
    sketch = jnp.swapaxes(back[:, :, :slice_runs], 0, 1).reshape(columns, devices * slice_runs)
    return sketch, jnp.sum(back[:, :, slice_runs:], axis=0)


def sliced_shards(matrix_slab, row_signs, sample_rows):
    columns, row_count = matrix_slab.shape
    sample_count = sample_rows.shape[0]
    devices = lax.axis_size(ORDER)
    run_length = row_count // sample_count
    sent = sliced_transform(matrix_slab, row_signs, sample_rows)
    received = exchange(sent.reshape(devices, -1), ORDER).reshape(sent.shape)
    scale = 1.0 / math.sqrt(row_count * devices)
    gram_scale = 1.0 / (sample_count * devices)
    picked = mix_and_pick(received, devices, run_length, scale, gram_scale)
    returned = exchange(picked.reshape(devices, -1), ORDER).reshape(picked.shape)
    return finish(returned, columns, sample_count)


def solution(mesh):
    wide, narrow = mesh.shape["wide"], mesh.shape["narrow"]
    axes, function = AXES, general_shards
    if wide * narrow == 32 and wide % 4 == 0:
        axes, function = SPLIT_AXES, sliced_shards
        mesh = jax.sharding.Mesh(mesh.devices.reshape(4, wide // 4, narrow), axes)
    in_specs = (P(None, axes), P(axes), P(axes))
    out_specs = (P(None, axes), P())
    return jax.shard_map(function, mesh=mesh, in_specs=in_specs, out_specs=out_specs, check_vma=False)
```

```python
import functools
import math

import jax
import jax.numpy as jnp
from jax import lax
from jax.experimental import pallas as pl
from jax.experimental.pallas import tpu as pltpu
from jax.sharding import PartitionSpec as P

LANES = 128
SUBLANES = 8
AXES = ("wide", "narrow")
SPLIT_AXES = ("line", "plane", "narrow")
ORDER = ("plane", "narrow", "line")
VMEM_LIMIT = 32 * 1024 * 1024
MESSAGE_ROWS = 6


def butterfly(values):
    values = list(values)
    apart = 1
    while apart < len(values):
        for low in range(len(values)):
            if not low & apart:
                first, second = values[low], values[low | apart]
                values[low], values[low | apart] = first + second, first - second
        apart *= 2
    return values


def sylvester(order_size):
    rows = lax.broadcasted_iota(jnp.int32, (order_size, order_size), 0)
    cols = lax.broadcasted_iota(jnp.int32, (order_size, order_size), 1)
    common = rows & cols
    parity = jnp.zeros_like(common)
    for bit_pos in range(order_size.bit_length() - 1):
        parity = parity ^ (common >> bit_pos)
    return (1 - 2 * (parity & 1)).astype(jnp.float32)


def split_dot(values, table, parts=3):
    total = None
    for _ in range(parts):
        part = values.astype(jnp.bfloat16)
        values = values - part.astype(jnp.float32)
        product = jnp.dot(part, table, preferred_element_type=jnp.float32)
        total = product if total is None else total + product
    return total


def butterfly_steps(count):
    steps = []
    apart = 1
    while apart < count:
        radix = min(8, count // apart)
        for start in range(count):
            if start // apart % radix == 0:
                steps.append((apart, [start + apart * index for index in range(radix)]))
        apart *= radix
    return steps


def signed_blocks(x_ref, signs_ref, out_ref):
    blocks, columns, _ = out_ref.shape
    table = sylvester(LANES).astype(jnp.bfloat16)
    signed = []
    for block in range(blocks):
        signs = signs_ref[block : block + 1, :].astype(jnp.float32)
        signed.append(x_ref[:, block * LANES : (block + 1) * LANES] * signs)
    mixed = split_dot(jnp.concatenate(signed, axis=0), table)
    out_ref[...] = mixed.reshape(blocks, columns, LANES)


def local_kernel(x_ref, signs_ref, out_ref):
    signed_blocks(x_ref, signs_ref, out_ref)
    for apart, places in butterfly_steps(out_ref.shape[0]):
        for place, value in zip(places, butterfly([out_ref[p] for p in places])):
            out_ref[place] = value


def sliced_kernel(x_ref, prepared_ref, final_ref, out_ref):
    signed_blocks(x_ref, prepared_ref, out_ref)
    blocks, columns, _ = out_ref.shape
    slices = blocks // 2
    rows = final_ref.shape[0] // slices
    samples = prepared_ref[blocks:]
    per_row = slices // samples.shape[0]
    for turn in range(per_row):
        shift = LANES - turn * LANES // per_row
        turned = pltpu.roll(samples, shift, 1) if turn else samples
        for index in range(turn, slices, per_row):
            tail = (index + 1) * rows - 1
            final_ref[tail : tail + 1, :] = turned[index // per_row : index // per_row + 1]
    steps = butterfly_steps(blocks)
    last = steps[-1][0]
    for apart, places in steps:
        for place, value in zip(places, butterfly([out_ref[p] for p in places])):
            if apart == last:
                start = place // 2 * rows + place % 2 * columns
                final_ref[start : start + columns, :] = value
            else:
                out_ref[place] = value


def in_vmem(count):
    return [pl.BlockSpec(memory_space=pltpu.VMEM)] * count


def local_transform(matrix_slab, row_signs):
    columns, row_count = matrix_slab.shape
    blocks = row_count // LANES
    return pl.pallas_call(
        local_kernel,
        out_shape=jax.ShapeDtypeStruct((blocks, columns, LANES), jnp.float32),
        in_specs=in_vmem(2),
        out_specs=in_vmem(1)[0],
        compiler_params=pltpu.CompilerParams(vmem_limit_bytes=VMEM_LIMIT),
    )(matrix_slab, row_signs.reshape(blocks, LANES))


def sliced_transform(matrix_slab, row_signs, sample_rows):
    columns, row_count = matrix_slab.shape
    blocks = row_count // LANES
    prepared = jnp.concatenate([row_signs, sample_rows]).astype(jnp.float32).reshape(-1, LANES)
    return pl.pallas_call(
        sliced_kernel,
        out_shape=jax.ShapeDtypeStruct((blocks // 2 * (2 * columns + 1), LANES), jnp.float32),
        in_specs=in_vmem(2),
        out_specs=in_vmem(1)[0],
        scratch_shapes=[pltpu.VMEM((blocks, columns, LANES), jnp.float32)],
        compiler_params=pltpu.CompilerParams(vmem_limit_bytes=VMEM_LIMIT),
    )(matrix_slab, prepared)


def mix_kernel(run_length, scale, gram_scale, x_ref, out_ref):
    devices = out_ref.shape[0] // MESSAGE_ROWS
    rows = x_ref.shape[0] // devices
    runs = LANES // run_length
    samples = jnp.concatenate(
        [x_ref[(s + 1) * rows - 1 : (s + 1) * rows, :] for s in range(devices)], axis=0
    ).astype(jnp.bfloat16)
    run_of = lax.broadcasted_iota(jnp.int32, (LANES, 2 * LANES), 0)
    row_of = lax.broadcasted_iota(jnp.int32, (LANES, 2 * LANES), 1)
    spread = jnp.where(row_of // run_length == run_of, 1.0, 0.0).astype(jnp.bfloat16)
    offsets = jnp.dot(samples, spread, preferred_element_type=jnp.float32)
    own = lax.broadcasted_iota(jnp.int32, offsets.shape, 1) % run_length
    mask = jnp.where(offsets == own.astype(jnp.float32), scale, 0.0)
    picked = []
    for part in range(4):
        block = part // 2
        starts = [s * rows + part * SUBLANES for s in range(devices)]
        mixed = butterfly([x_ref[start : start + SUBLANES, :] for start in starts])
        picked.append(
            jnp.concatenate(
                [
                    mixed[d] * mask[d : d + 1, block * LANES : (block + 1) * LANES]
                    for d in range(devices)
                ],
                axis=0,
            )
        )
    quarter = 2 * runs
    row = lax.broadcasted_iota(jnp.int32, (4 * LANES, 2 * LANES), 0)
    lane = lax.broadcasted_iota(jnp.int32, (4 * LANES, 2 * LANES), 1)
    in_block, in_half = row // (2 * LANES), row // LANES % 2
    group = lane // quarter
    half_here = jnp.where(group >= 6, 7 - group, group % 2)
    target = in_block * runs + row % LANES // run_length
    place = jnp.where((half_here == in_half) & (lane % quarter == target), 1.0, 0.0)
    gathered = split_dot(jnp.concatenate(picked, axis=1), place.astype(jnp.bfloat16), 2)
    straight, crossed = gathered[:, :LANES], gathered[:, LANES:]
    totals = []
    for turn in range(SUBLANES):
        total = None
        for d in range(devices):
            one = straight[d * SUBLANES : (d + 1) * SUBLANES]
            two = crossed[d * SUBLANES : (d + 1) * SUBLANES]
            if turn:
                two = pltpu.roll(two, SUBLANES - turn, 0)
            total = one * two if total is None else total + one * two
        totals.append(total)
    row = lax.broadcasted_iota(jnp.int32, (LANES, 4 * LANES), 0)
    lane = lax.broadcasted_iota(jnp.int32, (LANES, 4 * LANES), 1)
    together = jnp.where(row // quarter == lane // LANES, 1.0, 0.0).astype(jnp.bfloat16)
    sums = split_dot(jnp.concatenate(totals, axis=0), together) * gram_scale
    sub = lax.broadcasted_iota(jnp.int32, (SUBLANES, LANES), 0)
    lane = lax.broadcasted_iota(jnp.int32, (SUBLANES, LANES), 1)
    first, second = [jnp.zeros((SUBLANES, LANES), jnp.float32)] * 2
    for turn in range(SUBLANES):
        here = sums[turn * SUBLANES : (turn + 1) * SUBLANES]
        quarters = [here[:, q * LANES : (q + 1) * LANES] for q in range(4)]
        mine = lane % SUBLANES == (sub + turn) % SUBLANES
        left = lane // SUBLANES % 2 == 0
        first = jnp.where(mine, jnp.where(left, quarters[0], quarters[2]), first)
        second = jnp.where(mine, jnp.where(left, quarters[3], quarters[1]), second)
    in_place = lane // (2 * SUBLANES) == sub
    gram = jnp.concatenate(
        [jnp.sum(jnp.where(in_place, part, 0.0), axis=0, keepdims=True) for part in (first, second)],
        axis=0,
    )
    half = SUBLANES // 2
    lane = lax.broadcasted_iota(jnp.int32, (half, LANES), 1)
    for d in range(devices):
        one = straight[d * SUBLANES : (d + 1) * SUBLANES]
        start = d * MESSAGE_ROWS
        out_ref[start : start + half, :] = jnp.where(lane < LANES // 2, one[:half], one[half:])
        out_ref[start + half : start + MESSAGE_ROWS, :] = gram


def mix_and_pick(received, devices, run_length, scale, gram_scale):
    return pl.pallas_call(
        functools.partial(mix_kernel, run_length, scale, gram_scale),
        out_shape=jax.ShapeDtypeStruct((devices * MESSAGE_ROWS, LANES), jnp.float32),
        in_specs=in_vmem(1),
        out_specs=in_vmem(1)[0],
        compiler_params=pltpu.CompilerParams(vmem_limit_bytes=VMEM_LIMIT),
    )(received)


def finish_kernel(x_ref, sketch_ref, gram_ref):
    sources = x_ref.shape[0] // MESSAGE_ROWS
    quarter = LANES // 4
    half_rows = SUBLANES // 2
    sub = lax.broadcasted_iota(jnp.int32, (SUBLANES, LANES), 0)
    lane = lax.broadcasted_iota(jnp.int32, (SUBLANES, LANES), 1)
    gram = None
    for start in range(0, sources, 4):
        halves = [None, None]
        for index in range(4):
            place = (start + index) * MESSAGE_ROWS
            tail = x_ref[place + half_rows : place + MESSAGE_ROWS, :]
            gram = tail if gram is None else gram + tail
            piece = x_ref[place : place + half_rows, :]
            piece = jnp.concatenate([piece, piece], axis=0)
            piece = jnp.where(sub < half_rows, piece, pltpu.roll(piece, LANES // 2, 1))
            for half in range(2):
                shift = (index - half) % 4 * quarter
                moved = pltpu.roll(piece, shift, 1) if shift else piece
                if halves[half] is None:
                    halves[half] = moved
                else:
                    halves[half] = jnp.where(lane // quarter == index, moved, halves[half])
        for half in range(2):
            sketch_ref[
                half * SUBLANES : (half + 1) * SUBLANES, start * quarter : (start + 4) * quarter
            ] = halves[half]
    columns = gram_ref.shape[0]
    for half in range(2):
        for row in range(SUBLANES):
            line = gram[half : half + 1]
            line = pltpu.roll(line, LANES - row * columns, 1) if row else line
            gram_ref[half * SUBLANES + row : half * SUBLANES + row + 1, :] = line[:, :columns]


def finish(received, columns, sample_count):
    return pl.pallas_call(
        finish_kernel,
        out_shape=(
            jax.ShapeDtypeStruct((columns, sample_count), jnp.float32),
            jax.ShapeDtypeStruct((columns, columns), jnp.float32),
        ),
        in_specs=[pl.BlockSpec(memory_space=pltpu.VMEM)],
        out_specs=(pl.BlockSpec(memory_space=pltpu.VMEM),) * 2,
        compiler_params=pltpu.CompilerParams(vmem_limit_bytes=VMEM_LIMIT),
    )(received)


def exchange(values, axes):
    return lax.all_to_all(values, axes, split_axis=0, concat_axis=0, tiled=True)


def general_shards(matrix_slab, row_signs, sample_rows):
    columns, row_count = matrix_slab.shape
    sample_count = sample_rows.shape[0]
    devices = lax.axis_size("wide") * lax.axis_size("narrow")
    run_length = row_count // sample_count
    slice_rows = row_count // devices
    slice_runs = slice_rows // run_length
    values = jnp.swapaxes(local_transform(matrix_slab, row_signs), 0, 1)
    values = values.reshape(columns, devices, slice_rows)
    received = exchange(jnp.swapaxes(values, 0, 1), AXES)
    offsets = exchange(sample_rows.reshape(devices, slice_runs), AXES)
    mixed = jnp.einsum("ds,scr->dcr", sylvester(devices), received, precision=lax.Precision.HIGHEST)
    mixed = mixed.reshape(devices, columns, slice_runs, run_length)
    chosen = offsets[:, None, :, None] == lax.iota(jnp.int32, run_length)
    picked = jnp.sum(jnp.where(chosen, mixed, 0.0), axis=3)
    picked = picked * jnp.float32(1.0 / math.sqrt(row_count * devices))
    gram = jnp.einsum("dck,dek->ce", picked, picked, precision=lax.Precision.HIGHEST)
    gram = gram / jnp.float32(sample_count * devices)
    grams = jnp.broadcast_to(gram[None], (devices, columns, columns))
    back = exchange(jnp.concatenate([picked, grams], axis=2), AXES)
    sketch = jnp.swapaxes(back[:, :, :slice_runs], 0, 1).reshape(columns, devices * slice_runs)
    return sketch, jnp.sum(back[:, :, slice_runs:], axis=0)


def sliced_shards(matrix_slab, row_signs, sample_rows):
    columns, row_count = matrix_slab.shape
    sample_count = sample_rows.shape[0]
    devices = lax.axis_size(ORDER)
    run_length = row_count // sample_count
    sent = sliced_transform(matrix_slab, row_signs, sample_rows)
    received = exchange(sent.reshape(devices, -1), ORDER).reshape(sent.shape)
    scale = 1.0 / math.sqrt(row_count * devices)
    gram_scale = 1.0 / (sample_count * devices)
    picked = mix_and_pick(received, devices, run_length, scale, gram_scale)
    returned = exchange(picked.reshape(devices, -1), ORDER).reshape(picked.shape)
    return finish(returned, columns, sample_count)


def solution(mesh):
    wide, narrow = mesh.shape["wide"], mesh.shape["narrow"]
    axes, function = AXES, general_shards
    if wide * narrow == 32 and wide % 4 == 0:
        axes, function = SPLIT_AXES, sliced_shards
        mesh = jax.sharding.Mesh(mesh.devices.reshape(4, wide // 4, narrow), axes)
    in_specs = (P(None, axes), P(axes), P(axes))
    out_specs = (P(None, axes), P())
    return jax.shard_map(function, mesh=mesh, in_specs=in_specs, out_specs=out_specs, check_vma=False)
```

```python
import functools
import math

import jax
import jax.numpy as jnp
from jax import lax
from jax.experimental import pallas as pl
from jax.experimental.pallas import tpu as pltpu
from jax.sharding import PartitionSpec as P

LANES = 128
SUBLANES = 8
AXES = ("wide", "narrow")
SPLIT_AXES = ("line", "plane", "narrow")
ORDER = ("plane", "narrow", "line")
VMEM_LIMIT = 32 * 1024 * 1024
FETCHES = 4
MESSAGE_ROWS = 6


def butterfly(values):
    values = list(values)
    apart = 1
    while apart < len(values):
        for low in range(len(values)):
            if not low & apart:
                first, second = values[low], values[low | apart]
                values[low], values[low | apart] = first + second, first - second
        apart *= 2
    return values


def sylvester(order_size):
    rows = lax.broadcasted_iota(jnp.int32, (order_size, order_size), 0)
    cols = lax.broadcasted_iota(jnp.int32, (order_size, order_size), 1)
    common = rows & cols
    parity = jnp.zeros_like(common)
    for bit_pos in range(order_size.bit_length() - 1):
        parity = parity ^ (common >> bit_pos)
    return (1 - 2 * (parity & 1)).astype(jnp.float32)


def split_dot(values, table, parts=3):
    total = None
    for _ in range(parts):
        part = values.astype(jnp.bfloat16)
        values = values - part.astype(jnp.float32)
        product = jnp.dot(part, table, preferred_element_type=jnp.float32)
        total = product if total is None else total + product
    return total


def butterfly_steps(count):
    steps = []
    apart = 1
    while apart < count:
        radix = min(8, count // apart)
        for start in range(count):
            if start // apart % radix == 0:
                steps.append((apart, [start + apart * index for index in range(radix)]))
        apart *= radix
    return steps


def fetch_blocks(x_hbm, signs_hbm, out_ref, x_ref, signs_ref, arrived):
    blocks, columns, _ = out_ref.shape
    share = blocks // FETCHES
    fetches = [pltpu.make_async_copy(signs_hbm, signs_ref, arrived.at[0])]
    for piece in range(FETCHES):
        place = (slice(None), pl.ds(piece * share * LANES, share * LANES))
        fetches.append(
            pltpu.make_async_copy(x_hbm.at[place], x_ref.at[place], arrived.at[piece + 1])
        )
    for fetch in fetches:
        fetch.start()
    table = sylvester(LANES).astype(jnp.bfloat16)
    fetches[0].wait()
    for piece in range(FETCHES):
        fetches[piece + 1].wait()
        signed = []
        for block in range(piece * share, (piece + 1) * share):
            signs = signs_ref[block : block + 1, :].astype(jnp.float32)
            signed.append(x_ref[:, block * LANES : (block + 1) * LANES] * signs)
        mixed = split_dot(jnp.concatenate(signed, axis=0), table)
        out_ref[piece * share : (piece + 1) * share] = mixed.reshape(share, columns, LANES)


def local_kernel(x_hbm, signs_hbm, out_ref, x_ref, signs_ref, arrived):
    fetch_blocks(x_hbm, signs_hbm, out_ref, x_ref, signs_ref, arrived)
    for apart, places in butterfly_steps(out_ref.shape[0]):
        for place, value in zip(places, butterfly([out_ref[p] for p in places])):
            out_ref[place] = value


def sliced_kernel(
    x_hbm, signs_hbm, samples_hbm, final_ref, out_ref, x_ref, signs_ref, samples_ref, arrived, noted
):
    note = pltpu.make_async_copy(samples_hbm, samples_ref, noted)
    note.start()
    fetch_blocks(x_hbm, signs_hbm, out_ref, x_ref, signs_ref, arrived)
    blocks, columns, _ = out_ref.shape
    slices = blocks // 2
    rows = final_ref.shape[0] // slices
    note.wait()
    samples = samples_ref[...].astype(jnp.float32)
    per_row = slices // samples.shape[0]
    for turn in range(per_row):
        shift = LANES - turn * LANES // per_row
        turned = pltpu.roll(samples, shift, 1) if turn else samples
        for index in range(turn, slices, per_row):
            tail = (index + 1) * rows - 1
            final_ref[tail : tail + 1, :] = turned[index // per_row : index // per_row + 1]
    steps = butterfly_steps(blocks)
    last = steps[-1][0]
    for apart, places in steps:
        for place, value in zip(places, butterfly([out_ref[p] for p in places])):
            if apart == last:
                start = place // 2 * rows + place % 2 * columns
                final_ref[start : start + columns, :] = value
            else:
                out_ref[place] = value


def in_vmem(count):
    return [pl.BlockSpec(memory_space=pltpu.VMEM)] * count


def in_hbm(*arrays):
    return [pltpu.with_memory_space_constraint(array, pltpu.HBM) for array in arrays]


def fetch_scratch(matrix_slab, blocks):
    return [
        pltpu.VMEM(matrix_slab.shape, jnp.float32),
        pltpu.VMEM((blocks, LANES), jnp.int32),
    ]


def local_transform(matrix_slab, row_signs):
    columns, row_count = matrix_slab.shape
    blocks = row_count // LANES
    return pl.pallas_call(
        local_kernel,
        out_shape=jax.ShapeDtypeStruct((blocks, columns, LANES), jnp.float32),
        in_specs=[pl.BlockSpec(memory_space=pltpu.HBM)] * 2,
        out_specs=in_vmem(1)[0],
        scratch_shapes=[
            *fetch_scratch(matrix_slab, blocks),
            pltpu.SemaphoreType.DMA((FETCHES + 1,)),
        ],
        compiler_params=pltpu.CompilerParams(vmem_limit_bytes=VMEM_LIMIT),
    )(*in_hbm(matrix_slab, row_signs.reshape(blocks, LANES)))


def sliced_transform(matrix_slab, row_signs, sample_rows):
    columns, row_count = matrix_slab.shape
    blocks = row_count // LANES
    samples = sample_rows.reshape(-1, LANES)
    return pl.pallas_call(
        sliced_kernel,
        out_shape=jax.ShapeDtypeStruct((blocks // 2 * (2 * columns + 1), LANES), jnp.float32),
        in_specs=[pl.BlockSpec(memory_space=pltpu.HBM)] * 3,
        out_specs=in_vmem(1)[0],
        scratch_shapes=[
            pltpu.VMEM((blocks, columns, LANES), jnp.float32),
            *fetch_scratch(matrix_slab, blocks),
            pltpu.VMEM(samples.shape, jnp.int32),
            pltpu.SemaphoreType.DMA((FETCHES + 1,)),
            pltpu.SemaphoreType.DMA(()),
        ],
        compiler_params=pltpu.CompilerParams(vmem_limit_bytes=VMEM_LIMIT),
    )(*in_hbm(matrix_slab, row_signs.reshape(blocks, LANES), samples))


def mix_kernel(run_length, scale, gram_scale, x_ref, out_ref):
    devices = out_ref.shape[0] // MESSAGE_ROWS
    rows = x_ref.shape[0] // devices
    runs = LANES // run_length
    samples = jnp.concatenate(
        [x_ref[(s + 1) * rows - 1 : (s + 1) * rows, :] for s in range(devices)], axis=0
    ).astype(jnp.bfloat16)
    run_of = lax.broadcasted_iota(jnp.int32, (LANES, 2 * LANES), 0)
    row_of = lax.broadcasted_iota(jnp.int32, (LANES, 2 * LANES), 1)
    spread = jnp.where(row_of // run_length == run_of, 1.0, 0.0).astype(jnp.bfloat16)
    offsets = jnp.dot(samples, spread, preferred_element_type=jnp.float32)
    own = lax.broadcasted_iota(jnp.int32, offsets.shape, 1) % run_length
    mask = jnp.where(offsets == own.astype(jnp.float32), scale, 0.0)
    picked = []
    for part in range(4):
        block = part // 2
        starts = [s * rows + part * SUBLANES for s in range(devices)]
        mixed = butterfly([x_ref[start : start + SUBLANES, :] for start in starts])
        picked.append(
            jnp.concatenate(
                [
                    mixed[d] * mask[d : d + 1, block * LANES : (block + 1) * LANES]
                    for d in range(devices)
                ],
                axis=0,
            )
        )
    quarter = 2 * runs
    row = lax.broadcasted_iota(jnp.int32, (4 * LANES, 2 * LANES), 0)
    lane = lax.broadcasted_iota(jnp.int32, (4 * LANES, 2 * LANES), 1)
    in_block, in_half = row // (2 * LANES), row // LANES % 2
    group = lane // quarter
    half_here = jnp.where(group >= 6, 7 - group, group % 2)
    target = in_block * runs + row % LANES // run_length
    place = jnp.where((half_here == in_half) & (lane % quarter == target), 1.0, 0.0)
    gathered = split_dot(jnp.concatenate(picked, axis=1), place.astype(jnp.bfloat16), 2)
    straight, crossed = gathered[:, :LANES], gathered[:, LANES:]
    totals = []
    for turn in range(SUBLANES):
        total = None
        for d in range(devices):
            one = straight[d * SUBLANES : (d + 1) * SUBLANES]
            two = crossed[d * SUBLANES : (d + 1) * SUBLANES]
            if turn:
                two = pltpu.roll(two, SUBLANES - turn, 0)
            total = one * two if total is None else total + one * two
        totals.append(total)
    row = lax.broadcasted_iota(jnp.int32, (LANES, 4 * LANES), 0)
    lane = lax.broadcasted_iota(jnp.int32, (LANES, 4 * LANES), 1)
    together = jnp.where(row // quarter == lane // LANES, 1.0, 0.0).astype(jnp.bfloat16)
    sums = split_dot(jnp.concatenate(totals, axis=0), together) * gram_scale
    sub = lax.broadcasted_iota(jnp.int32, (SUBLANES, LANES), 0)
    lane = lax.broadcasted_iota(jnp.int32, (SUBLANES, LANES), 1)
    first, second = [jnp.zeros((SUBLANES, LANES), jnp.float32)] * 2
    for turn in range(SUBLANES):
        here = sums[turn * SUBLANES : (turn + 1) * SUBLANES]
        quarters = [here[:, q * LANES : (q + 1) * LANES] for q in range(4)]
        mine = lane % SUBLANES == (sub + turn) % SUBLANES
        left = lane // SUBLANES % 2 == 0
        first = jnp.where(mine, jnp.where(left, quarters[0], quarters[2]), first)
        second = jnp.where(mine, jnp.where(left, quarters[3], quarters[1]), second)
    in_place = lane // (2 * SUBLANES) == sub
    gram = jnp.concatenate(
        [jnp.sum(jnp.where(in_place, part, 0.0), axis=0, keepdims=True) for part in (first, second)],
        axis=0,
    )
    half = SUBLANES // 2
    lane = lax.broadcasted_iota(jnp.int32, (half, LANES), 1)
    for d in range(devices):
        one = straight[d * SUBLANES : (d + 1) * SUBLANES]
        start = d * MESSAGE_ROWS
        out_ref[start : start + half, :] = jnp.where(lane < LANES // 2, one[:half], one[half:])
        out_ref[start + half : start + MESSAGE_ROWS, :] = gram


def mix_and_pick(received, devices, run_length, scale, gram_scale):
    return pl.pallas_call(
        functools.partial(mix_kernel, run_length, scale, gram_scale),
        out_shape=jax.ShapeDtypeStruct((devices * MESSAGE_ROWS, LANES), jnp.float32),
        in_specs=in_vmem(1),
        out_specs=in_vmem(1)[0],
        compiler_params=pltpu.CompilerParams(vmem_limit_bytes=VMEM_LIMIT),
    )(received)


def finish_kernel(x_ref, sketch_ref, gram_ref):
    sources = x_ref.shape[0] // MESSAGE_ROWS
    quarter = LANES // 4
    half_rows = SUBLANES // 2
    sub = lax.broadcasted_iota(jnp.int32, (SUBLANES, LANES), 0)
    lane = lax.broadcasted_iota(jnp.int32, (SUBLANES, LANES), 1)
    gram = None
    for start in range(0, sources, 4):
        halves = [None, None]
        for index in range(4):
            place = (start + index) * MESSAGE_ROWS
            tail = x_ref[place + half_rows : place + MESSAGE_ROWS, :]
            gram = tail if gram is None else gram + tail
            piece = x_ref[place : place + half_rows, :]
            piece = jnp.concatenate([piece, piece], axis=0)
            piece = jnp.where(sub < half_rows, piece, pltpu.roll(piece, LANES // 2, 1))
            for half in range(2):
                shift = (index - half) % 4 * quarter
                moved = pltpu.roll(piece, shift, 1) if shift else piece
                if halves[half] is None:
                    halves[half] = moved
                else:
                    halves[half] = jnp.where(lane // quarter == index, moved, halves[half])
        for half in range(2):
            sketch_ref[
                half * SUBLANES : (half + 1) * SUBLANES, start * quarter : (start + 4) * quarter
            ] = halves[half]
    columns = gram_ref.shape[0]
    for half in range(2):
        for row in range(SUBLANES):
            line = gram[half : half + 1]
            line = pltpu.roll(line, LANES - row * columns, 1) if row else line
            gram_ref[half * SUBLANES + row : half * SUBLANES + row + 1, :] = line[:, :columns]


def finish(received, columns, sample_count):
    return pl.pallas_call(
        finish_kernel,
        out_shape=(
            jax.ShapeDtypeStruct((columns, sample_count), jnp.float32),
            jax.ShapeDtypeStruct((columns, columns), jnp.float32),
        ),
        in_specs=[pl.BlockSpec(memory_space=pltpu.VMEM)],
        out_specs=(pl.BlockSpec(memory_space=pltpu.VMEM),) * 2,
        compiler_params=pltpu.CompilerParams(vmem_limit_bytes=VMEM_LIMIT),
    )(received)


def exchange(values, axes):
    return lax.all_to_all(values, axes, split_axis=0, concat_axis=0, tiled=True)


def general_shards(matrix_slab, row_signs, sample_rows):
    columns, row_count = matrix_slab.shape
    sample_count = sample_rows.shape[0]
    devices = lax.axis_size("wide") * lax.axis_size("narrow")
    run_length = row_count // sample_count
    slice_rows = row_count // devices
    slice_runs = slice_rows // run_length
    values = jnp.swapaxes(local_transform(matrix_slab, row_signs), 0, 1)
    values = values.reshape(columns, devices, slice_rows)
    received = exchange(jnp.swapaxes(values, 0, 1), AXES)
    offsets = exchange(sample_rows.reshape(devices, slice_runs), AXES)
    mixed = jnp.einsum("ds,scr->dcr", sylvester(devices), received, precision=lax.Precision.HIGHEST)
    mixed = mixed.reshape(devices, columns, slice_runs, run_length)
    chosen = offsets[:, None, :, None] == lax.iota(jnp.int32, run_length)
    picked = jnp.sum(jnp.where(chosen, mixed, 0.0), axis=3)
    picked = picked * jnp.float32(1.0 / math.sqrt(row_count * devices))
    gram = jnp.einsum("dck,dek->ce", picked, picked, precision=lax.Precision.HIGHEST)
    gram = gram / jnp.float32(sample_count * devices)
    grams = jnp.broadcast_to(gram[None], (devices, columns, columns))
    back = exchange(jnp.concatenate([picked, grams], axis=2), AXES)
    sketch = jnp.swapaxes(back[:, :, :slice_runs], 0, 1).reshape(columns, devices * slice_runs)
    return sketch, jnp.sum(back[:, :, slice_runs:], axis=0)


def sliced_shards(matrix_slab, row_signs, sample_rows):
    columns, row_count = matrix_slab.shape
    sample_count = sample_rows.shape[0]
    devices = lax.axis_size(ORDER)
    run_length = row_count // sample_count
    sent = sliced_transform(matrix_slab, row_signs, sample_rows)
    received = exchange(sent.reshape(devices, -1), ORDER).reshape(sent.shape)
    scale = 1.0 / math.sqrt(row_count * devices)
    gram_scale = 1.0 / (sample_count * devices)
    picked = mix_and_pick(received, devices, run_length, scale, gram_scale)
    returned = exchange(picked.reshape(devices, -1), ORDER).reshape(picked.shape)
    return finish(returned, columns, sample_count)


def solution(mesh):
    wide, narrow = mesh.shape["wide"], mesh.shape["narrow"]
    axes, function = AXES, general_shards
    if wide * narrow == 32 and wide % 4 == 0:
        axes, function = SPLIT_AXES, sliced_shards
        mesh = jax.sharding.Mesh(mesh.devices.reshape(4, wide // 4, narrow), axes)
    in_specs = (P(None, axes), P(axes), P(axes))
    out_specs = (P(None, axes), P())
    return jax.shard_map(function, mesh=mesh, in_specs=in_specs, out_specs=out_specs, check_vma=False)
```

```python
import functools
import math

import jax
import jax.numpy as jnp
from jax import lax
from jax.experimental import pallas as pl
from jax.experimental.pallas import tpu as pltpu
from jax.sharding import PartitionSpec as P

LANES = 128
SUBLANES = 8
AXES = ("wide", "narrow")
SPLIT_AXES = ("line", "plane", "narrow")
ORDER = ("plane", "narrow", "line")
VMEM_LIMIT = 32 * 1024 * 1024
MESSAGE_ROWS = 6


def butterfly(values):
    values = list(values)
    apart = 1
    while apart < len(values):
        for low in range(len(values)):
            if not low & apart:
                first, second = values[low], values[low | apart]
                values[low], values[low | apart] = first + second, first - second
        apart *= 2
    return values


def sylvester(order_size):
    rows = lax.broadcasted_iota(jnp.int32, (order_size, order_size), 0)
    cols = lax.broadcasted_iota(jnp.int32, (order_size, order_size), 1)
    common = rows & cols
    parity = jnp.zeros_like(common)
    for bit_pos in range(order_size.bit_length() - 1):
        parity = parity ^ (common >> bit_pos)
    return (1 - 2 * (parity & 1)).astype(jnp.float32)


def split_dot(values, table, parts=3):
    total = None
    for _ in range(parts):
        part = values.astype(jnp.bfloat16)
        values = values - part.astype(jnp.float32)
        product = jnp.dot(part, table, preferred_element_type=jnp.float32)
        total = product if total is None else total + product
    return total


def butterfly_steps(count):
    steps = []
    apart = 1
    while apart < count:
        radix = min(8, count // apart)
        for start in range(count):
            if start // apart % radix == 0:
                steps.append((apart, [start + apart * index for index in range(radix)]))
        apart *= radix
    return steps


def fetch_blocks(x_hbm, signs_hbm, out_ref, x_ref, signs_ref, arrived):
    blocks, columns, _ = out_ref.shape
    fetches = [pltpu.make_async_copy(signs_hbm, signs_ref, arrived.at[0])]
    places = [pl.ds(start, SUBLANES) for start in range(0, columns, SUBLANES)]
    for index, place in enumerate(places):
        fetches.append(
            pltpu.make_async_copy(x_hbm.at[place], x_ref.at[place], arrived.at[index + 1])
        )
    for fetch in fetches:
        fetch.start()
    table = sylvester(LANES).astype(jnp.bfloat16)
    fetches[0].wait()
    for index, place in enumerate(places):
        fetches[index + 1].wait()
        signed = []
        for block in range(blocks):
            signs = signs_ref[block : block + 1, :].astype(jnp.float32)
            signed.append(x_ref[place, block * LANES : (block + 1) * LANES] * signs)
        mixed = split_dot(jnp.concatenate(signed, axis=0), table)
        out_ref[:, place, :] = mixed.reshape(blocks, SUBLANES, LANES)


def local_kernel(x_hbm, signs_hbm, out_ref, x_ref, signs_ref, arrived):
    fetch_blocks(x_hbm, signs_hbm, out_ref, x_ref, signs_ref, arrived)
    for apart, places in butterfly_steps(out_ref.shape[0]):
        for place, value in zip(places, butterfly([out_ref[p] for p in places])):
            out_ref[place] = value


def sliced_kernel(
    x_hbm, signs_hbm, samples_hbm, final_ref, out_ref, x_ref, signs_ref, samples_ref, arrived, noted
):
    note = pltpu.make_async_copy(samples_hbm, samples_ref, noted)
    note.start()
    fetch_blocks(x_hbm, signs_hbm, out_ref, x_ref, signs_ref, arrived)
    blocks, columns, _ = out_ref.shape
    slices = blocks // 2
    rows = final_ref.shape[0] // slices
    note.wait()
    samples = samples_ref[...].astype(jnp.float32)
    per_row = slices // samples.shape[0]
    for turn in range(per_row):
        shift = LANES - turn * LANES // per_row
        turned = pltpu.roll(samples, shift, 1) if turn else samples
        for index in range(turn, slices, per_row):
            tail = (index + 1) * rows - 1
            final_ref[tail : tail + 1, :] = turned[index // per_row : index // per_row + 1]
    steps = butterfly_steps(blocks)
    last = steps[-1][0]
    for apart, places in steps:
        for place, value in zip(places, butterfly([out_ref[p] for p in places])):
            if apart == last:
                start = place // 2 * rows + place % 2 * columns
                final_ref[start : start + columns, :] = value
            else:
                out_ref[place] = value


def in_vmem(count):
    return [pl.BlockSpec(memory_space=pltpu.VMEM)] * count


def in_hbm(*arrays):
    return [pltpu.with_memory_space_constraint(array, pltpu.HBM) for array in arrays]


def fetch_scratch(matrix_slab, blocks):
    return [
        pltpu.VMEM(matrix_slab.shape, jnp.float32),
        pltpu.VMEM((blocks, LANES), jnp.int32),
    ]


def local_transform(matrix_slab, row_signs):
    columns, row_count = matrix_slab.shape
    blocks = row_count // LANES
    return pl.pallas_call(
        local_kernel,
        out_shape=jax.ShapeDtypeStruct((blocks, columns, LANES), jnp.float32),
        in_specs=[pl.BlockSpec(memory_space=pltpu.HBM)] * 2,
        out_specs=in_vmem(1)[0],
        scratch_shapes=[
            *fetch_scratch(matrix_slab, blocks),
            pltpu.SemaphoreType.DMA((columns // SUBLANES + 1,)),
        ],
        compiler_params=pltpu.CompilerParams(vmem_limit_bytes=VMEM_LIMIT),
    )(*in_hbm(matrix_slab, row_signs.reshape(blocks, LANES)))


def sliced_transform(matrix_slab, row_signs, sample_rows):
    columns, row_count = matrix_slab.shape
    blocks = row_count // LANES
    samples = sample_rows.reshape(-1, LANES)
    return pl.pallas_call(
        sliced_kernel,
        out_shape=jax.ShapeDtypeStruct((blocks // 2 * (2 * columns + 1), LANES), jnp.float32),
        in_specs=[pl.BlockSpec(memory_space=pltpu.HBM)] * 3,
        out_specs=in_vmem(1)[0],
        scratch_shapes=[
            pltpu.VMEM((blocks, columns, LANES), jnp.float32),
            *fetch_scratch(matrix_slab, blocks),
            pltpu.VMEM(samples.shape, jnp.int32),
            pltpu.SemaphoreType.DMA((columns // SUBLANES + 1,)),
            pltpu.SemaphoreType.DMA(()),
        ],
        compiler_params=pltpu.CompilerParams(vmem_limit_bytes=VMEM_LIMIT),
    )(*in_hbm(matrix_slab, row_signs.reshape(blocks, LANES), samples))


def mix_kernel(run_length, scale, gram_scale, x_ref, out_ref):
    devices = out_ref.shape[0] // MESSAGE_ROWS
    rows = x_ref.shape[0] // devices
    runs = LANES // run_length
    samples = jnp.concatenate(
        [x_ref[(s + 1) * rows - 1 : (s + 1) * rows, :] for s in range(devices)], axis=0
    ).astype(jnp.bfloat16)
    run_of = lax.broadcasted_iota(jnp.int32, (LANES, 2 * LANES), 0)
    row_of = lax.broadcasted_iota(jnp.int32, (LANES, 2 * LANES), 1)
    spread = jnp.where(row_of // run_length == run_of, 1.0, 0.0).astype(jnp.bfloat16)
    offsets = jnp.dot(samples, spread, preferred_element_type=jnp.float32)
    own = lax.broadcasted_iota(jnp.int32, offsets.shape, 1) % run_length
    mask = jnp.where(offsets == own.astype(jnp.float32), scale, 0.0)
    picked = []
    for part in range(4):
        block = part // 2
        starts = [s * rows + part * SUBLANES for s in range(devices)]
        mixed = butterfly([x_ref[start : start + SUBLANES, :] for start in starts])
        picked.append(
            jnp.concatenate(
                [
                    mixed[d] * mask[d : d + 1, block * LANES : (block + 1) * LANES]
                    for d in range(devices)
                ],
                axis=0,
            )
        )
    quarter = 2 * runs
    row = lax.broadcasted_iota(jnp.int32, (LANES, LANES), 0)
    lane = lax.broadcasted_iota(jnp.int32, (LANES, LANES), 1)
    pattern = jnp.where(row // run_length == lane % runs, 1.0, 0.0)
    lane = lax.broadcasted_iota(jnp.int32, (1, LANES), 1)
    group = lane // quarter
    place = []
    for part in range(4):
        block, half = part // 2, part % 2
        here = lane // runs % 2 == block
        sides = [group % 2, jnp.where(group < 2, group, 3 - group)]
        masks = [jnp.where(here & (side == half), 1.0, 0.0) for side in sides]
        place.append(jnp.concatenate([(pattern * mask).astype(jnp.bfloat16) for mask in masks], axis=1))
    gathered = split_dot(jnp.concatenate(picked, axis=1), jnp.concatenate(place, axis=0), 2)
    straight, crossed = gathered[:, :LANES], gathered[:, LANES:]
    turns = SUBLANES // 2 + 1
    totals = []
    for turn in range(turns):
        total = None
        for d in range(devices):
            one = straight[d * SUBLANES : (d + 1) * SUBLANES]
            two = crossed[d * SUBLANES : (d + 1) * SUBLANES]
            if turn:
                two = pltpu.roll(two, SUBLANES - turn, 0)
            total = one * two if total is None else total + one * two
        totals.append(total)
    from_quarter = row // quarter
    together = [jnp.where(from_quarter == q, 1.0, 0.0).astype(jnp.bfloat16) for q in range(4)]
    sums = split_dot(jnp.concatenate(totals, axis=0), jnp.concatenate(together, axis=1)) * gram_scale
    sub = lax.broadcasted_iota(jnp.int32, (SUBLANES, LANES), 0)
    lane = lax.broadcasted_iota(jnp.int32, (SUBLANES, LANES), 1)
    first, second = [jnp.zeros((SUBLANES, LANES), jnp.float32)] * 2
    for turn in range(SUBLANES):
        known = min(turn, SUBLANES - turn)
        here = sums[known * SUBLANES : (known + 1) * SUBLANES]
        quarters = [here[:, q * LANES : (q + 1) * LANES] for q in range(4)]
        if known != turn:
            quarters = [pltpu.roll(quarters[q], known, 0) for q in (0, 1, 3, 2)]
        mine = lane % SUBLANES == (sub + turn) % SUBLANES
        left = lane // SUBLANES % 2 == 0
        first = jnp.where(mine, jnp.where(left, quarters[0], quarters[2]), first)
        second = jnp.where(mine, jnp.where(left, quarters[3], quarters[1]), second)
    in_place = lane // (2 * SUBLANES) == sub
    gram = jnp.concatenate(
        [jnp.sum(jnp.where(in_place, part, 0.0), axis=0, keepdims=True) for part in (first, second)],
        axis=0,
    )
    half = SUBLANES // 2
    lane = lax.broadcasted_iota(jnp.int32, (half, LANES), 1)
    for d in range(devices):
        one = straight[d * SUBLANES : (d + 1) * SUBLANES]
        start = d * MESSAGE_ROWS
        out_ref[start : start + half, :] = jnp.where(lane < LANES // 2, one[:half], one[half:])
        out_ref[start + half : start + MESSAGE_ROWS, :] = gram


def mix_and_pick(received, devices, run_length, scale, gram_scale):
    return pl.pallas_call(
        functools.partial(mix_kernel, run_length, scale, gram_scale),
        out_shape=jax.ShapeDtypeStruct((devices * MESSAGE_ROWS, LANES), jnp.float32),
        in_specs=in_vmem(1),
        out_specs=in_vmem(1)[0],
        compiler_params=pltpu.CompilerParams(vmem_limit_bytes=VMEM_LIMIT),
    )(received)


def finish_kernel(x_ref, sketch_ref, gram_ref):
    sources = x_ref.shape[0] // MESSAGE_ROWS
    quarter = LANES // 4
    half_rows = SUBLANES // 2
    sub = lax.broadcasted_iota(jnp.int32, (SUBLANES, LANES), 0)
    lane = lax.broadcasted_iota(jnp.int32, (SUBLANES, LANES), 1)
    gram = None
    for start in range(0, sources, 4):
        halves = [None, None]
        for index in range(4):
            place = (start + index) * MESSAGE_ROWS
            tail = x_ref[place + half_rows : place + MESSAGE_ROWS, :]
            gram = tail if gram is None else gram + tail
            piece = x_ref[place : place + half_rows, :]
            piece = jnp.concatenate([piece, piece], axis=0)
            piece = jnp.where(sub < half_rows, piece, pltpu.roll(piece, LANES // 2, 1))
            for half in range(2):
                shift = (index - half) % 4 * quarter
                moved = pltpu.roll(piece, shift, 1) if shift else piece
                if halves[half] is None:
                    halves[half] = moved
                else:
                    halves[half] = jnp.where(lane // quarter == index, moved, halves[half])
        for half in range(2):
            sketch_ref[
                half * SUBLANES : (half + 1) * SUBLANES, start * quarter : (start + 4) * quarter
            ] = halves[half]
    columns = gram_ref.shape[0]
    for half in range(2):
        for row in range(SUBLANES):
            line = gram[half : half + 1]
            line = pltpu.roll(line, LANES - row * columns, 1) if row else line
            gram_ref[half * SUBLANES + row : half * SUBLANES + row + 1, :] = line[:, :columns]


def finish(received, columns, sample_count):
    return pl.pallas_call(
        finish_kernel,
        out_shape=(
            jax.ShapeDtypeStruct((columns, sample_count), jnp.float32),
            jax.ShapeDtypeStruct((columns, columns), jnp.float32),
        ),
        in_specs=[pl.BlockSpec(memory_space=pltpu.VMEM)],
        out_specs=(pl.BlockSpec(memory_space=pltpu.VMEM),) * 2,
        compiler_params=pltpu.CompilerParams(vmem_limit_bytes=VMEM_LIMIT),
    )(received)


def exchange(values, axes):
    return lax.all_to_all(values, axes, split_axis=0, concat_axis=0, tiled=True)


def general_shards(matrix_slab, row_signs, sample_rows):
    columns, row_count = matrix_slab.shape
    sample_count = sample_rows.shape[0]
    devices = lax.axis_size("wide") * lax.axis_size("narrow")
    run_length = row_count // sample_count
    slice_rows = row_count // devices
    slice_runs = slice_rows // run_length
    values = jnp.swapaxes(local_transform(matrix_slab, row_signs), 0, 1)
    values = values.reshape(columns, devices, slice_rows)
    received = exchange(jnp.swapaxes(values, 0, 1), AXES)
    offsets = exchange(sample_rows.reshape(devices, slice_runs), AXES)
    mixed = jnp.einsum("ds,scr->dcr", sylvester(devices), received, precision=lax.Precision.HIGHEST)
    mixed = mixed.reshape(devices, columns, slice_runs, run_length)
    chosen = offsets[:, None, :, None] == lax.iota(jnp.int32, run_length)
    picked = jnp.sum(jnp.where(chosen, mixed, 0.0), axis=3)
    picked = picked * jnp.float32(1.0 / math.sqrt(row_count * devices))
    gram = jnp.einsum("dck,dek->ce", picked, picked, precision=lax.Precision.HIGHEST)
    gram = gram / jnp.float32(sample_count * devices)
    grams = jnp.broadcast_to(gram[None], (devices, columns, columns))
    back = exchange(jnp.concatenate([picked, grams], axis=2), AXES)
    sketch = jnp.swapaxes(back[:, :, :slice_runs], 0, 1).reshape(columns, devices * slice_runs)
    return sketch, jnp.sum(back[:, :, slice_runs:], axis=0)


def sliced_shards(matrix_slab, row_signs, sample_rows):
    columns, row_count = matrix_slab.shape
    sample_count = sample_rows.shape[0]
    devices = lax.axis_size(ORDER)
    run_length = row_count // sample_count
    sent = sliced_transform(matrix_slab, row_signs, sample_rows)
    received = exchange(sent.reshape(devices, -1), ORDER).reshape(sent.shape)
    scale = 1.0 / math.sqrt(row_count * devices)
    gram_scale = 1.0 / (sample_count * devices)
    picked = mix_and_pick(received, devices, run_length, scale, gram_scale)
    returned = exchange(picked.reshape(devices, -1), ORDER).reshape(picked.shape)
    return finish(returned, columns, sample_count)


def solution(mesh):
    wide, narrow = mesh.shape["wide"], mesh.shape["narrow"]
    axes, function = AXES, general_shards
    if wide * narrow == 32 and wide % 4 == 0:
        axes, function = SPLIT_AXES, sliced_shards
        mesh = jax.sharding.Mesh(mesh.devices.reshape(4, wide // 4, narrow), axes)
    in_specs = (P(None, axes), P(axes), P(axes))
    out_specs = (P(None, axes), P())
    return jax.shard_map(function, mesh=mesh, in_specs=in_specs, out_specs=out_specs, check_vma=False)
```

```python
import functools
import math

import jax
import jax.numpy as jnp
from jax import lax
from jax.experimental import pallas as pl
from jax.experimental.pallas import tpu as pltpu
from jax.sharding import PartitionSpec as P

LANES = 128
SUBLANES = 8
AXES = ("wide", "narrow")
SPLIT_AXES = ("line", "plane", "narrow")
ORDER = ("narrow", "plane", "line")
VMEM_LIMIT = 32 * 1024 * 1024
MESSAGE_ROWS = 6


def butterfly(values):
    values = list(values)
    apart = 1
    while apart < len(values):
        for low in range(len(values)):
            if not low & apart:
                first, second = values[low], values[low | apart]
                values[low], values[low | apart] = first + second, first - second
        apart *= 2
    return values


def sylvester(order_size):
    rows = lax.broadcasted_iota(jnp.int32, (order_size, order_size), 0)
    cols = lax.broadcasted_iota(jnp.int32, (order_size, order_size), 1)
    common = rows & cols
    parity = jnp.zeros_like(common)
    for bit_pos in range(order_size.bit_length() - 1):
        parity = parity ^ (common >> bit_pos)
    return (1 - 2 * (parity & 1)).astype(jnp.float32)


def split_dot(values, table, parts=3):
    total = None
    for _ in range(parts):
        part = values.astype(jnp.bfloat16)
        values = values - part.astype(jnp.float32)
        product = jnp.dot(part, table, preferred_element_type=jnp.float32)
        total = product if total is None else total + product
    return total


def butterfly_steps(count):
    steps = []
    apart = 1
    while apart < count:
        radix = min(8, count // apart)
        for start in range(count):
            if start // apart % radix == 0:
                steps.append((apart, [start + apart * index for index in range(radix)]))
        apart *= radix
    return steps


def fetch_blocks(x_hbm, signs_hbm, out_ref, x_ref, signs_ref, arrived):
    blocks, columns, _ = out_ref.shape
    fetches = [pltpu.make_async_copy(signs_hbm, signs_ref, arrived.at[0])]
    places = [pl.ds(start, SUBLANES) for start in range(0, columns, SUBLANES)]
    for index, place in enumerate(places):
        fetches.append(
            pltpu.make_async_copy(x_hbm.at[place], x_ref.at[place], arrived.at[index + 1])
        )
    for fetch in fetches:
        fetch.start()
    table = sylvester(LANES).astype(jnp.bfloat16)
    fetches[0].wait()
    for index, place in enumerate(places):
        fetches[index + 1].wait()
        signed = []
        for block in range(blocks):
            signs = signs_ref[block : block + 1, :].astype(jnp.float32)
            signed.append(x_ref[place, block * LANES : (block + 1) * LANES] * signs)
        mixed = split_dot(jnp.concatenate(signed, axis=0), table)
        out_ref[:, place, :] = mixed.reshape(blocks, SUBLANES, LANES)


def local_kernel(x_hbm, signs_hbm, out_ref, x_ref, signs_ref, arrived):
    fetch_blocks(x_hbm, signs_hbm, out_ref, x_ref, signs_ref, arrived)
    for apart, places in butterfly_steps(out_ref.shape[0]):
        for place, value in zip(places, butterfly([out_ref[p] for p in places])):
            out_ref[place] = value


def sliced_kernel(
    x_hbm, signs_hbm, samples_hbm, final_ref, out_ref, x_ref, signs_ref, samples_ref, arrived, noted
):
    note = pltpu.make_async_copy(samples_hbm, samples_ref, noted)
    note.start()
    fetch_blocks(x_hbm, signs_hbm, out_ref, x_ref, signs_ref, arrived)
    blocks, columns, _ = out_ref.shape
    slices = blocks // 2
    rows = final_ref.shape[0] // slices
    note.wait()
    samples = samples_ref[...].astype(jnp.float32)
    per_row = slices // samples.shape[0]
    for turn in range(per_row):
        shift = LANES - turn * LANES // per_row
        turned = pltpu.roll(samples, shift, 1) if turn else samples
        for index in range(turn, slices, per_row):
            tail = (index + 1) * rows - 1
            final_ref[tail : tail + 1, :] = turned[index // per_row : index // per_row + 1]
    steps = butterfly_steps(blocks)
    last = steps[-1][0]
    for apart, places in steps:
        for place, value in zip(places, butterfly([out_ref[p] for p in places])):
            if apart == last:
                start = place // 2 * rows + place % 2 * columns
                final_ref[start : start + columns, :] = value
            else:
                out_ref[place] = value


def in_vmem(count):
    return [pl.BlockSpec(memory_space=pltpu.VMEM)] * count


def in_hbm(*arrays):
    return [pltpu.with_memory_space_constraint(array, pltpu.HBM) for array in arrays]


def fetch_scratch(matrix_slab, blocks):
    return [
        pltpu.VMEM(matrix_slab.shape, jnp.float32),
        pltpu.VMEM((blocks, LANES), jnp.int32),
    ]


def local_transform(matrix_slab, row_signs):
    columns, row_count = matrix_slab.shape
    blocks = row_count // LANES
    return pl.pallas_call(
        local_kernel,
        out_shape=jax.ShapeDtypeStruct((blocks, columns, LANES), jnp.float32),
        in_specs=[pl.BlockSpec(memory_space=pltpu.HBM)] * 2,
        out_specs=in_vmem(1)[0],
        scratch_shapes=[
            *fetch_scratch(matrix_slab, blocks),
            pltpu.SemaphoreType.DMA((columns // SUBLANES + 1,)),
        ],
        compiler_params=pltpu.CompilerParams(vmem_limit_bytes=VMEM_LIMIT),
    )(*in_hbm(matrix_slab, row_signs.reshape(blocks, LANES)))


def sliced_transform(matrix_slab, row_signs, sample_rows):
    columns, row_count = matrix_slab.shape
    blocks = row_count // LANES
    samples = sample_rows.reshape(-1, LANES)
    return pl.pallas_call(
        sliced_kernel,
        out_shape=jax.ShapeDtypeStruct((blocks // 2 * (2 * columns + 1), LANES), jnp.float32),
        in_specs=[pl.BlockSpec(memory_space=pltpu.HBM)] * 3,
        out_specs=in_vmem(1)[0],
        scratch_shapes=[
            pltpu.VMEM((blocks, columns, LANES), jnp.float32),
            *fetch_scratch(matrix_slab, blocks),
            pltpu.VMEM(samples.shape, jnp.int32),
            pltpu.SemaphoreType.DMA((columns // SUBLANES + 1,)),
            pltpu.SemaphoreType.DMA(()),
        ],
        compiler_params=pltpu.CompilerParams(vmem_limit_bytes=VMEM_LIMIT),
    )(*in_hbm(matrix_slab, row_signs.reshape(blocks, LANES), samples))


def mix_kernel(run_length, scale, gram_scale, x_ref, out_ref):
    devices = out_ref.shape[0] // MESSAGE_ROWS
    rows = x_ref.shape[0] // devices
    runs = LANES // run_length
    samples = jnp.concatenate(
        [x_ref[(s + 1) * rows - 1 : (s + 1) * rows, :] for s in range(devices)], axis=0
    ).astype(jnp.bfloat16)
    run_of = lax.broadcasted_iota(jnp.int32, (LANES, 2 * LANES), 0)
    row_of = lax.broadcasted_iota(jnp.int32, (LANES, 2 * LANES), 1)
    spread = jnp.where(row_of // run_length == run_of, 1.0, 0.0).astype(jnp.bfloat16)
    offsets = jnp.dot(samples, spread, preferred_element_type=jnp.float32)
    own = lax.broadcasted_iota(jnp.int32, offsets.shape, 1) % run_length
    mask = jnp.where(offsets == own.astype(jnp.float32), scale, 0.0)
    picked = []
    for part in range(4):
        block = part // 2
        starts = [s * rows + part * SUBLANES for s in range(devices)]
        mixed = butterfly([x_ref[start : start + SUBLANES, :] for start in starts])
        picked.append(
            jnp.concatenate(
                [
                    mixed[d] * mask[d : d + 1, block * LANES : (block + 1) * LANES]
                    for d in range(devices)
                ],
                axis=0,
            )
        )
    quarter = 2 * runs
    row = lax.broadcasted_iota(jnp.int32, (LANES, LANES), 0)
    lane = lax.broadcasted_iota(jnp.int32, (LANES, LANES), 1)
    pattern = jnp.where(row // run_length == lane % runs, 1.0, 0.0)
    lane = lax.broadcasted_iota(jnp.int32, (1, LANES), 1)
    group = lane // quarter
    place = []
    for part in range(4):
        block, half = part // 2, part % 2
        here = lane // runs % 2 == block
        sides = [group % 2, jnp.where(group < 2, group, 3 - group)]
        masks = [jnp.where(here & (side == half), 1.0, 0.0) for side in sides]
        place.append(jnp.concatenate([(pattern * mask).astype(jnp.bfloat16) for mask in masks], axis=1))
    gathered = split_dot(jnp.concatenate(picked, axis=1), jnp.concatenate(place, axis=0), 2)
    straight, crossed = gathered[:, :LANES], gathered[:, LANES:]
    turns = SUBLANES // 2 + 1
    totals = []
    for turn in range(turns):
        total = None
        for d in range(devices):
            one = straight[d * SUBLANES : (d + 1) * SUBLANES]
            two = crossed[d * SUBLANES : (d + 1) * SUBLANES]
            if turn:
                two = pltpu.roll(two, SUBLANES - turn, 0)
            total = one * two if total is None else total + one * two
        totals.append(total)
    from_quarter = row // quarter
    together = [jnp.where(from_quarter == q, 1.0, 0.0).astype(jnp.bfloat16) for q in range(4)]
    sums = split_dot(jnp.concatenate(totals, axis=0), jnp.concatenate(together, axis=1)) * gram_scale
    sub = lax.broadcasted_iota(jnp.int32, (SUBLANES, LANES), 0)
    lane = lax.broadcasted_iota(jnp.int32, (SUBLANES, LANES), 1)
    first, second = [jnp.zeros((SUBLANES, LANES), jnp.float32)] * 2
    for turn in range(SUBLANES):
        known = min(turn, SUBLANES - turn)
        here = sums[known * SUBLANES : (known + 1) * SUBLANES]
        quarters = [here[:, q * LANES : (q + 1) * LANES] for q in range(4)]
        if known != turn:
            quarters = [pltpu.roll(quarters[q], known, 0) for q in (0, 1, 3, 2)]
        mine = lane % SUBLANES == (sub + turn) % SUBLANES
        left = lane // SUBLANES % 2 == 0
        first = jnp.where(mine, jnp.where(left, quarters[0], quarters[2]), first)
        second = jnp.where(mine, jnp.where(left, quarters[3], quarters[1]), second)
    in_place = lane // (2 * SUBLANES) == sub
    gram = jnp.concatenate(
        [jnp.sum(jnp.where(in_place, part, 0.0), axis=0, keepdims=True) for part in (first, second)],
        axis=0,
    )
    half = SUBLANES // 2
    lane = lax.broadcasted_iota(jnp.int32, (half, LANES), 1)
    for d in range(devices):
        one = straight[d * SUBLANES : (d + 1) * SUBLANES]
        start = d * MESSAGE_ROWS
        out_ref[start : start + half, :] = jnp.where(lane < LANES // 2, one[:half], one[half:])
        out_ref[start + half : start + MESSAGE_ROWS, :] = gram


def mix_and_pick(received, devices, run_length, scale, gram_scale):
    return pl.pallas_call(
        functools.partial(mix_kernel, run_length, scale, gram_scale),
        out_shape=jax.ShapeDtypeStruct((devices * MESSAGE_ROWS, LANES), jnp.float32),
        in_specs=in_vmem(1),
        out_specs=in_vmem(1)[0],
        compiler_params=pltpu.CompilerParams(vmem_limit_bytes=VMEM_LIMIT),
    )(received)


def finish_kernel(x_ref, sketch_ref, gram_ref):
    sources = x_ref.shape[0] // MESSAGE_ROWS
    quarter = LANES // 4
    half_rows = SUBLANES // 2
    sub = lax.broadcasted_iota(jnp.int32, (SUBLANES, LANES), 0)
    lane = lax.broadcasted_iota(jnp.int32, (SUBLANES, LANES), 1)
    gram = None
    for start in range(0, sources, 4):
        halves = [None, None]
        for index in range(4):
            place = (start + index) * MESSAGE_ROWS
            tail = x_ref[place + half_rows : place + MESSAGE_ROWS, :]
            gram = tail if gram is None else gram + tail
            piece = x_ref[place : place + half_rows, :]
            piece = jnp.concatenate([piece, piece], axis=0)
            piece = jnp.where(sub < half_rows, piece, pltpu.roll(piece, LANES // 2, 1))
            for half in range(2):
                shift = (index - half) % 4 * quarter
                moved = pltpu.roll(piece, shift, 1) if shift else piece
                if halves[half] is None:
                    halves[half] = moved
                else:
                    halves[half] = jnp.where(lane // quarter == index, moved, halves[half])
        for half in range(2):
            sketch_ref[
                half * SUBLANES : (half + 1) * SUBLANES, start * quarter : (start + 4) * quarter
            ] = halves[half]
    columns = gram_ref.shape[0]
    for half in range(2):
        for row in range(SUBLANES):
            line = gram[half : half + 1]
            line = pltpu.roll(line, LANES - row * columns, 1) if row else line
            gram_ref[half * SUBLANES + row : half * SUBLANES + row + 1, :] = line[:, :columns]


def finish(received, columns, sample_count):
    return pl.pallas_call(
        finish_kernel,
        out_shape=(
            jax.ShapeDtypeStruct((columns, sample_count), jnp.float32),
            jax.ShapeDtypeStruct((columns, columns), jnp.float32),
        ),
        in_specs=[pl.BlockSpec(memory_space=pltpu.VMEM)],
        out_specs=(pl.BlockSpec(memory_space=pltpu.VMEM),) * 2,
        compiler_params=pltpu.CompilerParams(vmem_limit_bytes=VMEM_LIMIT),
    )(received)


def exchange(values, axes):
    return lax.all_to_all(values, axes, split_axis=0, concat_axis=0, tiled=True)


def general_shards(matrix_slab, row_signs, sample_rows):
    columns, row_count = matrix_slab.shape
    sample_count = sample_rows.shape[0]
    devices = lax.axis_size("wide") * lax.axis_size("narrow")
    run_length = row_count // sample_count
    slice_rows = row_count // devices
    slice_runs = slice_rows // run_length
    values = jnp.swapaxes(local_transform(matrix_slab, row_signs), 0, 1)
    values = values.reshape(columns, devices, slice_rows)
    received = exchange(jnp.swapaxes(values, 0, 1), AXES)
    offsets = exchange(sample_rows.reshape(devices, slice_runs), AXES)
    mixed = jnp.einsum("ds,scr->dcr", sylvester(devices), received, precision=lax.Precision.HIGHEST)
    mixed = mixed.reshape(devices, columns, slice_runs, run_length)
    chosen = offsets[:, None, :, None] == lax.iota(jnp.int32, run_length)
    picked = jnp.sum(jnp.where(chosen, mixed, 0.0), axis=3)
    picked = picked * jnp.float32(1.0 / math.sqrt(row_count * devices))
    gram = jnp.einsum("dck,dek->ce", picked, picked, precision=lax.Precision.HIGHEST)
    gram = gram / jnp.float32(sample_count * devices)
    grams = jnp.broadcast_to(gram[None], (devices, columns, columns))
    back = exchange(jnp.concatenate([picked, grams], axis=2), AXES)
    sketch = jnp.swapaxes(back[:, :, :slice_runs], 0, 1).reshape(columns, devices * slice_runs)
    return sketch, jnp.sum(back[:, :, slice_runs:], axis=0)


def sliced_shards(matrix_slab, row_signs, sample_rows):
    columns, row_count = matrix_slab.shape
    sample_count = sample_rows.shape[0]
    devices = lax.axis_size(ORDER)
    run_length = row_count // sample_count
    sent = sliced_transform(matrix_slab, row_signs, sample_rows)
    received = exchange(sent.reshape(devices, -1), ORDER).reshape(sent.shape)
    scale = 1.0 / math.sqrt(row_count * devices)
    gram_scale = 1.0 / (sample_count * devices)
    picked = mix_and_pick(received, devices, run_length, scale, gram_scale)
    returned = exchange(picked.reshape(devices, -1), ORDER).reshape(picked.shape)
    return finish(returned, columns, sample_count)


def solution(mesh):
    wide, narrow = mesh.shape["wide"], mesh.shape["narrow"]
    axes, function = AXES, general_shards
    if wide * narrow == 32 and wide % 4 == 0:
        axes, function = SPLIT_AXES, sliced_shards
        mesh = jax.sharding.Mesh(mesh.devices.reshape(4, wide // 4, narrow), axes)
    in_specs = (P(None, axes), P(axes), P(axes))
    out_specs = (P(None, axes), P())
    return jax.shard_map(function, mesh=mesh, in_specs=in_specs, out_specs=out_specs, check_vma=False)
```

```python
import functools
import math

import jax
import jax.numpy as jnp
from jax import lax
from jax.experimental import pallas as pl
from jax.experimental.pallas import tpu as pltpu
from jax.sharding import PartitionSpec as P

LANES = 128
SUBLANES = 8
AXES = ("wide", "narrow")
BIT_AXES = ("bit3", "bit2", "bit1", "bit0", "narrow")
FIRST_ORDER = ("narrow", "bit1", "bit0", "bit3", "bit2")
SECOND_ORDER = ("bit1", "bit0", "narrow", "bit3", "bit2")
VMEM_LIMIT = 32 * 1024 * 1024
MESSAGE_ROWS = 6


def positions(order, other):
    count = 2 ** len(order)
    found = []
    for place in range(count):
        bits = {axis: place >> (len(order) - 1 - rank) & 1 for rank, axis in enumerate(order)}
        found.append(sum(bits[axis] << (len(other) - 1 - rank) for rank, axis in enumerate(other)))
    return tuple(found)


def butterfly(values):
    values = list(values)
    apart = 1
    while apart < len(values):
        for low in range(len(values)):
            if not low & apart:
                first, second = values[low], values[low | apart]
                values[low], values[low | apart] = first + second, first - second
        apart *= 2
    return values


def sylvester(order_size):
    rows = lax.broadcasted_iota(jnp.int32, (order_size, order_size), 0)
    cols = lax.broadcasted_iota(jnp.int32, (order_size, order_size), 1)
    common = rows & cols
    parity = jnp.zeros_like(common)
    for bit_pos in range(order_size.bit_length() - 1):
        parity = parity ^ (common >> bit_pos)
    return (1 - 2 * (parity & 1)).astype(jnp.float32)


def split_dot(values, table, parts=3):
    total = None
    for _ in range(parts):
        part = values.astype(jnp.bfloat16)
        values = values - part.astype(jnp.float32)
        product = jnp.dot(part, table, preferred_element_type=jnp.float32)
        total = product if total is None else total + product
    return total


def butterfly_steps(count):
    steps = []
    apart = 1
    while apart < count:
        radix = min(8, count // apart)
        for start in range(count):
            if start // apart % radix == 0:
                steps.append((apart, [start + apart * index for index in range(radix)]))
        apart *= radix
    return steps


def fetch_blocks(x_hbm, signs_hbm, out_ref, x_ref, signs_ref, arrived):
    blocks, columns, _ = out_ref.shape
    fetches = [pltpu.make_async_copy(signs_hbm, signs_ref, arrived.at[0])]
    places = [pl.ds(start, SUBLANES) for start in range(0, columns, SUBLANES)]
    for index, place in enumerate(places):
        fetches.append(
            pltpu.make_async_copy(x_hbm.at[place], x_ref.at[place], arrived.at[index + 1])
        )
    for fetch in fetches:
        fetch.start()
    table = sylvester(LANES).astype(jnp.bfloat16)
    fetches[0].wait()
    for index, place in enumerate(places):
        fetches[index + 1].wait()
        signed = []
        for block in range(blocks):
            signs = signs_ref[block : block + 1, :].astype(jnp.float32)
            signed.append(x_ref[place, block * LANES : (block + 1) * LANES] * signs)
        mixed = split_dot(jnp.concatenate(signed, axis=0), table)
        out_ref[:, place, :] = mixed.reshape(blocks, SUBLANES, LANES)


def local_kernel(x_hbm, signs_hbm, out_ref, x_ref, signs_ref, arrived):
    fetch_blocks(x_hbm, signs_hbm, out_ref, x_ref, signs_ref, arrived)
    for apart, places in butterfly_steps(out_ref.shape[0]):
        for place, value in zip(places, butterfly([out_ref[p] for p in places])):
            out_ref[place] = value


def sliced_kernel(
    x_hbm, signs_hbm, samples_hbm, final_ref, out_ref, x_ref, signs_ref, samples_ref, arrived, noted
):
    note = pltpu.make_async_copy(samples_hbm, samples_ref, noted)
    note.start()
    fetch_blocks(x_hbm, signs_hbm, out_ref, x_ref, signs_ref, arrived)
    blocks, columns, _ = out_ref.shape
    slices = blocks // 2
    rows = final_ref.shape[0] // slices
    note.wait()
    samples = samples_ref[...].astype(jnp.float32)
    per_row = slices // samples.shape[0]
    for turn in range(per_row):
        shift = LANES - turn * LANES // per_row
        turned = pltpu.roll(samples, shift, 1) if turn else samples
        for index in range(turn, slices, per_row):
            tail = (index + 1) * rows - 1
            final_ref[tail : tail + 1, :] = turned[index // per_row : index // per_row + 1]
    steps = butterfly_steps(blocks)
    last = steps[-1][0]
    for apart, places in steps:
        for place, value in zip(places, butterfly([out_ref[p] for p in places])):
            if apart == last:
                start = place // 2 * rows + place % 2 * columns
                final_ref[start : start + columns, :] = value
            else:
                out_ref[place] = value


def in_vmem(count):
    return [pl.BlockSpec(memory_space=pltpu.VMEM)] * count


def in_hbm(*arrays):
    return [pltpu.with_memory_space_constraint(array, pltpu.HBM) for array in arrays]


def fetch_scratch(matrix_slab, blocks):
    return [
        pltpu.VMEM(matrix_slab.shape, jnp.float32),
        pltpu.VMEM((blocks, LANES), jnp.int32),
    ]


def local_transform(matrix_slab, row_signs):
    columns, row_count = matrix_slab.shape
    blocks = row_count // LANES
    return pl.pallas_call(
        local_kernel,
        out_shape=jax.ShapeDtypeStruct((blocks, columns, LANES), jnp.float32),
        in_specs=[pl.BlockSpec(memory_space=pltpu.HBM)] * 2,
        out_specs=in_vmem(1)[0],
        scratch_shapes=[
            *fetch_scratch(matrix_slab, blocks),
            pltpu.SemaphoreType.DMA((columns // SUBLANES + 1,)),
        ],
        compiler_params=pltpu.CompilerParams(vmem_limit_bytes=VMEM_LIMIT),
    )(*in_hbm(matrix_slab, row_signs.reshape(blocks, LANES)))


def sliced_transform(matrix_slab, row_signs, sample_rows):
    columns, row_count = matrix_slab.shape
    blocks = row_count // LANES
    samples = sample_rows.reshape(-1, LANES)
    return pl.pallas_call(
        sliced_kernel,
        out_shape=jax.ShapeDtypeStruct((blocks // 2 * (2 * columns + 1), LANES), jnp.float32),
        in_specs=[pl.BlockSpec(memory_space=pltpu.HBM)] * 3,
        out_specs=in_vmem(1)[0],
        scratch_shapes=[
            pltpu.VMEM((blocks, columns, LANES), jnp.float32),
            *fetch_scratch(matrix_slab, blocks),
            pltpu.VMEM(samples.shape, jnp.int32),
            pltpu.SemaphoreType.DMA((columns // SUBLANES + 1,)),
            pltpu.SemaphoreType.DMA(()),
        ],
        compiler_params=pltpu.CompilerParams(vmem_limit_bytes=VMEM_LIMIT),
    )(*in_hbm(matrix_slab, row_signs.reshape(blocks, LANES), samples))


def mix_kernel(run_length, scale, gram_scale, places, x_ref, out_ref):
    devices = out_ref.shape[0] // MESSAGE_ROWS
    rows = x_ref.shape[0] // devices
    runs = LANES // run_length
    samples = jnp.concatenate(
        [x_ref[(s + 1) * rows - 1 : (s + 1) * rows, :] for s in range(devices)], axis=0
    ).astype(jnp.bfloat16)
    run_of = lax.broadcasted_iota(jnp.int32, (LANES, 2 * LANES), 0)
    row_of = lax.broadcasted_iota(jnp.int32, (LANES, 2 * LANES), 1)
    spread = jnp.where(row_of // run_length == run_of, 1.0, 0.0).astype(jnp.bfloat16)
    offsets = jnp.dot(samples, spread, preferred_element_type=jnp.float32)
    own = lax.broadcasted_iota(jnp.int32, offsets.shape, 1) % run_length
    mask = jnp.where(offsets == own.astype(jnp.float32), scale, 0.0)
    picked = []
    for part in range(4):
        block = part // 2
        starts = [s * rows + part * SUBLANES for s in range(devices)]
        mixed = butterfly([x_ref[start : start + SUBLANES, :] for start in starts])
        picked.append(
            jnp.concatenate(
                [
                    mixed[d] * mask[d : d + 1, block * LANES : (block + 1) * LANES]
                    for d in range(devices)
                ],
                axis=0,
            )
        )
    quarter = 2 * runs
    row = lax.broadcasted_iota(jnp.int32, (LANES, LANES), 0)
    lane = lax.broadcasted_iota(jnp.int32, (LANES, LANES), 1)
    pattern = jnp.where(row // run_length == lane % runs, 1.0, 0.0)
    lane = lax.broadcasted_iota(jnp.int32, (1, LANES), 1)
    group = lane // quarter
    place = []
    for part in range(4):
        block, half = part // 2, part % 2
        here = lane // runs % 2 == block
        sides = [group % 2, jnp.where(group < 2, group, 3 - group)]
        masks = [jnp.where(here & (side == half), 1.0, 0.0) for side in sides]
        place.append(jnp.concatenate([(pattern * mask).astype(jnp.bfloat16) for mask in masks], axis=1))
    gathered = split_dot(jnp.concatenate(picked, axis=1), jnp.concatenate(place, axis=0), 2)
    straight, crossed = gathered[:, :LANES], gathered[:, LANES:]
    turns = SUBLANES // 2 + 1
    totals = []
    for turn in range(turns):
        total = None
        for d in range(devices):
            one = straight[d * SUBLANES : (d + 1) * SUBLANES]
            two = crossed[d * SUBLANES : (d + 1) * SUBLANES]
            if turn:
                two = pltpu.roll(two, SUBLANES - turn, 0)
            total = one * two if total is None else total + one * two
        totals.append(total)
    from_quarter = row // quarter
    together = [jnp.where(from_quarter == q, 1.0, 0.0).astype(jnp.bfloat16) for q in range(4)]
    sums = split_dot(jnp.concatenate(totals, axis=0), jnp.concatenate(together, axis=1)) * gram_scale
    sub = lax.broadcasted_iota(jnp.int32, (SUBLANES, LANES), 0)
    lane = lax.broadcasted_iota(jnp.int32, (SUBLANES, LANES), 1)
    first, second = [jnp.zeros((SUBLANES, LANES), jnp.float32)] * 2
    for turn in range(SUBLANES):
        known = min(turn, SUBLANES - turn)
        here = sums[known * SUBLANES : (known + 1) * SUBLANES]
        quarters = [here[:, q * LANES : (q + 1) * LANES] for q in range(4)]
        if known != turn:
            quarters = [pltpu.roll(quarters[q], known, 0) for q in (0, 1, 3, 2)]
        mine = lane % SUBLANES == (sub + turn) % SUBLANES
        left = lane // SUBLANES % 2 == 0
        first = jnp.where(mine, jnp.where(left, quarters[0], quarters[2]), first)
        second = jnp.where(mine, jnp.where(left, quarters[3], quarters[1]), second)
    in_place = lane // (2 * SUBLANES) == sub
    gram = jnp.concatenate(
        [jnp.sum(jnp.where(in_place, part, 0.0), axis=0, keepdims=True) for part in (first, second)],
        axis=0,
    )
    half = SUBLANES // 2
    lane = lax.broadcasted_iota(jnp.int32, (half, LANES), 1)
    for d in range(devices):
        one = straight[d * SUBLANES : (d + 1) * SUBLANES]
        start = places[d] * MESSAGE_ROWS
        out_ref[start : start + half, :] = jnp.where(lane < LANES // 2, one[:half], one[half:])
        out_ref[start + half : start + MESSAGE_ROWS, :] = gram


def mix_and_pick(received, devices, run_length, scale, gram_scale, places):
    return pl.pallas_call(
        functools.partial(mix_kernel, run_length, scale, gram_scale, places),
        out_shape=jax.ShapeDtypeStruct((devices * MESSAGE_ROWS, LANES), jnp.float32),
        in_specs=in_vmem(1),
        out_specs=in_vmem(1)[0],
        compiler_params=pltpu.CompilerParams(vmem_limit_bytes=VMEM_LIMIT),
    )(received)


def finish_kernel(places, x_ref, sketch_ref, gram_ref):
    sources = x_ref.shape[0] // MESSAGE_ROWS
    quarter = LANES // 4
    half_rows = SUBLANES // 2
    sub = lax.broadcasted_iota(jnp.int32, (SUBLANES, LANES), 0)
    lane = lax.broadcasted_iota(jnp.int32, (SUBLANES, LANES), 1)
    gram = None
    for start in range(0, sources, 4):
        halves = [None, None]
        for index in range(4):
            place = places[start + index] * MESSAGE_ROWS
            tail = x_ref[place + half_rows : place + MESSAGE_ROWS, :]
            gram = tail if gram is None else gram + tail
            piece = x_ref[place : place + half_rows, :]
            piece = jnp.concatenate([piece, piece], axis=0)
            piece = jnp.where(sub < half_rows, piece, pltpu.roll(piece, LANES // 2, 1))
            for half in range(2):
                shift = (index - half) % 4 * quarter
                moved = pltpu.roll(piece, shift, 1) if shift else piece
                if halves[half] is None:
                    halves[half] = moved
                else:
                    halves[half] = jnp.where(lane // quarter == index, moved, halves[half])
        for half in range(2):
            sketch_ref[
                half * SUBLANES : (half + 1) * SUBLANES, start * quarter : (start + 4) * quarter
            ] = halves[half]
    columns = gram_ref.shape[0]
    for half in range(2):
        for row in range(SUBLANES):
            line = gram[half : half + 1]
            line = pltpu.roll(line, LANES - row * columns, 1) if row else line
            gram_ref[half * SUBLANES + row : half * SUBLANES + row + 1, :] = line[:, :columns]


def finish(received, columns, sample_count, places):
    return pl.pallas_call(
        functools.partial(finish_kernel, places),
        out_shape=(
            jax.ShapeDtypeStruct((columns, sample_count), jnp.float32),
            jax.ShapeDtypeStruct((columns, columns), jnp.float32),
        ),
        in_specs=[pl.BlockSpec(memory_space=pltpu.VMEM)],
        out_specs=(pl.BlockSpec(memory_space=pltpu.VMEM),) * 2,
        compiler_params=pltpu.CompilerParams(vmem_limit_bytes=VMEM_LIMIT),
    )(received)


def exchange(values, axes):
    return lax.all_to_all(values, axes, split_axis=0, concat_axis=0, tiled=True)


def general_shards(matrix_slab, row_signs, sample_rows):
    columns, row_count = matrix_slab.shape
    sample_count = sample_rows.shape[0]
    devices = lax.axis_size("wide") * lax.axis_size("narrow")
    run_length = row_count // sample_count
    slice_rows = row_count // devices
    slice_runs = slice_rows // run_length
    values = jnp.swapaxes(local_transform(matrix_slab, row_signs), 0, 1)
    values = values.reshape(columns, devices, slice_rows)
    received = exchange(jnp.swapaxes(values, 0, 1), AXES)
    offsets = exchange(sample_rows.reshape(devices, slice_runs), AXES)
    mixed = jnp.einsum("ds,scr->dcr", sylvester(devices), received, precision=lax.Precision.HIGHEST)
    mixed = mixed.reshape(devices, columns, slice_runs, run_length)
    chosen = offsets[:, None, :, None] == lax.iota(jnp.int32, run_length)
    picked = jnp.sum(jnp.where(chosen, mixed, 0.0), axis=3)
    picked = picked * jnp.float32(1.0 / math.sqrt(row_count * devices))
    gram = jnp.einsum("dck,dek->ce", picked, picked, precision=lax.Precision.HIGHEST)
    gram = gram / jnp.float32(sample_count * devices)
    grams = jnp.broadcast_to(gram[None], (devices, columns, columns))
    back = exchange(jnp.concatenate([picked, grams], axis=2), AXES)
    sketch = jnp.swapaxes(back[:, :, :slice_runs], 0, 1).reshape(columns, devices * slice_runs)
    return sketch, jnp.sum(back[:, :, slice_runs:], axis=0)


def sliced_shards(matrix_slab, row_signs, sample_rows):
    columns, row_count = matrix_slab.shape
    sample_count = sample_rows.shape[0]
    devices = lax.axis_size(FIRST_ORDER)
    places = positions(FIRST_ORDER, SECOND_ORDER)
    run_length = row_count // sample_count
    sent = sliced_transform(matrix_slab, row_signs, sample_rows)
    received = exchange(sent.reshape(devices, -1), FIRST_ORDER).reshape(sent.shape)
    scale = 1.0 / math.sqrt(row_count * devices)
    gram_scale = 1.0 / (sample_count * devices)
    picked = mix_and_pick(received, devices, run_length, scale, gram_scale, places)
    returned = exchange(picked.reshape(devices, -1), SECOND_ORDER).reshape(picked.shape)
    return finish(returned, columns, sample_count, places)


def solution(mesh):
    axes, function = AXES, general_shards
    if (mesh.shape["wide"], mesh.shape["narrow"]) == (16, 2):
        axes, function = BIT_AXES, sliced_shards
        mesh = jax.sharding.Mesh(mesh.devices.reshape((2,) * len(axes)), axes)
    in_specs = (P(None, axes), P(axes), P(axes))
    out_specs = (P(None, axes), P())
    return jax.shard_map(function, mesh=mesh, in_specs=in_specs, out_specs=out_specs, check_vma=False)
```

```python
import functools
import math

import jax
import jax.numpy as jnp
from jax import lax
from jax.experimental import pallas as pl
from jax.experimental.pallas import tpu as pltpu
from jax.sharding import PartitionSpec as P

LANES = 128
SUBLANES = 8
AXES = ("wide", "narrow")
BIT_AXES = ("bit3", "bit2", "bit1", "bit0", "narrow")
FIRST_ORDER = ("bit1", "bit0", "narrow", "bit2", "bit3")
SECOND_ORDER = ("bit1", "bit0", "narrow", "bit2", "bit3")
VMEM_LIMIT = 32 * 1024 * 1024
MESSAGE_ROWS = 6


def positions(order, other):
    count = 2 ** len(order)
    found = []
    for place in range(count):
        bits = {axis: place >> (len(order) - 1 - rank) & 1 for rank, axis in enumerate(order)}
        found.append(sum(bits[axis] << (len(other) - 1 - rank) for rank, axis in enumerate(other)))
    return tuple(found)


def butterfly(values):
    values = list(values)
    apart = 1
    while apart < len(values):
        for low in range(len(values)):
            if not low & apart:
                first, second = values[low], values[low | apart]
                values[low], values[low | apart] = first + second, first - second
        apart *= 2
    return values


def sylvester(order_size):
    rows = lax.broadcasted_iota(jnp.int32, (order_size, order_size), 0)
    cols = lax.broadcasted_iota(jnp.int32, (order_size, order_size), 1)
    common = rows & cols
    parity = jnp.zeros_like(common)
    for bit_pos in range(order_size.bit_length() - 1):
        parity = parity ^ (common >> bit_pos)
    return (1 - 2 * (parity & 1)).astype(jnp.float32)


def split_dot(values, table, parts=3):
    total = None
    for _ in range(parts):
        part = values.astype(jnp.bfloat16)
        values = values - part.astype(jnp.float32)
        product = jnp.dot(part, table, preferred_element_type=jnp.float32)
        total = product if total is None else total + product
    return total


def butterfly_steps(count):
    steps = []
    apart = 1
    while apart < count:
        radix = min(8, count // apart)
        for start in range(count):
            if start // apart % radix == 0:
                steps.append((apart, [start + apart * index for index in range(radix)]))
        apart *= radix
    return steps


def fetch_blocks(x_hbm, signs_hbm, out_ref, x_ref, signs_ref, arrived):
    blocks, columns, _ = out_ref.shape
    fetches = [pltpu.make_async_copy(signs_hbm, signs_ref, arrived.at[0])]
    places = [pl.ds(start, SUBLANES) for start in range(0, columns, SUBLANES)]
    for index, place in enumerate(places):
        fetches.append(
            pltpu.make_async_copy(x_hbm.at[place], x_ref.at[place], arrived.at[index + 1])
        )
    for fetch in fetches:
        fetch.start()
    table = sylvester(LANES).astype(jnp.bfloat16)
    fetches[0].wait()
    for index, place in enumerate(places):
        fetches[index + 1].wait()
        signed = []
        for block in range(blocks):
            signs = signs_ref[block : block + 1, :].astype(jnp.float32)
            signed.append(x_ref[place, block * LANES : (block + 1) * LANES] * signs)
        mixed = split_dot(jnp.concatenate(signed, axis=0), table)
        out_ref[:, place, :] = mixed.reshape(blocks, SUBLANES, LANES)


def local_kernel(x_hbm, signs_hbm, out_ref, x_ref, signs_ref, arrived):
    fetch_blocks(x_hbm, signs_hbm, out_ref, x_ref, signs_ref, arrived)
    for apart, places in butterfly_steps(out_ref.shape[0]):
        for place, value in zip(places, butterfly([out_ref[p] for p in places])):
            out_ref[place] = value


def sliced_kernel(
    x_hbm, signs_hbm, samples_hbm, final_ref, out_ref, x_ref, signs_ref, samples_ref, arrived, noted
):
    note = pltpu.make_async_copy(samples_hbm, samples_ref, noted)
    note.start()
    fetch_blocks(x_hbm, signs_hbm, out_ref, x_ref, signs_ref, arrived)
    blocks, columns, _ = out_ref.shape
    slices = blocks // 2
    rows = final_ref.shape[0] // slices
    note.wait()
    samples = samples_ref[...].astype(jnp.float32)
    per_row = slices // samples.shape[0]
    for turn in range(per_row):
        shift = LANES - turn * LANES // per_row
        turned = pltpu.roll(samples, shift, 1) if turn else samples
        for index in range(turn, slices, per_row):
            tail = (index + 1) * rows - 1
            final_ref[tail : tail + 1, :] = turned[index // per_row : index // per_row + 1]
    steps = butterfly_steps(blocks)
    last = steps[-1][0]
    for apart, places in steps:
        for place, value in zip(places, butterfly([out_ref[p] for p in places])):
            if apart == last:
                start = place // 2 * rows + place % 2 * columns
                final_ref[start : start + columns, :] = value
            else:
                out_ref[place] = value


def in_vmem(count):
    return [pl.BlockSpec(memory_space=pltpu.VMEM)] * count


def in_hbm(*arrays):
    return [pltpu.with_memory_space_constraint(array, pltpu.HBM) for array in arrays]


def fetch_scratch(matrix_slab, blocks):
    return [
        pltpu.VMEM(matrix_slab.shape, jnp.float32),
        pltpu.VMEM((blocks, LANES), jnp.int32),
    ]


def local_transform(matrix_slab, row_signs):
    columns, row_count = matrix_slab.shape
    blocks = row_count // LANES
    return pl.pallas_call(
        local_kernel,
        out_shape=jax.ShapeDtypeStruct((blocks, columns, LANES), jnp.float32),
        in_specs=[pl.BlockSpec(memory_space=pltpu.HBM)] * 2,
        out_specs=in_vmem(1)[0],
        scratch_shapes=[
            *fetch_scratch(matrix_slab, blocks),
            pltpu.SemaphoreType.DMA((columns // SUBLANES + 1,)),
        ],
        compiler_params=pltpu.CompilerParams(vmem_limit_bytes=VMEM_LIMIT),
    )(*in_hbm(matrix_slab, row_signs.reshape(blocks, LANES)))


def sliced_transform(matrix_slab, row_signs, sample_rows):
    columns, row_count = matrix_slab.shape
    blocks = row_count // LANES
    samples = sample_rows.reshape(-1, LANES)
    return pl.pallas_call(
        sliced_kernel,
        out_shape=jax.ShapeDtypeStruct((blocks // 2 * (2 * columns + 1), LANES), jnp.float32),
        in_specs=[pl.BlockSpec(memory_space=pltpu.HBM)] * 3,
        out_specs=in_vmem(1)[0],
        scratch_shapes=[
            pltpu.VMEM((blocks, columns, LANES), jnp.float32),
            *fetch_scratch(matrix_slab, blocks),
            pltpu.VMEM(samples.shape, jnp.int32),
            pltpu.SemaphoreType.DMA((columns // SUBLANES + 1,)),
            pltpu.SemaphoreType.DMA(()),
        ],
        compiler_params=pltpu.CompilerParams(vmem_limit_bytes=VMEM_LIMIT),
    )(*in_hbm(matrix_slab, row_signs.reshape(blocks, LANES), samples))


def mix_kernel(run_length, scale, gram_scale, places, x_ref, out_ref):
    devices = out_ref.shape[0] // MESSAGE_ROWS
    rows = x_ref.shape[0] // devices
    runs = LANES // run_length
    samples = jnp.concatenate(
        [x_ref[(s + 1) * rows - 1 : (s + 1) * rows, :] for s in range(devices)], axis=0
    ).astype(jnp.bfloat16)
    run_of = lax.broadcasted_iota(jnp.int32, (LANES, 2 * LANES), 0)
    row_of = lax.broadcasted_iota(jnp.int32, (LANES, 2 * LANES), 1)
    spread = jnp.where(row_of // run_length == run_of, 1.0, 0.0).astype(jnp.bfloat16)
    offsets = jnp.dot(samples, spread, preferred_element_type=jnp.float32)
    own = lax.broadcasted_iota(jnp.int32, offsets.shape, 1) % run_length
    mask = jnp.where(offsets == own.astype(jnp.float32), scale, 0.0)
    picked = []
    for part in range(4):
        block = part // 2
        starts = [s * rows + part * SUBLANES for s in range(devices)]
        mixed = butterfly([x_ref[start : start + SUBLANES, :] for start in starts])
        picked.append(
            jnp.concatenate(
                [
                    mixed[d] * mask[d : d + 1, block * LANES : (block + 1) * LANES]
                    for d in range(devices)
                ],
                axis=0,
            )
        )
    quarter = 2 * runs
    row = lax.broadcasted_iota(jnp.int32, (LANES, LANES), 0)
    lane = lax.broadcasted_iota(jnp.int32, (LANES, LANES), 1)
    pattern = jnp.where(row // run_length == lane % runs, 1.0, 0.0)
    lane = lax.broadcasted_iota(jnp.int32, (1, LANES), 1)
    group = lane // quarter
    place = []
    for part in range(4):
        block, half = part // 2, part % 2
        here = lane // runs % 2 == block
        sides = [group % 2, jnp.where(group < 2, group, 3 - group)]
        masks = [jnp.where(here & (side == half), 1.0, 0.0) for side in sides]
        place.append(jnp.concatenate([(pattern * mask).astype(jnp.bfloat16) for mask in masks], axis=1))
    gathered = split_dot(jnp.concatenate(picked, axis=1), jnp.concatenate(place, axis=0), 2)
    straight, crossed = gathered[:, :LANES], gathered[:, LANES:]
    turns = SUBLANES // 2 + 1
    totals = []
    for turn in range(turns):
        total = None
        for d in range(devices):
            one = straight[d * SUBLANES : (d + 1) * SUBLANES]
            two = crossed[d * SUBLANES : (d + 1) * SUBLANES]
            if turn:
                two = pltpu.roll(two, SUBLANES - turn, 0)
            total = one * two if total is None else total + one * two
        totals.append(total)
    from_quarter = row // quarter
    together = [jnp.where(from_quarter == q, 1.0, 0.0).astype(jnp.bfloat16) for q in range(4)]
    sums = split_dot(jnp.concatenate(totals, axis=0), jnp.concatenate(together, axis=1)) * gram_scale
    sub = lax.broadcasted_iota(jnp.int32, (SUBLANES, LANES), 0)
    lane = lax.broadcasted_iota(jnp.int32, (SUBLANES, LANES), 1)
    first, second = [jnp.zeros((SUBLANES, LANES), jnp.float32)] * 2
    for turn in range(SUBLANES):
        known = min(turn, SUBLANES - turn)
        here = sums[known * SUBLANES : (known + 1) * SUBLANES]
        quarters = [here[:, q * LANES : (q + 1) * LANES] for q in range(4)]
        if known != turn:
            quarters = [pltpu.roll(quarters[q], known, 0) for q in (0, 1, 3, 2)]
        mine = lane % SUBLANES == (sub + turn) % SUBLANES
        left = lane // SUBLANES % 2 == 0
        first = jnp.where(mine, jnp.where(left, quarters[0], quarters[2]), first)
        second = jnp.where(mine, jnp.where(left, quarters[3], quarters[1]), second)
    in_place = lane // (2 * SUBLANES) == sub
    gram = jnp.concatenate(
        [jnp.sum(jnp.where(in_place, part, 0.0), axis=0, keepdims=True) for part in (first, second)],
        axis=0,
    )
    half = SUBLANES // 2
    lane = lax.broadcasted_iota(jnp.int32, (half, LANES), 1)
    for d in range(devices):
        one = straight[d * SUBLANES : (d + 1) * SUBLANES]
        start = places[d] * MESSAGE_ROWS
        out_ref[start : start + half, :] = jnp.where(lane < LANES // 2, one[:half], one[half:])
        out_ref[start + half : start + MESSAGE_ROWS, :] = gram


def mix_and_pick(received, devices, run_length, scale, gram_scale, places):
    return pl.pallas_call(
        functools.partial(mix_kernel, run_length, scale, gram_scale, places),
        out_shape=jax.ShapeDtypeStruct((devices * MESSAGE_ROWS, LANES), jnp.float32),
        in_specs=in_vmem(1),
        out_specs=in_vmem(1)[0],
        compiler_params=pltpu.CompilerParams(vmem_limit_bytes=VMEM_LIMIT),
    )(received)


def finish_kernel(places, x_ref, sketch_ref, gram_ref):
    sources = x_ref.shape[0] // MESSAGE_ROWS
    quarter = LANES // 4
    half_rows = SUBLANES // 2
    sub = lax.broadcasted_iota(jnp.int32, (SUBLANES, LANES), 0)
    lane = lax.broadcasted_iota(jnp.int32, (SUBLANES, LANES), 1)
    gram = None
    for start in range(0, sources, 4):
        halves = [None, None]
        for index in range(4):
            place = places[start + index] * MESSAGE_ROWS
            tail = x_ref[place + half_rows : place + MESSAGE_ROWS, :]
            gram = tail if gram is None else gram + tail
            piece = x_ref[place : place + half_rows, :]
            piece = jnp.concatenate([piece, piece], axis=0)
            piece = jnp.where(sub < half_rows, piece, pltpu.roll(piece, LANES // 2, 1))
            for half in range(2):
                shift = (index - half) % 4 * quarter
                moved = pltpu.roll(piece, shift, 1) if shift else piece
                if halves[half] is None:
                    halves[half] = moved
                else:
                    halves[half] = jnp.where(lane // quarter == index, moved, halves[half])
        for half in range(2):
            sketch_ref[
                half * SUBLANES : (half + 1) * SUBLANES, start * quarter : (start + 4) * quarter
            ] = halves[half]
    columns = gram_ref.shape[0]
    for half in range(2):
        for row in range(SUBLANES):
            line = gram[half : half + 1]
            line = pltpu.roll(line, LANES - row * columns, 1) if row else line
            gram_ref[half * SUBLANES + row : half * SUBLANES + row + 1, :] = line[:, :columns]


def finish(received, columns, sample_count, places):
    return pl.pallas_call(
        functools.partial(finish_kernel, places),
        out_shape=(
            jax.ShapeDtypeStruct((columns, sample_count), jnp.float32),
            jax.ShapeDtypeStruct((columns, columns), jnp.float32),
        ),
        in_specs=[pl.BlockSpec(memory_space=pltpu.VMEM)],
        out_specs=(pl.BlockSpec(memory_space=pltpu.VMEM),) * 2,
        compiler_params=pltpu.CompilerParams(vmem_limit_bytes=VMEM_LIMIT),
    )(received)


def exchange(values, axes):
    return lax.all_to_all(values, axes, split_axis=0, concat_axis=0, tiled=True)


def general_shards(matrix_slab, row_signs, sample_rows):
    columns, row_count = matrix_slab.shape
    sample_count = sample_rows.shape[0]
    devices = lax.axis_size("wide") * lax.axis_size("narrow")
    run_length = row_count // sample_count
    slice_rows = row_count // devices
    slice_runs = slice_rows // run_length
    values = jnp.swapaxes(local_transform(matrix_slab, row_signs), 0, 1)
    values = values.reshape(columns, devices, slice_rows)
    received = exchange(jnp.swapaxes(values, 0, 1), AXES)
    offsets = exchange(sample_rows.reshape(devices, slice_runs), AXES)
    mixed = jnp.einsum("ds,scr->dcr", sylvester(devices), received, precision=lax.Precision.HIGHEST)
    mixed = mixed.reshape(devices, columns, slice_runs, run_length)
    chosen = offsets[:, None, :, None] == lax.iota(jnp.int32, run_length)
    picked = jnp.sum(jnp.where(chosen, mixed, 0.0), axis=3)
    picked = picked * jnp.float32(1.0 / math.sqrt(row_count * devices))
    gram = jnp.einsum("dck,dek->ce", picked, picked, precision=lax.Precision.HIGHEST)
    gram = gram / jnp.float32(sample_count * devices)
    grams = jnp.broadcast_to(gram[None], (devices, columns, columns))
    back = exchange(jnp.concatenate([picked, grams], axis=2), AXES)
    sketch = jnp.swapaxes(back[:, :, :slice_runs], 0, 1).reshape(columns, devices * slice_runs)
    return sketch, jnp.sum(back[:, :, slice_runs:], axis=0)


def sliced_shards(matrix_slab, row_signs, sample_rows):
    columns, row_count = matrix_slab.shape
    sample_count = sample_rows.shape[0]
    devices = lax.axis_size(FIRST_ORDER)
    places = positions(FIRST_ORDER, SECOND_ORDER)
    run_length = row_count // sample_count
    sent = sliced_transform(matrix_slab, row_signs, sample_rows)
    received = exchange(sent.reshape(devices, -1), FIRST_ORDER).reshape(sent.shape)
    scale = 1.0 / math.sqrt(row_count * devices)
    gram_scale = 1.0 / (sample_count * devices)
    picked = mix_and_pick(received, devices, run_length, scale, gram_scale, places)
    returned = exchange(picked.reshape(devices, -1), SECOND_ORDER).reshape(picked.shape)
    return finish(returned, columns, sample_count, places)


def solution(mesh):
    axes, function = AXES, general_shards
    if (mesh.shape["wide"], mesh.shape["narrow"]) == (16, 2):
        axes, function = BIT_AXES, sliced_shards
        mesh = jax.sharding.Mesh(mesh.devices.reshape((2,) * len(axes)), axes)
    in_specs = (P(None, axes), P(axes), P(axes))
    out_specs = (P(None, axes), P())
    return jax.shard_map(function, mesh=mesh, in_specs=in_specs, out_specs=out_specs, check_vma=False)
```

```python
import functools
import math

import jax
import jax.numpy as jnp
from jax import lax
from jax.experimental import pallas as pl
from jax.experimental.pallas import tpu as pltpu
from jax.sharding import PartitionSpec as P

LANES = 128
SUBLANES = 8
AXES = ("wide", "narrow")
SPLIT_AXES = ("line", "plane", "narrow")
ORDER = ("plane", "narrow", "line")
VMEM_LIMIT = 32 * 1024 * 1024
MESSAGE_ROWS = 6


def butterfly(values):
    values = list(values)
    apart = 1
    while apart < len(values):
        for low in range(len(values)):
            if not low & apart:
                first, second = values[low], values[low | apart]
                values[low], values[low | apart] = first + second, first - second
        apart *= 2
    return values


def sylvester(order_size):
    rows = lax.broadcasted_iota(jnp.int32, (order_size, order_size), 0)
    cols = lax.broadcasted_iota(jnp.int32, (order_size, order_size), 1)
    common = rows & cols
    parity = jnp.zeros_like(common)
    for bit_pos in range(order_size.bit_length() - 1):
        parity = parity ^ (common >> bit_pos)
    return (1 - 2 * (parity & 1)).astype(jnp.float32)


def split_dot(values, table, parts=3):
    total = None
    for _ in range(parts):
        part = values.astype(jnp.bfloat16)
        values = values - part.astype(jnp.float32)
        product = jnp.dot(part, table, preferred_element_type=jnp.float32)
        total = product if total is None else total + product
    return total


def butterfly_steps(count):
    steps = []
    apart = 1
    while apart < count:
        radix = min(8, count // apart)
        for start in range(count):
            if start // apart % radix == 0:
                steps.append((apart, [start + apart * index for index in range(radix)]))
        apart *= radix
    return steps


def fetch_blocks(x_hbm, signs_hbm, out_ref, x_ref, signs_ref, arrived):
    blocks, columns, _ = out_ref.shape
    fetches = [pltpu.make_async_copy(signs_hbm, signs_ref, arrived.at[0])]
    places = [pl.ds(start, SUBLANES) for start in range(0, columns, SUBLANES)]
    for index, place in enumerate(places):
        fetches.append(
            pltpu.make_async_copy(x_hbm.at[place], x_ref.at[place], arrived.at[index + 1])
        )
    for fetch in fetches:
        fetch.start()
    table = sylvester(LANES).astype(jnp.bfloat16)
    fetches[0].wait()
    for index, place in enumerate(places):
        fetches[index + 1].wait()
        signed = []
        for block in range(blocks):
            signs = signs_ref[block : block + 1, :].astype(jnp.float32)
            signed.append(x_ref[place, block * LANES : (block + 1) * LANES] * signs)
        mixed = split_dot(jnp.concatenate(signed, axis=0), table)
        out_ref[:, place, :] = mixed.reshape(blocks, SUBLANES, LANES)


def local_kernel(x_hbm, signs_hbm, out_ref, x_ref, signs_ref, arrived):
    fetch_blocks(x_hbm, signs_hbm, out_ref, x_ref, signs_ref, arrived)
    for apart, places in butterfly_steps(out_ref.shape[0]):
        for place, value in zip(places, butterfly([out_ref[p] for p in places])):
            out_ref[place] = value


def sliced_kernel(
    x_hbm, signs_hbm, samples_hbm, final_ref, out_ref, x_ref, signs_ref, samples_ref, arrived, noted
):
    note = pltpu.make_async_copy(samples_hbm, samples_ref, noted)
    note.start()
    fetch_blocks(x_hbm, signs_hbm, out_ref, x_ref, signs_ref, arrived)
    blocks, columns, _ = out_ref.shape
    slices = blocks // 2
    rows = final_ref.shape[0] // slices
    note.wait()
    samples = samples_ref[...].astype(jnp.float32)
    per_row = slices // samples.shape[0]
    for turn in range(per_row):
        shift = LANES - turn * LANES // per_row
        turned = pltpu.roll(samples, shift, 1) if turn else samples
        for index in range(turn, slices, per_row):
            tail = (index + 1) * rows - 1
            final_ref[tail : tail + 1, :] = turned[index // per_row : index // per_row + 1]
    steps = butterfly_steps(blocks)
    last = steps[-1][0]
    for apart, places in steps:
        for place, value in zip(places, butterfly([out_ref[p] for p in places])):
            if apart == last:
                start = place // 2 * rows + place % 2 * columns
                final_ref[start : start + columns, :] = value
            else:
                out_ref[place] = value


def in_vmem(count):
    return [pl.BlockSpec(memory_space=pltpu.VMEM)] * count


def in_hbm(*arrays):
    return [pltpu.with_memory_space_constraint(array, pltpu.HBM) for array in arrays]


def fetch_scratch(matrix_slab, blocks):
    return [
        pltpu.VMEM(matrix_slab.shape, jnp.float32),
        pltpu.VMEM((blocks, LANES), jnp.int32),
    ]


def local_transform(matrix_slab, row_signs):
    columns, row_count = matrix_slab.shape
    blocks = row_count // LANES
    return pl.pallas_call(
        local_kernel,
        out_shape=jax.ShapeDtypeStruct((blocks, columns, LANES), jnp.float32),
        in_specs=[pl.BlockSpec(memory_space=pltpu.HBM)] * 2,
        out_specs=in_vmem(1)[0],
        scratch_shapes=[
            *fetch_scratch(matrix_slab, blocks),
            pltpu.SemaphoreType.DMA((columns // SUBLANES + 1,)),
        ],
        compiler_params=pltpu.CompilerParams(vmem_limit_bytes=VMEM_LIMIT),
    )(*in_hbm(matrix_slab, row_signs.reshape(blocks, LANES)))


def sliced_transform(matrix_slab, row_signs, sample_rows):
    columns, row_count = matrix_slab.shape
    blocks = row_count // LANES
    samples = sample_rows.reshape(-1, LANES)
    return pl.pallas_call(
        sliced_kernel,
        out_shape=jax.ShapeDtypeStruct((blocks // 2 * (2 * columns + 1), LANES), jnp.float32),
        in_specs=[pl.BlockSpec(memory_space=pltpu.HBM)] * 3,
        out_specs=in_vmem(1)[0],
        scratch_shapes=[
            pltpu.VMEM((blocks, columns, LANES), jnp.float32),
            *fetch_scratch(matrix_slab, blocks),
            pltpu.VMEM(samples.shape, jnp.int32),
            pltpu.SemaphoreType.DMA((columns // SUBLANES + 1,)),
            pltpu.SemaphoreType.DMA(()),
        ],
        compiler_params=pltpu.CompilerParams(vmem_limit_bytes=VMEM_LIMIT),
    )(*in_hbm(matrix_slab, row_signs.reshape(blocks, LANES), samples))


def mix_kernel(run_length, scale, gram_scale, x_ref, out_ref):
    devices = out_ref.shape[0] // MESSAGE_ROWS
    rows = x_ref.shape[0] // devices
    runs = LANES // run_length
    samples = jnp.concatenate(
        [x_ref[(s + 1) * rows - 1 : (s + 1) * rows, :] for s in range(devices)], axis=0
    ).astype(jnp.bfloat16)
    run_of = lax.broadcasted_iota(jnp.int32, (LANES, 2 * LANES), 0)
    row_of = lax.broadcasted_iota(jnp.int32, (LANES, 2 * LANES), 1)
    spread = jnp.where(row_of // run_length == run_of, 1.0, 0.0).astype(jnp.bfloat16)
    offsets = jnp.dot(samples, spread, preferred_element_type=jnp.float32)
    own = lax.broadcasted_iota(jnp.int32, offsets.shape, 1) % run_length
    mask = jnp.where(offsets == own.astype(jnp.float32), scale, 0.0)
    picked = []
    for part in range(4):
        block = part // 2
        starts = [s * rows + part * SUBLANES for s in range(devices)]
        mixed = butterfly([x_ref[start : start + SUBLANES, :] for start in starts])
        picked.append(
            jnp.concatenate(
                [
                    mixed[d] * mask[d : d + 1, block * LANES : (block + 1) * LANES]
                    for d in range(devices)
                ],
                axis=0,
            )
        )
    quarter = 2 * runs
    row = lax.broadcasted_iota(jnp.int32, (LANES, LANES), 0)
    lane = lax.broadcasted_iota(jnp.int32, (LANES, LANES), 1)
    pattern = jnp.where(row // run_length == lane % runs, 1.0, 0.0)
    lane = lax.broadcasted_iota(jnp.int32, (1, LANES), 1)
    group = lane // quarter
    place = []
    for part in range(4):
        block, half = part // 2, part % 2
        here = lane // runs % 2 == block
        sides = [group % 2, jnp.where(group < 2, group, 3 - group)]
        masks = [jnp.where(here & (side == half), 1.0, 0.0) for side in sides]
        place.append(jnp.concatenate([(pattern * mask).astype(jnp.bfloat16) for mask in masks], axis=1))
    gathered = split_dot(jnp.concatenate(picked, axis=1), jnp.concatenate(place, axis=0), 2)
    straight, crossed = gathered[:, :LANES], gathered[:, LANES:]
    turns = SUBLANES // 2 + 1
    totals = []
    for turn in range(turns):
        total = None
        for d in range(devices):
            one = straight[d * SUBLANES : (d + 1) * SUBLANES]
            two = crossed[d * SUBLANES : (d + 1) * SUBLANES]
            if turn:
                two = pltpu.roll(two, SUBLANES - turn, 0)
            total = one * two if total is None else total + one * two
        totals.append(total)
    from_quarter = row // quarter
    together = [jnp.where(from_quarter == q, 1.0, 0.0).astype(jnp.bfloat16) for q in range(4)]
    sums = split_dot(jnp.concatenate(totals, axis=0), jnp.concatenate(together, axis=1)) * gram_scale
    sub = lax.broadcasted_iota(jnp.int32, (SUBLANES, LANES), 0)
    lane = lax.broadcasted_iota(jnp.int32, (SUBLANES, LANES), 1)
    first, second = [jnp.zeros((SUBLANES, LANES), jnp.float32)] * 2
    for turn in range(SUBLANES):
        known = min(turn, SUBLANES - turn)
        here = sums[known * SUBLANES : (known + 1) * SUBLANES]
        quarters = [here[:, q * LANES : (q + 1) * LANES] for q in range(4)]
        if known != turn:
            quarters = [pltpu.roll(quarters[q], known, 0) for q in (0, 1, 3, 2)]
        mine = lane % SUBLANES == (sub + turn) % SUBLANES
        left = lane // SUBLANES % 2 == 0
        first = jnp.where(mine, jnp.where(left, quarters[0], quarters[2]), first)
        second = jnp.where(mine, jnp.where(left, quarters[3], quarters[1]), second)
    in_place = lane // (2 * SUBLANES) == sub
    gram = jnp.concatenate(
        [jnp.sum(jnp.where(in_place, part, 0.0), axis=0, keepdims=True) for part in (first, second)],
        axis=0,
    )
    half = SUBLANES // 2
    lane = lax.broadcasted_iota(jnp.int32, (half, LANES), 1)
    for d in range(devices):
        one = straight[d * SUBLANES : (d + 1) * SUBLANES]
        start = d * MESSAGE_ROWS
        out_ref[start : start + half, :] = jnp.where(lane < LANES // 2, one[:half], one[half:])
        out_ref[start + half : start + MESSAGE_ROWS, :] = gram


def mix_and_pick(received, devices, run_length, scale, gram_scale):
    return pl.pallas_call(
        functools.partial(mix_kernel, run_length, scale, gram_scale),
        out_shape=jax.ShapeDtypeStruct((devices * MESSAGE_ROWS, LANES), jnp.float32),
        in_specs=in_vmem(1),
        out_specs=in_vmem(1)[0],
        compiler_params=pltpu.CompilerParams(vmem_limit_bytes=VMEM_LIMIT),
    )(received)


def finish_kernel(x_ref, sketch_hbm, gram_hbm, sketch_ref, gram_ref, sent):
    sources = x_ref.shape[0] // MESSAGE_ROWS
    columns = gram_ref.shape[0]
    quarter = LANES // 4
    half_rows = SUBLANES // 2
    gram = None
    for source in range(sources):
        place = source * MESSAGE_ROWS
        tail = x_ref[place + half_rows : place + MESSAGE_ROWS, :]
        gram = tail if gram is None else gram + tail
    for row in range(columns):
        half, shift = row // SUBLANES, LANES - row % SUBLANES * columns
        line = gram[half : half + 1]
        line = pltpu.roll(line, shift, 1) if shift < LANES else line
        gram_ref[row : row + 1, :] = line[:, :columns]
    sends = [pltpu.make_async_copy(gram_ref, gram_hbm, sent.at[0])]
    sends[0].start()
    sub = lax.broadcasted_iota(jnp.int32, (SUBLANES, LANES), 0)
    lane = lax.broadcasted_iota(jnp.int32, (SUBLANES, LANES), 1)
    pieces = []
    for source in range(sources):
        place = source * MESSAGE_ROWS
        piece = x_ref[place : place + half_rows, :]
        piece = jnp.concatenate([piece, piece], axis=0)
        pieces.append(jnp.where(sub < half_rows, piece, pltpu.roll(piece, LANES // 2, 1)))
    for half in range(2):
        rows = pl.ds(half * SUBLANES, SUBLANES)
        for start in range(0, sources, 4):
            joined = None
            for index in range(4):
                shift = (index - half) % 4 * quarter
                piece = pieces[start + index]
                moved = pltpu.roll(piece, shift, 1) if shift else piece
                joined = moved if joined is None else jnp.where(lane // quarter == index, moved, joined)
            sketch_ref[rows, start * quarter : (start + 4) * quarter] = joined
        sends.append(
            pltpu.make_async_copy(sketch_ref.at[rows], sketch_hbm.at[rows], sent.at[half + 1])
        )
        sends[-1].start()
    for send in sends:
        send.wait()


def finish(received, columns, sample_count):
    sketch, gram = (columns, sample_count), (columns, columns)
    return pl.pallas_call(
        finish_kernel,
        out_shape=(
            jax.ShapeDtypeStruct(sketch, jnp.float32),
            jax.ShapeDtypeStruct(gram, jnp.float32),
        ),
        in_specs=in_vmem(1),
        out_specs=(pl.BlockSpec(memory_space=pltpu.HBM),) * 2,
        scratch_shapes=[
            pltpu.VMEM(sketch, jnp.float32),
            pltpu.VMEM(gram, jnp.float32),
            pltpu.SemaphoreType.DMA((3,)),
        ],
        compiler_params=pltpu.CompilerParams(vmem_limit_bytes=VMEM_LIMIT),
    )(received)


def exchange(values, axes):
    return lax.all_to_all(values, axes, split_axis=0, concat_axis=0, tiled=True)


def general_shards(matrix_slab, row_signs, sample_rows):
    columns, row_count = matrix_slab.shape
    sample_count = sample_rows.shape[0]
    devices = lax.axis_size("wide") * lax.axis_size("narrow")
    run_length = row_count // sample_count
    slice_rows = row_count // devices
    slice_runs = slice_rows // run_length
    values = jnp.swapaxes(local_transform(matrix_slab, row_signs), 0, 1)
    values = values.reshape(columns, devices, slice_rows)
    received = exchange(jnp.swapaxes(values, 0, 1), AXES)
    offsets = exchange(sample_rows.reshape(devices, slice_runs), AXES)
    mixed = jnp.einsum("ds,scr->dcr", sylvester(devices), received, precision=lax.Precision.HIGHEST)
    mixed = mixed.reshape(devices, columns, slice_runs, run_length)
    chosen = offsets[:, None, :, None] == lax.iota(jnp.int32, run_length)
    picked = jnp.sum(jnp.where(chosen, mixed, 0.0), axis=3)
    picked = picked * jnp.float32(1.0 / math.sqrt(row_count * devices))
    gram = jnp.einsum("dck,dek->ce", picked, picked, precision=lax.Precision.HIGHEST)
    gram = gram / jnp.float32(sample_count * devices)
    grams = jnp.broadcast_to(gram[None], (devices, columns, columns))
    back = exchange(jnp.concatenate([picked, grams], axis=2), AXES)
    sketch = jnp.swapaxes(back[:, :, :slice_runs], 0, 1).reshape(columns, devices * slice_runs)
    return sketch, jnp.sum(back[:, :, slice_runs:], axis=0)


def sliced_shards(matrix_slab, row_signs, sample_rows):
    columns, row_count = matrix_slab.shape
    sample_count = sample_rows.shape[0]
    devices = lax.axis_size(ORDER)
    run_length = row_count // sample_count
    sent = sliced_transform(matrix_slab, row_signs, sample_rows)
    received = exchange(sent.reshape(devices, -1), ORDER).reshape(sent.shape)
    scale = 1.0 / math.sqrt(row_count * devices)
    gram_scale = 1.0 / (sample_count * devices)
    picked = mix_and_pick(received, devices, run_length, scale, gram_scale)
    returned = exchange(picked.reshape(devices, -1), ORDER).reshape(picked.shape)
    return finish(returned, columns, sample_count)


def solution(mesh):
    wide, narrow = mesh.shape["wide"], mesh.shape["narrow"]
    axes, function = AXES, general_shards
    if wide * narrow == 32 and wide % 4 == 0:
        axes, function = SPLIT_AXES, sliced_shards
        mesh = jax.sharding.Mesh(mesh.devices.reshape(4, wide // 4, narrow), axes)
    in_specs = (P(None, axes), P(axes), P(axes))
    out_specs = (P(None, axes), P())
    return jax.shard_map(function, mesh=mesh, in_specs=in_specs, out_specs=out_specs, check_vma=False)
```

```python
import functools
import math

import jax
import jax.numpy as jnp
from jax import lax
from jax.experimental import pallas as pl
from jax.experimental.pallas import tpu as pltpu
from jax.sharding import PartitionSpec as P

LANES = 128
SUBLANES = 8
AXES = ("wide", "narrow")
EVERYONE = ("everyone",)
VMEM_LIMIT = 32 * 1024 * 1024
MESSAGE_ROWS = 6


def butterfly(values):
    values = list(values)
    apart = 1
    while apart < len(values):
        for low in range(len(values)):
            if not low & apart:
                first, second = values[low], values[low | apart]
                values[low], values[low | apart] = first + second, first - second
        apart *= 2
    return values


def sylvester(order_size):
    rows = lax.broadcasted_iota(jnp.int32, (order_size, order_size), 0)
    cols = lax.broadcasted_iota(jnp.int32, (order_size, order_size), 1)
    common = rows & cols
    parity = jnp.zeros_like(common)
    for bit_pos in range(order_size.bit_length() - 1):
        parity = parity ^ (common >> bit_pos)
    return (1 - 2 * (parity & 1)).astype(jnp.float32)


def split_dot(values, table, parts=3):
    total = None
    for _ in range(parts):
        part = values.astype(jnp.bfloat16)
        values = values - part.astype(jnp.float32)
        product = jnp.dot(part, table, preferred_element_type=jnp.float32)
        total = product if total is None else total + product
    return total


def butterfly_steps(count):
    steps = []
    apart = 1
    while apart < count:
        radix = min(8, count // apart)
        for start in range(count):
            if start // apart % radix == 0:
                steps.append((apart, [start + apart * index for index in range(radix)]))
        apart *= radix
    return steps


def fetch_blocks(x_hbm, signs_hbm, out_ref, x_ref, signs_ref, arrived):
    blocks, columns, _ = out_ref.shape
    fetches = [pltpu.make_async_copy(signs_hbm, signs_ref, arrived.at[0])]
    places = [pl.ds(start, SUBLANES) for start in range(0, columns, SUBLANES)]
    for index, place in enumerate(places):
        fetches.append(
            pltpu.make_async_copy(x_hbm.at[place], x_ref.at[place], arrived.at[index + 1])
        )
    for fetch in fetches:
        fetch.start()
    table = sylvester(LANES).astype(jnp.bfloat16)
    fetches[0].wait()
    for index, place in enumerate(places):
        fetches[index + 1].wait()
        signed = []
        for block in range(blocks):
            signs = signs_ref[block : block + 1, :].astype(jnp.float32)
            signed.append(x_ref[place, block * LANES : (block + 1) * LANES] * signs)
        mixed = split_dot(jnp.concatenate(signed, axis=0), table)
        out_ref[:, place, :] = mixed.reshape(blocks, SUBLANES, LANES)


def local_kernel(x_hbm, signs_hbm, out_ref, x_ref, signs_ref, arrived):
    fetch_blocks(x_hbm, signs_hbm, out_ref, x_ref, signs_ref, arrived)
    for apart, places in butterfly_steps(out_ref.shape[0]):
        for place, value in zip(places, butterfly([out_ref[p] for p in places])):
            out_ref[place] = value


def sliced_kernel(
    x_hbm, signs_hbm, samples_hbm, final_ref, out_ref, x_ref, signs_ref, samples_ref, arrived, noted
):
    note = pltpu.make_async_copy(samples_hbm, samples_ref, noted)
    note.start()
    fetch_blocks(x_hbm, signs_hbm, out_ref, x_ref, signs_ref, arrived)
    blocks, columns, _ = out_ref.shape
    slices = blocks // 2
    rows = final_ref.shape[0] // slices
    note.wait()
    samples = samples_ref[...].astype(jnp.float32)
    per_row = slices // samples.shape[0]
    for turn in range(per_row):
        shift = LANES - turn * LANES // per_row
        turned = pltpu.roll(samples, shift, 1) if turn else samples
        for index in range(turn, slices, per_row):
            tail = (slices - index) * rows - 1
            final_ref[tail : tail + 1, :] = turned[index // per_row : index // per_row + 1]
    steps = butterfly_steps(blocks)
    last = steps[-1][0]
    for apart, places in steps:
        for place, value in zip(places, butterfly([out_ref[p] for p in places])):
            if apart == last:
                start = (slices - 1 - place // 2) * rows + place % 2 * columns
                final_ref[start : start + columns, :] = value
            else:
                out_ref[place] = value


def in_vmem(count):
    return [pl.BlockSpec(memory_space=pltpu.VMEM)] * count


def in_hbm(*arrays):
    return [pltpu.with_memory_space_constraint(array, pltpu.HBM) for array in arrays]


def fetch_scratch(matrix_slab, blocks):
    return [
        pltpu.VMEM(matrix_slab.shape, jnp.float32),
        pltpu.VMEM((blocks, LANES), jnp.int32),
    ]


def local_transform(matrix_slab, row_signs):
    columns, row_count = matrix_slab.shape
    blocks = row_count // LANES
    return pl.pallas_call(
        local_kernel,
        out_shape=jax.ShapeDtypeStruct((blocks, columns, LANES), jnp.float32),
        in_specs=[pl.BlockSpec(memory_space=pltpu.HBM)] * 2,
        out_specs=in_vmem(1)[0],
        scratch_shapes=[
            *fetch_scratch(matrix_slab, blocks),
            pltpu.SemaphoreType.DMA((columns // SUBLANES + 1,)),
        ],
        compiler_params=pltpu.CompilerParams(vmem_limit_bytes=VMEM_LIMIT),
    )(*in_hbm(matrix_slab, row_signs.reshape(blocks, LANES)))


def sliced_transform(matrix_slab, row_signs, sample_rows):
    columns, row_count = matrix_slab.shape
    blocks = row_count // LANES
    samples = sample_rows.reshape(-1, LANES)
    return pl.pallas_call(
        sliced_kernel,
        out_shape=jax.ShapeDtypeStruct((blocks // 2 * (2 * columns + 1), LANES), jnp.float32),
        in_specs=[pl.BlockSpec(memory_space=pltpu.HBM)] * 3,
        out_specs=in_vmem(1)[0],
        scratch_shapes=[
            pltpu.VMEM((blocks, columns, LANES), jnp.float32),
            *fetch_scratch(matrix_slab, blocks),
            pltpu.VMEM(samples.shape, jnp.int32),
            pltpu.SemaphoreType.DMA((columns // SUBLANES + 1,)),
            pltpu.SemaphoreType.DMA(()),
        ],
        compiler_params=pltpu.CompilerParams(vmem_limit_bytes=VMEM_LIMIT),
    )(*in_hbm(matrix_slab, row_signs.reshape(blocks, LANES), samples))


def mix_kernel(run_length, scale, gram_scale, x_ref, out_ref):
    devices = out_ref.shape[0] // MESSAGE_ROWS
    rows = x_ref.shape[0] // devices
    runs = LANES // run_length
    samples = jnp.concatenate(
        [x_ref[s * rows - 1 : s * rows, :] for s in range(devices, 0, -1)], axis=0
    ).astype(jnp.bfloat16)
    run_of = lax.broadcasted_iota(jnp.int32, (LANES, 2 * LANES), 0)
    row_of = lax.broadcasted_iota(jnp.int32, (LANES, 2 * LANES), 1)
    spread = jnp.where(row_of // run_length == run_of, 1.0, 0.0).astype(jnp.bfloat16)
    offsets = jnp.dot(samples, spread, preferred_element_type=jnp.float32)
    own = lax.broadcasted_iota(jnp.int32, offsets.shape, 1) % run_length
    mask = jnp.where(offsets == own.astype(jnp.float32), scale, 0.0)
    picked = []
    for part in range(4):
        block = part // 2
        starts = [s * rows + part * SUBLANES for s in reversed(range(devices))]
        mixed = butterfly([x_ref[start : start + SUBLANES, :] for start in starts])
        picked.append(
            jnp.concatenate(
                [
                    mixed[d] * mask[d : d + 1, block * LANES : (block + 1) * LANES]
                    for d in range(devices)
                ],
                axis=0,
            )
        )
    quarter = 2 * runs
    row = lax.broadcasted_iota(jnp.int32, (LANES, LANES), 0)
    lane = lax.broadcasted_iota(jnp.int32, (LANES, LANES), 1)
    pattern = jnp.where(row // run_length == lane % runs, 1.0, 0.0)
    lane = lax.broadcasted_iota(jnp.int32, (1, LANES), 1)
    group = lane // quarter
    place = []
    for part in range(4):
        block, half = part // 2, part % 2
        here = lane // runs % 2 == block
        sides = [group % 2, jnp.where(group < 2, group, 3 - group)]
        masks = [jnp.where(here & (side == half), 1.0, 0.0) for side in sides]
        place.append(jnp.concatenate([(pattern * mask).astype(jnp.bfloat16) for mask in masks], axis=1))
    gathered = split_dot(jnp.concatenate(picked, axis=1), jnp.concatenate(place, axis=0), 2)
    straight, crossed = gathered[:, :LANES], gathered[:, LANES:]
    turns = SUBLANES // 2 + 1
    totals = []
    for turn in range(turns):
        total = None
        for d in range(devices):
            one = straight[d * SUBLANES : (d + 1) * SUBLANES]
            two = crossed[d * SUBLANES : (d + 1) * SUBLANES]
            if turn:
                two = pltpu.roll(two, SUBLANES - turn, 0)
            total = one * two if total is None else total + one * two
        totals.append(total)
    from_quarter = row // quarter
    together = [jnp.where(from_quarter == q, 1.0, 0.0).astype(jnp.bfloat16) for q in range(4)]
    sums = split_dot(jnp.concatenate(totals, axis=0), jnp.concatenate(together, axis=1)) * gram_scale
    sub = lax.broadcasted_iota(jnp.int32, (SUBLANES, LANES), 0)
    lane = lax.broadcasted_iota(jnp.int32, (SUBLANES, LANES), 1)
    first, second = [jnp.zeros((SUBLANES, LANES), jnp.float32)] * 2
    for turn in range(SUBLANES):
        known = min(turn, SUBLANES - turn)
        here = sums[known * SUBLANES : (known + 1) * SUBLANES]
        quarters = [here[:, q * LANES : (q + 1) * LANES] for q in range(4)]
        if known != turn:
            quarters = [pltpu.roll(quarters[q], known, 0) for q in (0, 1, 3, 2)]
        mine = lane % SUBLANES == (sub + turn) % SUBLANES
        left = lane // SUBLANES % 2 == 0
        first = jnp.where(mine, jnp.where(left, quarters[0], quarters[2]), first)
        second = jnp.where(mine, jnp.where(left, quarters[3], quarters[1]), second)
    in_place = lane // (2 * SUBLANES) == sub
    gram = jnp.concatenate(
        [jnp.sum(jnp.where(in_place, part, 0.0), axis=0, keepdims=True) for part in (first, second)],
        axis=0,
    )
    half = SUBLANES // 2
    lane = lax.broadcasted_iota(jnp.int32, (half, LANES), 1)
    for d in range(devices):
        one = straight[d * SUBLANES : (d + 1) * SUBLANES]
        start = (devices - 1 - d) * MESSAGE_ROWS
        out_ref[start : start + half, :] = jnp.where(lane < LANES // 2, one[:half], one[half:])
        out_ref[start + half : start + MESSAGE_ROWS, :] = gram


def mix_and_pick(received, devices, run_length, scale, gram_scale):
    return pl.pallas_call(
        functools.partial(mix_kernel, run_length, scale, gram_scale),
        out_shape=jax.ShapeDtypeStruct((devices * MESSAGE_ROWS, LANES), jnp.float32),
        in_specs=in_vmem(1),
        out_specs=in_vmem(1)[0],
        compiler_params=pltpu.CompilerParams(vmem_limit_bytes=VMEM_LIMIT),
    )(received)


def finish_kernel(x_ref, sketch_ref, gram_ref):
    sources = x_ref.shape[0] // MESSAGE_ROWS
    quarter = LANES // 4
    half_rows = SUBLANES // 2
    sub = lax.broadcasted_iota(jnp.int32, (SUBLANES, LANES), 0)
    lane = lax.broadcasted_iota(jnp.int32, (SUBLANES, LANES), 1)
    gram = None
    for start in range(0, sources, 4):
        halves = [None, None]
        for index in range(4):
            place = (sources - 1 - start - index) * MESSAGE_ROWS
            tail = x_ref[place + half_rows : place + MESSAGE_ROWS, :]
            gram = tail if gram is None else gram + tail
            piece = x_ref[place : place + half_rows, :]
            piece = jnp.concatenate([piece, piece], axis=0)
            piece = jnp.where(sub < half_rows, piece, pltpu.roll(piece, LANES // 2, 1))
            for half in range(2):
                shift = (index - half) % 4 * quarter
                moved = pltpu.roll(piece, shift, 1) if shift else piece
                if halves[half] is None:
                    halves[half] = moved
                else:
                    halves[half] = jnp.where(lane // quarter == index, moved, halves[half])
        for half in range(2):
            sketch_ref[
                half * SUBLANES : (half + 1) * SUBLANES, start * quarter : (start + 4) * quarter
            ] = halves[half]
    columns = gram_ref.shape[0]
    for half in range(2):
        for row in range(SUBLANES):
            line = gram[half : half + 1]
            line = pltpu.roll(line, LANES - row * columns, 1) if row else line
            gram_ref[half * SUBLANES + row : half * SUBLANES + row + 1, :] = line[:, :columns]


def finish(received, columns, sample_count):
    return pl.pallas_call(
        finish_kernel,
        out_shape=(
            jax.ShapeDtypeStruct((columns, sample_count), jnp.float32),
            jax.ShapeDtypeStruct((columns, columns), jnp.float32),
        ),
        in_specs=[pl.BlockSpec(memory_space=pltpu.VMEM)],
        out_specs=(pl.BlockSpec(memory_space=pltpu.VMEM),) * 2,
        compiler_params=pltpu.CompilerParams(vmem_limit_bytes=VMEM_LIMIT),
    )(received)


def exchange(values, axes, groups=None):
    return lax.all_to_all(
        values, axes, split_axis=0, concat_axis=0, axis_index_groups=groups, tiled=True
    )


def backward_order(long, middle, short):
    order = [
        (line * middle + plane) * short + narrow
        for plane in range(middle)
        for narrow in range(short)
        for line in range(long)
    ]
    return order[::-1]


def general_shards(matrix_slab, row_signs, sample_rows):
    columns, row_count = matrix_slab.shape
    sample_count = sample_rows.shape[0]
    devices = lax.axis_size("wide") * lax.axis_size("narrow")
    run_length = row_count // sample_count
    slice_rows = row_count // devices
    slice_runs = slice_rows // run_length
    values = jnp.swapaxes(local_transform(matrix_slab, row_signs), 0, 1)
    values = values.reshape(columns, devices, slice_rows)
    received = exchange(jnp.swapaxes(values, 0, 1), AXES)
    offsets = exchange(sample_rows.reshape(devices, slice_runs), AXES)
    mixed = jnp.einsum("ds,scr->dcr", sylvester(devices), received, precision=lax.Precision.HIGHEST)
    mixed = mixed.reshape(devices, columns, slice_runs, run_length)
    chosen = offsets[:, None, :, None] == lax.iota(jnp.int32, run_length)
    picked = jnp.sum(jnp.where(chosen, mixed, 0.0), axis=3)
    picked = picked * jnp.float32(1.0 / math.sqrt(row_count * devices))
    gram = jnp.einsum("dck,dek->ce", picked, picked, precision=lax.Precision.HIGHEST)
    gram = gram / jnp.float32(sample_count * devices)
    grams = jnp.broadcast_to(gram[None], (devices, columns, columns))
    back = exchange(jnp.concatenate([picked, grams], axis=2), AXES)
    sketch = jnp.swapaxes(back[:, :, :slice_runs], 0, 1).reshape(columns, devices * slice_runs)
    return sketch, jnp.sum(back[:, :, slice_runs:], axis=0)


def sliced_shards(order, matrix_slab, row_signs, sample_rows):
    columns, row_count = matrix_slab.shape
    sample_count = sample_rows.shape[0]
    devices = len(order)
    run_length = row_count // sample_count
    sent = sliced_transform(matrix_slab, row_signs, sample_rows)
    received = exchange(sent.reshape(devices, -1), EVERYONE, [order]).reshape(sent.shape)
    scale = 1.0 / math.sqrt(row_count * devices)
    gram_scale = 1.0 / (sample_count * devices)
    picked = mix_and_pick(received, devices, run_length, scale, gram_scale)
    returned = exchange(picked.reshape(devices, -1), EVERYONE, [order]).reshape(picked.shape)
    return finish(returned, columns, sample_count)


def solution(mesh):
    wide, narrow = mesh.shape["wide"], mesh.shape["narrow"]
    axes, function = AXES, general_shards
    if wide * narrow == 32 and wide % 4 == 0:
        axes, function = EVERYONE, functools.partial(
            sliced_shards, backward_order(4, wide // 4, narrow)
        )
        mesh = jax.sharding.Mesh(mesh.devices.reshape(-1), axes)
    in_specs = (P(None, axes), P(axes), P(axes))
    out_specs = (P(None, axes), P())
    return jax.shard_map(function, mesh=mesh, in_specs=in_specs, out_specs=out_specs, check_vma=False)
```

```python
import functools
import math

import jax
import jax.numpy as jnp
from jax import lax
from jax.experimental import pallas as pl
from jax.experimental.pallas import tpu as pltpu
from jax.sharding import PartitionSpec as P

LANES = 128
SUBLANES = 8
AXES = ("wide", "narrow")
BIT_AXES = ("bit3", "bit2", "bit1", "bit0", "narrow")
FIRST_ORDER = ("bit0", "bit1", "narrow", "bit3", "bit2")
SECOND_ORDER = ("bit0", "bit1", "narrow", "bit3", "bit2")
VMEM_LIMIT = 32 * 1024 * 1024
MESSAGE_ROWS = 6


def positions(order, other):
    count = 2 ** len(order)
    found = []
    for place in range(count):
        bits = {axis: place >> (len(order) - 1 - rank) & 1 for rank, axis in enumerate(order)}
        found.append(sum(bits[axis] << (len(other) - 1 - rank) for rank, axis in enumerate(other)))
    return tuple(found)


def butterfly(values):
    values = list(values)
    apart = 1
    while apart < len(values):
        for low in range(len(values)):
            if not low & apart:
                first, second = values[low], values[low | apart]
                values[low], values[low | apart] = first + second, first - second
        apart *= 2
    return values


def sylvester(order_size):
    rows = lax.broadcasted_iota(jnp.int32, (order_size, order_size), 0)
    cols = lax.broadcasted_iota(jnp.int32, (order_size, order_size), 1)
    common = rows & cols
    parity = jnp.zeros_like(common)
    for bit_pos in range(order_size.bit_length() - 1):
        parity = parity ^ (common >> bit_pos)
    return (1 - 2 * (parity & 1)).astype(jnp.float32)


def split_dot(values, table, parts=3):
    total = None
    for _ in range(parts):
        part = values.astype(jnp.bfloat16)
        values = values - part.astype(jnp.float32)
        product = jnp.dot(part, table, preferred_element_type=jnp.float32)
        total = product if total is None else total + product
    return total


def butterfly_steps(count):
    steps = []
    apart = 1
    while apart < count:
        radix = min(8, count // apart)
        for start in range(count):
            if start // apart % radix == 0:
                steps.append((apart, [start + apart * index for index in range(radix)]))
        apart *= radix
    return steps


def fetch_blocks(x_hbm, signs_hbm, out_ref, x_ref, signs_ref, arrived):
    blocks, columns, _ = out_ref.shape
    fetches = [pltpu.make_async_copy(signs_hbm, signs_ref, arrived.at[0])]
    places = [pl.ds(start, SUBLANES) for start in range(0, columns, SUBLANES)]
    for index, place in enumerate(places):
        fetches.append(
            pltpu.make_async_copy(x_hbm.at[place], x_ref.at[place], arrived.at[index + 1])
        )
    for fetch in fetches:
        fetch.start()
    table = sylvester(LANES).astype(jnp.bfloat16)
    fetches[0].wait()
    for index, place in enumerate(places):
        fetches[index + 1].wait()
        signed = []
        for block in range(blocks):
            signs = signs_ref[block : block + 1, :].astype(jnp.float32)
            signed.append(x_ref[place, block * LANES : (block + 1) * LANES] * signs)
        mixed = split_dot(jnp.concatenate(signed, axis=0), table)
        out_ref[:, place, :] = mixed.reshape(blocks, SUBLANES, LANES)


def local_kernel(x_hbm, signs_hbm, out_ref, x_ref, signs_ref, arrived):
    fetch_blocks(x_hbm, signs_hbm, out_ref, x_ref, signs_ref, arrived)
    for apart, places in butterfly_steps(out_ref.shape[0]):
        for place, value in zip(places, butterfly([out_ref[p] for p in places])):
            out_ref[place] = value


def sliced_kernel(
    x_hbm, signs_hbm, samples_hbm, final_ref, out_ref, x_ref, signs_ref, samples_ref, arrived, noted
):
    note = pltpu.make_async_copy(samples_hbm, samples_ref, noted)
    note.start()
    fetch_blocks(x_hbm, signs_hbm, out_ref, x_ref, signs_ref, arrived)
    blocks, columns, _ = out_ref.shape
    slices = blocks // 2
    rows = final_ref.shape[0] // slices
    note.wait()
    samples = samples_ref[...].astype(jnp.float32)
    per_row = slices // samples.shape[0]
    for turn in range(per_row):
        shift = LANES - turn * LANES // per_row
        turned = pltpu.roll(samples, shift, 1) if turn else samples
        for index in range(turn, slices, per_row):
            tail = (index + 1) * rows - 1
            final_ref[tail : tail + 1, :] = turned[index // per_row : index // per_row + 1]
    steps = butterfly_steps(blocks)
    last = steps[-1][0]
    for apart, places in steps:
        for place, value in zip(places, butterfly([out_ref[p] for p in places])):
            if apart == last:
                start = place // 2 * rows + place % 2 * columns
                final_ref[start : start + columns, :] = value
            else:
                out_ref[place] = value


def in_vmem(count):
    return [pl.BlockSpec(memory_space=pltpu.VMEM)] * count


def in_hbm(*arrays):
    return [pltpu.with_memory_space_constraint(array, pltpu.HBM) for array in arrays]


def fetch_scratch(matrix_slab, blocks):
    return [
        pltpu.VMEM(matrix_slab.shape, jnp.float32),
        pltpu.VMEM((blocks, LANES), jnp.int32),
    ]


def local_transform(matrix_slab, row_signs):
    columns, row_count = matrix_slab.shape
    blocks = row_count // LANES
    return pl.pallas_call(
        local_kernel,
        out_shape=jax.ShapeDtypeStruct((blocks, columns, LANES), jnp.float32),
        in_specs=[pl.BlockSpec(memory_space=pltpu.HBM)] * 2,
        out_specs=in_vmem(1)[0],
        scratch_shapes=[
            *fetch_scratch(matrix_slab, blocks),
            pltpu.SemaphoreType.DMA((columns // SUBLANES + 1,)),
        ],
        compiler_params=pltpu.CompilerParams(vmem_limit_bytes=VMEM_LIMIT),
    )(*in_hbm(matrix_slab, row_signs.reshape(blocks, LANES)))


def sliced_transform(matrix_slab, row_signs, sample_rows):
    columns, row_count = matrix_slab.shape
    blocks = row_count // LANES
    samples = sample_rows.reshape(-1, LANES)
    return pl.pallas_call(
        sliced_kernel,
        out_shape=jax.ShapeDtypeStruct((blocks // 2 * (2 * columns + 1), LANES), jnp.float32),
        in_specs=[pl.BlockSpec(memory_space=pltpu.HBM)] * 3,
        out_specs=in_vmem(1)[0],
        scratch_shapes=[
            pltpu.VMEM((blocks, columns, LANES), jnp.float32),
            *fetch_scratch(matrix_slab, blocks),
            pltpu.VMEM(samples.shape, jnp.int32),
            pltpu.SemaphoreType.DMA((columns // SUBLANES + 1,)),
            pltpu.SemaphoreType.DMA(()),
        ],
        compiler_params=pltpu.CompilerParams(vmem_limit_bytes=VMEM_LIMIT),
    )(*in_hbm(matrix_slab, row_signs.reshape(blocks, LANES), samples))


def mix_kernel(run_length, scale, gram_scale, places, x_ref, out_ref):
    devices = out_ref.shape[0] // MESSAGE_ROWS
    rows = x_ref.shape[0] // devices
    runs = LANES // run_length
    samples = jnp.concatenate(
        [x_ref[(s + 1) * rows - 1 : (s + 1) * rows, :] for s in range(devices)], axis=0
    ).astype(jnp.bfloat16)
    run_of = lax.broadcasted_iota(jnp.int32, (LANES, 2 * LANES), 0)
    row_of = lax.broadcasted_iota(jnp.int32, (LANES, 2 * LANES), 1)
    spread = jnp.where(row_of // run_length == run_of, 1.0, 0.0).astype(jnp.bfloat16)
    offsets = jnp.dot(samples, spread, preferred_element_type=jnp.float32)
    own = lax.broadcasted_iota(jnp.int32, offsets.shape, 1) % run_length
    mask = jnp.where(offsets == own.astype(jnp.float32), scale, 0.0)
    picked = []
    for part in range(4):
        block = part // 2
        starts = [s * rows + part * SUBLANES for s in range(devices)]
        mixed = butterfly([x_ref[start : start + SUBLANES, :] for start in starts])
        picked.append(
            jnp.concatenate(
                [
                    mixed[d] * mask[d : d + 1, block * LANES : (block + 1) * LANES]
                    for d in range(devices)
                ],
                axis=0,
            )
        )
    quarter = 2 * runs
    row = lax.broadcasted_iota(jnp.int32, (LANES, LANES), 0)
    lane = lax.broadcasted_iota(jnp.int32, (LANES, LANES), 1)
    pattern = jnp.where(row // run_length == lane % runs, 1.0, 0.0)
    lane = lax.broadcasted_iota(jnp.int32, (1, LANES), 1)
    group = lane // quarter
    place = []
    for part in range(4):
        block, half = part // 2, part % 2
        here = lane // runs % 2 == block
        sides = [group % 2, jnp.where(group < 2, group, 3 - group)]
        masks = [jnp.where(here & (side == half), 1.0, 0.0) for side in sides]
        place.append(jnp.concatenate([(pattern * mask).astype(jnp.bfloat16) for mask in masks], axis=1))
    gathered = split_dot(jnp.concatenate(picked, axis=1), jnp.concatenate(place, axis=0), 2)
    straight, crossed = gathered[:, :LANES], gathered[:, LANES:]
    turns = SUBLANES // 2 + 1
    totals = []
    for turn in range(turns):
        total = None
        for d in range(devices):
            one = straight[d * SUBLANES : (d + 1) * SUBLANES]
            two = crossed[d * SUBLANES : (d + 1) * SUBLANES]
            if turn:
                two = pltpu.roll(two, SUBLANES - turn, 0)
            total = one * two if total is None else total + one * two
        totals.append(total)
    from_quarter = row // quarter
    together = [jnp.where(from_quarter == q, 1.0, 0.0).astype(jnp.bfloat16) for q in range(4)]
    sums = split_dot(jnp.concatenate(totals, axis=0), jnp.concatenate(together, axis=1)) * gram_scale
    sub = lax.broadcasted_iota(jnp.int32, (SUBLANES, LANES), 0)
    lane = lax.broadcasted_iota(jnp.int32, (SUBLANES, LANES), 1)
    first, second = [jnp.zeros((SUBLANES, LANES), jnp.float32)] * 2
    for turn in range(SUBLANES):
        known = min(turn, SUBLANES - turn)
        here = sums[known * SUBLANES : (known + 1) * SUBLANES]
        quarters = [here[:, q * LANES : (q + 1) * LANES] for q in range(4)]
        if known != turn:
            quarters = [pltpu.roll(quarters[q], known, 0) for q in (0, 1, 3, 2)]
        mine = lane % SUBLANES == (sub + turn) % SUBLANES
        left = lane // SUBLANES % 2 == 0
        first = jnp.where(mine, jnp.where(left, quarters[0], quarters[2]), first)
        second = jnp.where(mine, jnp.where(left, quarters[3], quarters[1]), second)
    in_place = lane // (2 * SUBLANES) == sub
    gram = jnp.concatenate(
        [jnp.sum(jnp.where(in_place, part, 0.0), axis=0, keepdims=True) for part in (first, second)],
        axis=0,
    )
    half = SUBLANES // 2
    lane = lax.broadcasted_iota(jnp.int32, (half, LANES), 1)
    for d in range(devices):
        one = straight[d * SUBLANES : (d + 1) * SUBLANES]
        start = places[d] * MESSAGE_ROWS
        out_ref[start : start + half, :] = jnp.where(lane < LANES // 2, one[:half], one[half:])
        out_ref[start + half : start + MESSAGE_ROWS, :] = gram


def mix_and_pick(received, devices, run_length, scale, gram_scale, places):
    return pl.pallas_call(
        functools.partial(mix_kernel, run_length, scale, gram_scale, places),
        out_shape=jax.ShapeDtypeStruct((devices * MESSAGE_ROWS, LANES), jnp.float32),
        in_specs=in_vmem(1),
        out_specs=in_vmem(1)[0],
        compiler_params=pltpu.CompilerParams(vmem_limit_bytes=VMEM_LIMIT),
    )(received)


def finish_kernel(places, x_ref, sketch_ref, gram_ref):
    sources = x_ref.shape[0] // MESSAGE_ROWS
    quarter = LANES // 4
    half_rows = SUBLANES // 2
    sub = lax.broadcasted_iota(jnp.int32, (SUBLANES, LANES), 0)
    lane = lax.broadcasted_iota(jnp.int32, (SUBLANES, LANES), 1)
    gram = None
    for start in range(0, sources, 4):
        halves = [None, None]
        for index in range(4):
            place = places[start + index] * MESSAGE_ROWS
            tail = x_ref[place + half_rows : place + MESSAGE_ROWS, :]
            gram = tail if gram is None else gram + tail
            piece = x_ref[place : place + half_rows, :]
            piece = jnp.concatenate([piece, piece], axis=0)
            piece = jnp.where(sub < half_rows, piece, pltpu.roll(piece, LANES // 2, 1))
            for half in range(2):
                shift = (index - half) % 4 * quarter
                moved = pltpu.roll(piece, shift, 1) if shift else piece
                if halves[half] is None:
                    halves[half] = moved
                else:
                    halves[half] = jnp.where(lane // quarter == index, moved, halves[half])
        for half in range(2):
            sketch_ref[
                half * SUBLANES : (half + 1) * SUBLANES, start * quarter : (start + 4) * quarter
            ] = halves[half]
    columns = gram_ref.shape[0]
    for half in range(2):
        for row in range(SUBLANES):
            line = gram[half : half + 1]
            line = pltpu.roll(line, LANES - row * columns, 1) if row else line
            gram_ref[half * SUBLANES + row : half * SUBLANES + row + 1, :] = line[:, :columns]


def finish(received, columns, sample_count, places):
    return pl.pallas_call(
        functools.partial(finish_kernel, places),
        out_shape=(
            jax.ShapeDtypeStruct((columns, sample_count), jnp.float32),
            jax.ShapeDtypeStruct((columns, columns), jnp.float32),
        ),
        in_specs=[pl.BlockSpec(memory_space=pltpu.VMEM)],
        out_specs=(pl.BlockSpec(memory_space=pltpu.VMEM),) * 2,
        compiler_params=pltpu.CompilerParams(vmem_limit_bytes=VMEM_LIMIT),
    )(received)


def exchange(values, axes):
    return lax.all_to_all(values, axes, split_axis=0, concat_axis=0, tiled=True)


def general_shards(matrix_slab, row_signs, sample_rows):
    columns, row_count = matrix_slab.shape
    sample_count = sample_rows.shape[0]
    devices = lax.axis_size("wide") * lax.axis_size("narrow")
    run_length = row_count // sample_count
    slice_rows = row_count // devices
    slice_runs = slice_rows // run_length
    values = jnp.swapaxes(local_transform(matrix_slab, row_signs), 0, 1)
    values = values.reshape(columns, devices, slice_rows)
    received = exchange(jnp.swapaxes(values, 0, 1), AXES)
    offsets = exchange(sample_rows.reshape(devices, slice_runs), AXES)
    mixed = jnp.einsum("ds,scr->dcr", sylvester(devices), received, precision=lax.Precision.HIGHEST)
    mixed = mixed.reshape(devices, columns, slice_runs, run_length)
    chosen = offsets[:, None, :, None] == lax.iota(jnp.int32, run_length)
    picked = jnp.sum(jnp.where(chosen, mixed, 0.0), axis=3)
    picked = picked * jnp.float32(1.0 / math.sqrt(row_count * devices))
    gram = jnp.einsum("dck,dek->ce", picked, picked, precision=lax.Precision.HIGHEST)
    gram = gram / jnp.float32(sample_count * devices)
    grams = jnp.broadcast_to(gram[None], (devices, columns, columns))
    back = exchange(jnp.concatenate([picked, grams], axis=2), AXES)
    sketch = jnp.swapaxes(back[:, :, :slice_runs], 0, 1).reshape(columns, devices * slice_runs)
    return sketch, jnp.sum(back[:, :, slice_runs:], axis=0)


def sliced_shards(matrix_slab, row_signs, sample_rows):
    columns, row_count = matrix_slab.shape
    sample_count = sample_rows.shape[0]
    devices = lax.axis_size(FIRST_ORDER)
    places = positions(FIRST_ORDER, SECOND_ORDER)
    run_length = row_count // sample_count
    sent = sliced_transform(matrix_slab, row_signs, sample_rows)
    received = exchange(sent.reshape(devices, -1), FIRST_ORDER).reshape(sent.shape)
    scale = 1.0 / math.sqrt(row_count * devices)
    gram_scale = 1.0 / (sample_count * devices)
    picked = mix_and_pick(received, devices, run_length, scale, gram_scale, places)
    returned = exchange(picked.reshape(devices, -1), SECOND_ORDER).reshape(picked.shape)
    return finish(returned, columns, sample_count, places)


def solution(mesh):
    axes, function = AXES, general_shards
    if (mesh.shape["wide"], mesh.shape["narrow"]) == (16, 2):
        axes, function = BIT_AXES, sliced_shards
        mesh = jax.sharding.Mesh(mesh.devices.reshape((2,) * len(axes)), axes)
    in_specs = (P(None, axes), P(axes), P(axes))
    out_specs = (P(None, axes), P())
    return jax.shard_map(function, mesh=mesh, in_specs=in_specs, out_specs=out_specs, check_vma=False)
```

```python
import functools
import math

import jax
import jax.numpy as jnp
from jax import lax
from jax.experimental import pallas as pl
from jax.experimental.pallas import tpu as pltpu
from jax.sharding import PartitionSpec as P

LANES = 128
SUBLANES = 8
AXES = ("wide", "narrow")
SPLIT_AXES = ("line", "plane", "narrow")
ORDER = ("plane", "narrow", "line")
VMEM_LIMIT = 32 * 1024 * 1024
MESSAGE_ROWS = 6


def butterfly(values):
    values = list(values)
    apart = 1
    while apart < len(values):
        for low in range(len(values)):
            if not low & apart:
                first, second = values[low], values[low | apart]
                values[low], values[low | apart] = first + second, first - second
        apart *= 2
    return values


def sylvester(order_size):
    rows = lax.broadcasted_iota(jnp.int32, (order_size, order_size), 0)
    cols = lax.broadcasted_iota(jnp.int32, (order_size, order_size), 1)
    common = rows & cols
    parity = jnp.zeros_like(common)
    for bit_pos in range(order_size.bit_length() - 1):
        parity = parity ^ (common >> bit_pos)
    return (1 - 2 * (parity & 1)).astype(jnp.float32)


def split_dot(values, table, parts=3):
    total = None
    for _ in range(parts):
        part = values.astype(jnp.bfloat16)
        values = values - part.astype(jnp.float32)
        product = jnp.dot(part, table, preferred_element_type=jnp.float32)
        total = product if total is None else total + product
    return total


def butterfly_steps(count):
    steps = []
    apart = 2
    while apart < count:
        radix = min(8, count // apart)
        for start in range(count):
            if start // apart % radix == 0:
                steps.append((apart, [start + apart * index for index in range(radix)]))
        apart *= radix
    return steps


def fetch_blocks(x_hbm, signs_hbm, out_ref, x_ref, signs_ref, arrived):
    blocks, columns, _ = out_ref.shape
    fetches = [pltpu.make_async_copy(signs_hbm, signs_ref, arrived.at[0])]
    places = [pl.ds(start, SUBLANES) for start in range(0, columns, SUBLANES)]
    for index, place in enumerate(places):
        fetches.append(
            pltpu.make_async_copy(x_hbm.at[place], x_ref.at[place], arrived.at[index + 1])
        )
    for fetch in fetches:
        fetch.start()
    table = sylvester(2 * LANES).astype(jnp.bfloat16)
    fetches[0].wait()
    signs = signs_ref[...].astype(jnp.float32)
    for index, place in enumerate(places):
        fetches[index + 1].wait()
        signed = []
        for block in range(0, blocks, 2):
            pair = jnp.concatenate([signs[block : block + 1], signs[block + 1 : block + 2]], axis=1)
            signed.append(x_ref[place, block * LANES : (block + 2) * LANES] * pair)
        mixed = split_dot(jnp.concatenate(signed, axis=0), table)
        for block in range(blocks):
            rows = slice(block // 2 * SUBLANES, (block // 2 + 1) * SUBLANES)
            out_ref[block, place, :] = mixed[rows, block % 2 * LANES : (block % 2 + 1) * LANES]


def local_kernel(x_hbm, signs_hbm, out_ref, x_ref, signs_ref, arrived):
    fetch_blocks(x_hbm, signs_hbm, out_ref, x_ref, signs_ref, arrived)
    for apart, places in butterfly_steps(out_ref.shape[0]):
        for place, value in zip(places, butterfly([out_ref[p] for p in places])):
            out_ref[place] = value


def sliced_kernel(
    x_hbm, signs_hbm, samples_hbm, final_ref, out_ref, x_ref, signs_ref, samples_ref, arrived, noted
):
    note = pltpu.make_async_copy(samples_hbm, samples_ref, noted)
    note.start()
    fetch_blocks(x_hbm, signs_hbm, out_ref, x_ref, signs_ref, arrived)
    blocks, columns, _ = out_ref.shape
    slices = blocks // 2
    rows = final_ref.shape[0] // slices
    note.wait()
    samples = samples_ref[...].astype(jnp.float32)
    per_row = slices // samples.shape[0]
    for turn in range(per_row):
        shift = LANES - turn * LANES // per_row
        turned = pltpu.roll(samples, shift, 1) if turn else samples
        for index in range(turn, slices, per_row):
            tail = (index + 1) * rows - 1
            final_ref[tail : tail + 1, :] = turned[index // per_row : index // per_row + 1]
    steps = butterfly_steps(blocks)
    last = steps[-1][0]
    for apart, places in steps:
        for place, value in zip(places, butterfly([out_ref[p] for p in places])):
            if apart == last:
                start = place // 2 * rows + place % 2 * columns
                final_ref[start : start + columns, :] = value
            else:
                out_ref[place] = value


def in_vmem(count):
    return [pl.BlockSpec(memory_space=pltpu.VMEM)] * count


def in_hbm(*arrays):
    return [pltpu.with_memory_space_constraint(array, pltpu.HBM) for array in arrays]


def fetch_scratch(matrix_slab, blocks):
    return [
        pltpu.VMEM(matrix_slab.shape, jnp.float32),
        pltpu.VMEM((blocks, LANES), jnp.int32),
    ]


def local_transform(matrix_slab, row_signs):
    columns, row_count = matrix_slab.shape
    blocks = row_count // LANES
    return pl.pallas_call(
        local_kernel,
        out_shape=jax.ShapeDtypeStruct((blocks, columns, LANES), jnp.float32),
        in_specs=[pl.BlockSpec(memory_space=pltpu.HBM)] * 2,
        out_specs=in_vmem(1)[0],
        scratch_shapes=[
            *fetch_scratch(matrix_slab, blocks),
            pltpu.SemaphoreType.DMA((columns // SUBLANES + 1,)),
        ],
        compiler_params=pltpu.CompilerParams(vmem_limit_bytes=VMEM_LIMIT),
    )(*in_hbm(matrix_slab, row_signs.reshape(blocks, LANES)))


def sliced_transform(matrix_slab, row_signs, sample_rows):
    columns, row_count = matrix_slab.shape
    blocks = row_count // LANES
    samples = sample_rows.reshape(-1, LANES)
    return pl.pallas_call(
        sliced_kernel,
        out_shape=jax.ShapeDtypeStruct((blocks // 2 * (2 * columns + 1), LANES), jnp.float32),
        in_specs=[pl.BlockSpec(memory_space=pltpu.HBM)] * 3,
        out_specs=in_vmem(1)[0],
        scratch_shapes=[
            pltpu.VMEM((blocks, columns, LANES), jnp.float32),
            *fetch_scratch(matrix_slab, blocks),
            pltpu.VMEM(samples.shape, jnp.int32),
            pltpu.SemaphoreType.DMA((columns // SUBLANES + 1,)),
            pltpu.SemaphoreType.DMA(()),
        ],
        compiler_params=pltpu.CompilerParams(vmem_limit_bytes=VMEM_LIMIT),
    )(*in_hbm(matrix_slab, row_signs.reshape(blocks, LANES), samples))


def mix_kernel(run_length, scale, gram_scale, x_ref, out_ref):
    devices = out_ref.shape[0] // MESSAGE_ROWS
    rows = x_ref.shape[0] // devices
    runs = LANES // run_length
    samples = jnp.concatenate(
        [x_ref[(s + 1) * rows - 1 : (s + 1) * rows, :] for s in range(devices)], axis=0
    ).astype(jnp.bfloat16)
    run_of = lax.broadcasted_iota(jnp.int32, (LANES, 2 * LANES), 0)
    row_of = lax.broadcasted_iota(jnp.int32, (LANES, 2 * LANES), 1)
    spread = jnp.where(row_of // run_length == run_of, 1.0, 0.0).astype(jnp.bfloat16)
    offsets = jnp.dot(samples, spread, preferred_element_type=jnp.float32)
    own = lax.broadcasted_iota(jnp.int32, offsets.shape, 1) % run_length
    mask = jnp.where(offsets == own.astype(jnp.float32), scale, 0.0)
    picked = []
    for part in range(4):
        block = part // 2
        starts = [s * rows + part * SUBLANES for s in range(devices)]
        mixed = butterfly([x_ref[start : start + SUBLANES, :] for start in starts])
        picked.append(
            jnp.concatenate(
                [
                    mixed[d] * mask[d : d + 1, block * LANES : (block + 1) * LANES]
                    for d in range(devices)
                ],
                axis=0,
            )
        )
    quarter = 2 * runs
    row = lax.broadcasted_iota(jnp.int32, (LANES, LANES), 0)
    lane = lax.broadcasted_iota(jnp.int32, (LANES, LANES), 1)
    pattern = jnp.where(row // run_length == lane % runs, 1.0, 0.0)
    lane = lax.broadcasted_iota(jnp.int32, (1, LANES), 1)
    group = lane // quarter
    place = []
    for part in range(4):
        block, half = part // 2, part % 2
        here = lane // runs % 2 == block
        sides = [group % 2, jnp.where(group < 2, group, 3 - group)]
        masks = [jnp.where(here & (side == half), 1.0, 0.0) for side in sides]
        place.append(jnp.concatenate([(pattern * mask).astype(jnp.bfloat16) for mask in masks], axis=1))
    gathered = split_dot(jnp.concatenate(picked, axis=1), jnp.concatenate(place, axis=0), 2)
    straight, crossed = gathered[:, :LANES], gathered[:, LANES:]
    turns = SUBLANES // 2 + 1
    totals = []
    for turn in range(turns):
        total = None
        for d in range(devices):
            one = straight[d * SUBLANES : (d + 1) * SUBLANES]
            two = crossed[d * SUBLANES : (d + 1) * SUBLANES]
            if turn:
                two = pltpu.roll(two, SUBLANES - turn, 0)
            total = one * two if total is None else total + one * two
        totals.append(total)
    from_quarter = row // quarter
    together = [jnp.where(from_quarter == q, 1.0, 0.0).astype(jnp.bfloat16) for q in range(4)]
    sums = split_dot(jnp.concatenate(totals, axis=0), jnp.concatenate(together, axis=1)) * gram_scale
    sub = lax.broadcasted_iota(jnp.int32, (SUBLANES, LANES), 0)
    lane = lax.broadcasted_iota(jnp.int32, (SUBLANES, LANES), 1)
    first, second = [jnp.zeros((SUBLANES, LANES), jnp.float32)] * 2
    for turn in range(SUBLANES):
        known = min(turn, SUBLANES - turn)
        here = sums[known * SUBLANES : (known + 1) * SUBLANES]
        quarters = [here[:, q * LANES : (q + 1) * LANES] for q in range(4)]
        if known != turn:
            quarters = [pltpu.roll(quarters[q], known, 0) for q in (0, 1, 3, 2)]
        mine = lane % SUBLANES == (sub + turn) % SUBLANES
        left = lane // SUBLANES % 2 == 0
        first = jnp.where(mine, jnp.where(left, quarters[0], quarters[2]), first)
        second = jnp.where(mine, jnp.where(left, quarters[3], quarters[1]), second)
    in_place = lane // (2 * SUBLANES) == sub
    gram = jnp.concatenate(
        [jnp.sum(jnp.where(in_place, part, 0.0), axis=0, keepdims=True) for part in (first, second)],
        axis=0,
    )
    half = SUBLANES // 2
    lane = lax.broadcasted_iota(jnp.int32, (half, LANES), 1)
    for d in range(devices):
        one = straight[d * SUBLANES : (d + 1) * SUBLANES]
        start = d * MESSAGE_ROWS
        out_ref[start : start + half, :] = jnp.where(lane < LANES // 2, one[:half], one[half:])
        out_ref[start + half : start + MESSAGE_ROWS, :] = gram


def mix_and_pick(received, devices, run_length, scale, gram_scale):
    return pl.pallas_call(
        functools.partial(mix_kernel, run_length, scale, gram_scale),
        out_shape=jax.ShapeDtypeStruct((devices * MESSAGE_ROWS, LANES), jnp.float32),
        in_specs=in_vmem(1),
        out_specs=in_vmem(1)[0],
        compiler_params=pltpu.CompilerParams(vmem_limit_bytes=VMEM_LIMIT),
    )(received)


def finish_kernel(x_ref, sketch_ref, gram_ref):
    sources = x_ref.shape[0] // MESSAGE_ROWS
    quarter = LANES // 4
    half_rows = SUBLANES // 2
    sub = lax.broadcasted_iota(jnp.int32, (SUBLANES, LANES), 0)
    lane = lax.broadcasted_iota(jnp.int32, (SUBLANES, LANES), 1)
    gram = None
    for start in range(0, sources, 4):
        halves = [None, None]
        for index in range(4):
            place = (start + index) * MESSAGE_ROWS
            tail = x_ref[place + half_rows : place + MESSAGE_ROWS, :]
            gram = tail if gram is None else gram + tail
            piece = x_ref[place : place + half_rows, :]
            piece = jnp.concatenate([piece, piece], axis=0)
            piece = jnp.where(sub < half_rows, piece, pltpu.roll(piece, LANES // 2, 1))
            for half in range(2):
                shift = (index - half) % 4 * quarter
                moved = pltpu.roll(piece, shift, 1) if shift else piece
                if halves[half] is None:
                    halves[half] = moved
                else:
                    halves[half] = jnp.where(lane // quarter == index, moved, halves[half])
        for half in range(2):
            sketch_ref[
                half * SUBLANES : (half + 1) * SUBLANES, start * quarter : (start + 4) * quarter
            ] = halves[half]
    columns = gram_ref.shape[0]
    for half in range(2):
        for row in range(SUBLANES):
            line = gram[half : half + 1]
            line = pltpu.roll(line, LANES - row * columns, 1) if row else line
            gram_ref[half * SUBLANES + row : half * SUBLANES + row + 1, :] = line[:, :columns]


def finish(received, columns, sample_count):
    return pl.pallas_call(
        finish_kernel,
        out_shape=(
            jax.ShapeDtypeStruct((columns, sample_count), jnp.float32),
            jax.ShapeDtypeStruct((columns, columns), jnp.float32),
        ),
        in_specs=[pl.BlockSpec(memory_space=pltpu.VMEM)],
        out_specs=(pl.BlockSpec(memory_space=pltpu.VMEM),) * 2,
        compiler_params=pltpu.CompilerParams(vmem_limit_bytes=VMEM_LIMIT),
    )(received)


def exchange(values, axes):
    return lax.all_to_all(values, axes, split_axis=0, concat_axis=0, tiled=True)


def general_shards(matrix_slab, row_signs, sample_rows):
    columns, row_count = matrix_slab.shape
    sample_count = sample_rows.shape[0]
    devices = lax.axis_size("wide") * lax.axis_size("narrow")
    run_length = row_count // sample_count
    slice_rows = row_count // devices
    slice_runs = slice_rows // run_length
    values = jnp.swapaxes(local_transform(matrix_slab, row_signs), 0, 1)
    values = values.reshape(columns, devices, slice_rows)
    received = exchange(jnp.swapaxes(values, 0, 1), AXES)
    offsets = exchange(sample_rows.reshape(devices, slice_runs), AXES)
    mixed = jnp.einsum("ds,scr->dcr", sylvester(devices), received, precision=lax.Precision.HIGHEST)
    mixed = mixed.reshape(devices, columns, slice_runs, run_length)
    chosen = offsets[:, None, :, None] == lax.iota(jnp.int32, run_length)
    picked = jnp.sum(jnp.where(chosen, mixed, 0.0), axis=3)
    picked = picked * jnp.float32(1.0 / math.sqrt(row_count * devices))
    gram = jnp.einsum("dck,dek->ce", picked, picked, precision=lax.Precision.HIGHEST)
    gram = gram / jnp.float32(sample_count * devices)
    grams = jnp.broadcast_to(gram[None], (devices, columns, columns))
    back = exchange(jnp.concatenate([picked, grams], axis=2), AXES)
    sketch = jnp.swapaxes(back[:, :, :slice_runs], 0, 1).reshape(columns, devices * slice_runs)
    return sketch, jnp.sum(back[:, :, slice_runs:], axis=0)


def sliced_shards(matrix_slab, row_signs, sample_rows):
    columns, row_count = matrix_slab.shape
    sample_count = sample_rows.shape[0]
    devices = lax.axis_size(ORDER)
    run_length = row_count // sample_count
    sent = sliced_transform(matrix_slab, row_signs, sample_rows)
    received = exchange(sent.reshape(devices, -1), ORDER).reshape(sent.shape)
    scale = 1.0 / math.sqrt(row_count * devices)
    gram_scale = 1.0 / (sample_count * devices)
    picked = mix_and_pick(received, devices, run_length, scale, gram_scale)
    returned = exchange(picked.reshape(devices, -1), ORDER).reshape(picked.shape)
    return finish(returned, columns, sample_count)


def solution(mesh):
    wide, narrow = mesh.shape["wide"], mesh.shape["narrow"]
    axes, function = AXES, general_shards
    if wide * narrow == 32 and wide % 4 == 0:
        axes, function = SPLIT_AXES, sliced_shards
        mesh = jax.sharding.Mesh(mesh.devices.reshape(4, wide // 4, narrow), axes)
    in_specs = (P(None, axes), P(axes), P(axes))
    out_specs = (P(None, axes), P())
    return jax.shard_map(function, mesh=mesh, in_specs=in_specs, out_specs=out_specs, check_vma=False)
```

```python
import functools
import math

import jax
import jax.numpy as jnp
from jax import lax
from jax.experimental import pallas as pl
from jax.experimental.pallas import tpu as pltpu
from jax.sharding import PartitionSpec as P

LANES = 128
SUBLANES = 8
AXES = ("wide", "narrow")
SPLIT_AXES = ("line", "plane", "narrow")
ORDER = ("plane", "narrow", "line")
VMEM_LIMIT = 32 * 1024 * 1024
MESSAGE_ROWS = 6


def butterfly(values):
    values = list(values)
    apart = 1
    while apart < len(values):
        for low in range(len(values)):
            if not low & apart:
                first, second = values[low], values[low | apart]
                values[low], values[low | apart] = first + second, first - second
        apart *= 2
    return values


def sylvester(order_size):
    rows = lax.broadcasted_iota(jnp.int32, (order_size, order_size), 0)
    cols = lax.broadcasted_iota(jnp.int32, (order_size, order_size), 1)
    common = rows & cols
    parity = jnp.zeros_like(common)
    for bit_pos in range(order_size.bit_length() - 1):
        parity = parity ^ (common >> bit_pos)
    return (1 - 2 * (parity & 1)).astype(jnp.float32)


def split_dot(values, table, parts=3):
    total = None
    for _ in range(parts):
        part = values.astype(jnp.bfloat16)
        values = values - part.astype(jnp.float32)
        product = jnp.dot(part, table, preferred_element_type=jnp.float32)
        total = product if total is None else total + product
    return total


def butterfly_steps(count):
    steps = []
    apart = 1
    while apart < count:
        radix = min(8, count // apart)
        for start in range(count):
            if start // apart % radix == 0:
                steps.append((apart, [start + apart * index for index in range(radix)]))
        apart *= radix
    return steps


def fetch_blocks(x_hbm, signs_hbm, out_ref, x_ref, signs_ref, arrived):
    blocks, columns, _ = out_ref.shape
    fetches = [pltpu.make_async_copy(signs_hbm, signs_ref, arrived.at[0])]
    places = [pl.ds(start, SUBLANES) for start in range(0, columns, SUBLANES)]
    for index, place in enumerate(places):
        fetches.append(
            pltpu.make_async_copy(x_hbm.at[place], x_ref.at[place], arrived.at[index + 1])
        )
    for fetch in fetches:
        fetch.start()
    table = sylvester(LANES).astype(jnp.bfloat16)
    fetches[0].wait()
    for index, place in enumerate(places):
        fetches[index + 1].wait()
        signed = []
        for block in range(blocks):
            signs = signs_ref[block : block + 1, :].astype(jnp.float32)
            signed.append(x_ref[place, block * LANES : (block + 1) * LANES] * signs)
        mixed = split_dot(jnp.concatenate(signed, axis=0), table)
        out_ref[:, place, :] = mixed.reshape(blocks, SUBLANES, LANES)


def local_kernel(x_hbm, signs_hbm, out_ref, x_ref, signs_ref, arrived):
    fetch_blocks(x_hbm, signs_hbm, out_ref, x_ref, signs_ref, arrived)
    for apart, places in butterfly_steps(out_ref.shape[0]):
        for place, value in zip(places, butterfly([out_ref[p] for p in places])):
            out_ref[place] = value


def sliced_kernel(
    x_hbm, signs_hbm, samples_hbm, final_ref, out_ref, x_ref, signs_ref, samples_ref, arrived, noted
):
    note = pltpu.make_async_copy(samples_hbm, samples_ref, noted)
    note.start()
    fetch_blocks(x_hbm, signs_hbm, out_ref, x_ref, signs_ref, arrived)
    blocks, columns, _ = out_ref.shape
    slices = blocks // 2
    rows = final_ref.shape[0] // slices
    note.wait()
    samples = samples_ref[...].astype(jnp.float32)
    per_row = slices // samples.shape[0]
    for turn in range(per_row):
        shift = LANES - turn * LANES // per_row
        turned = pltpu.roll(samples, shift, 1) if turn else samples
        for index in range(turn, slices, per_row):
            tail = (index + 1) * rows - 1
            final_ref[tail : tail + 1, :] = turned[index // per_row : index // per_row + 1]
    steps = butterfly_steps(blocks)
    last = steps[-1][0]
    for apart, places in steps:
        for place, value in zip(places, butterfly([out_ref[p] for p in places])):
            if apart == last:
                start = place // 2 * rows + place % 2 * columns
                final_ref[start : start + columns, :] = value
            else:
                out_ref[place] = value


def in_vmem(count):
    return [pl.BlockSpec(memory_space=pltpu.VMEM)] * count


def in_hbm(*arrays):
    return [pltpu.with_memory_space_constraint(array, pltpu.HBM) for array in arrays]


def fetch_scratch(matrix_slab, blocks):
    return [
        pltpu.VMEM(matrix_slab.shape, jnp.float32),
        pltpu.VMEM((blocks, LANES), jnp.int32),
    ]


def local_transform(matrix_slab, row_signs):
    columns, row_count = matrix_slab.shape
    blocks = row_count // LANES
    return pl.pallas_call(
        local_kernel,
        out_shape=jax.ShapeDtypeStruct((blocks, columns, LANES), jnp.float32),
        in_specs=[pl.BlockSpec(memory_space=pltpu.HBM)] * 2,
        out_specs=in_vmem(1)[0],
        scratch_shapes=[
            *fetch_scratch(matrix_slab, blocks),
            pltpu.SemaphoreType.DMA((columns // SUBLANES + 1,)),
        ],
        compiler_params=pltpu.CompilerParams(vmem_limit_bytes=VMEM_LIMIT),
    )(*in_hbm(matrix_slab, row_signs.reshape(blocks, LANES)))


def sliced_transform(matrix_slab, row_signs, sample_rows):
    columns, row_count = matrix_slab.shape
    blocks = row_count // LANES
    samples = sample_rows.reshape(-1, LANES)
    return pl.pallas_call(
        sliced_kernel,
        out_shape=jax.ShapeDtypeStruct((blocks // 2 * (2 * columns + 1), LANES), jnp.float32),
        in_specs=[pl.BlockSpec(memory_space=pltpu.HBM)] * 3,
        out_specs=in_vmem(1)[0],
        scratch_shapes=[
            pltpu.VMEM((blocks, columns, LANES), jnp.float32),
            *fetch_scratch(matrix_slab, blocks),
            pltpu.VMEM(samples.shape, jnp.int32),
            pltpu.SemaphoreType.DMA((columns // SUBLANES + 1,)),
            pltpu.SemaphoreType.DMA(()),
        ],
        compiler_params=pltpu.CompilerParams(vmem_limit_bytes=VMEM_LIMIT),
    )(*in_hbm(matrix_slab, row_signs.reshape(blocks, LANES), samples))


def table_kernel(run_length, spread_ref, place_ref, together_ref):
    runs = LANES // run_length
    run_of = lax.broadcasted_iota(jnp.int32, (LANES, 2 * LANES), 0)
    row_of = lax.broadcasted_iota(jnp.int32, (LANES, 2 * LANES), 1)
    spread_ref[...] = jnp.where(row_of // run_length == run_of, 1.0, 0.0).astype(jnp.bfloat16)
    quarter = 2 * runs
    row = lax.broadcasted_iota(jnp.int32, (LANES, LANES), 0)
    lane = lax.broadcasted_iota(jnp.int32, (LANES, LANES), 1)
    pattern = jnp.where(row // run_length == lane % runs, 1.0, 0.0)
    lane = lax.broadcasted_iota(jnp.int32, (1, LANES), 1)
    group = lane // quarter
    place = []
    for part in range(4):
        block, half = part // 2, part % 2
        here = lane // runs % 2 == block
        sides = [group % 2, jnp.where(group < 2, group, 3 - group)]
        masks = [jnp.where(here & (side == half), 1.0, 0.0) for side in sides]
        place.append(jnp.concatenate([(pattern * mask).astype(jnp.bfloat16) for mask in masks], axis=1))
    place_ref[...] = jnp.concatenate(place, axis=0)
    from_quarter = row // quarter
    together = [jnp.where(from_quarter == q, 1.0, 0.0).astype(jnp.bfloat16) for q in range(4)]
    together_ref[...] = jnp.concatenate(together, axis=1)


def tables(run_length):
    return pl.pallas_call(
        functools.partial(table_kernel, run_length),
        out_shape=tuple(
            jax.ShapeDtypeStruct(shape, jnp.bfloat16)
            for shape in ((LANES, 2 * LANES), (4 * LANES, 2 * LANES), (LANES, 4 * LANES))
        ),
        out_specs=tuple(in_vmem(3)),
        compiler_params=pltpu.CompilerParams(vmem_limit_bytes=VMEM_LIMIT),
    )()


def mix_kernel(
    run_length, scale, gram_scale, x_ref, spread_ref, place_ref, together_ref, out_ref
):
    devices = out_ref.shape[0] // MESSAGE_ROWS
    rows = x_ref.shape[0] // devices
    samples = jnp.concatenate(
        [x_ref[(s + 1) * rows - 1 : (s + 1) * rows, :] for s in range(devices)], axis=0
    ).astype(jnp.bfloat16)
    offsets = jnp.dot(samples, spread_ref[...], preferred_element_type=jnp.float32)
    own = lax.broadcasted_iota(jnp.int32, offsets.shape, 1) % run_length
    mask = jnp.where(offsets == own.astype(jnp.float32), scale, 0.0)
    picked = []
    for part in range(4):
        block = part // 2
        starts = [s * rows + part * SUBLANES for s in range(devices)]
        mixed = butterfly([x_ref[start : start + SUBLANES, :] for start in starts])
        picked.append(
            jnp.concatenate(
                [
                    mixed[d] * mask[d : d + 1, block * LANES : (block + 1) * LANES]
                    for d in range(devices)
                ],
                axis=0,
            )
        )
    gathered = split_dot(jnp.concatenate(picked, axis=1), place_ref[...], 2)
    straight, crossed = gathered[:, :LANES], gathered[:, LANES:]
    turns = SUBLANES // 2 + 1
    totals = []
    for turn in range(turns):
        total = None
        for d in range(devices):
            one = straight[d * SUBLANES : (d + 1) * SUBLANES]
            two = crossed[d * SUBLANES : (d + 1) * SUBLANES]
            if turn:
                two = pltpu.roll(two, SUBLANES - turn, 0)
            total = one * two if total is None else total + one * two
        totals.append(total)
    sums = split_dot(jnp.concatenate(totals, axis=0), together_ref[...]) * gram_scale
    sub = lax.broadcasted_iota(jnp.int32, (SUBLANES, LANES), 0)
    lane = lax.broadcasted_iota(jnp.int32, (SUBLANES, LANES), 1)
    first, second = [jnp.zeros((SUBLANES, LANES), jnp.float32)] * 2
    for turn in range(SUBLANES):
        known = min(turn, SUBLANES - turn)
        here = sums[known * SUBLANES : (known + 1) * SUBLANES]
        quarters = [here[:, q * LANES : (q + 1) * LANES] for q in range(4)]
        if known != turn:
            quarters = [pltpu.roll(quarters[q], known, 0) for q in (0, 1, 3, 2)]
        mine = lane % SUBLANES == (sub + turn) % SUBLANES
        left = lane // SUBLANES % 2 == 0
        first = jnp.where(mine, jnp.where(left, quarters[0], quarters[2]), first)
        second = jnp.where(mine, jnp.where(left, quarters[3], quarters[1]), second)
    in_place = lane // (2 * SUBLANES) == sub
    gram = jnp.concatenate(
        [jnp.sum(jnp.where(in_place, part, 0.0), axis=0, keepdims=True) for part in (first, second)],
        axis=0,
    )
    half = SUBLANES // 2
    lane = lax.broadcasted_iota(jnp.int32, (half, LANES), 1)
    for d in range(devices):
        one = straight[d * SUBLANES : (d + 1) * SUBLANES]
        start = d * MESSAGE_ROWS
        out_ref[start : start + half, :] = jnp.where(lane < LANES // 2, one[:half], one[half:])
        out_ref[start + half : start + MESSAGE_ROWS, :] = gram


def mix_and_pick(received, devices, run_length, scale, gram_scale):
    return pl.pallas_call(
        functools.partial(mix_kernel, run_length, scale, gram_scale),
        out_shape=jax.ShapeDtypeStruct((devices * MESSAGE_ROWS, LANES), jnp.float32),
        in_specs=in_vmem(4),
        out_specs=in_vmem(1)[0],
        compiler_params=pltpu.CompilerParams(vmem_limit_bytes=VMEM_LIMIT),
    )(received, *tables(run_length))


def finish_kernel(x_ref, sketch_ref, gram_ref):
    sources = x_ref.shape[0] // MESSAGE_ROWS
    quarter = LANES // 4
    half_rows = SUBLANES // 2
    sub = lax.broadcasted_iota(jnp.int32, (SUBLANES, LANES), 0)
    lane = lax.broadcasted_iota(jnp.int32, (SUBLANES, LANES), 1)
    gram = None
    for start in range(0, sources, 4):
        halves = [None, None]
        for index in range(4):
            place = (start + index) * MESSAGE_ROWS
            tail = x_ref[place + half_rows : place + MESSAGE_ROWS, :]
            gram = tail if gram is None else gram + tail
            piece = x_ref[place : place + half_rows, :]
            piece = jnp.concatenate([piece, piece], axis=0)
            piece = jnp.where(sub < half_rows, piece, pltpu.roll(piece, LANES // 2, 1))
            for half in range(2):
                shift = (index - half) % 4 * quarter
                moved = pltpu.roll(piece, shift, 1) if shift else piece
                if halves[half] is None:
                    halves[half] = moved
                else:
                    halves[half] = jnp.where(lane // quarter == index, moved, halves[half])
        for half in range(2):
            sketch_ref[
                half * SUBLANES : (half + 1) * SUBLANES, start * quarter : (start + 4) * quarter
            ] = halves[half]
    columns = gram_ref.shape[0]
    for half in range(2):
        for row in range(SUBLANES):
            line = gram[half : half + 1]
            line = pltpu.roll(line, LANES - row * columns, 1) if row else line
            gram_ref[half * SUBLANES + row : half * SUBLANES + row + 1, :] = line[:, :columns]


def finish(received, columns, sample_count):
    return pl.pallas_call(
        finish_kernel,
        out_shape=(
            jax.ShapeDtypeStruct((columns, sample_count), jnp.float32),
            jax.ShapeDtypeStruct((columns, columns), jnp.float32),
        ),
        in_specs=[pl.BlockSpec(memory_space=pltpu.VMEM)],
        out_specs=(pl.BlockSpec(memory_space=pltpu.VMEM),) * 2,
        compiler_params=pltpu.CompilerParams(vmem_limit_bytes=VMEM_LIMIT),
    )(received)


def exchange(values, axes):
    return lax.all_to_all(values, axes, split_axis=0, concat_axis=0, tiled=True)


def general_shards(matrix_slab, row_signs, sample_rows):
    columns, row_count = matrix_slab.shape
    sample_count = sample_rows.shape[0]
    devices = lax.axis_size("wide") * lax.axis_size("narrow")
    run_length = row_count // sample_count
    slice_rows = row_count // devices
    slice_runs = slice_rows // run_length
    values = jnp.swapaxes(local_transform(matrix_slab, row_signs), 0, 1)
    values = values.reshape(columns, devices, slice_rows)
    received = exchange(jnp.swapaxes(values, 0, 1), AXES)
    offsets = exchange(sample_rows.reshape(devices, slice_runs), AXES)
    mixed = jnp.einsum("ds,scr->dcr", sylvester(devices), received, precision=lax.Precision.HIGHEST)
    mixed = mixed.reshape(devices, columns, slice_runs, run_length)
    chosen = offsets[:, None, :, None] == lax.iota(jnp.int32, run_length)
    picked = jnp.sum(jnp.where(chosen, mixed, 0.0), axis=3)
    picked = picked * jnp.float32(1.0 / math.sqrt(row_count * devices))
    gram = jnp.einsum("dck,dek->ce", picked, picked, precision=lax.Precision.HIGHEST)
    gram = gram / jnp.float32(sample_count * devices)
    grams = jnp.broadcast_to(gram[None], (devices, columns, columns))
    back = exchange(jnp.concatenate([picked, grams], axis=2), AXES)
    sketch = jnp.swapaxes(back[:, :, :slice_runs], 0, 1).reshape(columns, devices * slice_runs)
    return sketch, jnp.sum(back[:, :, slice_runs:], axis=0)


def sliced_shards(matrix_slab, row_signs, sample_rows):
    columns, row_count = matrix_slab.shape
    sample_count = sample_rows.shape[0]
    devices = lax.axis_size(ORDER)
    run_length = row_count // sample_count
    sent = sliced_transform(matrix_slab, row_signs, sample_rows)
    received = exchange(sent.reshape(devices, -1), ORDER).reshape(sent.shape)
    scale = 1.0 / math.sqrt(row_count * devices)
    gram_scale = 1.0 / (sample_count * devices)
    picked = mix_and_pick(received, devices, run_length, scale, gram_scale)
    returned = exchange(picked.reshape(devices, -1), ORDER).reshape(picked.shape)
    return finish(returned, columns, sample_count)


def solution(mesh):
    wide, narrow = mesh.shape["wide"], mesh.shape["narrow"]
    axes, function = AXES, general_shards
    if wide * narrow == 32 and wide % 4 == 0:
        axes, function = SPLIT_AXES, sliced_shards
        mesh = jax.sharding.Mesh(mesh.devices.reshape(4, wide // 4, narrow), axes)
    in_specs = (P(None, axes), P(axes), P(axes))
    out_specs = (P(None, axes), P())
    return jax.shard_map(function, mesh=mesh, in_specs=in_specs, out_specs=out_specs, check_vma=False)
```

```python
import functools
import math

import jax
import jax.numpy as jnp
from jax import lax
from jax.experimental import pallas as pl
from jax.experimental.pallas import tpu as pltpu
from jax.sharding import PartitionSpec as P

LANES = 128
SUBLANES = 8
AXES = ("wide", "narrow")
SPLIT_AXES = ("line", "plane", "narrow")
ORDER = ("plane", "narrow", "line")
VMEM_LIMIT = 32 * 1024 * 1024
MESSAGE_ROWS = 6


def butterfly(values):
    values = list(values)
    apart = 1
    while apart < len(values):
        for low in range(len(values)):
            if not low & apart:
                first, second = values[low], values[low | apart]
                values[low], values[low | apart] = first + second, first - second
        apart *= 2
    return values


def sylvester(order_size):
    rows = lax.broadcasted_iota(jnp.int32, (order_size, order_size), 0)
    cols = lax.broadcasted_iota(jnp.int32, (order_size, order_size), 1)
    common = rows & cols
    parity = jnp.zeros_like(common)
    for bit_pos in range(order_size.bit_length() - 1):
        parity = parity ^ (common >> bit_pos)
    return (1 - 2 * (parity & 1)).astype(jnp.float32)


def split_dot(values, table, parts=3):
    total = None
    for _ in range(parts):
        part = values.astype(jnp.bfloat16)
        values = values - part.astype(jnp.float32)
        product = jnp.dot(part, table, preferred_element_type=jnp.float32)
        total = product if total is None else total + product
    return total


def butterfly_steps(count):
    steps = []
    apart = 1
    while apart < count:
        radix = min(8, count // apart)
        for start in range(count):
            if start // apart % radix == 0:
                steps.append((apart, [start + apart * index for index in range(radix)]))
        apart *= radix
    return steps


def fetch_blocks(x_hbm, signs_hbm, out_ref, x_ref, signs_ref, arrived):
    blocks, columns, _ = out_ref.shape
    fetches = [
        pltpu.make_async_copy(x_hbm, x_ref, arrived.at[0]),
        pltpu.make_async_copy(signs_hbm, signs_ref, arrived.at[1]),
    ]
    for fetch in fetches:
        fetch.start()
    table = sylvester(LANES).astype(jnp.bfloat16)
    for fetch in fetches:
        fetch.wait()
    signs = signs_ref[...].astype(jnp.float32)
    signed = [
        x_ref[:, block * LANES : (block + 1) * LANES] * signs[block : block + 1]
        for block in range(blocks)
    ]
    mixed = split_dot(jnp.concatenate(signed, axis=0), table)
    out_ref[...] = mixed.reshape(blocks, columns, LANES)


def local_kernel(x_hbm, signs_hbm, out_ref, x_ref, signs_ref, arrived):
    fetch_blocks(x_hbm, signs_hbm, out_ref, x_ref, signs_ref, arrived)
    for apart, places in butterfly_steps(out_ref.shape[0]):
        for place, value in zip(places, butterfly([out_ref[p] for p in places])):
            out_ref[place] = value


def sliced_kernel(
    x_hbm, signs_hbm, samples_hbm, final_ref, out_ref, x_ref, signs_ref, samples_ref, arrived, noted
):
    note = pltpu.make_async_copy(samples_hbm, samples_ref, noted)
    note.start()
    fetch_blocks(x_hbm, signs_hbm, out_ref, x_ref, signs_ref, arrived)
    blocks, columns, _ = out_ref.shape
    slices = blocks // 2
    rows = final_ref.shape[0] // slices
    note.wait()
    samples = samples_ref[...].astype(jnp.float32)
    per_row = slices // samples.shape[0]
    for turn in range(per_row):
        shift = LANES - turn * LANES // per_row
        turned = pltpu.roll(samples, shift, 1) if turn else samples
        for index in range(turn, slices, per_row):
            tail = (index + 1) * rows - 1
            final_ref[tail : tail + 1, :] = turned[index // per_row : index // per_row + 1]
    steps = butterfly_steps(blocks)
    last = steps[-1][0]
    for apart, places in steps:
        for place, value in zip(places, butterfly([out_ref[p] for p in places])):
            if apart == last:
                start = place // 2 * rows + place % 2 * columns
                final_ref[start : start + columns, :] = value
            else:
                out_ref[place] = value


def in_vmem(count):
    return [pl.BlockSpec(memory_space=pltpu.VMEM)] * count


def in_hbm(*arrays):
    return [pltpu.with_memory_space_constraint(array, pltpu.HBM) for array in arrays]


def fetch_scratch(matrix_slab, blocks):
    return [
        pltpu.VMEM(matrix_slab.shape, jnp.float32),
        pltpu.VMEM((blocks, LANES), jnp.int32),
    ]


def local_transform(matrix_slab, row_signs):
    columns, row_count = matrix_slab.shape
    blocks = row_count // LANES
    return pl.pallas_call(
        local_kernel,
        out_shape=jax.ShapeDtypeStruct((blocks, columns, LANES), jnp.float32),
        in_specs=[pl.BlockSpec(memory_space=pltpu.HBM)] * 2,
        out_specs=in_vmem(1)[0],
        scratch_shapes=[
            *fetch_scratch(matrix_slab, blocks),
            pltpu.SemaphoreType.DMA((2,)),
        ],
        compiler_params=pltpu.CompilerParams(vmem_limit_bytes=VMEM_LIMIT),
    )(*in_hbm(matrix_slab, row_signs.reshape(blocks, LANES)))


def sliced_transform(matrix_slab, row_signs, sample_rows):
    columns, row_count = matrix_slab.shape
    blocks = row_count // LANES
    samples = sample_rows.reshape(-1, LANES)
    return pl.pallas_call(
        sliced_kernel,
        out_shape=jax.ShapeDtypeStruct((blocks // 2 * (2 * columns + 1), LANES), jnp.float32),
        in_specs=[pl.BlockSpec(memory_space=pltpu.HBM)] * 3,
        out_specs=in_vmem(1)[0],
        scratch_shapes=[
            pltpu.VMEM((blocks, columns, LANES), jnp.float32),
            *fetch_scratch(matrix_slab, blocks),
            pltpu.VMEM(samples.shape, jnp.int32),
            pltpu.SemaphoreType.DMA((2,)),
            pltpu.SemaphoreType.DMA(()),
        ],
        compiler_params=pltpu.CompilerParams(vmem_limit_bytes=VMEM_LIMIT),
    )(*in_hbm(matrix_slab, row_signs.reshape(blocks, LANES), samples))


def mix_kernel(run_length, scale, gram_scale, x_ref, out_ref):
    devices = out_ref.shape[0] // MESSAGE_ROWS
    rows = x_ref.shape[0] // devices
    runs = LANES // run_length
    samples = jnp.concatenate(
        [x_ref[(s + 1) * rows - 1 : (s + 1) * rows, :] for s in range(devices)], axis=0
    ).astype(jnp.bfloat16)
    run_of = lax.broadcasted_iota(jnp.int32, (LANES, 2 * LANES), 0)
    row_of = lax.broadcasted_iota(jnp.int32, (LANES, 2 * LANES), 1)
    spread = jnp.where(row_of // run_length == run_of, 1.0, 0.0).astype(jnp.bfloat16)
    offsets = jnp.dot(samples, spread, preferred_element_type=jnp.float32)
    own = lax.broadcasted_iota(jnp.int32, offsets.shape, 1) % run_length
    mask = jnp.where(offsets == own.astype(jnp.float32), scale, 0.0)
    picked = []
    for part in range(4):
        block = part // 2
        starts = [s * rows + part * SUBLANES for s in range(devices)]
        mixed = butterfly([x_ref[start : start + SUBLANES, :] for start in starts])
        picked.append(
            jnp.concatenate(
                [
                    mixed[d] * mask[d : d + 1, block * LANES : (block + 1) * LANES]
                    for d in range(devices)
                ],
                axis=0,
            )
        )
    quarter = 2 * runs
    row = lax.broadcasted_iota(jnp.int32, (LANES, LANES), 0)
    lane = lax.broadcasted_iota(jnp.int32, (LANES, LANES), 1)
    pattern = jnp.where(row // run_length == lane % runs, 1.0, 0.0)
    lane = lax.broadcasted_iota(jnp.int32, (1, LANES), 1)
    group = lane // quarter
    place = []
    for part in range(4):
        block, half = part // 2, part % 2
        here = lane // runs % 2 == block
        sides = [group % 2, jnp.where(group < 2, group, 3 - group)]
        masks = [jnp.where(here & (side == half), 1.0, 0.0) for side in sides]
        place.append(jnp.concatenate([(pattern * mask).astype(jnp.bfloat16) for mask in masks], axis=1))
    gathered = split_dot(jnp.concatenate(picked, axis=1), jnp.concatenate(place, axis=0), 2)
    straight, crossed = gathered[:, :LANES], gathered[:, LANES:]
    turns = SUBLANES // 2 + 1
    totals = []
    for turn in range(turns):
        total = None
        for d in range(devices):
            one = straight[d * SUBLANES : (d + 1) * SUBLANES]
            two = crossed[d * SUBLANES : (d + 1) * SUBLANES]
            if turn:
                two = pltpu.roll(two, SUBLANES - turn, 0)
            total = one * two if total is None else total + one * two
        totals.append(total)
    from_quarter = row // quarter
    together = [jnp.where(from_quarter == q, 1.0, 0.0).astype(jnp.bfloat16) for q in range(4)]
    sums = split_dot(jnp.concatenate(totals, axis=0), jnp.concatenate(together, axis=1)) * gram_scale
    sub = lax.broadcasted_iota(jnp.int32, (SUBLANES, LANES), 0)
    lane = lax.broadcasted_iota(jnp.int32, (SUBLANES, LANES), 1)
    first, second = [jnp.zeros((SUBLANES, LANES), jnp.float32)] * 2
    for turn in range(SUBLANES):
        known = min(turn, SUBLANES - turn)
        here = sums[known * SUBLANES : (known + 1) * SUBLANES]
        quarters = [here[:, q * LANES : (q + 1) * LANES] for q in range(4)]
        if known != turn:
            quarters = [pltpu.roll(quarters[q], known, 0) for q in (0, 1, 3, 2)]
        mine = lane % SUBLANES == (sub + turn) % SUBLANES
        left = lane // SUBLANES % 2 == 0
        first = jnp.where(mine, jnp.where(left, quarters[0], quarters[2]), first)
        second = jnp.where(mine, jnp.where(left, quarters[3], quarters[1]), second)
    in_place = lane // (2 * SUBLANES) == sub
    gram = jnp.concatenate(
        [jnp.sum(jnp.where(in_place, part, 0.0), axis=0, keepdims=True) for part in (first, second)],
        axis=0,
    )
    half = SUBLANES // 2
    lane = lax.broadcasted_iota(jnp.int32, (half, LANES), 1)
    for d in range(devices):
        one = straight[d * SUBLANES : (d + 1) * SUBLANES]
        start = d * MESSAGE_ROWS
        out_ref[start : start + half, :] = jnp.where(lane < LANES // 2, one[:half], one[half:])
        out_ref[start + half : start + MESSAGE_ROWS, :] = gram


def mix_and_pick(received, devices, run_length, scale, gram_scale):
    return pl.pallas_call(
        functools.partial(mix_kernel, run_length, scale, gram_scale),
        out_shape=jax.ShapeDtypeStruct((devices * MESSAGE_ROWS, LANES), jnp.float32),
        in_specs=in_vmem(1),
        out_specs=in_vmem(1)[0],
        compiler_params=pltpu.CompilerParams(vmem_limit_bytes=VMEM_LIMIT),
    )(received)


def finish_kernel(x_ref, sketch_ref, gram_ref):
    sources = x_ref.shape[0] // MESSAGE_ROWS
    quarter = LANES // 4
    half_rows = SUBLANES // 2
    sub = lax.broadcasted_iota(jnp.int32, (SUBLANES, LANES), 0)
    lane = lax.broadcasted_iota(jnp.int32, (SUBLANES, LANES), 1)
    gram = None
    for start in range(0, sources, 4):
        halves = [None, None]
        for index in range(4):
            place = (start + index) * MESSAGE_ROWS
            tail = x_ref[place + half_rows : place + MESSAGE_ROWS, :]
            gram = tail if gram is None else gram + tail
            piece = x_ref[place : place + half_rows, :]
            piece = jnp.concatenate([piece, piece], axis=0)
            piece = jnp.where(sub < half_rows, piece, pltpu.roll(piece, LANES // 2, 1))
            for half in range(2):
                shift = (index - half) % 4 * quarter
                moved = pltpu.roll(piece, shift, 1) if shift else piece
                if halves[half] is None:
                    halves[half] = moved
                else:
                    halves[half] = jnp.where(lane // quarter == index, moved, halves[half])
        for half in range(2):
            sketch_ref[
                half * SUBLANES : (half + 1) * SUBLANES, start * quarter : (start + 4) * quarter
            ] = halves[half]
    columns = gram_ref.shape[0]
    for half in range(2):
        for row in range(SUBLANES):
            line = gram[half : half + 1]
            line = pltpu.roll(line, LANES - row * columns, 1) if row else line
            gram_ref[half * SUBLANES + row : half * SUBLANES + row + 1, :] = line[:, :columns]


def finish(received, columns, sample_count):
    return pl.pallas_call(
        finish_kernel,
        out_shape=(
            jax.ShapeDtypeStruct((columns, sample_count), jnp.float32),
            jax.ShapeDtypeStruct((columns, columns), jnp.float32),
        ),
        in_specs=[pl.BlockSpec(memory_space=pltpu.VMEM)],
        out_specs=(pl.BlockSpec(memory_space=pltpu.VMEM),) * 2,
        compiler_params=pltpu.CompilerParams(vmem_limit_bytes=VMEM_LIMIT),
    )(received)


def exchange(values, axes):
    return lax.all_to_all(values, axes, split_axis=0, concat_axis=0, tiled=True)


def general_shards(matrix_slab, row_signs, sample_rows):
    columns, row_count = matrix_slab.shape
    sample_count = sample_rows.shape[0]
    devices = lax.axis_size("wide") * lax.axis_size("narrow")
    run_length = row_count // sample_count
    slice_rows = row_count // devices
    slice_runs = slice_rows // run_length
    values = jnp.swapaxes(local_transform(matrix_slab, row_signs), 0, 1)
    values = values.reshape(columns, devices, slice_rows)
    received = exchange(jnp.swapaxes(values, 0, 1), AXES)
    offsets = exchange(sample_rows.reshape(devices, slice_runs), AXES)
    mixed = jnp.einsum("ds,scr->dcr", sylvester(devices), received, precision=lax.Precision.HIGHEST)
    mixed = mixed.reshape(devices, columns, slice_runs, run_length)
    chosen = offsets[:, None, :, None] == lax.iota(jnp.int32, run_length)
    picked = jnp.sum(jnp.where(chosen, mixed, 0.0), axis=3)
    picked = picked * jnp.float32(1.0 / math.sqrt(row_count * devices))
    gram = jnp.einsum("dck,dek->ce", picked, picked, precision=lax.Precision.HIGHEST)
    gram = gram / jnp.float32(sample_count * devices)
    grams = jnp.broadcast_to(gram[None], (devices, columns, columns))
    back = exchange(jnp.concatenate([picked, grams], axis=2), AXES)
    sketch = jnp.swapaxes(back[:, :, :slice_runs], 0, 1).reshape(columns, devices * slice_runs)
    return sketch, jnp.sum(back[:, :, slice_runs:], axis=0)


def sliced_shards(matrix_slab, row_signs, sample_rows):
    columns, row_count = matrix_slab.shape
    sample_count = sample_rows.shape[0]
    devices = lax.axis_size(ORDER)
    run_length = row_count // sample_count
    sent = sliced_transform(matrix_slab, row_signs, sample_rows)
    received = exchange(sent.reshape(devices, -1), ORDER).reshape(sent.shape)
    scale = 1.0 / math.sqrt(row_count * devices)
    gram_scale = 1.0 / (sample_count * devices)
    picked = mix_and_pick(received, devices, run_length, scale, gram_scale)
    returned = exchange(picked.reshape(devices, -1), ORDER).reshape(picked.shape)
    return finish(returned, columns, sample_count)


def solution(mesh):
    wide, narrow = mesh.shape["wide"], mesh.shape["narrow"]
    axes, function = AXES, general_shards
    if wide * narrow == 32 and wide % 4 == 0:
        axes, function = SPLIT_AXES, sliced_shards
        mesh = jax.sharding.Mesh(mesh.devices.reshape(4, wide // 4, narrow), axes)
    in_specs = (P(None, axes), P(axes), P(axes))
    out_specs = (P(None, axes), P())
    return jax.shard_map(function, mesh=mesh, in_specs=in_specs, out_specs=out_specs, check_vma=False)
```

```python
import functools
import math

import jax
import jax.numpy as jnp
from jax import lax
from jax.experimental import pallas as pl
from jax.experimental.pallas import tpu as pltpu
from jax.sharding import PartitionSpec as P

LANES = 128
SUBLANES = 8
AXES = ("wide", "narrow")
SPLIT_AXES = ("line", "plane", "narrow")
ORDER = ("plane", "narrow", "line")
VMEM_LIMIT = 32 * 1024 * 1024
MESSAGE_ROWS = 6


def butterfly(values):
    values = list(values)
    apart = 1
    while apart < len(values):
        for low in range(len(values)):
            if not low & apart:
                first, second = values[low], values[low | apart]
                values[low], values[low | apart] = first + second, first - second
        apart *= 2
    return values


def sylvester(order_size):
    rows = lax.broadcasted_iota(jnp.int32, (order_size, order_size), 0)
    cols = lax.broadcasted_iota(jnp.int32, (order_size, order_size), 1)
    common = rows & cols
    parity = jnp.zeros_like(common)
    for bit_pos in range(order_size.bit_length() - 1):
        parity = parity ^ (common >> bit_pos)
    return (1 - 2 * (parity & 1)).astype(jnp.float32)


def split_dot(values, table, parts=3):
    total = None
    for _ in range(parts):
        part = values.astype(jnp.bfloat16)
        values = values - part.astype(jnp.float32)
        product = jnp.dot(part, table, preferred_element_type=jnp.float32)
        total = product if total is None else total + product
    return total


def butterfly_steps(count):
    steps = []
    apart = 2
    while apart < count:
        radix = min(8, count // apart)
        for start in range(count):
            if start // apart % radix == 0:
                steps.append((apart, [start + apart * index for index in range(radix)]))
        apart *= radix
    return steps


def fetch_blocks(x_hbm, signs_hbm, out_ref, x_ref, signs_ref, arrived):
    blocks, columns, _ = out_ref.shape
    fetches = [
        pltpu.make_async_copy(x_hbm, x_ref, arrived.at[0]),
        pltpu.make_async_copy(signs_hbm, signs_ref, arrived.at[1]),
    ]
    for fetch in fetches:
        fetch.start()
    table = sylvester(2 * LANES).astype(jnp.bfloat16)
    for fetch in fetches:
        fetch.wait()
    signs = signs_ref[...].astype(jnp.float32)
    signed = []
    for block in range(0, blocks, 2):
        pair = jnp.concatenate([signs[block : block + 1], signs[block + 1 : block + 2]], axis=1)
        signed.append(x_ref[:, block * LANES : (block + 2) * LANES] * pair)
    mixed = split_dot(jnp.concatenate(signed, axis=0), table)
    for block in range(blocks):
        rows = slice(block // 2 * columns, (block // 2 + 1) * columns)
        out_ref[block] = mixed[rows, block % 2 * LANES : (block % 2 + 1) * LANES]


def local_kernel(x_hbm, signs_hbm, out_ref, x_ref, signs_ref, arrived):
    fetch_blocks(x_hbm, signs_hbm, out_ref, x_ref, signs_ref, arrived)
    for apart, places in butterfly_steps(out_ref.shape[0]):
        for place, value in zip(places, butterfly([out_ref[p] for p in places])):
            out_ref[place] = value


def sliced_kernel(
    x_hbm, signs_hbm, samples_hbm, final_ref, out_ref, x_ref, signs_ref, samples_ref, arrived, noted
):
    note = pltpu.make_async_copy(samples_hbm, samples_ref, noted)
    note.start()
    fetch_blocks(x_hbm, signs_hbm, out_ref, x_ref, signs_ref, arrived)
    blocks, columns, _ = out_ref.shape
    slices = blocks // 2
    rows = final_ref.shape[0] // slices
    note.wait()
    samples = samples_ref[...].astype(jnp.float32)
    per_row = slices // samples.shape[0]
    for turn in range(per_row):
        shift = LANES - turn * LANES // per_row
        turned = pltpu.roll(samples, shift, 1) if turn else samples
        for index in range(turn, slices, per_row):
            tail = (index + 1) * rows - 1
            final_ref[tail : tail + 1, :] = turned[index // per_row : index // per_row + 1]
    steps = butterfly_steps(blocks)
    last = steps[-1][0]
    for apart, places in steps:
        for place, value in zip(places, butterfly([out_ref[p] for p in places])):
            if apart == last:
                start = place // 2 * rows + place % 2 * columns
                final_ref[start : start + columns, :] = value
            else:
                out_ref[place] = value


def in_vmem(count):
    return [pl.BlockSpec(memory_space=pltpu.VMEM)] * count


def in_hbm(*arrays):
    return [pltpu.with_memory_space_constraint(array, pltpu.HBM) for array in arrays]


def fetch_scratch(matrix_slab, blocks):
    return [
        pltpu.VMEM(matrix_slab.shape, jnp.float32),
        pltpu.VMEM((blocks, LANES), jnp.int32),
    ]


def local_transform(matrix_slab, row_signs):
    columns, row_count = matrix_slab.shape
    blocks = row_count // LANES
    return pl.pallas_call(
        local_kernel,
        out_shape=jax.ShapeDtypeStruct((blocks, columns, LANES), jnp.float32),
        in_specs=[pl.BlockSpec(memory_space=pltpu.HBM)] * 2,
        out_specs=in_vmem(1)[0],
        scratch_shapes=[
            *fetch_scratch(matrix_slab, blocks),
            pltpu.SemaphoreType.DMA((2,)),
        ],
        compiler_params=pltpu.CompilerParams(vmem_limit_bytes=VMEM_LIMIT),
    )(*in_hbm(matrix_slab, row_signs.reshape(blocks, LANES)))


def sliced_transform(matrix_slab, row_signs, sample_rows):
    columns, row_count = matrix_slab.shape
    blocks = row_count // LANES
    samples = sample_rows.reshape(-1, LANES)
    return pl.pallas_call(
        sliced_kernel,
        out_shape=jax.ShapeDtypeStruct((blocks // 2 * (2 * columns + 1), LANES), jnp.float32),
        in_specs=[pl.BlockSpec(memory_space=pltpu.HBM)] * 3,
        out_specs=in_vmem(1)[0],
        scratch_shapes=[
            pltpu.VMEM((blocks, columns, LANES), jnp.float32),
            *fetch_scratch(matrix_slab, blocks),
            pltpu.VMEM(samples.shape, jnp.int32),
            pltpu.SemaphoreType.DMA((2,)),
            pltpu.SemaphoreType.DMA(()),
        ],
        compiler_params=pltpu.CompilerParams(vmem_limit_bytes=VMEM_LIMIT),
    )(*in_hbm(matrix_slab, row_signs.reshape(blocks, LANES), samples))


def mix_kernel(run_length, scale, gram_scale, x_ref, out_ref):
    devices = out_ref.shape[0] // MESSAGE_ROWS
    rows = x_ref.shape[0] // devices
    runs = LANES // run_length
    samples = jnp.concatenate(
        [x_ref[(s + 1) * rows - 1 : (s + 1) * rows, :] for s in range(devices)], axis=0
    ).astype(jnp.bfloat16)
    run_of = lax.broadcasted_iota(jnp.int32, (LANES, 2 * LANES), 0)
    row_of = lax.broadcasted_iota(jnp.int32, (LANES, 2 * LANES), 1)
    spread = jnp.where(row_of // run_length == run_of, 1.0, 0.0).astype(jnp.bfloat16)
    offsets = jnp.dot(samples, spread, preferred_element_type=jnp.float32)
    own = lax.broadcasted_iota(jnp.int32, offsets.shape, 1) % run_length
    mask = jnp.where(offsets == own.astype(jnp.float32), scale, 0.0)
    picked = []
    for part in range(4):
        block = part // 2
        starts = [s * rows + part * SUBLANES for s in range(devices)]
        mixed = butterfly([x_ref[start : start + SUBLANES, :] for start in starts])
        picked.append(
            jnp.concatenate(
                [
                    mixed[d] * mask[d : d + 1, block * LANES : (block + 1) * LANES]
                    for d in range(devices)
                ],
                axis=0,
            )
        )
    quarter = 2 * runs
    row = lax.broadcasted_iota(jnp.int32, (LANES, LANES), 0)
    lane = lax.broadcasted_iota(jnp.int32, (LANES, LANES), 1)
    pattern = jnp.where(row // run_length == lane % runs, 1.0, 0.0)
    lane = lax.broadcasted_iota(jnp.int32, (1, LANES), 1)
    group = lane // quarter
    place = []
    for part in range(4):
        block, half = part // 2, part % 2
        here = lane // runs % 2 == block
        sides = [group % 2, jnp.where(group < 2, group, 3 - group)]
        masks = [jnp.where(here & (side == half), 1.0, 0.0) for side in sides]
        place.append(jnp.concatenate([(pattern * mask).astype(jnp.bfloat16) for mask in masks], axis=1))
    gathered = split_dot(jnp.concatenate(picked, axis=1), jnp.concatenate(place, axis=0), 2)
    straight, crossed = gathered[:, :LANES], gathered[:, LANES:]
    turns = SUBLANES // 2 + 1
    totals = []
    for turn in range(turns):
        total = None
        for d in range(devices):
            one = straight[d * SUBLANES : (d + 1) * SUBLANES]
            two = crossed[d * SUBLANES : (d + 1) * SUBLANES]
            if turn:
                two = pltpu.roll(two, SUBLANES - turn, 0)
            total = one * two if total is None else total + one * two
        totals.append(total)
    from_quarter = row // quarter
    together = [jnp.where(from_quarter == q, 1.0, 0.0).astype(jnp.bfloat16) for q in range(4)]
    sums = split_dot(jnp.concatenate(totals, axis=0), jnp.concatenate(together, axis=1)) * gram_scale
    sub = lax.broadcasted_iota(jnp.int32, (SUBLANES, LANES), 0)
    lane = lax.broadcasted_iota(jnp.int32, (SUBLANES, LANES), 1)
    first, second = [jnp.zeros((SUBLANES, LANES), jnp.float32)] * 2
    for turn in range(SUBLANES):
        known = min(turn, SUBLANES - turn)
        here = sums[known * SUBLANES : (known + 1) * SUBLANES]
        quarters = [here[:, q * LANES : (q + 1) * LANES] for q in range(4)]
        if known != turn:
            quarters = [pltpu.roll(quarters[q], known, 0) for q in (0, 1, 3, 2)]
        mine = lane % SUBLANES == (sub + turn) % SUBLANES
        left = lane // SUBLANES % 2 == 0
        first = jnp.where(mine, jnp.where(left, quarters[0], quarters[2]), first)
        second = jnp.where(mine, jnp.where(left, quarters[3], quarters[1]), second)
    in_place = lane // (2 * SUBLANES) == sub
    gram = jnp.concatenate(
        [jnp.sum(jnp.where(in_place, part, 0.0), axis=0, keepdims=True) for part in (first, second)],
        axis=0,
    )
    half = SUBLANES // 2
    lane = lax.broadcasted_iota(jnp.int32, (half, LANES), 1)
    for d in range(devices):
        one = straight[d * SUBLANES : (d + 1) * SUBLANES]
        start = d * MESSAGE_ROWS
        out_ref[start : start + half, :] = jnp.where(lane < LANES // 2, one[:half], one[half:])
        out_ref[start + half : start + MESSAGE_ROWS, :] = gram


def mix_and_pick(received, devices, run_length, scale, gram_scale):
    return pl.pallas_call(
        functools.partial(mix_kernel, run_length, scale, gram_scale),
        out_shape=jax.ShapeDtypeStruct((devices * MESSAGE_ROWS, LANES), jnp.float32),
        in_specs=in_vmem(1),
        out_specs=in_vmem(1)[0],
        compiler_params=pltpu.CompilerParams(vmem_limit_bytes=VMEM_LIMIT),
    )(received)


def finish_kernel(x_ref, sketch_ref, gram_ref):
    sources = x_ref.shape[0] // MESSAGE_ROWS
    quarter = LANES // 4
    half_rows = SUBLANES // 2
    sub = lax.broadcasted_iota(jnp.int32, (SUBLANES, LANES), 0)
    lane = lax.broadcasted_iota(jnp.int32, (SUBLANES, LANES), 1)
    gram = None
    for start in range(0, sources, 4):
        halves = [None, None]
        for index in range(4):
            place = (start + index) * MESSAGE_ROWS
            tail = x_ref[place + half_rows : place + MESSAGE_ROWS, :]
            gram = tail if gram is None else gram + tail
            piece = x_ref[place : place + half_rows, :]
            piece = jnp.concatenate([piece, piece], axis=0)
            piece = jnp.where(sub < half_rows, piece, pltpu.roll(piece, LANES // 2, 1))
            for half in range(2):
                shift = (index - half) % 4 * quarter
                moved = pltpu.roll(piece, shift, 1) if shift else piece
                if halves[half] is None:
                    halves[half] = moved
                else:
                    halves[half] = jnp.where(lane // quarter == index, moved, halves[half])
        for half in range(2):
            sketch_ref[
                half * SUBLANES : (half + 1) * SUBLANES, start * quarter : (start + 4) * quarter
            ] = halves[half]
    columns = gram_ref.shape[0]
    for half in range(2):
        for row in range(SUBLANES):
            line = gram[half : half + 1]
            line = pltpu.roll(line, LANES - row * columns, 1) if row else line
            gram_ref[half * SUBLANES + row : half * SUBLANES + row + 1, :] = line[:, :columns]


def finish(received, columns, sample_count):
    return pl.pallas_call(
        finish_kernel,
        out_shape=(
            jax.ShapeDtypeStruct((columns, sample_count), jnp.float32),
            jax.ShapeDtypeStruct((columns, columns), jnp.float32),
        ),
        in_specs=[pl.BlockSpec(memory_space=pltpu.VMEM)],
        out_specs=(pl.BlockSpec(memory_space=pltpu.VMEM),) * 2,
        compiler_params=pltpu.CompilerParams(vmem_limit_bytes=VMEM_LIMIT),
    )(received)


def exchange(values, axes):
    return lax.all_to_all(values, axes, split_axis=0, concat_axis=0, tiled=True)


def general_shards(matrix_slab, row_signs, sample_rows):
    columns, row_count = matrix_slab.shape
    sample_count = sample_rows.shape[0]
    devices = lax.axis_size("wide") * lax.axis_size("narrow")
    run_length = row_count // sample_count
    slice_rows = row_count // devices
    slice_runs = slice_rows // run_length
    values = jnp.swapaxes(local_transform(matrix_slab, row_signs), 0, 1)
    values = values.reshape(columns, devices, slice_rows)
    received = exchange(jnp.swapaxes(values, 0, 1), AXES)
    offsets = exchange(sample_rows.reshape(devices, slice_runs), AXES)
    mixed = jnp.einsum("ds,scr->dcr", sylvester(devices), received, precision=lax.Precision.HIGHEST)
    mixed = mixed.reshape(devices, columns, slice_runs, run_length)
    chosen = offsets[:, None, :, None] == lax.iota(jnp.int32, run_length)
    picked = jnp.sum(jnp.where(chosen, mixed, 0.0), axis=3)
    picked = picked * jnp.float32(1.0 / math.sqrt(row_count * devices))
    gram = jnp.einsum("dck,dek->ce", picked, picked, precision=lax.Precision.HIGHEST)
    gram = gram / jnp.float32(sample_count * devices)
    grams = jnp.broadcast_to(gram[None], (devices, columns, columns))
    back = exchange(jnp.concatenate([picked, grams], axis=2), AXES)
    sketch = jnp.swapaxes(back[:, :, :slice_runs], 0, 1).reshape(columns, devices * slice_runs)
    return sketch, jnp.sum(back[:, :, slice_runs:], axis=0)


def sliced_shards(matrix_slab, row_signs, sample_rows):
    columns, row_count = matrix_slab.shape
    sample_count = sample_rows.shape[0]
    devices = lax.axis_size(ORDER)
    run_length = row_count // sample_count
    sent = sliced_transform(matrix_slab, row_signs, sample_rows)
    received = exchange(sent.reshape(devices, -1), ORDER).reshape(sent.shape)
    scale = 1.0 / math.sqrt(row_count * devices)
    gram_scale = 1.0 / (sample_count * devices)
    picked = mix_and_pick(received, devices, run_length, scale, gram_scale)
    returned = exchange(picked.reshape(devices, -1), ORDER).reshape(picked.shape)
    return finish(returned, columns, sample_count)


def solution(mesh):
    wide, narrow = mesh.shape["wide"], mesh.shape["narrow"]
    axes, function = AXES, general_shards
    if wide * narrow == 32 and wide % 4 == 0:
        axes, function = SPLIT_AXES, sliced_shards
        mesh = jax.sharding.Mesh(mesh.devices.reshape(4, wide // 4, narrow), axes)
    in_specs = (P(None, axes), P(axes), P(axes))
    out_specs = (P(None, axes), P())
    return jax.shard_map(function, mesh=mesh, in_specs=in_specs, out_specs=out_specs, check_vma=False)
```

```python
import functools
import math

import jax
import jax.numpy as jnp
from jax import lax
from jax.experimental import pallas as pl
from jax.experimental.pallas import tpu as pltpu
from jax.sharding import PartitionSpec as P

LANES = 128
SUBLANES = 8
AXES = ("wide", "narrow")
SPLIT_AXES = ("line", "plane", "narrow")
ORDER = ("plane", "narrow", "line")
VMEM_LIMIT = 32 * 1024 * 1024
MESSAGE_ROWS = 6


def butterfly(values):
    values = list(values)
    apart = 1
    while apart < len(values):
        for low in range(len(values)):
            if not low & apart:
                first, second = values[low], values[low | apart]
                values[low], values[low | apart] = first + second, first - second
        apart *= 2
    return values


def sylvester(order_size):
    rows = lax.broadcasted_iota(jnp.int32, (order_size, order_size), 0)
    cols = lax.broadcasted_iota(jnp.int32, (order_size, order_size), 1)
    common = rows & cols
    parity = jnp.zeros_like(common)
    for bit_pos in range(order_size.bit_length() - 1):
        parity = parity ^ (common >> bit_pos)
    return (1 - 2 * (parity & 1)).astype(jnp.float32)


def split_dot(values, table, parts=3):
    total = None
    for _ in range(parts):
        part = values.astype(jnp.bfloat16)
        values = values - part.astype(jnp.float32)
        product = jnp.dot(part, table, preferred_element_type=jnp.float32)
        total = product if total is None else total + product
    return total


def butterfly_steps(count):
    steps = []
    apart = 1
    while apart < count:
        radix = min(8, count // apart)
        for start in range(count):
            if start // apart % radix == 0:
                steps.append((apart, [start + apart * index for index in range(radix)]))
        apart *= radix
    return steps


def fetch_blocks(x_hbm, signs_hbm, out_ref, x_ref, signs_ref, arrived):
    blocks, columns, _ = out_ref.shape
    fetches = [
        pltpu.make_async_copy(x_hbm, x_ref, arrived.at[0]),
        pltpu.make_async_copy(signs_hbm, signs_ref, arrived.at[1]),
    ]
    for fetch in fetches:
        fetch.start()
    table = sylvester(LANES).astype(jnp.bfloat16)
    for fetch in fetches:
        fetch.wait()
    signs = signs_ref[...].astype(jnp.float32)
    signed = [
        x_ref[:, block * LANES : (block + 1) * LANES] * signs[block : block + 1]
        for block in range(blocks)
    ]
    mixed = split_dot(jnp.concatenate(signed, axis=0), table)
    out_ref[...] = mixed.reshape(blocks, columns, LANES)


def local_kernel(x_hbm, signs_hbm, out_ref, x_ref, signs_ref, arrived):
    fetch_blocks(x_hbm, signs_hbm, out_ref, x_ref, signs_ref, arrived)
    for apart, places in butterfly_steps(out_ref.shape[0]):
        for place, value in zip(places, butterfly([out_ref[p] for p in places])):
            out_ref[place] = value


def sliced_kernel(
    x_hbm, signs_hbm, samples_hbm, final_ref, out_ref, x_ref, signs_ref, samples_ref, arrived, noted
):
    note = pltpu.make_async_copy(samples_hbm, samples_ref, noted)
    note.start()
    fetch_blocks(x_hbm, signs_hbm, out_ref, x_ref, signs_ref, arrived)
    blocks, columns, _ = out_ref.shape
    slices = blocks // 2
    rows = final_ref.shape[0] // slices
    note.wait()
    samples = samples_ref[...].astype(jnp.float32)
    per_row = slices // samples.shape[0]
    for turn in range(per_row):
        shift = LANES - turn * LANES // per_row
        turned = pltpu.roll(samples, shift, 1) if turn else samples
        for index in range(turn, slices, per_row):
            tail = (index + 1) * rows - 1
            final_ref[tail : tail + 1, :] = turned[index // per_row : index // per_row + 1]
    steps = butterfly_steps(blocks)
    last = steps[-1][0]
    for apart, places in steps:
        for place, value in zip(places, butterfly([out_ref[p] for p in places])):
            if apart == last:
                start = place // 2 * rows + place % 2 * columns
                final_ref[start : start + columns, :] = value
            else:
                out_ref[place] = value


def in_vmem(count):
    return [pl.BlockSpec(memory_space=pltpu.VMEM)] * count


def in_hbm(*arrays):
    return [pltpu.with_memory_space_constraint(array, pltpu.HBM) for array in arrays]


def fetch_scratch(matrix_slab, blocks):
    return [
        pltpu.VMEM(matrix_slab.shape, jnp.float32),
        pltpu.VMEM((blocks, LANES), jnp.int32),
    ]


def local_transform(matrix_slab, row_signs):
    columns, row_count = matrix_slab.shape
    blocks = row_count // LANES
    return pl.pallas_call(
        local_kernel,
        out_shape=jax.ShapeDtypeStruct((blocks, columns, LANES), jnp.float32),
        in_specs=[pl.BlockSpec(memory_space=pltpu.HBM)] * 2,
        out_specs=in_vmem(1)[0],
        scratch_shapes=[
            *fetch_scratch(matrix_slab, blocks),
            pltpu.SemaphoreType.DMA((2,)),
        ],
        compiler_params=pltpu.CompilerParams(vmem_limit_bytes=VMEM_LIMIT),
    )(*in_hbm(matrix_slab, row_signs.reshape(blocks, LANES)))


def sliced_transform(matrix_slab, row_signs, sample_rows):
    columns, row_count = matrix_slab.shape
    blocks = row_count // LANES
    samples = sample_rows.reshape(-1, LANES)
    return pl.pallas_call(
        sliced_kernel,
        out_shape=jax.ShapeDtypeStruct((blocks // 2 * (2 * columns + 1), LANES), jnp.float32),
        in_specs=[pl.BlockSpec(memory_space=pltpu.HBM)] * 3,
        out_specs=in_vmem(1)[0],
        scratch_shapes=[
            pltpu.VMEM((blocks, columns, LANES), jnp.float32),
            *fetch_scratch(matrix_slab, blocks),
            pltpu.VMEM(samples.shape, jnp.int32),
            pltpu.SemaphoreType.DMA((2,)),
            pltpu.SemaphoreType.DMA(()),
        ],
        compiler_params=pltpu.CompilerParams(vmem_limit_bytes=VMEM_LIMIT),
    )(*in_hbm(matrix_slab, row_signs.reshape(blocks, LANES), samples))


def mix_kernel(run_length, scale, gram_scale, x_ref, out_ref):
    devices = out_ref.shape[0] // MESSAGE_ROWS
    rows = x_ref.shape[0] // devices
    runs = LANES // run_length
    samples = jnp.concatenate(
        [x_ref[(s + 1) * rows - 1 : (s + 1) * rows, :] for s in range(devices)], axis=0
    ).astype(jnp.bfloat16)
    run_of = lax.broadcasted_iota(jnp.int32, (LANES, 2 * LANES), 0)
    row_of = lax.broadcasted_iota(jnp.int32, (LANES, 2 * LANES), 1)
    spread = jnp.where(row_of // run_length == run_of, 1.0, 0.0).astype(jnp.bfloat16)
    offsets = jnp.dot(samples, spread, preferred_element_type=jnp.float32)
    own = lax.broadcasted_iota(jnp.int32, offsets.shape, 1) % run_length
    mask = jnp.where(offsets == own.astype(jnp.float32), scale, 0.0)
    picked = []
    for part in range(4):
        block = part // 2
        starts = [s * rows + part * SUBLANES for s in range(devices)]
        mixed = butterfly([x_ref[start : start + SUBLANES, :] for start in starts])
        picked.append(
            jnp.concatenate(
                [
                    mixed[d] * mask[d : d + 1, block * LANES : (block + 1) * LANES]
                    for d in range(devices)
                ],
                axis=0,
            )
        )
    quarter = 2 * runs
    row = lax.broadcasted_iota(jnp.int32, (LANES, LANES), 0)
    lane = lax.broadcasted_iota(jnp.int32, (LANES, LANES), 1)
    pattern = jnp.where(row // run_length == lane % runs, 1.0, 0.0)
    lane = lax.broadcasted_iota(jnp.int32, (1, LANES), 1)
    group = lane // quarter
    place = []
    for part in range(4):
        block, half = part // 2, part % 2
        here = lane // runs % 2 == block
        sides = [group % 2, jnp.where(group < 2, group, 3 - group)]
        masks = [jnp.where(here & (side == half), 1.0, 0.0) for side in sides]
        place.append(jnp.concatenate([(pattern * mask).astype(jnp.bfloat16) for mask in masks], axis=1))
    gathered = split_dot(jnp.concatenate(picked, axis=1), jnp.concatenate(place, axis=0), 2)
    straight, crossed = gathered[:, :LANES], gathered[:, LANES:]
    turns = SUBLANES // 2 + 1
    totals = []
    for turn in range(turns):
        total = None
        for d in range(devices):
            one = straight[d * SUBLANES : (d + 1) * SUBLANES]
            two = crossed[d * SUBLANES : (d + 1) * SUBLANES]
            if turn:
                two = pltpu.roll(two, SUBLANES - turn, 0)
            total = one * two if total is None else total + one * two
        totals.append(total)
    from_quarter = row // quarter
    together = [jnp.where(from_quarter == q, 1.0, 0.0).astype(jnp.bfloat16) for q in range(4)]
    sums = split_dot(jnp.concatenate(totals, axis=0), jnp.concatenate(together, axis=1)) * gram_scale
    sub = lax.broadcasted_iota(jnp.int32, (SUBLANES, LANES), 0)
    lane = lax.broadcasted_iota(jnp.int32, (SUBLANES, LANES), 1)
    first, second = [jnp.zeros((SUBLANES, LANES), jnp.float32)] * 2
    for turn in range(SUBLANES):
        known = min(turn, SUBLANES - turn)
        here = sums[known * SUBLANES : (known + 1) * SUBLANES]
        quarters = [here[:, q * LANES : (q + 1) * LANES] for q in range(4)]
        if known != turn:
            quarters = [pltpu.roll(quarters[q], known, 0) for q in (0, 1, 3, 2)]
        mine = lane % SUBLANES == (sub + turn) % SUBLANES
        left = lane // SUBLANES % 2 == 0
        first = jnp.where(mine, jnp.where(left, quarters[0], quarters[2]), first)
        second = jnp.where(mine, jnp.where(left, quarters[3], quarters[1]), second)
    in_place = lane // (2 * SUBLANES) == (SUBLANES - sub) % SUBLANES
    gram = jnp.concatenate(
        [jnp.sum(jnp.where(in_place, part, 0.0), axis=0, keepdims=True) for part in (first, second)],
        axis=0,
    )
    half = SUBLANES // 2
    lane = lax.broadcasted_iota(jnp.int32, (half, LANES), 1)
    for d in range(devices):
        one = straight[d * SUBLANES : (d + 1) * SUBLANES]
        start = d * MESSAGE_ROWS
        out_ref[start : start + half, :] = jnp.where(lane < LANES // 2, one[:half], one[half:])
        out_ref[start + half : start + MESSAGE_ROWS, :] = gram


def mix_and_pick(received, devices, run_length, scale, gram_scale):
    return pl.pallas_call(
        functools.partial(mix_kernel, run_length, scale, gram_scale),
        out_shape=jax.ShapeDtypeStruct((devices * MESSAGE_ROWS, LANES), jnp.float32),
        in_specs=in_vmem(1),
        out_specs=in_vmem(1)[0],
        compiler_params=pltpu.CompilerParams(vmem_limit_bytes=VMEM_LIMIT),
    )(received)


def finish_kernel(x_ref, sketch_ref, gram_ref):
    sources = x_ref.shape[0] // MESSAGE_ROWS
    quarter = LANES // 4
    half_rows = SUBLANES // 2
    sub = lax.broadcasted_iota(jnp.int32, (SUBLANES, LANES), 0)
    lane = lax.broadcasted_iota(jnp.int32, (SUBLANES, LANES), 1)
    even = lane // quarter % 2 == 0
    stays = (sub < half_rows) == (lane < LANES // 2)
    gram = None
    for start in range(0, sources, 4):
        rows = []
        for index in range(4):
            place = (start + index) * MESSAGE_ROWS
            tail = x_ref[place + half_rows : place + MESSAGE_ROWS, :]
            gram = tail if gram is None else gram + tail
            rows.append(x_ref[place : place + half_rows, :])
        one = jnp.concatenate([rows[0], rows[2]], axis=0)
        two = jnp.concatenate([rows[1], rows[3]], axis=0)
        halves = [
            jnp.where(even, one, pltpu.roll(two, quarter, 1)),
            jnp.where(even, pltpu.roll(one, LANES - quarter, 1), two),
        ]
        for half, value in enumerate(halves):
            crossed = pltpu.roll(pltpu.roll(value, half_rows, 0), LANES // 2, 1)
            sketch_ref[
                half * SUBLANES : (half + 1) * SUBLANES, start * quarter : (start + 4) * quarter
            ] = jnp.where(stays, value, crossed)
    columns = gram_ref.shape[0]
    for half in range(2):
        lines = jnp.broadcast_to(gram[half : half + 1], (SUBLANES, LANES))
        turned = pltpu.roll(lines, 0, 1, stride=columns, stride_axis=0)
        gram_ref[half * SUBLANES : (half + 1) * SUBLANES, :] = turned[:, :columns]


def finish(received, columns, sample_count):
    return pl.pallas_call(
        finish_kernel,
        out_shape=(
            jax.ShapeDtypeStruct((columns, sample_count), jnp.float32),
            jax.ShapeDtypeStruct((columns, columns), jnp.float32),
        ),
        in_specs=[pl.BlockSpec(memory_space=pltpu.VMEM)],
        out_specs=(pl.BlockSpec(memory_space=pltpu.VMEM),) * 2,
        compiler_params=pltpu.CompilerParams(vmem_limit_bytes=VMEM_LIMIT),
    )(received)


def exchange(values, axes):
    return lax.all_to_all(values, axes, split_axis=0, concat_axis=0, tiled=True)


def general_shards(matrix_slab, row_signs, sample_rows):
    columns, row_count = matrix_slab.shape
    sample_count = sample_rows.shape[0]
    devices = lax.axis_size("wide") * lax.axis_size("narrow")
    run_length = row_count // sample_count
    slice_rows = row_count // devices
    slice_runs = slice_rows // run_length
    values = jnp.swapaxes(local_transform(matrix_slab, row_signs), 0, 1)
    values = values.reshape(columns, devices, slice_rows)
    received = exchange(jnp.swapaxes(values, 0, 1), AXES)
    offsets = exchange(sample_rows.reshape(devices, slice_runs), AXES)
    mixed = jnp.einsum("ds,scr->dcr", sylvester(devices), received, precision=lax.Precision.HIGHEST)
    mixed = mixed.reshape(devices, columns, slice_runs, run_length)
    chosen = offsets[:, None, :, None] == lax.iota(jnp.int32, run_length)
    picked = jnp.sum(jnp.where(chosen, mixed, 0.0), axis=3)
    picked = picked * jnp.float32(1.0 / math.sqrt(row_count * devices))
    gram = jnp.einsum("dck,dek->ce", picked, picked, precision=lax.Precision.HIGHEST)
    gram = gram / jnp.float32(sample_count * devices)
    grams = jnp.broadcast_to(gram[None], (devices, columns, columns))
    back = exchange(jnp.concatenate([picked, grams], axis=2), AXES)
    sketch = jnp.swapaxes(back[:, :, :slice_runs], 0, 1).reshape(columns, devices * slice_runs)
    return sketch, jnp.sum(back[:, :, slice_runs:], axis=0)


def sliced_shards(matrix_slab, row_signs, sample_rows):
    columns, row_count = matrix_slab.shape
    sample_count = sample_rows.shape[0]
    devices = lax.axis_size(ORDER)
    run_length = row_count // sample_count
    sent = sliced_transform(matrix_slab, row_signs, sample_rows)
    received = exchange(sent.reshape(devices, -1), ORDER).reshape(sent.shape)
    scale = 1.0 / math.sqrt(row_count * devices)
    gram_scale = 1.0 / (sample_count * devices)
    picked = mix_and_pick(received, devices, run_length, scale, gram_scale)
    returned = exchange(picked.reshape(devices, -1), ORDER).reshape(picked.shape)
    return finish(returned, columns, sample_count)


def solution(mesh):
    wide, narrow = mesh.shape["wide"], mesh.shape["narrow"]
    axes, function = AXES, general_shards
    if wide * narrow == 32 and wide % 4 == 0:
        axes, function = SPLIT_AXES, sliced_shards
        mesh = jax.sharding.Mesh(mesh.devices.reshape(4, wide // 4, narrow), axes)
    in_specs = (P(None, axes), P(axes), P(axes))
    out_specs = (P(None, axes), P())
    return jax.shard_map(function, mesh=mesh, in_specs=in_specs, out_specs=out_specs, check_vma=False)
```

```python
import functools
import math

import jax
import jax.numpy as jnp
from jax import lax
from jax.experimental import pallas as pl
from jax.experimental.pallas import tpu as pltpu
from jax.sharding import PartitionSpec as P

LANES = 128
SUBLANES = 8
AXES = ("wide", "narrow")
SPLIT_AXES = ("line", "plane", "narrow")
ORDER = ("plane", "narrow", "line")
VMEM_LIMIT = 32 * 1024 * 1024
MESSAGE_ROWS = 6


def butterfly(values):
    values = list(values)
    apart = 1
    while apart < len(values):
        for low in range(len(values)):
            if not low & apart:
                first, second = values[low], values[low | apart]
                values[low], values[low | apart] = first + second, first - second
        apart *= 2
    return values


def sylvester(order_size):
    rows = lax.broadcasted_iota(jnp.int32, (order_size, order_size), 0)
    cols = lax.broadcasted_iota(jnp.int32, (order_size, order_size), 1)
    common = rows & cols
    parity = jnp.zeros_like(common)
    for bit_pos in range(order_size.bit_length() - 1):
        parity = parity ^ (common >> bit_pos)
    return (1 - 2 * (parity & 1)).astype(jnp.float32)


def split_dot(values, table, parts=3):
    total = None
    for _ in range(parts):
        part = values.astype(jnp.bfloat16)
        values = values - part.astype(jnp.float32)
        product = jnp.dot(part, table, preferred_element_type=jnp.float32)
        total = product if total is None else total + product
    return total


def butterfly_steps(count):
    steps = []
    apart = 1
    while apart < count:
        radix = min(8, count // apart)
        for start in range(count):
            if start // apart % radix == 0:
                steps.append((apart, [start + apart * index for index in range(radix)]))
        apart *= radix
    return steps


def fetch_blocks(x_hbm, signs_hbm, out_ref, x_ref, signs_ref, arrived, *others):
    blocks, columns, _ = out_ref.shape
    fetches = [
        pltpu.make_async_copy(x_hbm, x_ref, arrived.at[0]),
        pltpu.make_async_copy(signs_hbm, signs_ref, arrived.at[1]),
    ]
    for fetch in (*fetches, *others):
        fetch.start()
    table = sylvester(LANES).astype(jnp.bfloat16)
    for fetch in fetches:
        fetch.wait()
    signs = signs_ref[...].astype(jnp.float32)
    signed = [
        x_ref[:, block * LANES : (block + 1) * LANES] * signs[block : block + 1]
        for block in range(blocks)
    ]
    mixed = split_dot(jnp.concatenate(signed, axis=0), table)
    out_ref[...] = mixed.reshape(blocks, columns, LANES)


def local_kernel(x_hbm, signs_hbm, out_ref, x_ref, signs_ref, arrived):
    fetch_blocks(x_hbm, signs_hbm, out_ref, x_ref, signs_ref, arrived)
    for apart, places in butterfly_steps(out_ref.shape[0]):
        for place, value in zip(places, butterfly([out_ref[p] for p in places])):
            out_ref[place] = value


def sliced_kernel(
    x_hbm, signs_hbm, samples_hbm, final_ref, out_ref, x_ref, signs_ref, samples_ref, arrived, noted
):
    note = pltpu.make_async_copy(samples_hbm, samples_ref, noted)
    fetch_blocks(x_hbm, signs_hbm, out_ref, x_ref, signs_ref, arrived, note)
    blocks, columns, _ = out_ref.shape
    slices = blocks // 2
    rows = final_ref.shape[0] // slices
    note.wait()
    samples = samples_ref[...].astype(jnp.float32)
    per_row = slices // samples.shape[0]
    for turn in range(per_row):
        shift = LANES - turn * LANES // per_row
        turned = pltpu.roll(samples, shift, 1) if turn else samples
        for index in range(turn, slices, per_row):
            tail = (index + 1) * rows - 1
            final_ref[tail : tail + 1, :] = turned[index // per_row : index // per_row + 1]
    steps = butterfly_steps(blocks)
    last = steps[-1][0]
    for apart, places in steps:
        for place, value in zip(places, butterfly([out_ref[p] for p in places])):
            if apart == last:
                start = place // 2 * rows + place % 2 * columns
                final_ref[start : start + columns, :] = value
            else:
                out_ref[place] = value


def in_vmem(count):
    return [pl.BlockSpec(memory_space=pltpu.VMEM)] * count


def in_hbm(*arrays):
    return [pltpu.with_memory_space_constraint(array, pltpu.HBM) for array in arrays]


def fetch_scratch(matrix_slab, blocks):
    return [
        pltpu.VMEM(matrix_slab.shape, jnp.float32),
        pltpu.VMEM((blocks, LANES), jnp.int32),
    ]


def local_transform(matrix_slab, row_signs):
    columns, row_count = matrix_slab.shape
    blocks = row_count // LANES
    return pl.pallas_call(
        local_kernel,
        out_shape=jax.ShapeDtypeStruct((blocks, columns, LANES), jnp.float32),
        in_specs=[pl.BlockSpec(memory_space=pltpu.HBM)] * 2,
        out_specs=in_vmem(1)[0],
        scratch_shapes=[
            *fetch_scratch(matrix_slab, blocks),
            pltpu.SemaphoreType.DMA((2,)),
        ],
        compiler_params=pltpu.CompilerParams(vmem_limit_bytes=VMEM_LIMIT),
    )(*in_hbm(matrix_slab, row_signs.reshape(blocks, LANES)))


def sliced_transform(matrix_slab, row_signs, sample_rows):
    columns, row_count = matrix_slab.shape
    blocks = row_count // LANES
    samples = sample_rows.reshape(-1, LANES)
    return pl.pallas_call(
        sliced_kernel,
        out_shape=jax.ShapeDtypeStruct((blocks // 2 * (2 * columns + 1), LANES), jnp.float32),
        in_specs=[pl.BlockSpec(memory_space=pltpu.HBM)] * 3,
        out_specs=in_vmem(1)[0],
        scratch_shapes=[
            pltpu.VMEM((blocks, columns, LANES), jnp.float32),
            *fetch_scratch(matrix_slab, blocks),
            pltpu.VMEM(samples.shape, jnp.int32),
            pltpu.SemaphoreType.DMA((2,)),
            pltpu.SemaphoreType.DMA(()),
        ],
        compiler_params=pltpu.CompilerParams(vmem_limit_bytes=VMEM_LIMIT),
    )(*in_hbm(matrix_slab, row_signs.reshape(blocks, LANES), samples))


def mix_kernel(run_length, scale, gram_scale, x_ref, out_ref):
    devices = out_ref.shape[0] // MESSAGE_ROWS
    rows = x_ref.shape[0] // devices
    runs = LANES // run_length
    samples = jnp.concatenate(
        [x_ref[(s + 1) * rows - 1 : (s + 1) * rows, :] for s in range(devices)], axis=0
    ).astype(jnp.bfloat16)
    run_of = lax.broadcasted_iota(jnp.int32, (LANES, 2 * LANES), 0)
    row_of = lax.broadcasted_iota(jnp.int32, (LANES, 2 * LANES), 1)
    spread = jnp.where(row_of // run_length == run_of, 1.0, 0.0).astype(jnp.bfloat16)
    offsets = jnp.dot(samples, spread, preferred_element_type=jnp.float32)
    own = lax.broadcasted_iota(jnp.int32, offsets.shape, 1) % run_length
    mask = jnp.where(offsets == own.astype(jnp.float32), scale, 0.0)
    picked = []
    for part in range(4):
        block = part // 2
        starts = [s * rows + part * SUBLANES for s in range(devices)]
        mixed = butterfly([x_ref[start : start + SUBLANES, :] for start in starts])
        picked.append(
            jnp.concatenate(
                [
                    mixed[d] * mask[d : d + 1, block * LANES : (block + 1) * LANES]
                    for d in range(devices)
                ],
                axis=0,
            )
        )
    quarter = 2 * runs
    row = lax.broadcasted_iota(jnp.int32, (LANES, LANES), 0)
    lane = lax.broadcasted_iota(jnp.int32, (LANES, LANES), 1)
    pattern = jnp.where(row // run_length == lane % runs, 1.0, 0.0)
    lane = lax.broadcasted_iota(jnp.int32, (1, LANES), 1)
    group = lane // quarter
    place = []
    for part in range(4):
        block, half = part // 2, part % 2
        here = lane // runs % 2 == block
        sides = [group % 2, jnp.where(group < 2, group, 3 - group)]
        masks = [jnp.where(here & (side == half), 1.0, 0.0) for side in sides]
        place.append(jnp.concatenate([(pattern * mask).astype(jnp.bfloat16) for mask in masks], axis=1))
    gathered = split_dot(jnp.concatenate(picked, axis=1), jnp.concatenate(place, axis=0), 2)
    straight, crossed = gathered[:, :LANES], gathered[:, LANES:]
    turns = SUBLANES // 2 + 1
    totals = []
    for turn in range(turns):
        total = None
        for d in range(devices):
            one = straight[d * SUBLANES : (d + 1) * SUBLANES]
            two = crossed[d * SUBLANES : (d + 1) * SUBLANES]
            if turn:
                two = pltpu.roll(two, SUBLANES - turn, 0)
            total = one * two if total is None else total + one * two
        totals.append(total)
    from_quarter = row // quarter
    together = [jnp.where(from_quarter == q, 1.0, 0.0).astype(jnp.bfloat16) for q in range(4)]
    sums = split_dot(jnp.concatenate(totals, axis=0), jnp.concatenate(together, axis=1), 2)
    sums = sums * gram_scale
    sub = lax.broadcasted_iota(jnp.int32, (SUBLANES, LANES), 0)
    lane = lax.broadcasted_iota(jnp.int32, (SUBLANES, LANES), 1)
    first, second = [jnp.zeros((SUBLANES, LANES), jnp.float32)] * 2
    for turn in range(SUBLANES):
        known = min(turn, SUBLANES - turn)
        here = sums[known * SUBLANES : (known + 1) * SUBLANES]
        quarters = [here[:, q * LANES : (q + 1) * LANES] for q in range(4)]
        if known != turn:
            quarters = [pltpu.roll(quarters[q], known, 0) for q in (0, 1, 3, 2)]
        mine = lane % SUBLANES == (sub + turn) % SUBLANES
        left = lane // SUBLANES % 2 == 0
        first = jnp.where(mine, jnp.where(left, quarters[0], quarters[2]), first)
        second = jnp.where(mine, jnp.where(left, quarters[3], quarters[1]), second)
    in_place = lane // (2 * SUBLANES) == (SUBLANES - sub) % SUBLANES
    gram = jnp.concatenate(
        [jnp.sum(jnp.where(in_place, part, 0.0), axis=0, keepdims=True) for part in (first, second)],
        axis=0,
    )
    half = SUBLANES // 2
    lane = lax.broadcasted_iota(jnp.int32, (half, LANES), 1)
    for d in range(devices):
        one = straight[d * SUBLANES : (d + 1) * SUBLANES]
        start = d * MESSAGE_ROWS
        out_ref[start : start + half, :] = jnp.where(lane < LANES // 2, one[:half], one[half:])
        out_ref[start + half : start + MESSAGE_ROWS, :] = gram


def mix_and_pick(received, devices, run_length, scale, gram_scale):
    return pl.pallas_call(
        functools.partial(mix_kernel, run_length, scale, gram_scale),
        out_shape=jax.ShapeDtypeStruct((devices * MESSAGE_ROWS, LANES), jnp.float32),
        in_specs=in_vmem(1),
        out_specs=in_vmem(1)[0],
        compiler_params=pltpu.CompilerParams(vmem_limit_bytes=VMEM_LIMIT),
    )(received)


def finish_kernel(x_ref, sketch_ref, gram_ref):
    sources = x_ref.shape[0] // MESSAGE_ROWS
    quarter = LANES // 4
    half_rows = SUBLANES // 2
    sub = lax.broadcasted_iota(jnp.int32, (SUBLANES, LANES), 0)
    lane = lax.broadcasted_iota(jnp.int32, (SUBLANES, LANES), 1)
    even = lane // quarter % 2 == 0
    stays = (sub < half_rows) == (lane < LANES // 2)
    gram = None
    for start in range(0, sources, 4):
        rows = []
        for index in range(4):
            place = (start + index) * MESSAGE_ROWS
            tail = x_ref[place + half_rows : place + MESSAGE_ROWS, :]
            gram = tail if gram is None else gram + tail
            rows.append(x_ref[place : place + half_rows, :])
        one = jnp.concatenate([rows[0], rows[2]], axis=0)
        two = jnp.concatenate([rows[1], rows[3]], axis=0)
        halves = [
            jnp.where(even, one, pltpu.roll(two, quarter, 1)),
            jnp.where(even, pltpu.roll(one, LANES - quarter, 1), two),
        ]
        for half, value in enumerate(halves):
            crossed = pltpu.roll(pltpu.roll(value, half_rows, 0), LANES // 2, 1)
            sketch_ref[
                half * SUBLANES : (half + 1) * SUBLANES, start * quarter : (start + 4) * quarter
            ] = jnp.where(stays, value, crossed)
    columns = gram_ref.shape[0]
    for half in range(2):
        lines = jnp.broadcast_to(gram[half : half + 1], (SUBLANES, LANES))
        turned = pltpu.roll(lines, 0, 1, stride=columns, stride_axis=0)
        gram_ref[half * SUBLANES : (half + 1) * SUBLANES, :] = turned[:, :columns]


def finish(received, columns, sample_count):
    return pl.pallas_call(
        finish_kernel,
        out_shape=(
            jax.ShapeDtypeStruct((columns, sample_count), jnp.float32),
            jax.ShapeDtypeStruct((columns, columns), jnp.float32),
        ),
        in_specs=[pl.BlockSpec(memory_space=pltpu.VMEM)],
        out_specs=(pl.BlockSpec(memory_space=pltpu.VMEM),) * 2,
        compiler_params=pltpu.CompilerParams(vmem_limit_bytes=VMEM_LIMIT),
    )(received)


def exchange(values, axes):
    return lax.all_to_all(values, axes, split_axis=0, concat_axis=0, tiled=True)


def general_shards(matrix_slab, row_signs, sample_rows):
    columns, row_count = matrix_slab.shape
    sample_count = sample_rows.shape[0]
    devices = lax.axis_size("wide") * lax.axis_size("narrow")
    run_length = row_count // sample_count
    slice_rows = row_count // devices
    slice_runs = slice_rows // run_length
    values = jnp.swapaxes(local_transform(matrix_slab, row_signs), 0, 1)
    values = values.reshape(columns, devices, slice_rows)
    received = exchange(jnp.swapaxes(values, 0, 1), AXES)
    offsets = exchange(sample_rows.reshape(devices, slice_runs), AXES)
    mixed = jnp.einsum("ds,scr->dcr", sylvester(devices), received, precision=lax.Precision.HIGHEST)
    mixed = mixed.reshape(devices, columns, slice_runs, run_length)
    chosen = offsets[:, None, :, None] == lax.iota(jnp.int32, run_length)
    picked = jnp.sum(jnp.where(chosen, mixed, 0.0), axis=3)
    picked = picked * jnp.float32(1.0 / math.sqrt(row_count * devices))
    gram = jnp.einsum("dck,dek->ce", picked, picked, precision=lax.Precision.HIGHEST)
    gram = gram / jnp.float32(sample_count * devices)
    grams = jnp.broadcast_to(gram[None], (devices, columns, columns))
    back = exchange(jnp.concatenate([picked, grams], axis=2), AXES)
    sketch = jnp.swapaxes(back[:, :, :slice_runs], 0, 1).reshape(columns, devices * slice_runs)
    return sketch, jnp.sum(back[:, :, slice_runs:], axis=0)


def sliced_shards(matrix_slab, row_signs, sample_rows):
    columns, row_count = matrix_slab.shape
    sample_count = sample_rows.shape[0]
    devices = lax.axis_size(ORDER)
    run_length = row_count // sample_count
    sent = sliced_transform(matrix_slab, row_signs, sample_rows)
    received = exchange(sent.reshape(devices, -1), ORDER).reshape(sent.shape)
    scale = 1.0 / math.sqrt(row_count * devices)
    gram_scale = 1.0 / (sample_count * devices)
    picked = mix_and_pick(received, devices, run_length, scale, gram_scale)
    returned = exchange(picked.reshape(devices, -1), ORDER).reshape(picked.shape)
    return finish(returned, columns, sample_count)


def solution(mesh):
    wide, narrow = mesh.shape["wide"], mesh.shape["narrow"]
    axes, function = AXES, general_shards
    if wide * narrow == 32 and wide % 4 == 0:
        axes, function = SPLIT_AXES, sliced_shards
        mesh = jax.sharding.Mesh(mesh.devices.reshape(4, wide // 4, narrow), axes)
    in_specs = (P(None, axes), P(axes), P(axes))
    out_specs = (P(None, axes), P())
    return jax.shard_map(function, mesh=mesh, in_specs=in_specs, out_specs=out_specs, check_vma=False)
```

```python
import functools
import math

import jax
import jax.numpy as jnp
from jax import lax
from jax.experimental import pallas as pl
from jax.experimental.pallas import tpu as pltpu
from jax.sharding import PartitionSpec as P

LANES = 128
SUBLANES = 8
AXES = ("wide", "narrow")
SPLIT_AXES = ("line", "plane", "narrow")
ORDER = ("plane", "narrow", "line")
VMEM_LIMIT = 32 * 1024 * 1024
MESSAGE_ROWS = 6


def butterfly(values):
    values = list(values)
    apart = 1
    while apart < len(values):
        for low in range(len(values)):
            if not low & apart:
                first, second = values[low], values[low | apart]
                values[low], values[low | apart] = first + second, first - second
        apart *= 2
    return values


def sylvester(order_size):
    rows = lax.broadcasted_iota(jnp.int32, (order_size, order_size), 0)
    cols = lax.broadcasted_iota(jnp.int32, (order_size, order_size), 1)
    common = rows & cols
    parity = jnp.zeros_like(common)
    for bit_pos in range(order_size.bit_length() - 1):
        parity = parity ^ (common >> bit_pos)
    return (1 - 2 * (parity & 1)).astype(jnp.float32)


def split_dot(values, table, parts=3):
    pieces = []
    for _ in range(parts):
        pieces.append(values.astype(jnp.bfloat16))
        values = values - pieces[-1].astype(jnp.float32)
    return jnp.dot(
        jnp.concatenate(pieces, axis=1),
        jnp.concatenate([table] * parts, axis=0),
        preferred_element_type=jnp.float32,
    )


def butterfly_steps(count):
    steps = []
    apart = 1
    while apart < count:
        radix = min(8, count // apart)
        for start in range(count):
            if start // apart % radix == 0:
                steps.append((apart, [start + apart * index for index in range(radix)]))
        apart *= radix
    return steps


def fetch_blocks(x_hbm, signs_hbm, out_ref, x_ref, signs_ref, arrived, *others):
    blocks, columns, _ = out_ref.shape
    fetches = [
        pltpu.make_async_copy(x_hbm, x_ref, arrived.at[0]),
        pltpu.make_async_copy(signs_hbm, signs_ref, arrived.at[1]),
    ]
    for fetch in (*fetches, *others):
        fetch.start()
    table = sylvester(LANES).astype(jnp.bfloat16)
    for fetch in fetches:
        fetch.wait()
    signs = signs_ref[...].astype(jnp.float32)
    signed = [
        x_ref[:, block * LANES : (block + 1) * LANES] * signs[block : block + 1]
        for block in range(blocks)
    ]
    mixed = split_dot(jnp.concatenate(signed, axis=0), table)
    out_ref[...] = mixed.reshape(blocks, columns, LANES)


def local_kernel(x_hbm, signs_hbm, out_ref, x_ref, signs_ref, arrived):
    fetch_blocks(x_hbm, signs_hbm, out_ref, x_ref, signs_ref, arrived)
    for apart, places in butterfly_steps(out_ref.shape[0]):
        for place, value in zip(places, butterfly([out_ref[p] for p in places])):
            out_ref[place] = value


def sliced_kernel(
    x_hbm, signs_hbm, samples_hbm, final_ref, out_ref, x_ref, signs_ref, samples_ref, arrived, noted
):
    note = pltpu.make_async_copy(samples_hbm, samples_ref, noted)
    fetch_blocks(x_hbm, signs_hbm, out_ref, x_ref, signs_ref, arrived, note)
    blocks, columns, _ = out_ref.shape
    slices = blocks // 2
    rows = final_ref.shape[0] // slices
    note.wait()
    samples = samples_ref[...].astype(jnp.float32)
    per_row = slices // samples.shape[0]
    for turn in range(per_row):
        shift = LANES - turn * LANES // per_row
        turned = pltpu.roll(samples, shift, 1) if turn else samples
        for index in range(turn, slices, per_row):
            tail = (index + 1) * rows - 1
            final_ref[tail : tail + 1, :] = turned[index // per_row : index // per_row + 1]
    steps = butterfly_steps(blocks)
    last = steps[-1][0]
    for apart, places in steps:
        for place, value in zip(places, butterfly([out_ref[p] for p in places])):
            if apart == last:
                start = place // 2 * rows + place % 2 * columns
                final_ref[start : start + columns, :] = value
            else:
                out_ref[place] = value


def in_vmem(count):
    return [pl.BlockSpec(memory_space=pltpu.VMEM)] * count


def in_hbm(*arrays):
    return [pltpu.with_memory_space_constraint(array, pltpu.HBM) for array in arrays]


def fetch_scratch(matrix_slab, blocks):
    return [
        pltpu.VMEM(matrix_slab.shape, jnp.float32),
        pltpu.VMEM((blocks, LANES), jnp.int32),
    ]


def local_transform(matrix_slab, row_signs):
    columns, row_count = matrix_slab.shape
    blocks = row_count // LANES
    return pl.pallas_call(
        local_kernel,
        out_shape=jax.ShapeDtypeStruct((blocks, columns, LANES), jnp.float32),
        in_specs=[pl.BlockSpec(memory_space=pltpu.HBM)] * 2,
        out_specs=in_vmem(1)[0],
        scratch_shapes=[
            *fetch_scratch(matrix_slab, blocks),
            pltpu.SemaphoreType.DMA((2,)),
        ],
        compiler_params=pltpu.CompilerParams(vmem_limit_bytes=VMEM_LIMIT),
    )(*in_hbm(matrix_slab, row_signs.reshape(blocks, LANES)))


def sliced_transform(matrix_slab, row_signs, sample_rows):
    columns, row_count = matrix_slab.shape
    blocks = row_count // LANES
    samples = sample_rows.reshape(-1, LANES)
    return pl.pallas_call(
        sliced_kernel,
        out_shape=jax.ShapeDtypeStruct((blocks // 2 * (2 * columns + 1), LANES), jnp.float32),
        in_specs=[pl.BlockSpec(memory_space=pltpu.HBM)] * 3,
        out_specs=in_vmem(1)[0],
        scratch_shapes=[
            pltpu.VMEM((blocks, columns, LANES), jnp.float32),
            *fetch_scratch(matrix_slab, blocks),
            pltpu.VMEM(samples.shape, jnp.int32),
            pltpu.SemaphoreType.DMA((2,)),
            pltpu.SemaphoreType.DMA(()),
        ],
        compiler_params=pltpu.CompilerParams(vmem_limit_bytes=VMEM_LIMIT),
    )(*in_hbm(matrix_slab, row_signs.reshape(blocks, LANES), samples))


def mix_kernel(run_length, scale, gram_scale, x_ref, out_ref):
    devices = out_ref.shape[0] // MESSAGE_ROWS
    rows = x_ref.shape[0] // devices
    runs = LANES // run_length
    samples = jnp.concatenate(
        [x_ref[(s + 1) * rows - 1 : (s + 1) * rows, :] for s in range(devices)], axis=0
    ).astype(jnp.bfloat16)
    run_of = lax.broadcasted_iota(jnp.int32, (LANES, 2 * LANES), 0)
    row_of = lax.broadcasted_iota(jnp.int32, (LANES, 2 * LANES), 1)
    spread = jnp.where(row_of // run_length == run_of, 1.0, 0.0).astype(jnp.bfloat16)
    offsets = jnp.dot(samples, spread, preferred_element_type=jnp.float32)
    own = lax.broadcasted_iota(jnp.int32, offsets.shape, 1) % run_length
    mask = jnp.where(offsets == own.astype(jnp.float32), scale, 0.0)
    picked = []
    for part in range(4):
        block = part // 2
        starts = [s * rows + part * SUBLANES for s in range(devices)]
        mixed = butterfly([x_ref[start : start + SUBLANES, :] for start in starts])
        picked.append(
            jnp.concatenate(
                [
                    mixed[d] * mask[d : d + 1, block * LANES : (block + 1) * LANES]
                    for d in range(devices)
                ],
                axis=0,
            )
        )
    quarter = 2 * runs
    row = lax.broadcasted_iota(jnp.int32, (LANES, LANES), 0)
    lane = lax.broadcasted_iota(jnp.int32, (LANES, LANES), 1)
    pattern = jnp.where(row // run_length == lane % runs, 1.0, 0.0)
    lane = lax.broadcasted_iota(jnp.int32, (1, LANES), 1)
    group = lane // quarter
    place = []
    for part in range(4):
        block, half = part // 2, part % 2
        here = lane // runs % 2 == block
        sides = [group % 2, jnp.where(group < 2, group, 3 - group)]
        masks = [jnp.where(here & (side == half), 1.0, 0.0) for side in sides]
        place.append(jnp.concatenate([(pattern * mask).astype(jnp.bfloat16) for mask in masks], axis=1))
    gathered = split_dot(jnp.concatenate(picked, axis=1), jnp.concatenate(place, axis=0), 2)
    straight, crossed = gathered[:, :LANES], gathered[:, LANES:]
    turns = SUBLANES // 2 + 1
    totals = []
    for turn in range(turns):
        total = None
        for d in range(devices):
            one = straight[d * SUBLANES : (d + 1) * SUBLANES]
            two = crossed[d * SUBLANES : (d + 1) * SUBLANES]
            if turn:
                two = pltpu.roll(two, SUBLANES - turn, 0)
            total = one * two if total is None else total + one * two
        totals.append(total)
    from_quarter = row // quarter
    together = [jnp.where(from_quarter == q, 1.0, 0.0).astype(jnp.bfloat16) for q in range(4)]
    sums = split_dot(jnp.concatenate(totals, axis=0), jnp.concatenate(together, axis=1), 2)
    sums = sums * gram_scale
    sub = lax.broadcasted_iota(jnp.int32, (SUBLANES, LANES), 0)
    lane = lax.broadcasted_iota(jnp.int32, (SUBLANES, LANES), 1)
    first, second = [jnp.zeros((SUBLANES, LANES), jnp.float32)] * 2
    for turn in range(SUBLANES):
        known = min(turn, SUBLANES - turn)
        here = sums[known * SUBLANES : (known + 1) * SUBLANES]
        quarters = [here[:, q * LANES : (q + 1) * LANES] for q in range(4)]
        if known != turn:
            quarters = [pltpu.roll(quarters[q], known, 0) for q in (0, 1, 3, 2)]
        mine = lane % SUBLANES == (sub + turn) % SUBLANES
        left = lane // SUBLANES % 2 == 0
        first = jnp.where(mine, jnp.where(left, quarters[0], quarters[2]), first)
        second = jnp.where(mine, jnp.where(left, quarters[3], quarters[1]), second)
    in_place = lane // (2 * SUBLANES) == (SUBLANES - sub) % SUBLANES
    gram = jnp.concatenate(
        [jnp.sum(jnp.where(in_place, part, 0.0), axis=0, keepdims=True) for part in (first, second)],
        axis=0,
    )
    half = SUBLANES // 2
    lane = lax.broadcasted_iota(jnp.int32, (half, LANES), 1)
    for d in range(devices):
        one = straight[d * SUBLANES : (d + 1) * SUBLANES]
        start = d * MESSAGE_ROWS
        out_ref[start : start + half, :] = jnp.where(lane < LANES // 2, one[:half], one[half:])
        out_ref[start + half : start + MESSAGE_ROWS, :] = gram


def mix_and_pick(received, devices, run_length, scale, gram_scale):
    return pl.pallas_call(
        functools.partial(mix_kernel, run_length, scale, gram_scale),
        out_shape=jax.ShapeDtypeStruct((devices * MESSAGE_ROWS, LANES), jnp.float32),
        in_specs=in_vmem(1),
        out_specs=in_vmem(1)[0],
        compiler_params=pltpu.CompilerParams(vmem_limit_bytes=VMEM_LIMIT),
    )(received)


def finish_kernel(x_ref, sketch_ref, gram_ref):
    sources = x_ref.shape[0] // MESSAGE_ROWS
    quarter = LANES // 4
    half_rows = SUBLANES // 2
    sub = lax.broadcasted_iota(jnp.int32, (SUBLANES, LANES), 0)
    lane = lax.broadcasted_iota(jnp.int32, (SUBLANES, LANES), 1)
    even = lane // quarter % 2 == 0
    stays = (sub < half_rows) == (lane < LANES // 2)
    gram = None
    for start in range(0, sources, 4):
        rows = []
        for index in range(4):
            place = (start + index) * MESSAGE_ROWS
            tail = x_ref[place + half_rows : place + MESSAGE_ROWS, :]
            gram = tail if gram is None else gram + tail
            rows.append(x_ref[place : place + half_rows, :])
        one = jnp.concatenate([rows[0], rows[2]], axis=0)
        two = jnp.concatenate([rows[1], rows[3]], axis=0)
        halves = [
            jnp.where(even, one, pltpu.roll(two, quarter, 1)),
            jnp.where(even, pltpu.roll(one, LANES - quarter, 1), two),
        ]
        for half, value in enumerate(halves):
            crossed = pltpu.roll(pltpu.roll(value, half_rows, 0), LANES // 2, 1)
            sketch_ref[
                half * SUBLANES : (half + 1) * SUBLANES, start * quarter : (start + 4) * quarter
            ] = jnp.where(stays, value, crossed)
    columns = gram_ref.shape[0]
    for half in range(2):
        lines = jnp.broadcast_to(gram[half : half + 1], (SUBLANES, LANES))
        turned = pltpu.roll(lines, 0, 1, stride=columns, stride_axis=0)
        gram_ref[half * SUBLANES : (half + 1) * SUBLANES, :] = turned[:, :columns]


def finish(received, columns, sample_count):
    return pl.pallas_call(
        finish_kernel,
        out_shape=(
            jax.ShapeDtypeStruct((columns, sample_count), jnp.float32),
            jax.ShapeDtypeStruct((columns, columns), jnp.float32),
        ),
        in_specs=[pl.BlockSpec(memory_space=pltpu.VMEM)],
        out_specs=(pl.BlockSpec(memory_space=pltpu.VMEM),) * 2,
        compiler_params=pltpu.CompilerParams(vmem_limit_bytes=VMEM_LIMIT),
    )(received)


def exchange(values, axes):
    return lax.all_to_all(values, axes, split_axis=0, concat_axis=0, tiled=True)


def general_shards(matrix_slab, row_signs, sample_rows):
    columns, row_count = matrix_slab.shape
    sample_count = sample_rows.shape[0]
    devices = lax.axis_size("wide") * lax.axis_size("narrow")
    run_length = row_count // sample_count
    slice_rows = row_count // devices
    slice_runs = slice_rows // run_length
    values = jnp.swapaxes(local_transform(matrix_slab, row_signs), 0, 1)
    values = values.reshape(columns, devices, slice_rows)
    received = exchange(jnp.swapaxes(values, 0, 1), AXES)
    offsets = exchange(sample_rows.reshape(devices, slice_runs), AXES)
    mixed = jnp.einsum("ds,scr->dcr", sylvester(devices), received, precision=lax.Precision.HIGHEST)
    mixed = mixed.reshape(devices, columns, slice_runs, run_length)
    chosen = offsets[:, None, :, None] == lax.iota(jnp.int32, run_length)
    picked = jnp.sum(jnp.where(chosen, mixed, 0.0), axis=3)
    picked = picked * jnp.float32(1.0 / math.sqrt(row_count * devices))
    gram = jnp.einsum("dck,dek->ce", picked, picked, precision=lax.Precision.HIGHEST)
    gram = gram / jnp.float32(sample_count * devices)
    grams = jnp.broadcast_to(gram[None], (devices, columns, columns))
    back = exchange(jnp.concatenate([picked, grams], axis=2), AXES)
    sketch = jnp.swapaxes(back[:, :, :slice_runs], 0, 1).reshape(columns, devices * slice_runs)
    return sketch, jnp.sum(back[:, :, slice_runs:], axis=0)


def sliced_shards(matrix_slab, row_signs, sample_rows):
    columns, row_count = matrix_slab.shape
    sample_count = sample_rows.shape[0]
    devices = lax.axis_size(ORDER)
    run_length = row_count // sample_count
    sent = sliced_transform(matrix_slab, row_signs, sample_rows)
    received = exchange(sent.reshape(devices, -1), ORDER).reshape(sent.shape)
    scale = 1.0 / math.sqrt(row_count * devices)
    gram_scale = 1.0 / (sample_count * devices)
    picked = mix_and_pick(received, devices, run_length, scale, gram_scale)
    returned = exchange(picked.reshape(devices, -1), ORDER).reshape(picked.shape)
    return finish(returned, columns, sample_count)


def solution(mesh):
    wide, narrow = mesh.shape["wide"], mesh.shape["narrow"]
    axes, function = AXES, general_shards
    if wide * narrow == 32 and wide % 4 == 0:
        axes, function = SPLIT_AXES, sliced_shards
        mesh = jax.sharding.Mesh(mesh.devices.reshape(4, wide // 4, narrow), axes)
    in_specs = (P(None, axes), P(axes), P(axes))
    out_specs = (P(None, axes), P())
    return jax.shard_map(function, mesh=mesh, in_specs=in_specs, out_specs=out_specs, check_vma=False)
```

```python
import functools
import math

import jax
import jax.numpy as jnp
from jax import lax
from jax.experimental import pallas as pl
from jax.experimental.pallas import tpu as pltpu
from jax.sharding import PartitionSpec as P

LANES = 128
SUBLANES = 8
AXES = ("wide", "narrow")
SPLIT_AXES = ("line", "plane", "narrow")
ORDER = ("plane", "narrow", "line")
VMEM_LIMIT = 32 * 1024 * 1024
MESSAGE_ROWS = 6


def butterfly(values):
    values = list(values)
    apart = 1
    while apart < len(values):
        for low in range(len(values)):
            if not low & apart:
                first, second = values[low], values[low | apart]
                values[low], values[low | apart] = first + second, first - second
        apart *= 2
    return values


def sylvester(order_size):
    rows = lax.broadcasted_iota(jnp.int32, (order_size, order_size), 0)
    cols = lax.broadcasted_iota(jnp.int32, (order_size, order_size), 1)
    common = rows & cols
    parity = jnp.zeros_like(common)
    for bit_pos in range(order_size.bit_length() - 1):
        parity = parity ^ (common >> bit_pos)
    return (1 - 2 * (parity & 1)).astype(jnp.float32)


def split_dot(values, table, parts=3):
    pieces = []
    for _ in range(parts):
        pieces.append(values.astype(jnp.bfloat16))
        values = values - pieces[-1].astype(jnp.float32)
    return jnp.dot(
        jnp.concatenate(pieces, axis=1),
        jnp.concatenate([table] * parts, axis=0),
        preferred_element_type=jnp.float32,
    )


def butterfly_steps(count):
    steps = []
    apart = 1
    while apart < count:
        radix = min(8, count // apart)
        for start in range(count):
            if start // apart % radix == 0:
                steps.append((apart, [start + apart * index for index in range(radix)]))
        apart *= radix
    return steps


def fetch_blocks(x_hbm, signs_hbm, x_ref, signs_ref, arrived, *others):
    columns, blocks = x_ref.shape[0], x_ref.shape[1] // LANES
    fetches = [
        pltpu.make_async_copy(x_hbm, x_ref, arrived.at[0]),
        pltpu.make_async_copy(signs_hbm, signs_ref, arrived.at[1]),
    ]
    for fetch in (*fetches, *others):
        fetch.start()
    table = sylvester(LANES).astype(jnp.bfloat16)
    for fetch in fetches:
        fetch.wait()
    signs = signs_ref[...].astype(jnp.float32)
    signed = [
        x_ref[:, block * LANES : (block + 1) * LANES] * signs[block : block + 1]
        for block in range(blocks)
    ]
    mixed = split_dot(jnp.concatenate(signed, axis=0), table)
    return [mixed[block * columns : (block + 1) * columns] for block in range(blocks)]


def local_kernel(x_hbm, signs_hbm, out_ref, x_ref, signs_ref, arrived):
    mixed = fetch_blocks(x_hbm, signs_hbm, x_ref, signs_ref, arrived)
    for apart, places in butterfly_steps(out_ref.shape[0]):
        values = [mixed[p] if apart == 1 else out_ref[p] for p in places]
        for place, value in zip(places, butterfly(values)):
            out_ref[place] = value


def sliced_kernel(
    x_hbm, signs_hbm, samples_hbm, final_ref, out_ref, x_ref, signs_ref, samples_ref, arrived, noted
):
    note = pltpu.make_async_copy(samples_hbm, samples_ref, noted)
    mixed = fetch_blocks(x_hbm, signs_hbm, x_ref, signs_ref, arrived, note)
    blocks, columns, _ = out_ref.shape
    slices = blocks // 2
    rows = final_ref.shape[0] // slices
    note.wait()
    samples = samples_ref[...].astype(jnp.float32)
    per_row = slices // samples.shape[0]
    for turn in range(per_row):
        shift = LANES - turn * LANES // per_row
        turned = pltpu.roll(samples, shift, 1) if turn else samples
        for index in range(turn, slices, per_row):
            tail = (index + 1) * rows - 1
            final_ref[tail : tail + 1, :] = turned[index // per_row : index // per_row + 1]
    steps = butterfly_steps(blocks)
    last = steps[-1][0]
    for apart, places in steps:
        values = [mixed[p] if apart == 1 else out_ref[p] for p in places]
        for place, value in zip(places, butterfly(values)):
            if apart == last:
                start = place // 2 * rows + place % 2 * columns
                final_ref[start : start + columns, :] = value
            else:
                out_ref[place] = value


def in_vmem(count):
    return [pl.BlockSpec(memory_space=pltpu.VMEM)] * count


def in_hbm(*arrays):
    return [pltpu.with_memory_space_constraint(array, pltpu.HBM) for array in arrays]


def fetch_scratch(matrix_slab, blocks):
    return [
        pltpu.VMEM(matrix_slab.shape, jnp.float32),
        pltpu.VMEM((blocks, LANES), jnp.int32),
    ]


def local_transform(matrix_slab, row_signs):
    columns, row_count = matrix_slab.shape
    blocks = row_count // LANES
    return pl.pallas_call(
        local_kernel,
        out_shape=jax.ShapeDtypeStruct((blocks, columns, LANES), jnp.float32),
        in_specs=[pl.BlockSpec(memory_space=pltpu.HBM)] * 2,
        out_specs=in_vmem(1)[0],
        scratch_shapes=[
            *fetch_scratch(matrix_slab, blocks),
            pltpu.SemaphoreType.DMA((2,)),
        ],
        compiler_params=pltpu.CompilerParams(vmem_limit_bytes=VMEM_LIMIT),
    )(*in_hbm(matrix_slab, row_signs.reshape(blocks, LANES)))


def sliced_transform(matrix_slab, row_signs, sample_rows):
    columns, row_count = matrix_slab.shape
    blocks = row_count // LANES
    samples = sample_rows.reshape(-1, LANES)
    return pl.pallas_call(
        sliced_kernel,
        out_shape=jax.ShapeDtypeStruct((blocks // 2 * (2 * columns + 1), LANES), jnp.float32),
        in_specs=[pl.BlockSpec(memory_space=pltpu.HBM)] * 3,
        out_specs=in_vmem(1)[0],
        scratch_shapes=[
            pltpu.VMEM((blocks, columns, LANES), jnp.float32),
            *fetch_scratch(matrix_slab, blocks),
            pltpu.VMEM(samples.shape, jnp.int32),
            pltpu.SemaphoreType.DMA((2,)),
            pltpu.SemaphoreType.DMA(()),
        ],
        compiler_params=pltpu.CompilerParams(vmem_limit_bytes=VMEM_LIMIT),
    )(*in_hbm(matrix_slab, row_signs.reshape(blocks, LANES), samples))


def mix_kernel(run_length, scale, gram_scale, x_ref, out_ref):
    devices = out_ref.shape[0] // MESSAGE_ROWS
    rows = x_ref.shape[0] // devices
    runs = LANES // run_length
    samples = jnp.concatenate(
        [x_ref[(s + 1) * rows - 1 : (s + 1) * rows, :] for s in range(devices)], axis=0
    ).astype(jnp.bfloat16)
    run_of = lax.broadcasted_iota(jnp.int32, (LANES, 2 * LANES), 0)
    row_of = lax.broadcasted_iota(jnp.int32, (LANES, 2 * LANES), 1)
    spread = jnp.where(row_of // run_length == run_of, 1.0, 0.0).astype(jnp.bfloat16)
    offsets = jnp.dot(samples, spread, preferred_element_type=jnp.float32)
    own = lax.broadcasted_iota(jnp.int32, offsets.shape, 1) % run_length
    mask = jnp.where(offsets == own.astype(jnp.float32), scale, 0.0)
    picked = []
    for part in range(4):
        block = part // 2
        starts = [s * rows + part * SUBLANES for s in range(devices)]
        mixed = butterfly([x_ref[start : start + SUBLANES, :] for start in starts])
        picked.append(
            jnp.concatenate(
                [
                    mixed[d] * mask[d : d + 1, block * LANES : (block + 1) * LANES]
                    for d in range(devices)
                ],
                axis=0,
            )
        )
    quarter = 2 * runs
    row = lax.broadcasted_iota(jnp.int32, (LANES, LANES), 0)
    lane = lax.broadcasted_iota(jnp.int32, (LANES, LANES), 1)
    pattern = jnp.where(row // run_length == lane % runs, 1.0, 0.0)
    lane = lax.broadcasted_iota(jnp.int32, (1, LANES), 1)
    group = lane // quarter
    place = []
    for part in range(4):
        block, half = part // 2, part % 2
        here = lane // runs % 2 == block
        sides = [group % 2, jnp.where(group < 2, group, 3 - group)]
        masks = [jnp.where(here & (side == half), 1.0, 0.0) for side in sides]
        place.append(jnp.concatenate([(pattern * mask).astype(jnp.bfloat16) for mask in masks], axis=1))
    gathered = split_dot(jnp.concatenate(picked, axis=1), jnp.concatenate(place, axis=0), 2)
    straight, crossed = gathered[:, :LANES], gathered[:, LANES:]
    turns = SUBLANES // 2 + 1
    totals = []
    for turn in range(turns):
        total = None
        for d in range(devices):
            one = straight[d * SUBLANES : (d + 1) * SUBLANES]
            two = crossed[d * SUBLANES : (d + 1) * SUBLANES]
            if turn:
                two = pltpu.roll(two, SUBLANES - turn, 0)
            total = one * two if total is None else total + one * two
        totals.append(total)
    from_quarter = row // quarter
    together = [jnp.where(from_quarter == q, 1.0, 0.0).astype(jnp.bfloat16) for q in range(4)]
    sums = split_dot(jnp.concatenate(totals, axis=0), jnp.concatenate(together, axis=1), 2)
    sums = sums * gram_scale
    sub = lax.broadcasted_iota(jnp.int32, (SUBLANES, LANES), 0)
    lane = lax.broadcasted_iota(jnp.int32, (SUBLANES, LANES), 1)
    first, second = [jnp.zeros((SUBLANES, LANES), jnp.float32)] * 2
    for turn in range(SUBLANES):
        known = min(turn, SUBLANES - turn)
        here = sums[known * SUBLANES : (known + 1) * SUBLANES]
        quarters = [here[:, q * LANES : (q + 1) * LANES] for q in range(4)]
        if known != turn:
            quarters = [pltpu.roll(quarters[q], known, 0) for q in (0, 1, 3, 2)]
        mine = lane % SUBLANES == (sub + turn) % SUBLANES
        left = lane // SUBLANES % 2 == 0
        first = jnp.where(mine, jnp.where(left, quarters[0], quarters[2]), first)
        second = jnp.where(mine, jnp.where(left, quarters[3], quarters[1]), second)
    in_place = lane // (2 * SUBLANES) == (SUBLANES - sub) % SUBLANES
    gram = jnp.concatenate(
        [jnp.sum(jnp.where(in_place, part, 0.0), axis=0, keepdims=True) for part in (first, second)],
        axis=0,
    )
    half = SUBLANES // 2
    lane = lax.broadcasted_iota(jnp.int32, (half, LANES), 1)
    for d in range(devices):
        one = straight[d * SUBLANES : (d + 1) * SUBLANES]
        start = d * MESSAGE_ROWS
        out_ref[start : start + half, :] = jnp.where(lane < LANES // 2, one[:half], one[half:])
        out_ref[start + half : start + MESSAGE_ROWS, :] = gram


def mix_and_pick(received, devices, run_length, scale, gram_scale):
    return pl.pallas_call(
        functools.partial(mix_kernel, run_length, scale, gram_scale),
        out_shape=jax.ShapeDtypeStruct((devices * MESSAGE_ROWS, LANES), jnp.float32),
        in_specs=in_vmem(1),
        out_specs=in_vmem(1)[0],
        compiler_params=pltpu.CompilerParams(vmem_limit_bytes=VMEM_LIMIT),
    )(received)


def finish_kernel(x_ref, sketch_ref, gram_ref):
    sources = x_ref.shape[0] // MESSAGE_ROWS
    quarter = LANES // 4
    half_rows = SUBLANES // 2
    sub = lax.broadcasted_iota(jnp.int32, (SUBLANES, LANES), 0)
    lane = lax.broadcasted_iota(jnp.int32, (SUBLANES, LANES), 1)
    even = lane // quarter % 2 == 0
    stays = (sub < half_rows) == (lane < LANES // 2)
    gram = None
    for start in range(0, sources, 4):
        rows = []
        for index in range(4):
            place = (start + index) * MESSAGE_ROWS
            tail = x_ref[place + half_rows : place + MESSAGE_ROWS, :]
            gram = tail if gram is None else gram + tail
            rows.append(x_ref[place : place + half_rows, :])
        one = jnp.concatenate([rows[0], rows[2]], axis=0)
        two = jnp.concatenate([rows[1], rows[3]], axis=0)
        halves = [
            jnp.where(even, one, pltpu.roll(two, quarter, 1)),
            jnp.where(even, pltpu.roll(one, LANES - quarter, 1), two),
        ]
        for half, value in enumerate(halves):
            crossed = pltpu.roll(pltpu.roll(value, half_rows, 0), LANES // 2, 1)
            sketch_ref[
                half * SUBLANES : (half + 1) * SUBLANES, start * quarter : (start + 4) * quarter
            ] = jnp.where(stays, value, crossed)
    columns = gram_ref.shape[0]
    for half in range(2):
        lines = jnp.broadcast_to(gram[half : half + 1], (SUBLANES, LANES))
        turned = pltpu.roll(lines, 0, 1, stride=columns, stride_axis=0)
        gram_ref[half * SUBLANES : (half + 1) * SUBLANES, :] = turned[:, :columns]


def finish(received, columns, sample_count):
    return pl.pallas_call(
        finish_kernel,
        out_shape=(
            jax.ShapeDtypeStruct((columns, sample_count), jnp.float32),
            jax.ShapeDtypeStruct((columns, columns), jnp.float32),
        ),
        in_specs=[pl.BlockSpec(memory_space=pltpu.VMEM)],
        out_specs=(pl.BlockSpec(memory_space=pltpu.VMEM),) * 2,
        compiler_params=pltpu.CompilerParams(vmem_limit_bytes=VMEM_LIMIT),
    )(received)


def exchange(values, axes):
    return lax.all_to_all(values, axes, split_axis=0, concat_axis=0, tiled=True)


def general_shards(matrix_slab, row_signs, sample_rows):
    columns, row_count = matrix_slab.shape
    sample_count = sample_rows.shape[0]
    devices = lax.axis_size("wide") * lax.axis_size("narrow")
    run_length = row_count // sample_count
    slice_rows = row_count // devices
    slice_runs = slice_rows // run_length
    values = jnp.swapaxes(local_transform(matrix_slab, row_signs), 0, 1)
    values = values.reshape(columns, devices, slice_rows)
    received = exchange(jnp.swapaxes(values, 0, 1), AXES)
    offsets = exchange(sample_rows.reshape(devices, slice_runs), AXES)
    mixed = jnp.einsum("ds,scr->dcr", sylvester(devices), received, precision=lax.Precision.HIGHEST)
    mixed = mixed.reshape(devices, columns, slice_runs, run_length)
    chosen = offsets[:, None, :, None] == lax.iota(jnp.int32, run_length)
    picked = jnp.sum(jnp.where(chosen, mixed, 0.0), axis=3)
    picked = picked * jnp.float32(1.0 / math.sqrt(row_count * devices))
    gram = jnp.einsum("dck,dek->ce", picked, picked, precision=lax.Precision.HIGHEST)
    gram = gram / jnp.float32(sample_count * devices)
    grams = jnp.broadcast_to(gram[None], (devices, columns, columns))
    back = exchange(jnp.concatenate([picked, grams], axis=2), AXES)
    sketch = jnp.swapaxes(back[:, :, :slice_runs], 0, 1).reshape(columns, devices * slice_runs)
    return sketch, jnp.sum(back[:, :, slice_runs:], axis=0)


def sliced_shards(matrix_slab, row_signs, sample_rows):
    columns, row_count = matrix_slab.shape
    sample_count = sample_rows.shape[0]
    devices = lax.axis_size(ORDER)
    run_length = row_count // sample_count
    sent = sliced_transform(matrix_slab, row_signs, sample_rows)
    received = exchange(sent.reshape(devices, -1), ORDER).reshape(sent.shape)
    scale = 1.0 / math.sqrt(row_count * devices)
    gram_scale = 1.0 / (sample_count * devices)
    picked = mix_and_pick(received, devices, run_length, scale, gram_scale)
    returned = exchange(picked.reshape(devices, -1), ORDER).reshape(picked.shape)
    return finish(returned, columns, sample_count)


def solution(mesh):
    wide, narrow = mesh.shape["wide"], mesh.shape["narrow"]
    axes, function = AXES, general_shards
    if wide * narrow == 32 and wide % 4 == 0:
        axes, function = SPLIT_AXES, sliced_shards
        mesh = jax.sharding.Mesh(mesh.devices.reshape(4, wide // 4, narrow), axes)
    in_specs = (P(None, axes), P(axes), P(axes))
    out_specs = (P(None, axes), P())
    return jax.shard_map(function, mesh=mesh, in_specs=in_specs, out_specs=out_specs, check_vma=False)
```

```python
import functools
import math

import jax
import jax.numpy as jnp
from jax import lax
from jax.experimental import pallas as pl
from jax.experimental.pallas import tpu as pltpu
from jax.sharding import PartitionSpec as P

LANES = 128
SUBLANES = 8
AXES = ("wide", "narrow")
SPLIT_AXES = ("line", "plane", "narrow")
ORDER = ("plane", "narrow", "line")
VMEM_LIMIT = 32 * 1024 * 1024
MESSAGE_ROWS = 6


def butterfly(values):
    values = list(values)
    apart = 1
    while apart < len(values):
        for low in range(len(values)):
            if not low & apart:
                first, second = values[low], values[low | apart]
                values[low], values[low | apart] = first + second, first - second
        apart *= 2
    return values


def sylvester(order_size):
    rows = lax.broadcasted_iota(jnp.int32, (order_size, order_size), 0)
    cols = lax.broadcasted_iota(jnp.int32, (order_size, order_size), 1)
    common = rows & cols
    parity = jnp.zeros_like(common)
    for bit_pos in range(order_size.bit_length() - 1):
        parity = parity ^ (common >> bit_pos)
    return (1 - 2 * (parity & 1)).astype(jnp.float32)


def split_dot(values, table, parts=3):
    pieces = []
    for _ in range(parts):
        pieces.append(values.astype(jnp.bfloat16))
        values = values - pieces[-1].astype(jnp.float32)
    return jnp.dot(
        jnp.concatenate(pieces, axis=1),
        jnp.concatenate([table] * parts, axis=0),
        preferred_element_type=jnp.float32,
    )


def butterfly_steps(count):
    steps = []
    apart = 1
    while apart < count:
        radix = min(8, count // apart)
        for start in range(count):
            if start // apart % radix == 0:
                steps.append((apart, [start + apart * index for index in range(radix)]))
        apart *= radix
    return steps


def fetch_blocks(x_hbm, signs_hbm, x_ref, signs_ref, spread_ref, arrived, *others):
    columns, blocks = x_ref.shape[0], x_ref.shape[1] // LANES
    fetches = [
        pltpu.make_async_copy(x_hbm, x_ref, arrived.at[0]),
        pltpu.make_async_copy(signs_hbm, signs_ref, arrived.at[1]),
    ]
    for fetch in (*fetches, *others):
        fetch.start()
    table = sylvester(LANES).astype(jnp.bfloat16)
    fetches[1].wait()
    signs = signs_ref[...].astype(jnp.float32)
    for block in range(blocks):
        spread_ref[block] = jnp.broadcast_to(signs[block : block + 1], (SUBLANES, LANES))
    fetches[0].wait()
    signed = []
    for block in range(blocks):
        for start in range(0, columns, SUBLANES):
            place = (slice(start, start + SUBLANES), slice(block * LANES, (block + 1) * LANES))
            signed.append(x_ref[place] * spread_ref[block])
    mixed = split_dot(jnp.concatenate(signed, axis=0), table)
    return [mixed[block * columns : (block + 1) * columns] for block in range(blocks)]


def local_kernel(x_hbm, signs_hbm, out_ref, x_ref, signs_ref, spread_ref, arrived):
    mixed = fetch_blocks(x_hbm, signs_hbm, x_ref, signs_ref, spread_ref, arrived)
    for apart, places in butterfly_steps(out_ref.shape[0]):
        values = [mixed[p] if apart == 1 else out_ref[p] for p in places]
        for place, value in zip(places, butterfly(values)):
            out_ref[place] = value


def sliced_kernel(
    x_hbm, signs_hbm, samples_hbm, final_ref, out_ref, x_ref, signs_ref, spread_ref, samples_ref, arrived, noted
):
    note = pltpu.make_async_copy(samples_hbm, samples_ref, noted)
    mixed = fetch_blocks(x_hbm, signs_hbm, x_ref, signs_ref, spread_ref, arrived, note)
    blocks, columns, _ = out_ref.shape
    slices = blocks // 2
    rows = final_ref.shape[0] // slices
    note.wait()
    samples = samples_ref[...].astype(jnp.float32)
    per_row = slices // samples.shape[0]
    for turn in range(per_row):
        shift = LANES - turn * LANES // per_row
        turned = pltpu.roll(samples, shift, 1) if turn else samples
        for index in range(turn, slices, per_row):
            tail = (index + 1) * rows - 1
            final_ref[tail : tail + 1, :] = turned[index // per_row : index // per_row + 1]
    steps = butterfly_steps(blocks)
    last = steps[-1][0]
    for apart, places in steps:
        values = [mixed[p] if apart == 1 else out_ref[p] for p in places]
        for place, value in zip(places, butterfly(values)):
            if apart == last:
                start = place // 2 * rows + place % 2 * columns
                final_ref[start : start + columns, :] = value
            else:
                out_ref[place] = value


def in_vmem(count):
    return [pl.BlockSpec(memory_space=pltpu.VMEM)] * count


def in_hbm(*arrays):
    return [pltpu.with_memory_space_constraint(array, pltpu.HBM) for array in arrays]


def fetch_scratch(matrix_slab, blocks):
    return [
        pltpu.VMEM(matrix_slab.shape, jnp.float32),
        pltpu.VMEM((blocks, LANES), jnp.int32),
        pltpu.VMEM((blocks, SUBLANES, LANES), jnp.float32),
    ]


def local_transform(matrix_slab, row_signs):
    columns, row_count = matrix_slab.shape
    blocks = row_count // LANES
    return pl.pallas_call(
        local_kernel,
        out_shape=jax.ShapeDtypeStruct((blocks, columns, LANES), jnp.float32),
        in_specs=[pl.BlockSpec(memory_space=pltpu.HBM)] * 2,
        out_specs=in_vmem(1)[0],
        scratch_shapes=[
            *fetch_scratch(matrix_slab, blocks),
            pltpu.SemaphoreType.DMA((2,)),
        ],
        compiler_params=pltpu.CompilerParams(vmem_limit_bytes=VMEM_LIMIT),
    )(*in_hbm(matrix_slab, row_signs.reshape(blocks, LANES)))


def sliced_transform(matrix_slab, row_signs, sample_rows):
    columns, row_count = matrix_slab.shape
    blocks = row_count // LANES
    samples = sample_rows.reshape(-1, LANES)
    return pl.pallas_call(
        sliced_kernel,
        out_shape=jax.ShapeDtypeStruct((blocks // 2 * (2 * columns + 1), LANES), jnp.float32),
        in_specs=[pl.BlockSpec(memory_space=pltpu.HBM)] * 3,
        out_specs=in_vmem(1)[0],
        scratch_shapes=[
            pltpu.VMEM((blocks, columns, LANES), jnp.float32),
            *fetch_scratch(matrix_slab, blocks),
            pltpu.VMEM(samples.shape, jnp.int32),
            pltpu.SemaphoreType.DMA((2,)),
            pltpu.SemaphoreType.DMA(()),
        ],
        compiler_params=pltpu.CompilerParams(vmem_limit_bytes=VMEM_LIMIT),
    )(*in_hbm(matrix_slab, row_signs.reshape(blocks, LANES), samples))


def mix_kernel(run_length, scale, gram_scale, x_ref, out_ref):
    devices = out_ref.shape[0] // MESSAGE_ROWS
    rows = x_ref.shape[0] // devices
    runs = LANES // run_length
    samples = jnp.concatenate(
        [x_ref[(s + 1) * rows - 1 : (s + 1) * rows, :] for s in range(devices)], axis=0
    ).astype(jnp.bfloat16)
    run_of = lax.broadcasted_iota(jnp.int32, (LANES, 2 * LANES), 0)
    row_of = lax.broadcasted_iota(jnp.int32, (LANES, 2 * LANES), 1)
    spread = jnp.where(row_of // run_length == run_of, 1.0, 0.0).astype(jnp.bfloat16)
    offsets = jnp.dot(samples, spread, preferred_element_type=jnp.float32)
    own = lax.broadcasted_iota(jnp.int32, offsets.shape, 1) % run_length
    mask = jnp.where(offsets == own.astype(jnp.float32), scale, 0.0)
    picked = []
    for part in range(4):
        block = part // 2
        starts = [s * rows + part * SUBLANES for s in range(devices)]
        mixed = butterfly([x_ref[start : start + SUBLANES, :] for start in starts])
        picked.append(
            jnp.concatenate(
                [
                    mixed[d] * mask[d : d + 1, block * LANES : (block + 1) * LANES]
                    for d in range(devices)
                ],
                axis=0,
            )
        )
    quarter = 2 * runs
    row = lax.broadcasted_iota(jnp.int32, (LANES, LANES), 0)
    lane = lax.broadcasted_iota(jnp.int32, (LANES, LANES), 1)
    pattern = jnp.where(row // run_length == lane % runs, 1.0, 0.0)
    lane = lax.broadcasted_iota(jnp.int32, (1, LANES), 1)
    group = lane // quarter
    place = []
    for part in range(4):
        block, half = part // 2, part % 2
        here = lane // runs % 2 == block
        sides = [group % 2, jnp.where(group < 2, group, 3 - group)]
        masks = [jnp.where(here & (side == half), 1.0, 0.0) for side in sides]
        place.append(jnp.concatenate([(pattern * mask).astype(jnp.bfloat16) for mask in masks], axis=1))
    gathered = split_dot(jnp.concatenate(picked, axis=1), jnp.concatenate(place, axis=0), 2)
    straight, crossed = gathered[:, :LANES], gathered[:, LANES:]
    turns = SUBLANES // 2 + 1
    totals = []
    for turn in range(turns):
        total = None
        for d in range(devices):
            one = straight[d * SUBLANES : (d + 1) * SUBLANES]
            two = crossed[d * SUBLANES : (d + 1) * SUBLANES]
            if turn:
                two = pltpu.roll(two, SUBLANES - turn, 0)
            total = one * two if total is None else total + one * two
        totals.append(total)
    from_quarter = row // quarter
    together = [jnp.where(from_quarter == q, 1.0, 0.0).astype(jnp.bfloat16) for q in range(4)]
    sums = split_dot(jnp.concatenate(totals, axis=0), jnp.concatenate(together, axis=1), 2)
    sums = sums * gram_scale
    sub = lax.broadcasted_iota(jnp.int32, (SUBLANES, LANES), 0)
    lane = lax.broadcasted_iota(jnp.int32, (SUBLANES, LANES), 1)
    first, second = [jnp.zeros((SUBLANES, LANES), jnp.float32)] * 2
    for turn in range(SUBLANES):
        known = min(turn, SUBLANES - turn)
        here = sums[known * SUBLANES : (known + 1) * SUBLANES]
        quarters = [here[:, q * LANES : (q + 1) * LANES] for q in range(4)]
        if known != turn:
            quarters = [pltpu.roll(quarters[q], known, 0) for q in (0, 1, 3, 2)]
        mine = lane % SUBLANES == (sub + turn) % SUBLANES
        left = lane // SUBLANES % 2 == 0
        first = jnp.where(mine, jnp.where(left, quarters[0], quarters[2]), first)
        second = jnp.where(mine, jnp.where(left, quarters[3], quarters[1]), second)
    in_place = lane // (2 * SUBLANES) == (SUBLANES - sub) % SUBLANES
    gram = jnp.concatenate(
        [jnp.sum(jnp.where(in_place, part, 0.0), axis=0, keepdims=True) for part in (first, second)],
        axis=0,
    )
    half = SUBLANES // 2
    lane = lax.broadcasted_iota(jnp.int32, (half, LANES), 1)
    for d in range(devices):
        one = straight[d * SUBLANES : (d + 1) * SUBLANES]
        start = d * MESSAGE_ROWS
        out_ref[start : start + half, :] = jnp.where(lane < LANES // 2, one[:half], one[half:])
        out_ref[start + half : start + MESSAGE_ROWS, :] = gram


def mix_and_pick(received, devices, run_length, scale, gram_scale):
    return pl.pallas_call(
        functools.partial(mix_kernel, run_length, scale, gram_scale),
        out_shape=jax.ShapeDtypeStruct((devices * MESSAGE_ROWS, LANES), jnp.float32),
        in_specs=in_vmem(1),
        out_specs=in_vmem(1)[0],
        compiler_params=pltpu.CompilerParams(vmem_limit_bytes=VMEM_LIMIT),
    )(received)


def finish_kernel(x_ref, sketch_ref, gram_ref):
    sources = x_ref.shape[0] // MESSAGE_ROWS
    quarter = LANES // 4
    half_rows = SUBLANES // 2
    sub = lax.broadcasted_iota(jnp.int32, (SUBLANES, LANES), 0)
    lane = lax.broadcasted_iota(jnp.int32, (SUBLANES, LANES), 1)
    even = lane // quarter % 2 == 0
    stays = (sub < half_rows) == (lane < LANES // 2)
    gram = None
    for start in range(0, sources, 4):
        rows = []
        for index in range(4):
            place = (start + index) * MESSAGE_ROWS
            tail = x_ref[place + half_rows : place + MESSAGE_ROWS, :]
            gram = tail if gram is None else gram + tail
            rows.append(x_ref[place : place + half_rows, :])
        one = jnp.concatenate([rows[0], rows[2]], axis=0)
        two = jnp.concatenate([rows[1], rows[3]], axis=0)
        halves = [
            jnp.where(even, one, pltpu.roll(two, quarter, 1)),
            jnp.where(even, pltpu.roll(one, LANES - quarter, 1), two),
        ]
        for half, value in enumerate(halves):
            crossed = pltpu.roll(pltpu.roll(value, half_rows, 0), LANES // 2, 1)
            sketch_ref[
                half * SUBLANES : (half + 1) * SUBLANES, start * quarter : (start + 4) * quarter
            ] = jnp.where(stays, value, crossed)
    columns = gram_ref.shape[0]
    for half in range(2):
        lines = jnp.broadcast_to(gram[half : half + 1], (SUBLANES, LANES))
        turned = pltpu.roll(lines, 0, 1, stride=columns, stride_axis=0)
        gram_ref[half * SUBLANES : (half + 1) * SUBLANES, :] = turned[:, :columns]


def finish(received, columns, sample_count):
    return pl.pallas_call(
        finish_kernel,
        out_shape=(
            jax.ShapeDtypeStruct((columns, sample_count), jnp.float32),
            jax.ShapeDtypeStruct((columns, columns), jnp.float32),
        ),
        in_specs=[pl.BlockSpec(memory_space=pltpu.VMEM)],
        out_specs=(pl.BlockSpec(memory_space=pltpu.VMEM),) * 2,
        compiler_params=pltpu.CompilerParams(vmem_limit_bytes=VMEM_LIMIT),
    )(received)


def exchange(values, axes):
    return lax.all_to_all(values, axes, split_axis=0, concat_axis=0, tiled=True)


def general_shards(matrix_slab, row_signs, sample_rows):
    columns, row_count = matrix_slab.shape
    sample_count = sample_rows.shape[0]
    devices = lax.axis_size("wide") * lax.axis_size("narrow")
    run_length = row_count // sample_count
    slice_rows = row_count // devices
    slice_runs = slice_rows // run_length
    values = jnp.swapaxes(local_transform(matrix_slab, row_signs), 0, 1)
    values = values.reshape(columns, devices, slice_rows)
    received = exchange(jnp.swapaxes(values, 0, 1), AXES)
    offsets = exchange(sample_rows.reshape(devices, slice_runs), AXES)
    mixed = jnp.einsum("ds,scr->dcr", sylvester(devices), received, precision=lax.Precision.HIGHEST)
    mixed = mixed.reshape(devices, columns, slice_runs, run_length)
    chosen = offsets[:, None, :, None] == lax.iota(jnp.int32, run_length)
    picked = jnp.sum(jnp.where(chosen, mixed, 0.0), axis=3)
    picked = picked * jnp.float32(1.0 / math.sqrt(row_count * devices))
    gram = jnp.einsum("dck,dek->ce", picked, picked, precision=lax.Precision.HIGHEST)
    gram = gram / jnp.float32(sample_count * devices)
    grams = jnp.broadcast_to(gram[None], (devices, columns, columns))
    back = exchange(jnp.concatenate([picked, grams], axis=2), AXES)
    sketch = jnp.swapaxes(back[:, :, :slice_runs], 0, 1).reshape(columns, devices * slice_runs)
    return sketch, jnp.sum(back[:, :, slice_runs:], axis=0)


def sliced_shards(matrix_slab, row_signs, sample_rows):
    columns, row_count = matrix_slab.shape
    sample_count = sample_rows.shape[0]
    devices = lax.axis_size(ORDER)
    run_length = row_count // sample_count
    sent = sliced_transform(matrix_slab, row_signs, sample_rows)
    received = exchange(sent.reshape(devices, -1), ORDER).reshape(sent.shape)
    scale = 1.0 / math.sqrt(row_count * devices)
    gram_scale = 1.0 / (sample_count * devices)
    picked = mix_and_pick(received, devices, run_length, scale, gram_scale)
    returned = exchange(picked.reshape(devices, -1), ORDER).reshape(picked.shape)
    return finish(returned, columns, sample_count)


def solution(mesh):
    wide, narrow = mesh.shape["wide"], mesh.shape["narrow"]
    axes, function = AXES, general_shards
    if wide * narrow == 32 and wide % 4 == 0:
        axes, function = SPLIT_AXES, sliced_shards
        mesh = jax.sharding.Mesh(mesh.devices.reshape(4, wide // 4, narrow), axes)
    in_specs = (P(None, axes), P(axes), P(axes))
    out_specs = (P(None, axes), P())
    return jax.shard_map(function, mesh=mesh, in_specs=in_specs, out_specs=out_specs, check_vma=False)
```

```python
import functools
import math

import jax
import jax.numpy as jnp
from jax import lax
from jax.experimental import pallas as pl
from jax.experimental.pallas import tpu as pltpu
from jax.sharding import PartitionSpec as P

LANES = 128
SUBLANES = 8
AXES = ("wide", "narrow")
SPLIT_AXES = ("line", "plane", "narrow")
ORDER = ("plane", "line", "narrow")
VMEM_LIMIT = 32 * 1024 * 1024
MESSAGE_ROWS = 6


def butterfly(values):
    values = list(values)
    apart = 1
    while apart < len(values):
        for low in range(len(values)):
            if not low & apart:
                first, second = values[low], values[low | apart]
                values[low], values[low | apart] = first + second, first - second
        apart *= 2
    return values


def sylvester(order_size):
    rows = lax.broadcasted_iota(jnp.int32, (order_size, order_size), 0)
    cols = lax.broadcasted_iota(jnp.int32, (order_size, order_size), 1)
    common = rows & cols
    parity = jnp.zeros_like(common)
    for bit_pos in range(order_size.bit_length() - 1):
        parity = parity ^ (common >> bit_pos)
    return (1 - 2 * (parity & 1)).astype(jnp.float32)


def split_dot(values, table, parts=3):
    pieces = []
    for _ in range(parts):
        pieces.append(values.astype(jnp.bfloat16))
        values = values - pieces[-1].astype(jnp.float32)
    return jnp.dot(
        jnp.concatenate(pieces, axis=1),
        jnp.concatenate([table] * parts, axis=0),
        preferred_element_type=jnp.float32,
    )


def butterfly_steps(count):
    steps = []
    apart = 1
    while apart < count:
        radix = min(8, count // apart)
        for start in range(count):
            if start // apart % radix == 0:
                steps.append((apart, [start + apart * index for index in range(radix)]))
        apart *= radix
    return steps


def fetch_blocks(x_hbm, signs_hbm, x_ref, signs_ref, arrived, *others):
    columns, blocks = x_ref.shape[0], x_ref.shape[1] // LANES
    fetches = [
        pltpu.make_async_copy(x_hbm, x_ref, arrived.at[0]),
        pltpu.make_async_copy(signs_hbm, signs_ref, arrived.at[1]),
    ]
    for fetch in (*fetches, *others):
        fetch.start()
    table = sylvester(LANES).astype(jnp.bfloat16)
    for fetch in fetches:
        fetch.wait()
    signs = signs_ref[...].astype(jnp.float32)
    signed = [
        x_ref[:, block * LANES : (block + 1) * LANES] * signs[block : block + 1]
        for block in range(blocks)
    ]
    mixed = split_dot(jnp.concatenate(signed, axis=0), table)
    return [mixed[block * columns : (block + 1) * columns] for block in range(blocks)]


def local_kernel(x_hbm, signs_hbm, out_ref, x_ref, signs_ref, arrived):
    mixed = fetch_blocks(x_hbm, signs_hbm, x_ref, signs_ref, arrived)
    for apart, places in butterfly_steps(out_ref.shape[0]):
        values = [mixed[p] if apart == 1 else out_ref[p] for p in places]
        for place, value in zip(places, butterfly(values)):
            out_ref[place] = value


def sliced_kernel(
    x_hbm, signs_hbm, samples_hbm, final_ref, out_ref, x_ref, signs_ref, samples_ref, arrived, noted
):
    note = pltpu.make_async_copy(samples_hbm, samples_ref, noted)
    mixed = fetch_blocks(x_hbm, signs_hbm, x_ref, signs_ref, arrived, note)
    blocks, columns, _ = out_ref.shape
    slices = blocks // 2
    rows = final_ref.shape[0] // slices
    note.wait()
    samples = samples_ref[...].astype(jnp.float32)
    per_row = slices // samples.shape[0]
    for turn in range(per_row):
        shift = LANES - turn * LANES // per_row
        turned = pltpu.roll(samples, shift, 1) if turn else samples
        for index in range(turn, slices, per_row):
            tail = (index + 1) * rows - 1
            final_ref[tail : tail + 1, :] = turned[index // per_row : index // per_row + 1]
    steps = butterfly_steps(blocks)
    last = steps[-1][0]
    for apart, places in steps:
        values = [mixed[p] if apart == 1 else out_ref[p] for p in places]
        for place, value in zip(places, butterfly(values)):
            if apart == last:
                start = place // 2 * rows + place % 2 * columns
                final_ref[start : start + columns, :] = value
            else:
                out_ref[place] = value


def in_vmem(count):
    return [pl.BlockSpec(memory_space=pltpu.VMEM)] * count


def in_hbm(*arrays):
    return [pltpu.with_memory_space_constraint(array, pltpu.HBM) for array in arrays]


def fetch_scratch(matrix_slab, blocks):
    return [
        pltpu.VMEM(matrix_slab.shape, jnp.float32),
        pltpu.VMEM((blocks, LANES), jnp.int32),
    ]


def local_transform(matrix_slab, row_signs):
    columns, row_count = matrix_slab.shape
    blocks = row_count // LANES
    return pl.pallas_call(
        local_kernel,
        out_shape=jax.ShapeDtypeStruct((blocks, columns, LANES), jnp.float32),
        in_specs=[pl.BlockSpec(memory_space=pltpu.HBM)] * 2,
        out_specs=in_vmem(1)[0],
        scratch_shapes=[
            *fetch_scratch(matrix_slab, blocks),
            pltpu.SemaphoreType.DMA((2,)),
        ],
        compiler_params=pltpu.CompilerParams(vmem_limit_bytes=VMEM_LIMIT),
    )(*in_hbm(matrix_slab, row_signs.reshape(blocks, LANES)))


def sliced_transform(matrix_slab, row_signs, sample_rows):
    columns, row_count = matrix_slab.shape
    blocks = row_count // LANES
    samples = sample_rows.reshape(-1, LANES)
    return pl.pallas_call(
        sliced_kernel,
        out_shape=jax.ShapeDtypeStruct((blocks // 2 * (2 * columns + 1), LANES), jnp.float32),
        in_specs=[pl.BlockSpec(memory_space=pltpu.HBM)] * 3,
        out_specs=in_vmem(1)[0],
        scratch_shapes=[
            pltpu.VMEM((blocks, columns, LANES), jnp.float32),
            *fetch_scratch(matrix_slab, blocks),
            pltpu.VMEM(samples.shape, jnp.int32),
            pltpu.SemaphoreType.DMA((2,)),
            pltpu.SemaphoreType.DMA(()),
        ],
        compiler_params=pltpu.CompilerParams(vmem_limit_bytes=VMEM_LIMIT),
    )(*in_hbm(matrix_slab, row_signs.reshape(blocks, LANES), samples))


def mix_kernel(run_length, scale, gram_scale, x_ref, out_ref):
    devices = out_ref.shape[0] // MESSAGE_ROWS
    rows = x_ref.shape[0] // devices
    runs = LANES // run_length
    samples = jnp.concatenate(
        [x_ref[(s + 1) * rows - 1 : (s + 1) * rows, :] for s in range(devices)], axis=0
    ).astype(jnp.bfloat16)
    run_of = lax.broadcasted_iota(jnp.int32, (LANES, 2 * LANES), 0)
    row_of = lax.broadcasted_iota(jnp.int32, (LANES, 2 * LANES), 1)
    spread = jnp.where(row_of // run_length == run_of, 1.0, 0.0).astype(jnp.bfloat16)
    offsets = jnp.dot(samples, spread, preferred_element_type=jnp.float32)
    own = lax.broadcasted_iota(jnp.int32, offsets.shape, 1) % run_length
    mask = jnp.where(offsets == own.astype(jnp.float32), scale, 0.0)
    picked = []
    for part in range(4):
        block = part // 2
        starts = [s * rows + part * SUBLANES for s in range(devices)]
        mixed = butterfly([x_ref[start : start + SUBLANES, :] for start in starts])
        picked.append(
            jnp.concatenate(
                [
                    mixed[d] * mask[d : d + 1, block * LANES : (block + 1) * LANES]
                    for d in range(devices)
                ],
                axis=0,
            )
        )
    quarter = 2 * runs
    row = lax.broadcasted_iota(jnp.int32, (LANES, LANES), 0)
    lane = lax.broadcasted_iota(jnp.int32, (LANES, LANES), 1)
    pattern = jnp.where(row // run_length == lane % runs, 1.0, 0.0)
    lane = lax.broadcasted_iota(jnp.int32, (1, LANES), 1)
    group = lane // quarter
    place = []
    for part in range(4):
        block, half = part // 2, part % 2
        here = lane // runs % 2 == block
        sides = [group % 2, jnp.where(group < 2, group, 3 - group)]
        masks = [jnp.where(here & (side == half), 1.0, 0.0) for side in sides]
        place.append(jnp.concatenate([(pattern * mask).astype(jnp.bfloat16) for mask in masks], axis=1))
    gathered = split_dot(jnp.concatenate(picked, axis=1), jnp.concatenate(place, axis=0), 2)
    straight, crossed = gathered[:, :LANES], gathered[:, LANES:]
    turns = SUBLANES // 2 + 1
    totals = []
    for turn in range(turns):
        total = None
        for d in range(devices):
            one = straight[d * SUBLANES : (d + 1) * SUBLANES]
            two = crossed[d * SUBLANES : (d + 1) * SUBLANES]
            if turn:
                two = pltpu.roll(two, SUBLANES - turn, 0)
            total = one * two if total is None else total + one * two
        totals.append(total)
    from_quarter = row // quarter
    together = [jnp.where(from_quarter == q, 1.0, 0.0).astype(jnp.bfloat16) for q in range(4)]
    sums = split_dot(jnp.concatenate(totals, axis=0), jnp.concatenate(together, axis=1), 2)
    sums = sums * gram_scale
    sub = lax.broadcasted_iota(jnp.int32, (SUBLANES, LANES), 0)
    lane = lax.broadcasted_iota(jnp.int32, (SUBLANES, LANES), 1)
    first, second = [jnp.zeros((SUBLANES, LANES), jnp.float32)] * 2
    for turn in range(SUBLANES):
        known = min(turn, SUBLANES - turn)
        here = sums[known * SUBLANES : (known + 1) * SUBLANES]
        quarters = [here[:, q * LANES : (q + 1) * LANES] for q in range(4)]
        if known != turn:
            quarters = [pltpu.roll(quarters[q], known, 0) for q in (0, 1, 3, 2)]
        mine = lane % SUBLANES == (sub + turn) % SUBLANES
        left = lane // SUBLANES % 2 == 0
        first = jnp.where(mine, jnp.where(left, quarters[0], quarters[2]), first)
        second = jnp.where(mine, jnp.where(left, quarters[3], quarters[1]), second)
    in_place = lane // (2 * SUBLANES) == (SUBLANES - sub) % SUBLANES
    gram = jnp.concatenate(
        [jnp.sum(jnp.where(in_place, part, 0.0), axis=0, keepdims=True) for part in (first, second)],
        axis=0,
    )
    half = SUBLANES // 2
    lane = lax.broadcasted_iota(jnp.int32, (half, LANES), 1)
    for d in range(devices):
        one = straight[d * SUBLANES : (d + 1) * SUBLANES]
        start = d * MESSAGE_ROWS
        out_ref[start : start + half, :] = jnp.where(lane < LANES // 2, one[:half], one[half:])
        out_ref[start + half : start + MESSAGE_ROWS, :] = gram


def mix_and_pick(received, devices, run_length, scale, gram_scale):
    return pl.pallas_call(
        functools.partial(mix_kernel, run_length, scale, gram_scale),
        out_shape=jax.ShapeDtypeStruct((devices * MESSAGE_ROWS, LANES), jnp.float32),
        in_specs=in_vmem(1),
        out_specs=in_vmem(1)[0],
        compiler_params=pltpu.CompilerParams(vmem_limit_bytes=VMEM_LIMIT),
    )(received)


def finish_kernel(x_ref, sketch_ref, gram_ref):
    sources = x_ref.shape[0] // MESSAGE_ROWS
    quarter = LANES // 4
    half_rows = SUBLANES // 2
    sub = lax.broadcasted_iota(jnp.int32, (SUBLANES, LANES), 0)
    lane = lax.broadcasted_iota(jnp.int32, (SUBLANES, LANES), 1)
    even = lane // quarter % 2 == 0
    stays = (sub < half_rows) == (lane < LANES // 2)
    gram = None
    for start in range(0, sources, 4):
        rows = []
        for index in range(4):
            place = (start + index) * MESSAGE_ROWS
            tail = x_ref[place + half_rows : place + MESSAGE_ROWS, :]
            gram = tail if gram is None else gram + tail
            rows.append(x_ref[place : place + half_rows, :])
        one = jnp.concatenate([rows[0], rows[2]], axis=0)
        two = jnp.concatenate([rows[1], rows[3]], axis=0)
        halves = [
            jnp.where(even, one, pltpu.roll(two, quarter, 1)),
            jnp.where(even, pltpu.roll(one, LANES - quarter, 1), two),
        ]
        for half, value in enumerate(halves):
            crossed = pltpu.roll(pltpu.roll(value, half_rows, 0), LANES // 2, 1)
            sketch_ref[
                half * SUBLANES : (half + 1) * SUBLANES, start * quarter : (start + 4) * quarter
            ] = jnp.where(stays, value, crossed)
    columns = gram_ref.shape[0]
    for half in range(2):
        lines = jnp.broadcast_to(gram[half : half + 1], (SUBLANES, LANES))
        turned = pltpu.roll(lines, 0, 1, stride=columns, stride_axis=0)
        gram_ref[half * SUBLANES : (half + 1) * SUBLANES, :] = turned[:, :columns]


def finish(received, columns, sample_count):
    return pl.pallas_call(
        finish_kernel,
        out_shape=(
            jax.ShapeDtypeStruct((columns, sample_count), jnp.float32),
            jax.ShapeDtypeStruct((columns, columns), jnp.float32),
        ),
        in_specs=[pl.BlockSpec(memory_space=pltpu.VMEM)],
        out_specs=(pl.BlockSpec(memory_space=pltpu.VMEM),) * 2,
        compiler_params=pltpu.CompilerParams(vmem_limit_bytes=VMEM_LIMIT),
    )(received)


def exchange(values, axes):
    return lax.all_to_all(values, axes, split_axis=0, concat_axis=0, tiled=True)


def general_shards(matrix_slab, row_signs, sample_rows):
    columns, row_count = matrix_slab.shape
    sample_count = sample_rows.shape[0]
    devices = lax.axis_size("wide") * lax.axis_size("narrow")
    run_length = row_count // sample_count
    slice_rows = row_count // devices
    slice_runs = slice_rows // run_length
    values = jnp.swapaxes(local_transform(matrix_slab, row_signs), 0, 1)
    values = values.reshape(columns, devices, slice_rows)
    received = exchange(jnp.swapaxes(values, 0, 1), AXES)
    offsets = exchange(sample_rows.reshape(devices, slice_runs), AXES)
    mixed = jnp.einsum("ds,scr->dcr", sylvester(devices), received, precision=lax.Precision.HIGHEST)
    mixed = mixed.reshape(devices, columns, slice_runs, run_length)
    chosen = offsets[:, None, :, None] == lax.iota(jnp.int32, run_length)
    picked = jnp.sum(jnp.where(chosen, mixed, 0.0), axis=3)
    picked = picked * jnp.float32(1.0 / math.sqrt(row_count * devices))
    gram = jnp.einsum("dck,dek->ce", picked, picked, precision=lax.Precision.HIGHEST)
    gram = gram / jnp.float32(sample_count * devices)
    grams = jnp.broadcast_to(gram[None], (devices, columns, columns))
    back = exchange(jnp.concatenate([picked, grams], axis=2), AXES)
    sketch = jnp.swapaxes(back[:, :, :slice_runs], 0, 1).reshape(columns, devices * slice_runs)
    return sketch, jnp.sum(back[:, :, slice_runs:], axis=0)


def sliced_shards(matrix_slab, row_signs, sample_rows):
    columns, row_count = matrix_slab.shape
    sample_count = sample_rows.shape[0]
    devices = lax.axis_size(ORDER)
    run_length = row_count // sample_count
    sent = sliced_transform(matrix_slab, row_signs, sample_rows)
    received = exchange(sent.reshape(devices, -1), ORDER).reshape(sent.shape)
    scale = 1.0 / math.sqrt(row_count * devices)
    gram_scale = 1.0 / (sample_count * devices)
    picked = mix_and_pick(received, devices, run_length, scale, gram_scale)
    returned = exchange(picked.reshape(devices, -1), ORDER).reshape(picked.shape)
    return finish(returned, columns, sample_count)


def solution(mesh):
    wide, narrow = mesh.shape["wide"], mesh.shape["narrow"]
    axes, function = AXES, general_shards
    if wide * narrow == 32 and wide % 4 == 0:
        axes, function = SPLIT_AXES, sliced_shards
        mesh = jax.sharding.Mesh(mesh.devices.reshape(4, wide // 4, narrow), axes)
    in_specs = (P(None, axes), P(axes), P(axes))
    out_specs = (P(None, axes), P())
    return jax.shard_map(function, mesh=mesh, in_specs=in_specs, out_specs=out_specs, check_vma=False)
```

```python
import functools
import math

import jax
import jax.numpy as jnp
from jax import lax
from jax.experimental import pallas as pl
from jax.experimental.pallas import tpu as pltpu
from jax.sharding import PartitionSpec as P

LANES = 128
SUBLANES = 8
AXES = ("wide", "narrow")
SPLIT_AXES = ("line", "plane", "narrow")
ORDER = ("plane", "narrow", "line")
VMEM_LIMIT = 32 * 1024 * 1024
MESSAGE_ROWS = 6


def butterfly(values):
    values = list(values)
    apart = 1
    while apart < len(values):
        for low in range(len(values)):
            if not low & apart:
                first, second = values[low], values[low | apart]
                values[low], values[low | apart] = first + second, first - second
        apart *= 2
    return values


def sylvester(order_size):
    rows = lax.broadcasted_iota(jnp.int32, (order_size, order_size), 0)
    cols = lax.broadcasted_iota(jnp.int32, (order_size, order_size), 1)
    common = rows & cols
    parity = jnp.zeros_like(common)
    for bit_pos in range(order_size.bit_length() - 1):
        parity = parity ^ (common >> bit_pos)
    return (1 - 2 * (parity & 1)).astype(jnp.float32)


def split_dot(values, table, parts=3):
    pieces = []
    for _ in range(parts):
        pieces.append(values.astype(jnp.bfloat16))
        values = values - pieces[-1].astype(jnp.float32)
    return jnp.dot(
        jnp.concatenate(pieces, axis=1),
        jnp.concatenate([table] * parts, axis=0),
        preferred_element_type=jnp.float32,
    )


def butterfly_steps(count):
    steps = []
    apart = 1
    while apart < count:
        radix = min(8, count // apart)
        for start in range(count):
            if start // apart % radix == 0:
                steps.append((apart, [start + apart * index for index in range(radix)]))
        apart *= radix
    return steps


def fetch_blocks(x_hbm, signs_hbm, x_ref, signs_ref, spread_ref, arrived, *others, meanwhile=None):
    columns, blocks = x_ref.shape[0], x_ref.shape[1] // LANES
    fetches = [
        pltpu.make_async_copy(x_hbm, x_ref, arrived.at[0]),
        pltpu.make_async_copy(signs_hbm, signs_ref, arrived.at[1]),
    ]
    for fetch in (*fetches, *others):
        fetch.start()
    table = sylvester(LANES).astype(jnp.bfloat16)
    fetches[1].wait()
    signs = signs_ref[...].astype(jnp.float32)
    for block in range(blocks):
        spread_ref[block] = jnp.broadcast_to(signs[block : block + 1], (SUBLANES, LANES))
    if meanwhile:
        meanwhile()
    fetches[0].wait()
    signed = []
    for block in range(blocks):
        for start in range(0, columns, SUBLANES):
            place = (slice(start, start + SUBLANES), slice(block * LANES, (block + 1) * LANES))
            signed.append(x_ref[place] * spread_ref[block])
    mixed = split_dot(jnp.concatenate(signed, axis=0), table)
    return [mixed[block * columns : (block + 1) * columns] for block in range(blocks)]


def local_kernel(x_hbm, signs_hbm, out_ref, x_ref, signs_ref, spread_ref, arrived):
    mixed = fetch_blocks(x_hbm, signs_hbm, x_ref, signs_ref, spread_ref, arrived)
    for apart, places in butterfly_steps(out_ref.shape[0]):
        values = [mixed[p] if apart == 1 else out_ref[p] for p in places]
        for place, value in zip(places, butterfly(values)):
            out_ref[place] = value


def sliced_kernel(
    x_hbm, signs_hbm, samples_hbm, final_ref, out_ref, x_ref, signs_ref, spread_ref, samples_ref, arrived, noted
):
    note = pltpu.make_async_copy(samples_hbm, samples_ref, noted)
    blocks, columns, _ = out_ref.shape
    slices = blocks // 2
    rows = final_ref.shape[0] // slices

    def place_offsets():
        note.wait()
        samples = samples_ref[...].astype(jnp.float32)
        per_row = slices // samples.shape[0]
        for turn in range(per_row):
            shift = LANES - turn * LANES // per_row
            turned = pltpu.roll(samples, shift, 1) if turn else samples
            for index in range(turn, slices, per_row):
                tail = (index + 1) * rows - 1
                final_ref[tail : tail + 1, :] = turned[index // per_row : index // per_row + 1]

    mixed = fetch_blocks(
        x_hbm, signs_hbm, x_ref, signs_ref, spread_ref, arrived, note, meanwhile=place_offsets
    )
    steps = butterfly_steps(blocks)
    last = steps[-1][0]
    for apart, places in steps:
        values = [mixed[p] if apart == 1 else out_ref[p] for p in places]
        for place, value in zip(places, butterfly(values)):
            if apart == last:
                start = place // 2 * rows + place % 2 * columns
                final_ref[start : start + columns, :] = value
            else:
                out_ref[place] = value


def in_vmem(count):
    return [pl.BlockSpec(memory_space=pltpu.VMEM)] * count


def in_hbm(*arrays):
    return [pltpu.with_memory_space_constraint(array, pltpu.HBM) for array in arrays]


def fetch_scratch(matrix_slab, blocks):
    return [
        pltpu.VMEM(matrix_slab.shape, jnp.float32),
        pltpu.VMEM((blocks, LANES), jnp.int32),
        pltpu.VMEM((blocks, SUBLANES, LANES), jnp.float32),
    ]


def local_transform(matrix_slab, row_signs):
    columns, row_count = matrix_slab.shape
    blocks = row_count // LANES
    return pl.pallas_call(
        local_kernel,
        out_shape=jax.ShapeDtypeStruct((blocks, columns, LANES), jnp.float32),
        in_specs=[pl.BlockSpec(memory_space=pltpu.HBM)] * 2,
        out_specs=in_vmem(1)[0],
        scratch_shapes=[
            *fetch_scratch(matrix_slab, blocks),
            pltpu.SemaphoreType.DMA((2,)),
        ],
        compiler_params=pltpu.CompilerParams(vmem_limit_bytes=VMEM_LIMIT),
    )(*in_hbm(matrix_slab, row_signs.reshape(blocks, LANES)))


def sliced_transform(matrix_slab, row_signs, sample_rows):
    columns, row_count = matrix_slab.shape
    blocks = row_count // LANES
    samples = sample_rows.reshape(-1, LANES)
    return pl.pallas_call(
        sliced_kernel,
        out_shape=jax.ShapeDtypeStruct((blocks // 2 * (2 * columns + 1), LANES), jnp.float32),
        in_specs=[pl.BlockSpec(memory_space=pltpu.HBM)] * 3,
        out_specs=in_vmem(1)[0],
        scratch_shapes=[
            pltpu.VMEM((blocks, columns, LANES), jnp.float32),
            *fetch_scratch(matrix_slab, blocks),
            pltpu.VMEM(samples.shape, jnp.int32),
            pltpu.SemaphoreType.DMA((2,)),
            pltpu.SemaphoreType.DMA(()),
        ],
        compiler_params=pltpu.CompilerParams(vmem_limit_bytes=VMEM_LIMIT),
    )(*in_hbm(matrix_slab, row_signs.reshape(blocks, LANES), samples))


def mix_kernel(run_length, scale, gram_scale, x_ref, out_ref):
    devices = out_ref.shape[0] // MESSAGE_ROWS
    rows = x_ref.shape[0] // devices
    runs = LANES // run_length
    samples = jnp.concatenate(
        [x_ref[(s + 1) * rows - 1 : (s + 1) * rows, :] for s in range(devices)], axis=0
    ).astype(jnp.bfloat16)
    run_of = lax.broadcasted_iota(jnp.int32, (LANES, 2 * LANES), 0)
    row_of = lax.broadcasted_iota(jnp.int32, (LANES, 2 * LANES), 1)
    spread = jnp.where(row_of // run_length == run_of, 1.0, 0.0).astype(jnp.bfloat16)
    offsets = jnp.dot(samples, spread, preferred_element_type=jnp.float32)
    own = lax.broadcasted_iota(jnp.int32, offsets.shape, 1) % run_length
    mask = jnp.where(offsets == own.astype(jnp.float32), scale, 0.0)
    picked = []
    for part in range(4):
        block = part // 2
        starts = [s * rows + part * SUBLANES for s in range(devices)]
        mixed = butterfly([x_ref[start : start + SUBLANES, :] for start in starts])
        picked.append(
            jnp.concatenate(
                [
                    mixed[d] * mask[d : d + 1, block * LANES : (block + 1) * LANES]
                    for d in range(devices)
                ],
                axis=0,
            )
        )
    quarter = 2 * runs
    row = lax.broadcasted_iota(jnp.int32, (LANES, LANES), 0)
    lane = lax.broadcasted_iota(jnp.int32, (LANES, LANES), 1)
    pattern = jnp.where(row // run_length == lane % runs, 1.0, 0.0)
    lane = lax.broadcasted_iota(jnp.int32, (1, LANES), 1)
    group = lane // quarter
    place = []
    for part in range(4):
        block, half = part // 2, part % 2
        here = lane // runs % 2 == block
        sides = [group % 2, jnp.where(group < 2, group, 3 - group)]
        masks = [jnp.where(here & (side == half), 1.0, 0.0) for side in sides]
        place.append(jnp.concatenate([(pattern * mask).astype(jnp.bfloat16) for mask in masks], axis=1))
    gathered = split_dot(jnp.concatenate(picked, axis=1), jnp.concatenate(place, axis=0), 2)
    straight, crossed = gathered[:, :LANES], gathered[:, LANES:]
    turns = SUBLANES // 2 + 1
    totals = []
    for turn in range(turns):
        total = None
        for d in range(devices):
            one = straight[d * SUBLANES : (d + 1) * SUBLANES]
            two = crossed[d * SUBLANES : (d + 1) * SUBLANES]
            if turn:
                two = pltpu.roll(two, SUBLANES - turn, 0)
            total = one * two if total is None else total + one * two
        totals.append(total)
    from_quarter = row // quarter
    together = [jnp.where(from_quarter == q, 1.0, 0.0).astype(jnp.bfloat16) for q in range(4)]
    sums = split_dot(jnp.concatenate(totals, axis=0), jnp.concatenate(together, axis=1), 2)
    sums = sums * gram_scale
    sub = lax.broadcasted_iota(jnp.int32, (SUBLANES, LANES), 0)
    lane = lax.broadcasted_iota(jnp.int32, (SUBLANES, LANES), 1)
    first, second = [jnp.zeros((SUBLANES, LANES), jnp.float32)] * 2
    for turn in range(SUBLANES):
        known = min(turn, SUBLANES - turn)
        here = sums[known * SUBLANES : (known + 1) * SUBLANES]
        quarters = [here[:, q * LANES : (q + 1) * LANES] for q in range(4)]
        if known != turn:
            quarters = [pltpu.roll(quarters[q], known, 0) for q in (0, 1, 3, 2)]
        mine = lane % SUBLANES == (sub + turn) % SUBLANES
        left = lane // SUBLANES % 2 == 0
        first = jnp.where(mine, jnp.where(left, quarters[0], quarters[2]), first)
        second = jnp.where(mine, jnp.where(left, quarters[3], quarters[1]), second)
    in_place = lane // (2 * SUBLANES) == (SUBLANES - sub) % SUBLANES
    gram = jnp.concatenate(
        [jnp.sum(jnp.where(in_place, part, 0.0), axis=0, keepdims=True) for part in (first, second)],
        axis=0,
    )
    half = SUBLANES // 2
    lane = lax.broadcasted_iota(jnp.int32, (half, LANES), 1)
    for d in range(devices):
        one = straight[d * SUBLANES : (d + 1) * SUBLANES]
        start = d * MESSAGE_ROWS
        out_ref[start : start + half, :] = jnp.where(lane < LANES // 2, one[:half], one[half:])
        out_ref[start + half : start + MESSAGE_ROWS, :] = gram


def mix_and_pick(received, devices, run_length, scale, gram_scale):
    return pl.pallas_call(
        functools.partial(mix_kernel, run_length, scale, gram_scale),
        out_shape=jax.ShapeDtypeStruct((devices * MESSAGE_ROWS, LANES), jnp.float32),
        in_specs=in_vmem(1),
        out_specs=in_vmem(1)[0],
        compiler_params=pltpu.CompilerParams(vmem_limit_bytes=VMEM_LIMIT),
    )(received)


def finish_kernel(x_ref, sketch_ref, gram_ref):
    sources = x_ref.shape[0] // MESSAGE_ROWS
    quarter = LANES // 4
    half_rows = SUBLANES // 2
    sub = lax.broadcasted_iota(jnp.int32, (SUBLANES, LANES), 0)
    lane = lax.broadcasted_iota(jnp.int32, (SUBLANES, LANES), 1)
    even = lane // quarter % 2 == 0
    stays = (sub < half_rows) == (lane < LANES // 2)
    gram = None
    for start in range(0, sources, 4):
        rows = []
        for index in range(4):
            place = (start + index) * MESSAGE_ROWS
            tail = x_ref[place + half_rows : place + MESSAGE_ROWS, :]
            gram = tail if gram is None else gram + tail
            rows.append(x_ref[place : place + half_rows, :])
        one = jnp.concatenate([rows[0], rows[2]], axis=0)
        two = jnp.concatenate([rows[1], rows[3]], axis=0)
        halves = [
            jnp.where(even, one, pltpu.roll(two, quarter, 1)),
            jnp.where(even, pltpu.roll(one, LANES - quarter, 1), two),
        ]
        for half, value in enumerate(halves):
            crossed = pltpu.roll(pltpu.roll(value, half_rows, 0), LANES // 2, 1)
            sketch_ref[
                half * SUBLANES : (half + 1) * SUBLANES, start * quarter : (start + 4) * quarter
            ] = jnp.where(stays, value, crossed)
    columns = gram_ref.shape[0]
    for half in range(2):
        lines = jnp.broadcast_to(gram[half : half + 1], (SUBLANES, LANES))
        turned = pltpu.roll(lines, 0, 1, stride=columns, stride_axis=0)
        gram_ref[half * SUBLANES : (half + 1) * SUBLANES, :] = turned[:, :columns]


def finish(received, columns, sample_count):
    return pl.pallas_call(
        finish_kernel,
        out_shape=(
            jax.ShapeDtypeStruct((columns, sample_count), jnp.float32),
            jax.ShapeDtypeStruct((columns, columns), jnp.float32),
        ),
        in_specs=[pl.BlockSpec(memory_space=pltpu.VMEM)],
        out_specs=(pl.BlockSpec(memory_space=pltpu.VMEM),) * 2,
        compiler_params=pltpu.CompilerParams(vmem_limit_bytes=VMEM_LIMIT),
    )(received)


def exchange(values, axes):
    return lax.all_to_all(values, axes, split_axis=0, concat_axis=0, tiled=True)


def general_shards(matrix_slab, row_signs, sample_rows):
    columns, row_count = matrix_slab.shape
    sample_count = sample_rows.shape[0]
    devices = lax.axis_size("wide") * lax.axis_size("narrow")
    run_length = row_count // sample_count
    slice_rows = row_count // devices
    slice_runs = slice_rows // run_length
    values = jnp.swapaxes(local_transform(matrix_slab, row_signs), 0, 1)
    values = values.reshape(columns, devices, slice_rows)
    received = exchange(jnp.swapaxes(values, 0, 1), AXES)
    offsets = exchange(sample_rows.reshape(devices, slice_runs), AXES)
    mixed = jnp.einsum("ds,scr->dcr", sylvester(devices), received, precision=lax.Precision.HIGHEST)
    mixed = mixed.reshape(devices, columns, slice_runs, run_length)
    chosen = offsets[:, None, :, None] == lax.iota(jnp.int32, run_length)
    picked = jnp.sum(jnp.where(chosen, mixed, 0.0), axis=3)
    picked = picked * jnp.float32(1.0 / math.sqrt(row_count * devices))
    gram = jnp.einsum("dck,dek->ce", picked, picked, precision=lax.Precision.HIGHEST)
    gram = gram / jnp.float32(sample_count * devices)
    grams = jnp.broadcast_to(gram[None], (devices, columns, columns))
    back = exchange(jnp.concatenate([picked, grams], axis=2), AXES)
    sketch = jnp.swapaxes(back[:, :, :slice_runs], 0, 1).reshape(columns, devices * slice_runs)
    return sketch, jnp.sum(back[:, :, slice_runs:], axis=0)


def sliced_shards(matrix_slab, row_signs, sample_rows):
    columns, row_count = matrix_slab.shape
    sample_count = sample_rows.shape[0]
    devices = lax.axis_size(ORDER)
    run_length = row_count // sample_count
    sent = sliced_transform(matrix_slab, row_signs, sample_rows)
    received = exchange(sent.reshape(devices, -1), ORDER).reshape(sent.shape)
    scale = 1.0 / math.sqrt(row_count * devices)
    gram_scale = 1.0 / (sample_count * devices)
    picked = mix_and_pick(received, devices, run_length, scale, gram_scale)
    returned = exchange(picked.reshape(devices, -1), ORDER).reshape(picked.shape)
    return finish(returned, columns, sample_count)


def solution(mesh):
    wide, narrow = mesh.shape["wide"], mesh.shape["narrow"]
    axes, function = AXES, general_shards
    if wide * narrow == 32 and wide % 4 == 0:
        axes, function = SPLIT_AXES, sliced_shards
        mesh = jax.sharding.Mesh(mesh.devices.reshape(4, wide // 4, narrow), axes)
    in_specs = (P(None, axes), P(axes), P(axes))
    out_specs = (P(None, axes), P())
    return jax.shard_map(function, mesh=mesh, in_specs=in_specs, out_specs=out_specs, check_vma=False)
```
